32 devices in a mesh: ga: 16 (over z, x, core), band: 2 (over y).
Axes of the slice: x: 2, y: 2, z: 4, core: 2. Of those that a mesh axis runs over, the one named last changes fastest.
Arguments:
- orbitals: bfloat16 [2, 2, 128, 192], P(None, None, ('ga', 'band')), may hold values from -6 to 6
- projectors: bfloat16 [512, 2, 128, 192], P(None, None, ('ga', 'band')), may hold values from -0.09375 to 0.09375
- potential: float32 [192, 192, 192], P('ga'), may hold values from -2 to 0.5
- couplings: float32 [512, 512], replicated, may hold values from -3 to 3
- atom_index: int32 [512], replicated, may hold values from 0 to 63
- column_site: int32 [128], replicated, may hold values from 0 to 36863, as said below
- column_count: int32 [16], replicated, may hold values from 2 to 8, as said below
Outputs:
- applied: float32 [2, 2, 128, 192], P(None, None, ('ga', 'band'))
The draws below stay inside these ranges and needn't reach their ends.
Inputs may be any that keep to these rules, and one draw needn't show every extreme that they name: `column_site`: distinct positions kx * 192 + ky in the 192 x 192 plane of frequencies. `column_count`: the slot b * 4 + j of band index b in a ga block is used where it lies below that block's count; some ga block has all 8 slots used.
All inputs are finite; a program needn't handle non-finite values.
Results may differ from the reference program's by a relative error of at most 0.0027.
Values may be sent and summed in bfloat16 or wider, within the bound.
No kernel may reach another device: no remote copies, remote signals or barrier semaphores. Data moves between devices by JAX's collectives and lax.ppermute only.
A program may use at most 128 MiB of HBM per device.

```python
import jax
import jax.numpy as jnp
from jax import lax

GRID = 192
NPROJ = 512
NATOM = 64
NB = 2
CMAX = 8
NCOLS = 128
NXY = 36864
N_GA = 16


def draw_column_site(key, part):
    first_key, second_key = jax.random.split(key, 2)
    inner = 1 + jax.random.permutation(first_key, NXY - 2)[:NCOLS - 2]
    ends = jnp.array([0, NXY - 1], dtype=jnp.int32)
    sites = jnp.concatenate([ends, inner.astype(jnp.int32)])
    shuffle = jax.random.permutation(second_key, NCOLS)
    return sites[shuffle].astype(jnp.int32)


def draw_column_count(key, part):
    first_key, second_key = jax.random.split(key, 2)
    lowest = max(1, CMAX // 4)
    counts = jax.random.randint(first_key, (N_GA,), lowest, CMAX + 1)
    shuffle = jax.random.permutation(second_key, N_GA)
    counts = counts.at[shuffle[0]].set(CMAX).at[shuffle[1]].set(lowest)
    return counts.astype(jnp.int32)


def set_ends(values, own_key, smallest, high):
    index_at = [jax.random.randint(jax.random.fold_in(own_key, axis), (), 0, length) for axis, length in enumerate(values.shape)]
    main_axis = values.shape.index(max(values.shape))
    next_to = index_at[:main_axis] + [(index_at[main_axis] + 1) % values.shape[main_axis]] + index_at[main_axis + 1:]
    return values.at[tuple(index_at)].set(smallest).at[tuple(next_to)].set(high)


def steps_of(own_key, shape, pieces, low, largest):
    gain, own = 1.0, jax.random.fold_in(own_key, 6)
    for position, blocks in pieces:
        heights = jnp.exp(jax.random.uniform(jax.random.fold_in(own, position), (blocks,), jnp.float32, low / len(pieces), largest / len(pieces)))
        gain = gain * jnp.repeat(heights, shape[position] // blocks).reshape([-1 if axis == position else 1 for axis in range(len(shape))])
    return gain


def scatter_about(own_key, dims, scale, bound, cuts=(), kind=jnp.bfloat16):
    entries = scale * jax.random.normal(own_key, dims, jnp.float32)
    if cuts:
        entries = entries * steps_of(own_key, dims, cuts, -0.22, 0.18)
    return jnp.clip(entries, -bound, bound).astype(kind)


def setup_inputs(seed: int = 0) -> dict:
    key_of = jax.random.split(jax.random.key(seed), 8)
    orbitals = scatter_about(key_of[0], (NB, 2, NCOLS, GRID), 1.0, 6.0, ((2, 32),))
    projectors = scatter_about(key_of[1], (NPROJ, 2, NCOLS, GRID), ((NCOLS * GRID * NPROJ) ** 0.5) ** -0.5, 0.09375, ((2, 32),))
    potential = jnp.clip(-2.0 + 2.5 * jax.random.uniform(key_of[2], (GRID, GRID, GRID), jnp.float32) ** steps_of(key_of[2], (GRID, GRID, GRID), ((0, 16),), -0.2, 0.2), -2.0, 0.5)
    couplings = scatter_about(key_of[3], (NPROJ, NPROJ), 0.5, 3.0, (), jnp.float32)
    atom_index = set_ends(jax.random.randint(key_of[4], (NPROJ,), 0, NATOM), jax.random.fold_in(key_of[4], 1), 0, NATOM - 1).astype(jnp.int32)
    column_site = draw_column_site(jax.random.fold_in(key_of[7], 71), 0)
    column_count = draw_column_count(jax.random.fold_in(key_of[7], 71), 0)
    return {"orbitals": orbitals, "projectors": projectors, "potential": potential, "couplings": couplings, "atom_index": atom_index, "column_site": column_site, "column_count": column_count}


def reference(orbitals, projectors, potential, couplings, atom_index, column_site, column_count):
    slot_ids = jnp.arange(NCOLS, dtype=jnp.int32)
    active = ((slot_ids % CMAX) < column_count[slot_ids // CMAX]).astype(jnp.float32)
    coefficients = orbitals * active[None, None, :, None].astype(jnp.bfloat16)
    flat_projectors = projectors.reshape(NPROJ * 2, NCOLS * GRID)
    intersections = lax.dot_general(flat_projectors, coefficients.reshape(NB * 2, NCOLS * GRID),
                               (((1,), (1,)), ((), ())), preferred_element_type=jnp.float32)
    intersections = intersections.reshape(NPROJ, 2, NB, 2)
    partial_real = intersections[:, 0, :, 0] + intersections[:, 1, :, 1]
    partial_imag = intersections[:, 0, :, 1] - intersections[:, 1, :, 0]
    summed = jnp.stack([partial_real, partial_imag])
    coupled = jnp.where(atom_index[:, None] == atom_index[None, :], couplings, jnp.zeros_like(couplings))
    weighted = jnp.einsum('pq,cqn->cpn', coupled, summed, precision=lax.Precision.HIGHEST).astype(jnp.bfloat16)
    weight_real = weighted[0].T
    weight_imag = weighted[1].T
    row_real = jnp.stack([weight_real, -weight_imag], axis=-1)
    row_imag = jnp.stack([weight_imag, weight_real], axis=-1)
    mixing = jnp.stack([row_real, row_imag], axis=1).reshape(NB * 2, NPROJ * 2)
    projected = jnp.dot(mixing, flat_projectors, preferred_element_type=jnp.float32).reshape(NB, 2, NCOLS, GRID)
    potential_xyz = jnp.transpose(potential, (1, 2, 0))

    def one_orbital(single):
        values = lax.complex(single[0].astype(jnp.float32), single[1].astype(jnp.float32))
        spectrum = jnp.zeros((GRID * GRID, GRID), values.dtype).at[column_site].set(values)
        spectrum = spectrum.reshape(GRID, GRID, GRID)
        real_field = jnp.fft.ifftn(spectrum) * (GRID ** 3)
        weighted_field = real_field * potential_xyz
        back = jnp.fft.fftn(weighted_field) / (GRID ** 3)
        picked = back.reshape(GRID * GRID, GRID)[column_site]
        return jnp.stack([jnp.real(picked), jnp.imag(picked)])

    local_term = lax.map(one_orbital, coefficients)
    return (local_term + projected) * active[None, None, :, None]
```

```python
import functools

import jax
import jax.numpy as jnp
import ml_dtypes
import numpy as np
from jax import lax
from jax.experimental import pallas as pl
from jax.experimental.pallas import tpu as pltpu
from jax.sharding import PartitionSpec as P

LANES = 128
BF16 = jnp.bfloat16
F32 = jnp.float32


def pieces_of(table):
    table = np.asarray(table, np.float32)
    head = table.astype(ml_dtypes.bfloat16)
    return np.stack([head, (table - head.astype(np.float32)).astype(ml_dtypes.bfloat16)])


def grid_table(length):
    points = np.arange(length)
    phases = (points[:, None] * points[None, :] % length) * (2.0 * np.pi / length)
    return pieces_of(np.stack([np.cos(phases), np.sin(phases)]))


def line_table(length, blocks, planes, width):
    kz = np.arange(length)
    out = np.zeros((2, length, blocks, width), np.float64)
    for block in range(blocks):
        z = block * planes + np.arange(planes)
        phases = (kz[:, None] * z[None, :] % length) * (2.0 * np.pi / length)
        out[0, :, block, :planes] = np.cos(phases)
        out[0, :, block, width // 2 : width // 2 + planes] = np.sin(phases)
        out[1, :, block, :planes] = -np.sin(phases)
        out[1, :, block, width // 2 : width // 2 + planes] = np.cos(phases)
    return pieces_of(out.reshape(2, length, blocks * width))


def split(values):
    head = values.astype(BF16)
    return head, (values - head.astype(F32)).astype(BF16)


def dot(left, right):
    return lax.dot_general(left, right, (((1,), (0,)), ((), ())), preferred_element_type=F32)


def dot_nt(left, right):
    return lax.dot_general(left, right, (((1,), (1,)), ((), ())), preferred_element_type=F32)


def lane_ids(rows):
    return lax.broadcasted_iota(jnp.int32, (rows, LANES), 1)


def used_slots(count_ref, slots):
    used = count_ref[lax.axis_index("ga")] - lax.axis_index("band") * slots
    return lax.broadcasted_iota(jnp.int32, (slots, 1), 0) < used


def project_kernel(sizes, count_ref, orbitals_ref, projectors_ref, table_ref, out_ref, coef, spread):
    blocks, groups, orbitals, slots, length, projectors, width = sizes
    kinds = orbitals * 2
    devices = blocks * groups
    share = projectors // devices
    used = used_slots(count_ref, slots)
    for n in range(orbitals):
        for part in range(2):
            values = jnp.where(used, orbitals_ref[n, part].astype(F32), 0.0)
            at = (n * 2 + part) * slots
            coef[0, at : at + slots, :] = values
            at = (n * 2 + 1 - part) * slots
            coef[1, at : at + slots, :] = values if part == 1 else -values
            at = n * slots
            coef[2 + part, at : at + slots, :] = values
    row_slot = lax.broadcasted_iota(jnp.int32, (kinds * slots, length), 0) % slots
    sums = jnp.zeros((kinds * slots, projectors), F32)
    for part in range(2):
        rows = coef[part]
        for slot in range(slots):
            at = (part * slots + slot) * length
            left = jnp.where(row_slot == slot, rows, 0.0).astype(BF16)
            sums += dot(left, projectors_ref[at : at + length, :])
    for row in range(kinds):
        spread[row : row + 1, :] = jnp.sum(sums[row * slots : (row + 1) * slots, :], axis=0, keepdims=True)
    columns = jnp.zeros((orbitals * slots, blocks * width), F32)
    for part in range(2):
        left = coef[2 + part, : orbitals * slots, :].astype(BF16)
        columns += dot(left, table_ref[0, part]) + dot(left, table_ref[1, part])
    lanes = lane_ids(slots)
    groups_of_rows = kinds // slots
    for block in range(blocks):
        at = block * width
        base = at // LANES * LANES
        chunk = pltpu.roll(columns[:, base : base + LANES], (base - at) % LANES, 1)
        for group in range(groups):
            device = block * groups + group
            piece = jnp.where(lanes < width, chunk[group * slots : (group + 1) * slots, :], 0.0)
            first = device * share
            base = first // LANES * LANES
            for rows in range(groups_of_rows):
                low = width + rows * share
                own = spread[rows * slots : (rows + 1) * slots, base : base + LANES]
                own = pltpu.roll(own, (base + low - first) % LANES, 1)
                piece = jnp.where((lanes >= low) & (lanes < low + share), own, piece)
            out_ref[device] = piece


def table_kernel(sizes, site_ref, atom_ref, couplings_ref, grid_ref, x_ref, plus_ref, minus_ref, coupled_ref):
    columns, length, projectors, wide = sizes
    eye = lax.broadcasted_iota(jnp.int32, (LANES, LANES), 0) == lane_ids(LANES)
    plus_ref[...] = jnp.zeros_like(plus_ref)
    minus_ref[...] = jnp.zeros_like(minus_ref)
    row_ids = lax.broadcasted_iota(jnp.int32, (length, LANES), 0).astype(F32)
    column_ids = lax.broadcasted_iota(jnp.int32, (LANES, length), 1).astype(F32)
    for at in range(0, columns, LANES):
        site = site_ref[:, at : at + LANES].astype(F32)
        site_x = jnp.floor((site + 0.5) * (1.0 / length))
        site_y = site - site_x * length
        hot_x = (row_ids == site_x).astype(F32).astype(BF16)
        hot_y = (row_ids == site_y).astype(F32).astype(BF16)
        along = jnp.sum(jnp.where(eye, site_y, 0.0), axis=1, keepdims=True)
        hot_y_rows = (column_ids == along).astype(F32).astype(BF16)
        for part in range(2):
            value = dot(grid_ref[0, part], hot_x) + dot(grid_ref[1, part], hot_x)
            x_ref[:, part * columns + at : part * columns + at + LANES] = value
        for piece in range(2):
            cosine = dot(hot_y_rows, grid_ref[piece, 0])
            sine = dot(hot_y_rows, grid_ref[piece, 1])
            plus_ref[piece, at : at + LANES, :length] = cosine.astype(BF16)
            plus_ref[piece, at : at + LANES, wide : wide + length] = sine.astype(BF16)
            plus_ref[piece, columns + at : columns + at + LANES, :length] = (-sine).astype(BF16)
            plus_ref[piece, columns + at : columns + at + LANES, wide : wide + length] = cosine.astype(BF16)
            cosine = dot(grid_ref[piece, 0], hot_y)
            sine = dot(grid_ref[piece, 1], hot_y)
            minus_ref[piece, :length, at : at + LANES] = cosine.astype(BF16)
            minus_ref[piece, :length, columns + at : columns + at + LANES] = (-sine).astype(BF16)
            minus_ref[piece, wide : wide + length, at : at + LANES] = sine.astype(BF16)
            minus_ref[piece, wide : wide + length, columns + at : columns + at + LANES] = cosine.astype(BF16)
    atoms = atom_ref[...].astype(F32)
    for at in range(0, projectors, LANES):
        along = jnp.sum(jnp.where(eye, atoms[:, at : at + LANES], 0.0), axis=1, keepdims=True)
        head, rest = split(jnp.where(along == atoms, couplings_ref[at : at + LANES, :], 0.0))
        coupled_ref[0, at : at + LANES, :] = head
        coupled_ref[1, at : at + LANES, :] = rest


def plane_kernel(sizes, columns_ref, x_ref, plus_ref, minus_ref, potential_ref, out_ref, gathered, lines, back):
    devices, slots, planes, length, wide, width, carried = sizes
    count = devices * slots
    total = jnp.zeros((slots, LANES), F32)
    for device in range(devices):
        piece = columns_ref[device]
        gathered[device * slots : (device + 1) * slots, :] = piece
        total += piece
    for at in range(0, count, LANES):
        lines[:, at : at + LANES] = gathered[at : at + LANES, :].T
    back[...] = jnp.zeros_like(back)

    def one_plane(plane, carry):
        real = lines[pl.ds(plane, 1), :]
        imag = lines[pl.ds(plane + width // 2, 1), :]
        cosine = x_ref[:, :count]
        sine = x_ref[:, count:]
        left = jnp.concatenate([cosine * real - sine * imag, cosine * imag + sine * real], axis=1)
        head, rest = split(left)
        field = dot(head, plus_ref[0]) + (dot(head, plus_ref[1]) + dot(rest, plus_ref[0]))
        weights = jnp.concatenate([potential_ref[plane], jnp.zeros((length, wide - length), F32)], axis=1)
        head, rest = split(field * jnp.concatenate([weights, weights], axis=1))
        half = dot(head, minus_ref[0]) + (dot(head, minus_ref[1]) + dot(rest, minus_ref[0]))
        real = half[:, :count]
        imag = half[:, count:]
        back[pl.ds(plane, 1), :] = jnp.sum(cosine * real + sine * imag, axis=0, keepdims=True)
        back[pl.ds(plane + width // 2, 1), :] = jnp.sum(cosine * imag - sine * real, axis=0, keepdims=True)
        return carry

    lax.fori_loop(0, planes, one_plane, 0)
    for at in range(0, count, LANES):
        gathered[at : at + LANES, :] = back[:, at : at + LANES].T
    lanes = lane_ids(slots)
    for device in range(devices):
        piece = gathered[device * slots : (device + 1) * slots, :]
        out_ref[device] = jnp.where((lanes >= width) & (lanes < carried), total, piece)


def finish_kernel(sizes, count_ref, columns_ref, coupled_ref, projectors_ref, table_ref, out_ref, summed, lined, mixed):
    blocks, groups, orbitals, slots, length, projectors, width, normalizer = sizes
    kinds = orbitals * 2
    devices = blocks * groups
    share = projectors // devices
    groups_of_rows = kinds // slots
    lanes = lane_ids(slots)
    for chunk in range(projectors // LANES):
        in_chunk = range(chunk * LANES // share, (chunk + 1) * LANES // share)
        for rows in range(groups_of_rows):
            low = width + rows * share
            total = jnp.zeros((slots, LANES), F32)
            for device in in_chunk:
                own = columns_ref[device]
                own = pltpu.roll(jnp.where((lanes >= low) & (lanes < low + share), own, 0.0), (device * share - low) % LANES, 1)
                total += own
            summed[rows * slots : (rows + 1) * slots, chunk * LANES : (chunk + 1) * LANES] = total
    for n in range(orbitals):
        at = kinds + n * 2
        summed[at : at + 1, :] = -summed[n * 2 + 1 : n * 2 + 2, :]
        summed[at + 1 : at + 2, :] = summed[n * 2 : n * 2 + 1, :]
    head, rest = split(summed[...])
    weighted = dot_nt(head, coupled_ref[0]) + (dot_nt(head, coupled_ref[1]) + dot_nt(rest, coupled_ref[0]))
    weighted = weighted.astype(BF16)
    for slot in range(slots):
        rows = projectors_ref[slot * length : (slot + 1) * length, :]
        value = dot_nt(weighted, rows)[:kinds]
        rows = projectors_ref[(slots + slot) * length : (slots + slot + 1) * length, :]
        mixed[slot * kinds : (slot + 1) * kinds, :] = value + dot_nt(weighted, rows)[kinds:]
    for chunk in range(blocks * width // LANES):
        for group in range(groups):
            total = jnp.zeros((slots, LANES), F32)
            for inner in range(LANES // width):
                block = chunk * (LANES // width) + inner
                own = jnp.where(lanes < width, columns_ref[block * groups + group], 0.0)
                total += pltpu.roll(own, inner * width, 1)
            lined[group * slots : (group + 1) * slots, chunk * LANES : (chunk + 1) * LANES] = total
    head, rest = split(lined[...])
    used = used_slots(count_ref, slots)
    for part in range(2):
        local = dot_nt(head, table_ref[0, part]) + (dot_nt(head, table_ref[1, part]) + dot_nt(rest, table_ref[0, part]))
        local = local * normalizer
        for n in range(orbitals):
            row = n * 2 + part
            for slot in range(slots):
                at = n * slots + slot
                value = local[at : at + 1, :] + mixed[slot * kinds + row : slot * kinds + row + 1, :]
                out_ref[n, part, slot : slot + 1, :] = value
            out_ref[n, part] = jnp.where(used, out_ref[n, part], 0.0)


def on_device(orbitals, projectors, potential, couplings, atom_index, column_site, column_count):
    blocks = lax.axis_size("ga")
    groups = lax.axis_size("band")
    devices = blocks * groups
    orbital_count, _, slots, length = orbitals.shape
    planes = potential.shape[0]
    projector_count = projectors.shape[0]
    columns = column_site.shape[0]
    kinds = orbital_count * 2
    assert orbital_count == groups and kinds % slots == 0 and columns % LANES == 0
    share = projector_count // devices
    width = 2
    while width < 2 * planes:
        width *= 2
    carried = width + kinds // slots * share
    assert carried <= LANES and width <= LANES and share * devices == projector_count
    wide = -(-length // LANES) * LANES
    flat = jnp.transpose(projectors, (1, 2, 3, 0)).reshape(2 * slots * length, projector_count)
    z_table = line_table(length, blocks, planes, width)
    smem = pl.BlockSpec(memory_space=pltpu.SMEM)
    vmem = pl.BlockSpec(memory_space=pltpu.VMEM)
    params = pltpu.CompilerParams(vmem_limit_bytes=40 * 1024 * 1024)
    payload = jax.ShapeDtypeStruct((devices, slots, LANES), F32)

    sent = pl.pallas_call(
        functools.partial(
            project_kernel, (blocks, groups, orbital_count, slots, length, projector_count, width)
        ),
        out_shape=payload,
        in_specs=[smem, vmem, vmem, vmem],
        out_specs=vmem,
        scratch_shapes=[
            pltpu.VMEM((4, kinds * slots, length), F32),
            pltpu.VMEM((kinds, projector_count), F32),
        ],
        compiler_params=params,
        name="project",
    )(column_count, orbitals, flat, z_table)
    arrived = lax.all_to_all(sent, ("ga", "band"), split_axis=0, concat_axis=0, tiled=True)

    x_rows, plus, minus, coupled = pl.pallas_call(
        functools.partial(table_kernel, (columns, length, projector_count, wide)),
        out_shape=(
            jax.ShapeDtypeStruct((length, 2 * columns), F32),
            jax.ShapeDtypeStruct((2, 2 * columns, 2 * wide), BF16),
            jax.ShapeDtypeStruct((2, 2 * wide, 2 * columns), BF16),
            jax.ShapeDtypeStruct((2, projector_count, projector_count), BF16),
        ),
        in_specs=[vmem] * 4,
        out_specs=(vmem,) * 4,
        compiler_params=params,
        name="tables",
    )(column_site.reshape(1, columns), atom_index.reshape(1, projector_count), couplings, grid_table(length))

    sent = pl.pallas_call(
        functools.partial(plane_kernel, (devices, slots, planes, length, wide, width, carried)),
        out_shape=payload,
        in_specs=[vmem] * 5,
        out_specs=vmem,
        scratch_shapes=[
            pltpu.VMEM((columns, LANES), F32),
            pltpu.VMEM((LANES, columns), F32),
            pltpu.VMEM((LANES, columns), F32),
        ],
        compiler_params=params,
        name="planes",
    )(arrived, x_rows, plus, minus, potential)
    arrived = lax.all_to_all(sent, ("ga", "band"), split_axis=0, concat_axis=0, tiled=True)

    normalizer = 1.0 / float(length**3)
    return pl.pallas_call(
        functools.partial(
            finish_kernel,
            (blocks, groups, orbital_count, slots, length, projector_count, width, normalizer),
        ),
        out_shape=jax.ShapeDtypeStruct(orbitals.shape, F32),
        in_specs=[smem, vmem, vmem, vmem, vmem],
        out_specs=vmem,
        scratch_shapes=[
            pltpu.VMEM((2 * kinds, projector_count), F32),
            pltpu.VMEM((groups * slots, blocks * width), F32),
            pltpu.VMEM((slots * kinds, length), F32),
        ],
        compiler_params=params,
        name="finish",
    )(column_count, arrived, coupled, flat, z_table)


def solution(mesh):
    return jax.shard_map(
        on_device,
        mesh=mesh,
        in_specs=(
            P(None, None, ("ga", "band"), None),
            P(None, None, ("ga", "band"), None),
            P("ga", None, None),
            P(),
            P(),
            P(),
            P(),
        ),
        out_specs=P(None, None, ("ga", "band"), None),
        check_vma=False,
    )
```

```python
import functools

import jax
import jax.numpy as jnp
import ml_dtypes
import numpy as np
from jax import lax
from jax.experimental import pallas as pl
from jax.experimental.pallas import tpu as pltpu
from jax.sharding import PartitionSpec as P

LANES = 128
PIECES = ((0, 1), (2,))
BF16 = jnp.bfloat16
F32 = jnp.float32


def pieces_of(table):
    table = np.asarray(table, np.float32)
    head = table.astype(ml_dtypes.bfloat16)
    return np.stack([head, (table - head.astype(np.float32)).astype(ml_dtypes.bfloat16)])


def grid_table(length):
    points = np.arange(length)
    phases = (points[:, None] * points[None, :] % length) * (2.0 * np.pi / length)
    return pieces_of(np.stack([np.cos(phases), np.sin(phases)]))


def line_table(length, blocks, planes, width):
    kz = np.arange(length)
    out = np.zeros((2, length, blocks, width), np.float64)
    for block in range(blocks):
        z = block * planes + np.arange(planes)
        phases = (kz[:, None] * z[None, :] % length) * (2.0 * np.pi / length)
        out[0, :, block, :planes] = np.cos(phases)
        out[0, :, block, width // 2 : width // 2 + planes] = np.sin(phases)
        out[1, :, block, :planes] = -np.sin(phases)
        out[1, :, block, width // 2 : width // 2 + planes] = np.cos(phases)
    return pieces_of(out.reshape(2, length, blocks * width))


def split(values):
    head = values.astype(BF16)
    return head, (values - head.astype(F32)).astype(BF16)


def tripled(values):
    head, rest = split(values)
    return jnp.concatenate([head, rest, head], axis=1)


def dot(left, right):
    return lax.dot_general(left, right, (((1,), (0,)), ((), ())), preferred_element_type=F32)


def dot_nt(left, right):
    return lax.dot_general(left, right, (((1,), (1,)), ((), ())), preferred_element_type=F32)


def lane_ids(rows):
    return lax.broadcasted_iota(jnp.int32, (rows, LANES), 1)


def used_slots(count_ref, slots):
    used = count_ref[lax.axis_index("ga")] - lax.axis_index("band") * slots
    return lax.broadcasted_iota(jnp.int32, (slots, 1), 0) < used


def project_kernel(sizes, count_hbm, orbitals_hbm, projectors_hbm, table_hbm, out_ref, *scratch):
    blocks, groups, orbitals, slots, length, projectors, width = sizes
    count_ref, orbitals_ref, projectors_ref, table_ref, coef, spread, small_sems, sems = scratch
    kinds = orbitals * 2
    devices = blocks * groups
    share = projectors // devices
    small = [
        pltpu.make_async_copy(count_hbm, count_ref, small_sems.at[0]),
        pltpu.make_async_copy(orbitals_hbm, orbitals_ref, small_sems.at[1]),
        pltpu.make_async_copy(table_hbm, table_ref, small_sems.at[2]),
    ]
    copies = []
    for piece in range(2 * slots):
        rows = pl.ds(piece * length, length)
        copies.append(pltpu.make_async_copy(projectors_hbm.at[rows], projectors_ref.at[rows], sems.at[piece]))
    for copy in small + copies:
        copy.start()
    small[0].wait()
    small[1].wait()
    used = used_slots(count_ref, slots)
    for n in range(orbitals):
        for part in range(2):
            values = jnp.where(used, orbitals_ref[n, part].astype(F32), 0.0)
            at = (n * 2 + part) * slots
            coef[0, at : at + slots, :] = values
            at = (n * 2 + 1 - part) * slots
            coef[1, at : at + slots, :] = values if part == 1 else -values
            at = n * slots
            coef[2 + part, at : at + slots, :] = values
    small[2].wait()
    columns = jnp.zeros((orbitals * slots, blocks * width), F32)
    for part in range(2):
        left = coef[2 + part, : orbitals * slots, :].astype(BF16)
        columns += dot(left, table_ref[0, part]) + dot(left, table_ref[1, part])
    row_slot = lax.broadcasted_iota(jnp.int32, (kinds * slots, length), 0) % slots
    sums = jnp.zeros((kinds * slots, projectors), F32)
    for part in range(2):
        rows = coef[part]
        for slot in range(slots):
            piece = part * slots + slot
            left = jnp.where(row_slot == slot, rows, 0.0).astype(BF16)
            copies[piece].wait()
            sums += dot(left, projectors_ref[piece * length : (piece + 1) * length, :])
    for row in range(kinds):
        spread[row : row + 1, :] = jnp.sum(sums[row * slots : (row + 1) * slots, :], axis=0, keepdims=True)
    lanes = lane_ids(slots)
    groups_of_rows = kinds // slots
    for block in range(blocks):
        at = block * width
        base = at // LANES * LANES
        chunk = pltpu.roll(columns[:, base : base + LANES], (base - at) % LANES, 1)
        for group in range(groups):
            device = block * groups + group
            piece = jnp.where(lanes < width, chunk[group * slots : (group + 1) * slots, :], 0.0)
            first = device * share
            base = first // LANES * LANES
            for rows in range(groups_of_rows):
                low = width + rows * share
                own = spread[rows * slots : (rows + 1) * slots, base : base + LANES]
                own = pltpu.roll(own, (base + low - first) % LANES, 1)
                piece = jnp.where((lanes >= low) & (lanes < low + share), own, piece)
            out_ref[device] = piece


def table_kernel(sizes, site_ref, atom_ref, couplings_ref, grid_ref, x_ref, plus_ref, minus_ref, coupled_ref):
    columns, length, projectors, wide = sizes
    eye = lax.broadcasted_iota(jnp.int32, (LANES, LANES), 0) == lane_ids(LANES)
    plus_ref[...] = jnp.zeros_like(plus_ref)
    minus_ref[...] = jnp.zeros_like(minus_ref)
    row_ids = lax.broadcasted_iota(jnp.int32, (length, LANES), 0).astype(F32)
    column_ids = lax.broadcasted_iota(jnp.int32, (LANES, length), 1).astype(F32)
    for at in range(0, columns, LANES):
        site = site_ref[:, at : at + LANES].astype(F32)
        site_x = jnp.floor((site + 0.5) * (1.0 / length))
        site_y = site - site_x * length
        hot_x = (row_ids == site_x).astype(F32).astype(BF16)
        hot_y = (row_ids == site_y).astype(F32).astype(BF16)
        along = jnp.sum(jnp.where(eye, site_y, 0.0), axis=1, keepdims=True)
        hot_y_rows = (column_ids == along).astype(F32).astype(BF16)
        for part in range(2):
            value = dot(grid_ref[0, part], hot_x) + dot(grid_ref[1, part], hot_x)
            x_ref[:, part * columns + at : part * columns + at + LANES] = value
        for piece in range(2):
            cosine = dot(hot_y_rows, grid_ref[piece, 0])
            sine = dot(hot_y_rows, grid_ref[piece, 1])
            for copy in PIECES[piece]:
                rows = pl.ds(copy * 2 * columns + at, LANES)
                plus_ref[rows, :length] = cosine.astype(BF16)
                plus_ref[rows, wide : wide + length] = sine.astype(BF16)
                rows = pl.ds((copy * 2 + 1) * columns + at, LANES)
                plus_ref[rows, :length] = (-sine).astype(BF16)
                plus_ref[rows, wide : wide + length] = cosine.astype(BF16)
            cosine = dot(grid_ref[piece, 0], hot_y)
            sine = dot(grid_ref[piece, 1], hot_y)
            for copy in PIECES[piece]:
                rows = pl.ds(copy * 2 * wide, length)
                minus_ref[rows, at : at + LANES] = cosine.astype(BF16)
                minus_ref[rows, columns + at : columns + at + LANES] = (-sine).astype(BF16)
                rows = pl.ds((copy * 2 + 1) * wide, length)
                minus_ref[rows, at : at + LANES] = sine.astype(BF16)
                minus_ref[rows, columns + at : columns + at + LANES] = cosine.astype(BF16)
    atoms = atom_ref[...].astype(F32)
    for at in range(0, projectors, LANES):
        along = jnp.sum(jnp.where(eye, atoms[:, at : at + LANES], 0.0), axis=1, keepdims=True)
        head, rest = split(jnp.where(along == atoms, couplings_ref[at : at + LANES, :], 0.0))
        coupled_ref[0, at : at + LANES, :] = head
        coupled_ref[1, at : at + LANES, :] = rest


def plane_kernel(sizes, columns_ref, x_hbm, plus_hbm, minus_hbm, potential_hbm, out_ref, *scratch):
    devices, slots, planes, length, wide, width, carried, batch = sizes
    gathered, lines, back, x_ref, plus_ref, minus_ref, potential_ref, table_sems, sems = scratch
    count = devices * slots
    tables = [
        pltpu.make_async_copy(source, target, table_sems.at[i])
        for i, (source, target) in enumerate(((x_hbm, x_ref), (plus_hbm, plus_ref), (minus_hbm, minus_ref)))
    ]
    copies = []
    for i in range(planes // batch):
        some = pl.ds(i * batch, batch)
        copies.append(pltpu.make_async_copy(potential_hbm.at[some], potential_ref.at[some], sems.at[i]))
    for copy in tables[:2] + copies[:1] + tables[2:] + copies[1:]:
        copy.start()
    total = jnp.zeros((slots, LANES), F32)
    for device in range(devices):
        piece = columns_ref[device]
        gathered[device * slots : (device + 1) * slots, :] = piece
        total += piece
    for at in range(0, count, LANES):
        lines[:, at : at + LANES] = gathered[at : at + LANES, :].T
    back[...] = jnp.zeros_like(back)
    tables[0].wait()
    cosine = x_ref[:, :count]
    sine = x_ref[:, count:]
    padding = jnp.zeros((length, wide - length), F32)
    for i in range(planes // batch):
        left = []
        for plane in range(i * batch, (i + 1) * batch):
            real = lines[plane : plane + 1, :]
            imag = lines[plane + width // 2 : plane + width // 2 + 1, :]
            left.append(jnp.concatenate([cosine * real - sine * imag, cosine * imag + sine * real], axis=1))
        left = tripled(jnp.concatenate(left, axis=0))
        if i == 0:
            tables[1].wait()
        field = dot(left, plus_ref[...])
        copies[i].wait()
        weights = []
        for plane in range(i * batch, (i + 1) * batch):
            own = jnp.concatenate([potential_ref[plane], padding], axis=1)
            weights.append(jnp.concatenate([own, own], axis=1))
        left = tripled(field * jnp.concatenate(weights, axis=0))
        if i == 0:
            tables[2].wait()
        half = dot(left, minus_ref[...])
        for j in range(batch):
            plane = i * batch + j
            real = half[j * length : (j + 1) * length, :count]
            imag = half[j * length : (j + 1) * length, count:]
            back[plane : plane + 1, :] = jnp.sum(cosine * real + sine * imag, axis=0, keepdims=True)
            at = plane + width // 2
            back[at : at + 1, :] = jnp.sum(cosine * imag - sine * real, axis=0, keepdims=True)
    for at in range(0, count, LANES):
        gathered[at : at + LANES, :] = back[:, at : at + LANES].T
    lanes = lane_ids(slots)
    for device in range(devices):
        piece = gathered[device * slots : (device + 1) * slots, :]
        out_ref[device] = jnp.where((lanes >= width) & (lanes < carried), total, piece)


def finish_kernel(sizes, count_ref, columns_ref, coupled_ref, projectors_ref, table_ref, out_ref, summed, lined, mixed):
    blocks, groups, orbitals, slots, length, projectors, width, normalizer = sizes
    kinds = orbitals * 2
    devices = blocks * groups
    share = projectors // devices
    groups_of_rows = kinds // slots
    lanes = lane_ids(slots)
    for chunk in range(projectors // LANES):
        in_chunk = range(chunk * LANES // share, (chunk + 1) * LANES // share)
        for rows in range(groups_of_rows):
            low = width + rows * share
            total = jnp.zeros((slots, LANES), F32)
            for device in in_chunk:
                own = columns_ref[device]
                own = pltpu.roll(jnp.where((lanes >= low) & (lanes < low + share), own, 0.0), (device * share - low) % LANES, 1)
                total += own
            summed[rows * slots : (rows + 1) * slots, chunk * LANES : (chunk + 1) * LANES] = total
    for n in range(orbitals):
        at = kinds + n * 2
        summed[at : at + 1, :] = -summed[n * 2 + 1 : n * 2 + 2, :]
        summed[at + 1 : at + 2, :] = summed[n * 2 : n * 2 + 1, :]
    head, rest = split(summed[...])
    weighted = dot_nt(head, coupled_ref[0]) + (dot_nt(head, coupled_ref[1]) + dot_nt(rest, coupled_ref[0]))
    weighted = weighted.astype(BF16)
    for slot in range(slots):
        rows = projectors_ref[slot * length : (slot + 1) * length, :]
        value = dot_nt(weighted, rows)[:kinds]
        rows = projectors_ref[(slots + slot) * length : (slots + slot + 1) * length, :]
        mixed[slot * kinds : (slot + 1) * kinds, :] = value + dot_nt(weighted, rows)[kinds:]
    for chunk in range(blocks * width // LANES):
        for group in range(groups):
            total = jnp.zeros((slots, LANES), F32)
            for inner in range(LANES // width):
                block = chunk * (LANES // width) + inner
                own = jnp.where(lanes < width, columns_ref[block * groups + group], 0.0)
                total += pltpu.roll(own, inner * width, 1)
            lined[group * slots : (group + 1) * slots, chunk * LANES : (chunk + 1) * LANES] = total
    head, rest = split(lined[...])
    used = used_slots(count_ref, slots)
    for part in range(2):
        local = dot_nt(head, table_ref[0, part]) + (dot_nt(head, table_ref[1, part]) + dot_nt(rest, table_ref[0, part]))
        local = local * normalizer
        for n in range(orbitals):
            row = n * 2 + part
            for slot in range(slots):
                at = n * slots + slot
                value = local[at : at + 1, :] + mixed[slot * kinds + row : slot * kinds + row + 1, :]
                out_ref[n, part, slot : slot + 1, :] = value
            out_ref[n, part] = jnp.where(used, out_ref[n, part], 0.0)


def on_device(orbitals, projectors, potential, couplings, atom_index, column_site, column_count):
    blocks = lax.axis_size("ga")
    groups = lax.axis_size("band")
    devices = blocks * groups
    orbital_count, _, slots, length = orbitals.shape
    planes = potential.shape[0]
    projector_count = projectors.shape[0]
    columns = column_site.shape[0]
    kinds = orbital_count * 2
    assert orbital_count == groups and kinds % slots == 0 and columns % LANES == 0
    share = projector_count // devices
    width = 2
    while width < 2 * planes:
        width *= 2
    carried = width + kinds // slots * share
    assert carried <= LANES and width <= LANES and share * devices == projector_count
    wide = -(-length // LANES) * LANES
    flat = jnp.transpose(projectors, (1, 2, 3, 0)).reshape(2 * slots * length, projector_count)
    z_table = line_table(length, blocks, planes, width)
    batch = next(i for i in (4, 3, 2, 1) if planes % i == 0) if columns <= 512 else 1
    smem = pl.BlockSpec(memory_space=pltpu.SMEM)
    vmem = pl.BlockSpec(memory_space=pltpu.VMEM)
    hbm = pl.BlockSpec(memory_space=pltpu.HBM)
    params = pltpu.CompilerParams(vmem_limit_bytes=56 * 1024 * 1024)
    payload = jax.ShapeDtypeStruct((devices, slots, LANES), F32)

    sent = pl.pallas_call(
        functools.partial(
            project_kernel, (blocks, groups, orbital_count, slots, length, projector_count, width)
        ),
        out_shape=payload,
        in_specs=[hbm] * 4,
        out_specs=vmem,
        scratch_shapes=[
            pltpu.SMEM(column_count.shape, jnp.int32),
            pltpu.VMEM(orbitals.shape, BF16),
            pltpu.VMEM(flat.shape, BF16),
            pltpu.VMEM(z_table.shape, BF16),
            pltpu.VMEM((4, kinds * slots, length), F32),
            pltpu.VMEM((kinds, projector_count), F32),
            pltpu.SemaphoreType.DMA((3,)),
            pltpu.SemaphoreType.DMA((2 * slots,)),
        ],
        compiler_params=params,
        name="project",
    )(column_count, orbitals, flat, z_table)
    arrived = lax.all_to_all(sent, ("ga", "band"), split_axis=0, concat_axis=0, tiled=True)

    tables = (
        jax.ShapeDtypeStruct((length, 2 * columns), F32),
        jax.ShapeDtypeStruct((3 * 2 * columns, 2 * wide), BF16),
        jax.ShapeDtypeStruct((3 * 2 * wide, 2 * columns), BF16),
    )
    x_rows, plus, minus, coupled = pl.pallas_call(
        functools.partial(table_kernel, (columns, length, projector_count, wide)),
        out_shape=tables + (jax.ShapeDtypeStruct((2, projector_count, projector_count), BF16),),
        in_specs=[vmem] * 4,
        out_specs=(vmem,) * 4,
        compiler_params=params,
        name="tables",
    )(column_site.reshape(1, columns), atom_index.reshape(1, projector_count), couplings, grid_table(length))

    sent = pl.pallas_call(
        functools.partial(plane_kernel, (devices, slots, planes, length, wide, width, carried, batch)),
        out_shape=payload,
        in_specs=[vmem] + [hbm] * 4,
        out_specs=vmem,
        scratch_shapes=[
            pltpu.VMEM((columns, LANES), F32),
            pltpu.VMEM((LANES, columns), F32),
            pltpu.VMEM((LANES, columns), F32),
        ]
        + [pltpu.VMEM(table.shape, table.dtype) for table in tables]
        + [
            pltpu.VMEM(potential.shape, F32),
            pltpu.SemaphoreType.DMA((3,)),
            pltpu.SemaphoreType.DMA((planes // batch,)),
        ],
        compiler_params=params,
        name="planes",
    )(arrived, x_rows, plus, minus, potential)
    arrived = lax.all_to_all(sent, ("ga", "band"), split_axis=0, concat_axis=0, tiled=True)

    normalizer = 1.0 / float(length**3)
    return pl.pallas_call(
        functools.partial(
            finish_kernel,
            (blocks, groups, orbital_count, slots, length, projector_count, width, normalizer),
        ),
        out_shape=jax.ShapeDtypeStruct(orbitals.shape, F32),
        in_specs=[smem, vmem, vmem, vmem, vmem],
        out_specs=vmem,
        scratch_shapes=[
            pltpu.VMEM((2 * kinds, projector_count), F32),
            pltpu.VMEM((groups * slots, blocks * width), F32),
            pltpu.VMEM((slots * kinds, length), F32),
        ],
        compiler_params=pltpu.CompilerParams(vmem_limit_bytes=40 * 1024 * 1024),
        name="finish",
    )(column_count, arrived, coupled, flat, z_table)


def solution(mesh):
    return jax.shard_map(
        on_device,
        mesh=mesh,
        in_specs=(
            P(None, None, ("ga", "band"), None),
            P(None, None, ("ga", "band"), None),
            P("ga", None, None),
            P(),
            P(),
            P(),
            P(),
        ),
        out_specs=P(None, None, ("ga", "band"), None),
        check_vma=False,
    )
```

```python
import functools

import jax
import jax.numpy as jnp
import ml_dtypes
import numpy as np
from jax import lax
from jax.experimental import pallas as pl
from jax.experimental.pallas import tpu as pltpu
from jax.sharding import PartitionSpec as P

LANES = 128
BF16 = jnp.bfloat16
F32 = jnp.float32


def pieces_of(table):
    table = np.asarray(table, np.float32)
    head = table.astype(ml_dtypes.bfloat16)
    return np.stack([head, (table - head.astype(np.float32)).astype(ml_dtypes.bfloat16)])


def grid_table(length):
    points = np.arange(length)
    phases = (points[:, None] * points[None, :] % length) * (2.0 * np.pi / length)
    return pieces_of(np.stack([np.cos(phases), np.sin(phases)]))


def line_table(length, blocks, planes, width):
    kz = np.arange(length)
    out = np.zeros((2, length, blocks, width), np.float64)
    for block in range(blocks):
        z = block * planes + np.arange(planes)
        phases = (kz[:, None] * z[None, :] % length) * (2.0 * np.pi / length)
        out[0, :, block, :planes] = np.cos(phases)
        out[0, :, block, width // 2 : width // 2 + planes] = np.sin(phases)
        out[1, :, block, :planes] = -np.sin(phases)
        out[1, :, block, width // 2 : width // 2 + planes] = np.cos(phases)
    return pieces_of(out.reshape(2, length, blocks * width))


def split(values):
    head = values.astype(BF16)
    return head, (values - head.astype(F32)).astype(BF16)


def doubled(values):
    values = values.astype(BF16)
    return jnp.concatenate([values, values], axis=1)


def dot(left, right):
    return lax.dot_general(left, right, (((1,), (0,)), ((), ())), preferred_element_type=F32)


def dot_nt(left, right):
    return lax.dot_general(left, right, (((1,), (1,)), ((), ())), preferred_element_type=F32)


def lane_ids(rows):
    return lax.broadcasted_iota(jnp.int32, (rows, LANES), 1)


def used_slots(count_ref, slots):
    used = count_ref[lax.axis_index("ga")] - lax.axis_index("band") * slots
    return lax.broadcasted_iota(jnp.int32, (slots, 1), 0) < used


def project_kernel(sizes, count_hbm, orbitals_hbm, projectors_hbm, table_hbm, out_ref, *scratch):
    blocks, groups, orbitals, slots, length, projectors, width = sizes
    count_ref, orbitals_ref, projectors_ref, table_ref, coef, spread, small_sems, sems = scratch
    kinds = orbitals * 2
    devices = blocks * groups
    share = projectors // devices
    small = [
        pltpu.make_async_copy(count_hbm, count_ref, small_sems.at[0]),
        pltpu.make_async_copy(orbitals_hbm, orbitals_ref, small_sems.at[1]),
        pltpu.make_async_copy(table_hbm, table_ref, small_sems.at[2]),
    ]
    copies = []
    for piece in range(2 * slots):
        rows = pl.ds(piece * length, length)
        copies.append(pltpu.make_async_copy(projectors_hbm.at[rows], projectors_ref.at[rows], sems.at[piece]))
    for copy in small + copies:
        copy.start()
    small[0].wait()
    small[1].wait()
    used = used_slots(count_ref, slots)
    for n in range(orbitals):
        for part in range(2):
            values = jnp.where(used, orbitals_ref[n, part].astype(F32), 0.0)
            at = (n * 2 + part) * slots
            coef[0, at : at + slots, :] = values
            at = (n * 2 + 1 - part) * slots
            coef[1, at : at + slots, :] = values if part == 1 else -values
            at = n * slots
            coef[2 + part, at : at + slots, :] = values
    small[2].wait()
    columns = jnp.zeros((orbitals * slots, blocks * width), F32)
    for part in range(2):
        left = coef[2 + part, : orbitals * slots, :].astype(BF16)
        columns += dot(left, table_ref[0, part]) + dot(left, table_ref[1, part])
    row_slot = lax.broadcasted_iota(jnp.int32, (kinds * slots, length), 0) % slots
    sums = jnp.zeros((kinds * slots, projectors), F32)
    for part in range(2):
        rows = coef[part]
        for slot in range(slots):
            piece = part * slots + slot
            left = jnp.where(row_slot == slot, rows, 0.0).astype(BF16)
            copies[piece].wait()
            sums += dot(left, projectors_ref[piece * length : (piece + 1) * length, :])
    for row in range(kinds):
        spread[row : row + 1, :] = jnp.sum(sums[row * slots : (row + 1) * slots, :], axis=0, keepdims=True)
    lanes = lane_ids(slots)
    groups_of_rows = kinds // slots
    for block in range(blocks):
        at = block * width
        base = at // LANES * LANES
        chunk = pltpu.roll(columns[:, base : base + LANES], (base - at) % LANES, 1)
        for group in range(groups):
            device = block * groups + group
            piece = jnp.where(lanes < width, chunk[group * slots : (group + 1) * slots, :], 0.0)
            first = device * share
            base = first // LANES * LANES
            for rows in range(groups_of_rows):
                low = width + rows * share
                own = spread[rows * slots : (rows + 1) * slots, base : base + LANES]
                own = pltpu.roll(own, (base + low - first) % LANES, 1)
                piece = jnp.where((lanes >= low) & (lanes < low + share), own, piece)
            out_ref[device] = piece


def table_kernel(sizes, site_ref, atom_ref, couplings_ref, grid_ref, x_ref, plus_ref, minus_ref, coupled_ref):
    columns, length, projectors, wide = sizes
    eye = lax.broadcasted_iota(jnp.int32, (LANES, LANES), 0) == lane_ids(LANES)
    plus_ref[...] = jnp.zeros_like(plus_ref)
    minus_ref[...] = jnp.zeros_like(minus_ref)
    row_ids = lax.broadcasted_iota(jnp.int32, (length, LANES), 0).astype(F32)
    column_ids = lax.broadcasted_iota(jnp.int32, (LANES, length), 1).astype(F32)
    for at in range(0, columns, LANES):
        site = site_ref[:, at : at + LANES].astype(F32)
        site_x = jnp.floor((site + 0.5) * (1.0 / length))
        site_y = site - site_x * length
        hot_x = (row_ids == site_x).astype(F32).astype(BF16)
        hot_y = (row_ids == site_y).astype(F32).astype(BF16)
        along = jnp.sum(jnp.where(eye, site_y, 0.0), axis=1, keepdims=True)
        hot_y_rows = (column_ids == along).astype(F32).astype(BF16)
        for part in range(2):
            value = dot(grid_ref[0, part], hot_x) + dot(grid_ref[1, part], hot_x)
            x_ref[:, part * columns + at : part * columns + at + LANES] = value
        for piece in range(2):
            cosine = dot(hot_y_rows, grid_ref[piece, 0])
            sine = dot(hot_y_rows, grid_ref[piece, 1])
            rows = pl.ds(piece * 2 * columns + at, LANES)
            plus_ref[rows, :length] = cosine.astype(BF16)
            plus_ref[rows, wide : wide + length] = sine.astype(BF16)
            rows = pl.ds((piece * 2 + 1) * columns + at, LANES)
            plus_ref[rows, :length] = (-sine).astype(BF16)
            plus_ref[rows, wide : wide + length] = cosine.astype(BF16)
            cosine = dot(grid_ref[piece, 0], hot_y)
            sine = dot(grid_ref[piece, 1], hot_y)
            rows = pl.ds(piece * 2 * wide, length)
            minus_ref[rows, at : at + LANES] = cosine.astype(BF16)
            minus_ref[rows, columns + at : columns + at + LANES] = (-sine).astype(BF16)
            rows = pl.ds((piece * 2 + 1) * wide, length)
            minus_ref[rows, at : at + LANES] = sine.astype(BF16)
            minus_ref[rows, columns + at : columns + at + LANES] = cosine.astype(BF16)
    atoms = atom_ref[...].astype(F32)
    for at in range(0, projectors, LANES):
        along = jnp.sum(jnp.where(eye, atoms[:, at : at + LANES], 0.0), axis=1, keepdims=True)
        head, rest = split(jnp.where(along == atoms, couplings_ref[at : at + LANES, :], 0.0))
        coupled_ref[0, at : at + LANES, :] = head
        coupled_ref[1, at : at + LANES, :] = rest


def plane_kernel(sizes, columns_ref, x_hbm, plus_hbm, minus_hbm, potential_hbm, out_ref, *scratch):
    devices, slots, planes, length, wide, width, carried, batch = sizes
    gathered, lines, back, x_ref, plus_ref, minus_ref, potential_ref, table_sems, sems = scratch
    count = devices * slots
    tables = [
        pltpu.make_async_copy(source, target, table_sems.at[i])
        for i, (source, target) in enumerate(((x_hbm, x_ref), (plus_hbm, plus_ref), (minus_hbm, minus_ref)))
    ]
    copies = []
    for i in range(planes // batch):
        some = pl.ds(i * batch, batch)
        copies.append(pltpu.make_async_copy(potential_hbm.at[some], potential_ref.at[some], sems.at[i]))
    for copy in tables[:2] + copies[:1] + tables[2:] + copies[1:]:
        copy.start()
    total = jnp.zeros((slots, LANES), F32)
    for device in range(devices):
        piece = columns_ref[device]
        gathered[device * slots : (device + 1) * slots, :] = piece
        total += piece
    for at in range(0, count, LANES):
        lines[:, at : at + LANES] = gathered[at : at + LANES, :].T
    back[...] = jnp.zeros_like(back)
    tables[0].wait()
    cosine = x_ref[:, :count]
    sine = x_ref[:, count:]
    padding = jnp.zeros((length, wide - length), F32)
    for i in range(planes // batch):
        left = []
        for plane in range(i * batch, (i + 1) * batch):
            real = lines[plane : plane + 1, :]
            imag = lines[plane + width // 2 : plane + width // 2 + 1, :]
            left.append(jnp.concatenate([cosine * real - sine * imag, cosine * imag + sine * real], axis=1))
        left = doubled(jnp.concatenate(left, axis=0))
        if i == 0:
            tables[1].wait()
        field = dot(left, plus_ref[...])
        copies[i].wait()
        weights = []
        for plane in range(i * batch, (i + 1) * batch):
            own = jnp.concatenate([potential_ref[plane], padding], axis=1)
            weights.append(jnp.concatenate([own, own], axis=1))
        left = doubled(field * jnp.concatenate(weights, axis=0))
        if i == 0:
            tables[2].wait()
        half = dot(left, minus_ref[...])
        for j in range(batch):
            plane = i * batch + j
            real = half[j * length : (j + 1) * length, :count]
            imag = half[j * length : (j + 1) * length, count:]
            back[plane : plane + 1, :] = jnp.sum(cosine * real + sine * imag, axis=0, keepdims=True)
            at = plane + width // 2
            back[at : at + 1, :] = jnp.sum(cosine * imag - sine * real, axis=0, keepdims=True)
    for at in range(0, count, LANES):
        gathered[at : at + LANES, :] = back[:, at : at + LANES].T
    lanes = lane_ids(slots)
    for device in range(devices):
        piece = gathered[device * slots : (device + 1) * slots, :]
        out_ref[device] = jnp.where((lanes >= width) & (lanes < carried), total, piece)


def finish_kernel(sizes, count_ref, columns_ref, coupled_ref, projectors_ref, table_ref, out_ref, summed, lined, mixed):
    blocks, groups, orbitals, slots, length, projectors, width, normalizer = sizes
    kinds = orbitals * 2
    devices = blocks * groups
    share = projectors // devices
    groups_of_rows = kinds // slots
    lanes = lane_ids(slots)
    for chunk in range(projectors // LANES):
        in_chunk = range(chunk * LANES // share, (chunk + 1) * LANES // share)
        for rows in range(groups_of_rows):
            low = width + rows * share
            total = jnp.zeros((slots, LANES), F32)
            for device in in_chunk:
                own = columns_ref[device]
                own = pltpu.roll(jnp.where((lanes >= low) & (lanes < low + share), own, 0.0), (device * share - low) % LANES, 1)
                total += own
            summed[rows * slots : (rows + 1) * slots, chunk * LANES : (chunk + 1) * LANES] = total
    for n in range(orbitals):
        at = kinds + n * 2
        summed[at : at + 1, :] = -summed[n * 2 + 1 : n * 2 + 2, :]
        summed[at + 1 : at + 2, :] = summed[n * 2 : n * 2 + 1, :]
    head, rest = split(summed[...])
    weighted = dot_nt(head, coupled_ref[0]) + (dot_nt(head, coupled_ref[1]) + dot_nt(rest, coupled_ref[0]))
    weighted = weighted.astype(BF16)
    for slot in range(slots):
        rows = projectors_ref[slot * length : (slot + 1) * length, :]
        value = dot_nt(weighted, rows)[:kinds]
        rows = projectors_ref[(slots + slot) * length : (slots + slot + 1) * length, :]
        mixed[slot * kinds : (slot + 1) * kinds, :] = value + dot_nt(weighted, rows)[kinds:]
    for chunk in range(blocks * width // LANES):
        for group in range(groups):
            total = jnp.zeros((slots, LANES), F32)
            for inner in range(LANES // width):
                block = chunk * (LANES // width) + inner
                own = jnp.where(lanes < width, columns_ref[block * groups + group], 0.0)
                total += pltpu.roll(own, inner * width, 1)
            lined[group * slots : (group + 1) * slots, chunk * LANES : (chunk + 1) * LANES] = total
    head, rest = split(lined[...])
    used = used_slots(count_ref, slots)
    for part in range(2):
        local = dot_nt(head, table_ref[0, part]) + (dot_nt(head, table_ref[1, part]) + dot_nt(rest, table_ref[0, part]))
        local = local * normalizer
        for n in range(orbitals):
            row = n * 2 + part
            for slot in range(slots):
                at = n * slots + slot
                value = local[at : at + 1, :] + mixed[slot * kinds + row : slot * kinds + row + 1, :]
                out_ref[n, part, slot : slot + 1, :] = value
            out_ref[n, part] = jnp.where(used, out_ref[n, part], 0.0)


def on_device(orbitals, projectors, potential, couplings, atom_index, column_site, column_count):
    blocks = lax.axis_size("ga")
    groups = lax.axis_size("band")
    devices = blocks * groups
    orbital_count, _, slots, length = orbitals.shape
    planes = potential.shape[0]
    projector_count = projectors.shape[0]
    columns = column_site.shape[0]
    kinds = orbital_count * 2
    assert orbital_count == groups and kinds % slots == 0 and columns % LANES == 0
    share = projector_count // devices
    width = 2
    while width < 2 * planes:
        width *= 2
    carried = width + kinds // slots * share
    assert carried <= LANES and width <= LANES and share * devices == projector_count
    wide = -(-length // LANES) * LANES
    flat = jnp.transpose(projectors, (1, 2, 3, 0)).reshape(2 * slots * length, projector_count)
    z_table = line_table(length, blocks, planes, width)
    batch = next(i for i in (4, 3, 2, 1) if planes % i == 0) if columns <= 512 else 1
    smem = pl.BlockSpec(memory_space=pltpu.SMEM)
    vmem = pl.BlockSpec(memory_space=pltpu.VMEM)
    hbm = pl.BlockSpec(memory_space=pltpu.HBM)
    params = pltpu.CompilerParams(vmem_limit_bytes=56 * 1024 * 1024)
    small = pltpu.CompilerParams(vmem_limit_bytes=40 * 1024 * 1024)
    payload = jax.ShapeDtypeStruct((devices, slots, LANES), F32)

    sent = pl.pallas_call(
        functools.partial(
            project_kernel, (blocks, groups, orbital_count, slots, length, projector_count, width)
        ),
        out_shape=payload,
        in_specs=[hbm] * 4,
        out_specs=vmem,
        scratch_shapes=[
            pltpu.SMEM(column_count.shape, jnp.int32),
            pltpu.VMEM(orbitals.shape, BF16),
            pltpu.VMEM(flat.shape, BF16),
            pltpu.VMEM(z_table.shape, BF16),
            pltpu.VMEM((4, kinds * slots, length), F32),
            pltpu.VMEM((kinds, projector_count), F32),
            pltpu.SemaphoreType.DMA((3,)),
            pltpu.SemaphoreType.DMA((2 * slots,)),
        ],
        compiler_params=params,
        name="project",
    )(column_count, orbitals, flat, z_table)
    arrived = lax.all_to_all(sent, ("ga", "band"), split_axis=0, concat_axis=0, tiled=True)

    tables = (
        jax.ShapeDtypeStruct((length, 2 * columns), F32),
        jax.ShapeDtypeStruct((4 * columns, 2 * wide), BF16),
        jax.ShapeDtypeStruct((4 * wide, 2 * columns), BF16),
    )
    x_rows, plus, minus, coupled = pl.pallas_call(
        functools.partial(table_kernel, (columns, length, projector_count, wide)),
        out_shape=tables + (jax.ShapeDtypeStruct((2, projector_count, projector_count), BF16),),
        in_specs=[vmem] * 4,
        out_specs=(vmem,) * 4,
        compiler_params=params,
        name="tables",
    )(column_site.reshape(1, columns), atom_index.reshape(1, projector_count), couplings, grid_table(length))

    sent = pl.pallas_call(
        functools.partial(plane_kernel, (devices, slots, planes, length, wide, width, carried, batch)),
        out_shape=payload,
        in_specs=[vmem] + [hbm] * 4,
        out_specs=vmem,
        scratch_shapes=[
            pltpu.VMEM((columns, LANES), F32),
            pltpu.VMEM((LANES, columns), F32),
            pltpu.VMEM((LANES, columns), F32),
        ]
        + [pltpu.VMEM(table.shape, table.dtype) for table in tables]
        + [
            pltpu.VMEM(potential.shape, F32),
            pltpu.SemaphoreType.DMA((3,)),
            pltpu.SemaphoreType.DMA((planes // batch,)),
        ],
        compiler_params=small,
        name="planes",
    )(arrived, x_rows, plus, minus, potential)
    arrived = lax.all_to_all(sent, ("ga", "band"), split_axis=0, concat_axis=0, tiled=True)

    normalizer = 1.0 / float(length**3)
    return pl.pallas_call(
        functools.partial(
            finish_kernel,
            (blocks, groups, orbital_count, slots, length, projector_count, width, normalizer),
        ),
        out_shape=jax.ShapeDtypeStruct(orbitals.shape, F32),
        in_specs=[smem, vmem, vmem, vmem, vmem],
        out_specs=vmem,
        scratch_shapes=[
            pltpu.VMEM((2 * kinds, projector_count), F32),
            pltpu.VMEM((groups * slots, blocks * width), F32),
            pltpu.VMEM((slots * kinds, length), F32),
        ],
        compiler_params=small,
        name="finish",
    )(column_count, arrived, coupled, flat, z_table)


def solution(mesh):
    return jax.shard_map(
        on_device,
        mesh=mesh,
        in_specs=(
            P(None, None, ("ga", "band"), None),
            P(None, None, ("ga", "band"), None),
            P("ga", None, None),
            P(),
            P(),
            P(),
            P(),
        ),
        out_specs=P(None, None, ("ga", "band"), None),
        check_vma=False,
    )
```

```python
import functools

import jax
import jax.numpy as jnp
import ml_dtypes
import numpy as np
from jax import lax
from jax.experimental import pallas as pl
from jax.experimental.pallas import tpu as pltpu
from jax.sharding import PartitionSpec as P

LANES = 128
BF16 = jnp.bfloat16
F32 = jnp.float32


def pieces_of(table):
    table = np.asarray(table, np.float32)
    head = table.astype(ml_dtypes.bfloat16)
    return np.stack([head, (table - head.astype(np.float32)).astype(ml_dtypes.bfloat16)])


def grid_table(length):
    points = np.arange(length)
    phases = (points[:, None] * points[None, :] % length) * (2.0 * np.pi / length)
    return pieces_of(np.stack([np.cos(phases), np.sin(phases)]))


def line_table(length, blocks, planes, width):
    kz = np.arange(length)
    out = np.zeros((2, length, blocks, width), np.float64)
    for block in range(blocks):
        z = block * planes + np.arange(planes)
        phases = (kz[:, None] * z[None, :] % length) * (2.0 * np.pi / length)
        out[0, :, block, :planes] = np.cos(phases)
        out[0, :, block, width // 2 : width // 2 + planes] = np.sin(phases)
        out[1, :, block, :planes] = -np.sin(phases)
        out[1, :, block, width // 2 : width // 2 + planes] = np.cos(phases)
    return pieces_of(out.reshape(2, length, blocks * width))


def split(values):
    head = values.astype(BF16)
    return head, (values - head.astype(F32)).astype(BF16)


def doubled(values):
    values = values.astype(BF16)
    return jnp.concatenate([values, values], axis=1)


def dot(left, right):
    return lax.dot_general(left, right, (((1,), (0,)), ((), ())), preferred_element_type=F32)


def dot_nt(left, right):
    return lax.dot_general(left, right, (((1,), (1,)), ((), ())), preferred_element_type=F32)


def lane_ids(rows):
    return lax.broadcasted_iota(jnp.int32, (rows, LANES), 1)


def used_slots(count_ref, slots):
    used = count_ref[lax.axis_index("ga")] - lax.axis_index("band") * slots
    return lax.broadcasted_iota(jnp.int32, (slots, 1), 0) < used


def project_kernel(sizes, count_hbm, orbitals_hbm, projectors_hbm, table_hbm, out_ref, *scratch):
    blocks, groups, orbitals, slots, length, projectors, width = sizes
    count_ref, orbitals_ref, projectors_ref, table_ref, coef, spread, small_sems, sems = scratch
    kinds = orbitals * 2
    devices = blocks * groups
    share = projectors // devices
    small = [
        pltpu.make_async_copy(count_hbm, count_ref, small_sems.at[0]),
        pltpu.make_async_copy(orbitals_hbm, orbitals_ref, small_sems.at[1]),
        pltpu.make_async_copy(table_hbm, table_ref, small_sems.at[2]),
    ]
    copies = []
    for piece in range(2 * slots):
        rows = pl.ds(piece * length, length)
        copies.append(pltpu.make_async_copy(projectors_hbm.at[rows], projectors_ref.at[rows], sems.at[piece]))
    for copy in small + copies:
        copy.start()
    small[0].wait()
    small[1].wait()
    used = used_slots(count_ref, slots)
    for n in range(orbitals):
        for part in range(2):
            values = jnp.where(used, orbitals_ref[n, part].astype(F32), 0.0)
            at = (n * 2 + part) * slots
            coef[0, at : at + slots, :] = values
            at = (n * 2 + 1 - part) * slots
            coef[1, at : at + slots, :] = values if part == 1 else -values
            at = n * slots
            coef[2 + part, at : at + slots, :] = values
    small[2].wait()
    columns = jnp.zeros((orbitals * slots, blocks * width), F32)
    for part in range(2):
        left = coef[2 + part, : orbitals * slots, :].astype(BF16)
        columns += dot(left, table_ref[0, part]) + dot(left, table_ref[1, part])
    row_slot = lax.broadcasted_iota(jnp.int32, (kinds * slots, length), 0) % slots
    sums = jnp.zeros((kinds * slots, projectors), F32)
    for part in range(2):
        rows = coef[part]
        for slot in range(slots):
            piece = part * slots + slot
            left = jnp.where(row_slot == slot, rows, 0.0).astype(BF16)
            copies[piece].wait()
            sums += dot(left, projectors_ref[piece * length : (piece + 1) * length, :])
    for row in range(kinds):
        spread[row : row + 1, :] = jnp.sum(sums[row * slots : (row + 1) * slots, :], axis=0, keepdims=True)
    lanes = lane_ids(slots)
    groups_of_rows = kinds // slots
    for block in range(blocks):
        at = block * width
        base = at // LANES * LANES
        chunk = pltpu.roll(columns[:, base : base + LANES], (base - at) % LANES, 1)
        for group in range(groups):
            device = block * groups + group
            piece = jnp.where(lanes < width, chunk[group * slots : (group + 1) * slots, :], 0.0)
            first = device * share
            base = first // LANES * LANES
            for rows in range(groups_of_rows):
                low = width + rows * share
                own = spread[rows * slots : (rows + 1) * slots, base : base + LANES]
                own = pltpu.roll(own, (base + low - first) % LANES, 1)
                piece = jnp.where((lanes >= low) & (lanes < low + share), own, piece)
            out_ref[device] = piece


def table_kernel(sizes, site_ref, atom_ref, couplings_ref, grid_ref, x_ref, plus_ref, minus_ref, coupled_ref):
    columns, length, projectors, wide = sizes
    eye = lax.broadcasted_iota(jnp.int32, (LANES, LANES), 0) == lane_ids(LANES)
    plus_ref[...] = jnp.zeros_like(plus_ref)
    minus_ref[...] = jnp.zeros_like(minus_ref)
    row_ids = lax.broadcasted_iota(jnp.int32, (length, LANES), 0).astype(F32)
    column_ids = lax.broadcasted_iota(jnp.int32, (LANES, length), 1).astype(F32)
    for at in range(0, columns, LANES):
        site = site_ref[:, at : at + LANES].astype(F32)
        site_x = jnp.floor((site + 0.5) * (1.0 / length))
        site_y = site - site_x * length
        hot_x = (row_ids == site_x).astype(F32).astype(BF16)
        hot_y = (row_ids == site_y).astype(F32).astype(BF16)
        along = jnp.sum(jnp.where(eye, site_y, 0.0), axis=1, keepdims=True)
        hot_y_rows = (column_ids == along).astype(F32).astype(BF16)
        for part in range(2):
            value = dot(grid_ref[0, part], hot_x) + dot(grid_ref[1, part], hot_x)
            x_ref[:, part * columns + at : part * columns + at + LANES] = value
        for piece in range(2):
            cosine = dot(hot_y_rows, grid_ref[piece, 0])
            sine = dot(hot_y_rows, grid_ref[piece, 1])
            rows = pl.ds(piece * 2 * columns + at, LANES)
            plus_ref[rows, :length] = cosine.astype(BF16)
            plus_ref[rows, wide : wide + length] = sine.astype(BF16)
            rows = pl.ds((piece * 2 + 1) * columns + at, LANES)
            plus_ref[rows, :length] = (-sine).astype(BF16)
            plus_ref[rows, wide : wide + length] = cosine.astype(BF16)
            cosine = dot(grid_ref[piece, 0], hot_y)
            sine = dot(grid_ref[piece, 1], hot_y)
            rows = pl.ds(piece * 2 * wide, length)
            minus_ref[rows, at : at + LANES] = cosine.astype(BF16)
            minus_ref[rows, columns + at : columns + at + LANES] = (-sine).astype(BF16)
            rows = pl.ds((piece * 2 + 1) * wide, length)
            minus_ref[rows, at : at + LANES] = sine.astype(BF16)
            minus_ref[rows, columns + at : columns + at + LANES] = cosine.astype(BF16)
    atoms = atom_ref[...].astype(F32)
    for at in range(0, projectors, LANES):
        along = jnp.sum(jnp.where(eye, atoms[:, at : at + LANES], 0.0), axis=1, keepdims=True)
        head, rest = split(jnp.where(along == atoms, couplings_ref[at : at + LANES, :], 0.0))
        coupled_ref[0, at : at + LANES, :] = head
        coupled_ref[1, at : at + LANES, :] = rest


def plane_kernel(sizes, columns_ref, x_ref, plus_ref, minus_ref, potential_ref, out_ref, gathered, lines, back):
    devices, slots, planes, length, wide, width, carried, batch = sizes
    count = devices * slots
    total = jnp.zeros((slots, LANES), F32)
    for device in range(devices):
        piece = columns_ref[device]
        gathered[device * slots : (device + 1) * slots, :] = piece
        total += piece
    for at in range(0, count, LANES):
        lines[:, at : at + LANES] = gathered[at : at + LANES, :].T
    back[...] = jnp.zeros_like(back)
    cosine = x_ref[:, :count]
    sine = x_ref[:, count:]
    padding = jnp.zeros((length, wide - length), F32)
    for i in range(planes // batch):
        left = []
        for plane in range(i * batch, (i + 1) * batch):
            real = lines[plane : plane + 1, :]
            imag = lines[plane + width // 2 : plane + width // 2 + 1, :]
            left.append(jnp.concatenate([cosine * real - sine * imag, cosine * imag + sine * real], axis=1))
        left = doubled(jnp.concatenate(left, axis=0))
        field = dot(left, plus_ref[...])
        weights = []
        for plane in range(i * batch, (i + 1) * batch):
            own = jnp.concatenate([potential_ref[plane], padding], axis=1)
            weights.append(jnp.concatenate([own, own], axis=1))
        left = doubled(field * jnp.concatenate(weights, axis=0))
        half = dot(left, minus_ref[...])
        for j in range(batch):
            plane = i * batch + j
            real = half[j * length : (j + 1) * length, :count]
            imag = half[j * length : (j + 1) * length, count:]
            back[plane : plane + 1, :] = jnp.sum(cosine * real + sine * imag, axis=0, keepdims=True)
            at = plane + width // 2
            back[at : at + 1, :] = jnp.sum(cosine * imag - sine * real, axis=0, keepdims=True)
    for at in range(0, count, LANES):
        gathered[at : at + LANES, :] = back[:, at : at + LANES].T
    lanes = lane_ids(slots)
    for device in range(devices):
        piece = gathered[device * slots : (device + 1) * slots, :]
        out_ref[device] = jnp.where((lanes >= width) & (lanes < carried), total, piece)


def finish_kernel(sizes, count_hbm, columns_hbm, coupled_hbm, projectors_hbm, table_hbm, out_ref, *scratch):
    blocks, groups, orbitals, slots, length, projectors, width, normalizer = sizes
    count_ref, columns_ref, coupled_ref, projectors_ref, table_ref, summed, lined, mixed, sems = scratch
    pairs = (
        (columns_hbm, columns_ref),
        (coupled_hbm, coupled_ref),
        (projectors_hbm, projectors_ref),
        (table_hbm, table_ref),
        (count_hbm, count_ref),
    )
    copies = [pltpu.make_async_copy(source, target, sems.at[i]) for i, (source, target) in enumerate(pairs)]
    for copy in copies:
        copy.start()
    copies[0].wait()
    kinds = orbitals * 2
    devices = blocks * groups
    share = projectors // devices
    groups_of_rows = kinds // slots
    lanes = lane_ids(slots)
    for chunk in range(projectors // LANES):
        in_chunk = range(chunk * LANES // share, (chunk + 1) * LANES // share)
        for rows in range(groups_of_rows):
            low = width + rows * share
            total = jnp.zeros((slots, LANES), F32)
            for device in in_chunk:
                own = columns_ref[device]
                own = pltpu.roll(jnp.where((lanes >= low) & (lanes < low + share), own, 0.0), (device * share - low) % LANES, 1)
                total += own
            summed[rows * slots : (rows + 1) * slots, chunk * LANES : (chunk + 1) * LANES] = total
    for n in range(orbitals):
        at = kinds + n * 2
        summed[at : at + 1, :] = -summed[n * 2 + 1 : n * 2 + 2, :]
        summed[at + 1 : at + 2, :] = summed[n * 2 : n * 2 + 1, :]
    head, rest = split(summed[...])
    copies[1].wait()
    weighted = dot_nt(head, coupled_ref[0]) + (dot_nt(head, coupled_ref[1]) + dot_nt(rest, coupled_ref[0]))
    weighted = weighted.astype(BF16)
    copies[2].wait()
    for slot in range(slots):
        rows = projectors_ref[slot * length : (slot + 1) * length, :]
        value = dot_nt(weighted, rows)[:kinds]
        rows = projectors_ref[(slots + slot) * length : (slots + slot + 1) * length, :]
        mixed[slot * kinds : (slot + 1) * kinds, :] = value + dot_nt(weighted, rows)[kinds:]
    for chunk in range(blocks * width // LANES):
        for group in range(groups):
            total = jnp.zeros((slots, LANES), F32)
            for inner in range(LANES // width):
                block = chunk * (LANES // width) + inner
                own = jnp.where(lanes < width, columns_ref[block * groups + group], 0.0)
                total += pltpu.roll(own, inner * width, 1)
            lined[group * slots : (group + 1) * slots, chunk * LANES : (chunk + 1) * LANES] = total
    head, rest = split(lined[...])
    copies[3].wait()
    copies[4].wait()
    used = used_slots(count_ref, slots)
    for part in range(2):
        local = dot_nt(head, table_ref[0, part]) + (dot_nt(head, table_ref[1, part]) + dot_nt(rest, table_ref[0, part]))
        local = local * normalizer
        for n in range(orbitals):
            row = n * 2 + part
            for slot in range(slots):
                at = n * slots + slot
                value = local[at : at + 1, :] + mixed[slot * kinds + row : slot * kinds + row + 1, :]
                out_ref[n, part, slot : slot + 1, :] = value
            out_ref[n, part] = jnp.where(used, out_ref[n, part], 0.0)


def on_device(orbitals, projectors, potential, couplings, atom_index, column_site, column_count):
    blocks = lax.axis_size("ga")
    groups = lax.axis_size("band")
    devices = blocks * groups
    orbital_count, _, slots, length = orbitals.shape
    planes = potential.shape[0]
    projector_count = projectors.shape[0]
    columns = column_site.shape[0]
    kinds = orbital_count * 2
    assert orbital_count == groups and kinds % slots == 0 and columns % LANES == 0
    share = projector_count // devices
    width = 2
    while width < 2 * planes:
        width *= 2
    carried = width + kinds // slots * share
    assert carried <= LANES and width <= LANES and share * devices == projector_count
    wide = -(-length // LANES) * LANES
    flat = jnp.transpose(projectors, (1, 2, 3, 0)).reshape(2 * slots * length, projector_count)
    z_table = line_table(length, blocks, planes, width)
    batch = next(i for i in (4, 3, 2, 1) if planes % i == 0) if columns <= 512 else 1
    vmem = pl.BlockSpec(memory_space=pltpu.VMEM)
    hbm = pl.BlockSpec(memory_space=pltpu.HBM)
    params = pltpu.CompilerParams(vmem_limit_bytes=56 * 1024 * 1024)
    small = pltpu.CompilerParams(vmem_limit_bytes=40 * 1024 * 1024)
    payload = jax.ShapeDtypeStruct((devices, slots, LANES), F32)

    sent = pl.pallas_call(
        functools.partial(
            project_kernel, (blocks, groups, orbital_count, slots, length, projector_count, width)
        ),
        out_shape=payload,
        in_specs=[hbm] * 4,
        out_specs=vmem,
        scratch_shapes=[
            pltpu.SMEM(column_count.shape, jnp.int32),
            pltpu.VMEM(orbitals.shape, BF16),
            pltpu.VMEM(flat.shape, BF16),
            pltpu.VMEM(z_table.shape, BF16),
            pltpu.VMEM((4, kinds * slots, length), F32),
            pltpu.VMEM((kinds, projector_count), F32),
            pltpu.SemaphoreType.DMA((3,)),
            pltpu.SemaphoreType.DMA((2 * slots,)),
        ],
        compiler_params=params,
        name="project",
    )(column_count, orbitals, flat, z_table)
    arrived = lax.all_to_all(sent, ("ga", "band"), split_axis=0, concat_axis=0, tiled=True)

    tables = (
        jax.ShapeDtypeStruct((length, 2 * columns), F32),
        jax.ShapeDtypeStruct((4 * columns, 2 * wide), BF16),
        jax.ShapeDtypeStruct((4 * wide, 2 * columns), BF16),
    )
    x_rows, plus, minus, coupled = pl.pallas_call(
        functools.partial(table_kernel, (columns, length, projector_count, wide)),
        out_shape=tables + (jax.ShapeDtypeStruct((2, projector_count, projector_count), BF16),),
        in_specs=[vmem] * 4,
        out_specs=(vmem,) * 4,
        compiler_params=params,
        name="tables",
    )(column_site.reshape(1, columns), atom_index.reshape(1, projector_count), couplings, grid_table(length))

    sent = pl.pallas_call(
        functools.partial(plane_kernel, (devices, slots, planes, length, wide, width, carried, batch)),
        out_shape=payload,
        in_specs=[vmem] * 5,
        out_specs=vmem,
        scratch_shapes=[
            pltpu.VMEM((columns, LANES), F32),
            pltpu.VMEM((LANES, columns), F32),
            pltpu.VMEM((LANES, columns), F32),
        ],
        compiler_params=small,
        name="planes",
    )(arrived, x_rows, plus, minus, potential)
    arrived = lax.all_to_all(sent, ("ga", "band"), split_axis=0, concat_axis=0, tiled=True)

    normalizer = 1.0 / float(length**3)
    return pl.pallas_call(
        functools.partial(
            finish_kernel,
            (blocks, groups, orbital_count, slots, length, projector_count, width, normalizer),
        ),
        out_shape=jax.ShapeDtypeStruct(orbitals.shape, F32),
        in_specs=[hbm] * 5,
        out_specs=vmem,
        scratch_shapes=[
            pltpu.SMEM(column_count.shape, jnp.int32),
            pltpu.VMEM(payload.shape, F32),
            pltpu.VMEM(coupled.shape, BF16),
            pltpu.VMEM(flat.shape, BF16),
            pltpu.VMEM(z_table.shape, BF16),
            pltpu.VMEM((2 * kinds, projector_count), F32),
            pltpu.VMEM((groups * slots, blocks * width), F32),
            pltpu.VMEM((slots * kinds, length), F32),
            pltpu.SemaphoreType.DMA((5,)),
        ],
        compiler_params=pltpu.CompilerParams(vmem_limit_bytes=60 * 1024 * 1024),
        name="finish",
    )(column_count, arrived, coupled, flat, z_table)


def solution(mesh):
    return jax.shard_map(
        on_device,
        mesh=mesh,
        in_specs=(
            P(None, None, ("ga", "band"), None),
            P(None, None, ("ga", "band"), None),
            P("ga", None, None),
            P(),
            P(),
            P(),
            P(),
        ),
        out_specs=P(None, None, ("ga", "band"), None),
        check_vma=False,
    )
```

```python
import functools

import jax
import jax.numpy as jnp
import ml_dtypes
import numpy as np
from jax import lax
from jax.experimental import pallas as pl
from jax.experimental.pallas import tpu as pltpu
from jax.sharding import PartitionSpec as P

LANES = 128
BF16 = jnp.bfloat16
F32 = jnp.float32


def pieces_of(table):
    table = np.asarray(table, np.float32)
    head = table.astype(ml_dtypes.bfloat16)
    return np.stack([head, (table - head.astype(np.float32)).astype(ml_dtypes.bfloat16)])


def grid_table(length):
    points = np.arange(length)
    phases = (points[:, None] * points[None, :] % length) * (2.0 * np.pi / length)
    return pieces_of(np.stack([np.cos(phases), np.sin(phases)]))


def line_table(length, blocks, planes, width):
    kz = np.arange(length)
    out = np.zeros((2, length, blocks, width), np.float64)
    for block in range(blocks):
        z = block * planes + np.arange(planes)
        phases = (kz[:, None] * z[None, :] % length) * (2.0 * np.pi / length)
        out[0, :, block, :planes] = np.cos(phases)
        out[0, :, block, width // 2 : width // 2 + planes] = np.sin(phases)
        out[1, :, block, :planes] = -np.sin(phases)
        out[1, :, block, width // 2 : width // 2 + planes] = np.cos(phases)
    return pieces_of(out.reshape(2, length, blocks * width))


def split(values):
    head = values.astype(BF16)
    return head, (values - head.astype(F32)).astype(BF16)


def stacked(values):
    head, rest = split(values)
    return jnp.concatenate([head.astype(F32), rest.astype(F32)], axis=0).astype(BF16)


def doubled(values):
    values = values.astype(BF16)
    return jnp.concatenate([values, values], axis=1)


def dot(left, right):
    return lax.dot_general(left, right, (((1,), (0,)), ((), ())), preferred_element_type=F32)


def dot_nt(left, right):
    return lax.dot_general(left, right, (((1,), (1,)), ((), ())), preferred_element_type=F32)


def lane_ids(rows):
    return lax.broadcasted_iota(jnp.int32, (rows, LANES), 1)


def used_slots(count_ref, slots):
    used = count_ref[lax.axis_index("ga")] - lax.axis_index("band") * slots
    return lax.broadcasted_iota(jnp.int32, (slots, 1), 0) < used


def project_kernel(sizes, count_hbm, orbitals_hbm, projectors_hbm, table_hbm, out_ref, *scratch):
    blocks, groups, orbitals, slots, length, projectors, width = sizes
    count_ref, orbitals_ref, projectors_ref, table_ref, coef, spread, small_sems, sems = scratch
    kinds = orbitals * 2
    devices = blocks * groups
    share = projectors // devices
    small = [
        pltpu.make_async_copy(count_hbm, count_ref, small_sems.at[0]),
        pltpu.make_async_copy(orbitals_hbm, orbitals_ref, small_sems.at[1]),
        pltpu.make_async_copy(table_hbm, table_ref, small_sems.at[2]),
    ]
    copies = []
    for piece in range(2 * slots):
        rows = pl.ds(piece * length, length)
        copies.append(pltpu.make_async_copy(projectors_hbm.at[rows], projectors_ref.at[rows], sems.at[piece]))
    for copy in small + copies:
        copy.start()
    small[0].wait()
    small[1].wait()
    used = used_slots(count_ref, slots)
    for n in range(orbitals):
        for part in range(2):
            values = jnp.where(used, orbitals_ref[n, part].astype(F32), 0.0)
            at = (n * 2 + part) * slots
            coef[0, at : at + slots, :] = values
            at = (n * 2 + 1 - part) * slots
            coef[1, at : at + slots, :] = values if part == 1 else -values
            at = n * slots
            coef[2 + part, at : at + slots, :] = values
    small[2].wait()
    columns = jnp.zeros((orbitals * slots, blocks * width), F32)
    for part in range(2):
        left = coef[2 + part, : orbitals * slots, :].astype(BF16)
        columns += dot(left, table_ref[0, part]) + dot(left, table_ref[1, part])
    row_slot = lax.broadcasted_iota(jnp.int32, (kinds * slots, length), 0) % slots
    sums = jnp.zeros((kinds * slots, projectors), F32)
    for part in range(2):
        rows = coef[part]
        for slot in range(slots):
            piece = part * slots + slot
            left = jnp.where(row_slot == slot, rows, 0.0).astype(BF16)
            copies[piece].wait()
            sums += dot(left, projectors_ref[piece * length : (piece + 1) * length, :])
    for row in range(kinds):
        spread[row : row + 1, :] = jnp.sum(sums[row * slots : (row + 1) * slots, :], axis=0, keepdims=True)
    lanes = lane_ids(slots)
    groups_of_rows = kinds // slots
    for block in range(blocks):
        at = block * width
        base = at // LANES * LANES
        chunk = pltpu.roll(columns[:, base : base + LANES], (base - at) % LANES, 1)
        for group in range(groups):
            device = block * groups + group
            piece = jnp.where(lanes < width, chunk[group * slots : (group + 1) * slots, :], 0.0)
            first = device * share
            base = first // LANES * LANES
            for rows in range(groups_of_rows):
                low = width + rows * share
                own = spread[rows * slots : (rows + 1) * slots, base : base + LANES]
                own = pltpu.roll(own, (base + low - first) % LANES, 1)
                piece = jnp.where((lanes >= low) & (lanes < low + share), own, piece)
            out_ref[device] = piece


def couple_kernel(projectors, atom_ref, couplings_ref, coupled_ref):
    eye = lax.broadcasted_iota(jnp.int32, (LANES, LANES), 0) == lane_ids(LANES)
    atoms = atom_ref[...].astype(F32)
    for at in range(0, projectors, LANES):
        along = jnp.sum(jnp.where(eye, atoms[:, at : at + LANES], 0.0), axis=1, keepdims=True)
        masked = jnp.where(along == atoms, couplings_ref[at : at + LANES, :], 0.0)
        for other in range(0, projectors, LANES):
            head, rest = split(masked[:, other : other + LANES].T)
            coupled_ref[0, other : other + LANES, at : at + LANES] = head
            coupled_ref[1, other : other + LANES, at : at + LANES] = rest


def make_tables(columns, length, wide, site_ref, grid_ref, x_ref, plus_ref, minus_ref):
    eye = lax.broadcasted_iota(jnp.int32, (LANES, LANES), 0) == lane_ids(LANES)
    plus_ref[:, length:wide] = jnp.zeros((4 * columns, wide - length), BF16)
    plus_ref[:, wide + length :] = jnp.zeros((4 * columns, wide - length), BF16)
    for part in range(4):
        minus_ref[part * wide + length : (part + 1) * wide, :] = jnp.zeros((wide - length, 2 * columns), BF16)
    row_ids = lax.broadcasted_iota(jnp.int32, (length, LANES), 0).astype(F32)
    column_ids = lax.broadcasted_iota(jnp.int32, (LANES, length), 1).astype(F32)
    for at in range(0, columns, LANES):
        site = site_ref[:, at : at + LANES].astype(F32)
        site_x = jnp.floor((site + 0.5) * (1.0 / length))
        site_y = site - site_x * length
        hot_x = (row_ids == site_x).astype(F32).astype(BF16)
        hot_y = (row_ids == site_y).astype(F32).astype(BF16)
        along = jnp.sum(jnp.where(eye, site_y, 0.0), axis=1, keepdims=True)
        hot_y_rows = (column_ids == along).astype(F32).astype(BF16)
        for part in range(2):
            value = dot(grid_ref[0, part], hot_x) + dot(grid_ref[1, part], hot_x)
            x_ref[:, part * columns + at : part * columns + at + LANES] = value
        for piece in range(2):
            cosine = dot(hot_y_rows, grid_ref[piece, 0])
            sine = dot(hot_y_rows, grid_ref[piece, 1])
            rows = pl.ds(piece * 2 * columns + at, LANES)
            plus_ref[rows, :length] = cosine.astype(BF16)
            plus_ref[rows, wide : wide + length] = sine.astype(BF16)
            rows = pl.ds((piece * 2 + 1) * columns + at, LANES)
            plus_ref[rows, :length] = (-sine).astype(BF16)
            plus_ref[rows, wide : wide + length] = cosine.astype(BF16)
            cosine = dot(grid_ref[piece, 0], hot_y)
            sine = dot(grid_ref[piece, 1], hot_y)
            rows = pl.ds(piece * 2 * wide, length)
            minus_ref[rows, at : at + LANES] = cosine.astype(BF16)
            minus_ref[rows, columns + at : columns + at + LANES] = (-sine).astype(BF16)
            rows = pl.ds((piece * 2 + 1) * wide, length)
            minus_ref[rows, at : at + LANES] = sine.astype(BF16)
            minus_ref[rows, columns + at : columns + at + LANES] = cosine.astype(BF16)


def plane_kernel(sizes, columns_ref, site_ref, grid_ref, potential_ref, out_ref, *scratch):
    devices, slots, planes, length, wide, width, carried, batch = sizes
    gathered, lines, back, x_ref, plus_ref, minus_ref = scratch
    count = devices * slots
    make_tables(count, length, wide, site_ref, grid_ref, x_ref, plus_ref, minus_ref)
    total = jnp.zeros((slots, LANES), F32)
    for device in range(devices):
        piece = columns_ref[device]
        gathered[device * slots : (device + 1) * slots, :] = piece
        total += piece
    for at in range(0, count, LANES):
        lines[:, at : at + LANES] = gathered[at : at + LANES, :].T
    back[...] = jnp.zeros_like(back)
    cosine = x_ref[:, :count]
    sine = x_ref[:, count:]
    padding = jnp.zeros((length, wide - length), F32)
    for i in range(planes // batch):
        left = []
        for plane in range(i * batch, (i + 1) * batch):
            real = lines[plane : plane + 1, :]
            imag = lines[plane + width // 2 : plane + width // 2 + 1, :]
            left.append(jnp.concatenate([cosine * real - sine * imag, cosine * imag + sine * real], axis=1))
        left = doubled(jnp.concatenate(left, axis=0))
        field = dot(left, plus_ref[...])
        weights = []
        for plane in range(i * batch, (i + 1) * batch):
            own = jnp.concatenate([potential_ref[plane], padding], axis=1)
            weights.append(jnp.concatenate([own, own], axis=1))
        left = doubled(field * jnp.concatenate(weights, axis=0))
        half = dot(left, minus_ref[...])
        for j in range(batch):
            plane = i * batch + j
            real = half[j * length : (j + 1) * length, :count]
            imag = half[j * length : (j + 1) * length, count:]
            back[plane : plane + 1, :] = jnp.sum(cosine * real + sine * imag, axis=0, keepdims=True)
            at = plane + width // 2
            back[at : at + 1, :] = jnp.sum(cosine * imag - sine * real, axis=0, keepdims=True)
    for at in range(0, count, LANES):
        gathered[at : at + LANES, :] = back[:, at : at + LANES].T
    lanes = lane_ids(slots)
    for device in range(devices):
        piece = gathered[device * slots : (device + 1) * slots, :]
        out_ref[device] = jnp.where((lanes >= width) & (lanes < carried), total, piece)


def finish_kernel(sizes, count_hbm, columns_hbm, coupled_hbm, projectors_hbm, table_hbm, out_ref, *scratch):
    blocks, groups, orbitals, slots, length, projectors, width, normalizer = sizes
    count_ref, columns_ref, coupled_ref, projectors_ref, table_ref, summed, lined, mixed, sems = scratch
    pairs = (
        (columns_hbm, columns_ref),
        (coupled_hbm, coupled_ref),
        (projectors_hbm, projectors_ref),
        (table_hbm, table_ref),
        (count_hbm, count_ref),
    )
    copies = [pltpu.make_async_copy(source, target, sems.at[i]) for i, (source, target) in enumerate(pairs)]
    for copy in copies:
        copy.start()
    copies[0].wait()
    kinds = orbitals * 2
    devices = blocks * groups
    share = projectors // devices
    groups_of_rows = kinds // slots
    lanes = lane_ids(slots)
    for chunk in range(projectors // LANES):
        in_chunk = range(chunk * LANES // share, (chunk + 1) * LANES // share)
        for rows in range(groups_of_rows):
            low = width + rows * share
            total = jnp.zeros((slots, LANES), F32)
            for device in in_chunk:
                own = columns_ref[device]
                own = pltpu.roll(jnp.where((lanes >= low) & (lanes < low + share), own, 0.0), (device * share - low) % LANES, 1)
                total += own
            summed[rows * slots : (rows + 1) * slots, chunk * LANES : (chunk + 1) * LANES] = total
    for n in range(orbitals):
        at = kinds + n * 2
        summed[at : at + 1, :] = -summed[n * 2 + 1 : n * 2 + 2, :]
        summed[at + 1 : at + 2, :] = summed[n * 2 : n * 2 + 1, :]
    both = stacked(summed[...])
    copies[1].wait()
    head = dot(both, coupled_ref[0])
    rest = dot(both, coupled_ref[1])
    weighted = (head[: 2 * kinds] + (head[2 * kinds :] + rest[: 2 * kinds])).astype(BF16)
    copies[2].wait()
    for slot in range(slots):
        rows = projectors_ref[slot * length : (slot + 1) * length, :]
        value = dot_nt(weighted, rows)[:kinds]
        rows = projectors_ref[(slots + slot) * length : (slots + slot + 1) * length, :]
        mixed[slot * kinds : (slot + 1) * kinds, :] = value + dot_nt(weighted, rows)[kinds:]
    for chunk in range(blocks * width // LANES):
        for group in range(groups):
            total = jnp.zeros((slots, LANES), F32)
            for inner in range(LANES // width):
                block = chunk * (LANES // width) + inner
                own = jnp.where(lanes < width, columns_ref[block * groups + group], 0.0)
                total += pltpu.roll(own, inner * width, 1)
            lined[group * slots : (group + 1) * slots, chunk * LANES : (chunk + 1) * LANES] = total
    both = stacked(lined[...])
    rows_of_lines = groups * slots
    copies[3].wait()
    copies[4].wait()
    used = used_slots(count_ref, slots)
    for part in range(2):
        head = dot_nt(both, table_ref[0, part])
        rest = dot_nt(both, table_ref[1, part])
        local = (head[:rows_of_lines] + (head[rows_of_lines:] + rest[:rows_of_lines])) * normalizer
        for n in range(orbitals):
            row = n * 2 + part
            for slot in range(slots):
                at = n * slots + slot
                value = local[at : at + 1, :] + mixed[slot * kinds + row : slot * kinds + row + 1, :]
                out_ref[n, part, slot : slot + 1, :] = value
            out_ref[n, part] = jnp.where(used, out_ref[n, part], 0.0)


def on_device(orbitals, projectors, potential, couplings, atom_index, column_site, column_count):
    blocks = lax.axis_size("ga")
    groups = lax.axis_size("band")
    devices = blocks * groups
    orbital_count, _, slots, length = orbitals.shape
    planes = potential.shape[0]
    projector_count = projectors.shape[0]
    columns = column_site.shape[0]
    kinds = orbital_count * 2
    assert orbital_count == groups and kinds % slots == 0 and columns % LANES == 0
    share = projector_count // devices
    width = 2
    while width < 2 * planes:
        width *= 2
    carried = width + kinds // slots * share
    assert carried <= LANES and width <= LANES and share * devices == projector_count
    wide = -(-length // LANES) * LANES
    flat = jnp.transpose(projectors, (1, 2, 3, 0)).reshape(2 * slots * length, projector_count)
    z_table = line_table(length, blocks, planes, width)
    batch = next(i for i in (4, 3, 2, 1) if planes % i == 0) if columns <= 512 else 1
    vmem = pl.BlockSpec(memory_space=pltpu.VMEM)
    hbm = pl.BlockSpec(memory_space=pltpu.HBM)
    params = pltpu.CompilerParams(vmem_limit_bytes=56 * 1024 * 1024)
    small = pltpu.CompilerParams(vmem_limit_bytes=40 * 1024 * 1024)
    payload = jax.ShapeDtypeStruct((devices, slots, LANES), F32)

    sent = pl.pallas_call(
        functools.partial(
            project_kernel, (blocks, groups, orbital_count, slots, length, projector_count, width)
        ),
        out_shape=payload,
        in_specs=[hbm] * 4,
        out_specs=vmem,
        scratch_shapes=[
            pltpu.SMEM(column_count.shape, jnp.int32),
            pltpu.VMEM(orbitals.shape, BF16),
            pltpu.VMEM(flat.shape, BF16),
            pltpu.VMEM(z_table.shape, BF16),
            pltpu.VMEM((4, kinds * slots, length), F32),
            pltpu.VMEM((kinds, projector_count), F32),
            pltpu.SemaphoreType.DMA((3,)),
            pltpu.SemaphoreType.DMA((2 * slots,)),
        ],
        compiler_params=params,
        name="project",
    )(column_count, orbitals, flat, z_table)
    arrived = lax.all_to_all(sent, ("ga", "band"), split_axis=0, concat_axis=0, tiled=True)

    coupled = pl.pallas_call(
        functools.partial(couple_kernel, projector_count),
        out_shape=jax.ShapeDtypeStruct((2, projector_count, projector_count), BF16),
        in_specs=[vmem] * 2,
        out_specs=vmem,
        compiler_params=params,
        name="couple",
    )(atom_index.reshape(1, projector_count), couplings)

    sent = pl.pallas_call(
        functools.partial(plane_kernel, (devices, slots, planes, length, wide, width, carried, batch)),
        out_shape=payload,
        in_specs=[vmem] * 4,
        out_specs=vmem,
        scratch_shapes=[
            pltpu.VMEM((columns, LANES), F32),
            pltpu.VMEM((LANES, columns), F32),
            pltpu.VMEM((LANES, columns), F32),
            pltpu.VMEM((length, 2 * columns), F32),
            pltpu.VMEM((4 * columns, 2 * wide), BF16),
            pltpu.VMEM((4 * wide, 2 * columns), BF16),
        ],
        compiler_params=small,
        name="planes",
    )(arrived, column_site.reshape(1, columns), grid_table(length), potential)
    arrived = lax.all_to_all(sent, ("ga", "band"), split_axis=0, concat_axis=0, tiled=True)

    normalizer = 1.0 / float(length**3)
    return pl.pallas_call(
        functools.partial(
            finish_kernel,
            (blocks, groups, orbital_count, slots, length, projector_count, width, normalizer),
        ),
        out_shape=jax.ShapeDtypeStruct(orbitals.shape, F32),
        in_specs=[hbm] * 5,
        out_specs=vmem,
        scratch_shapes=[
            pltpu.SMEM(column_count.shape, jnp.int32),
            pltpu.VMEM(payload.shape, F32),
            pltpu.VMEM(coupled.shape, BF16),
            pltpu.VMEM(flat.shape, BF16),
            pltpu.VMEM(z_table.shape, BF16),
            pltpu.VMEM((2 * kinds, projector_count), F32),
            pltpu.VMEM((groups * slots, blocks * width), F32),
            pltpu.VMEM((slots * kinds, length), F32),
            pltpu.SemaphoreType.DMA((5,)),
        ],
        compiler_params=pltpu.CompilerParams(vmem_limit_bytes=60 * 1024 * 1024),
        name="finish",
    )(column_count, arrived, coupled, flat, z_table)


def solution(mesh):
    return jax.shard_map(
        on_device,
        mesh=mesh,
        in_specs=(
            P(None, None, ("ga", "band"), None),
            P(None, None, ("ga", "band"), None),
            P("ga", None, None),
            P(),
            P(),
            P(),
            P(),
        ),
        out_specs=P(None, None, ("ga", "band"), None),
        check_vma=False,
    )
```

```python
import functools

import jax
import jax.numpy as jnp
import ml_dtypes
import numpy as np
from jax import lax
from jax.experimental import pallas as pl
from jax.experimental.pallas import tpu as pltpu
from jax.sharding import PartitionSpec as P

LANES = 128
BF16 = jnp.bfloat16
F32 = jnp.float32


def pieces_of(table):
    table = np.asarray(table, np.float32)
    head = table.astype(ml_dtypes.bfloat16)
    return np.stack([head, (table - head.astype(np.float32)).astype(ml_dtypes.bfloat16)])


def grid_table(length):
    points = np.arange(length)
    phases = (points[:, None] * points[None, :] % length) * (2.0 * np.pi / length)
    return pieces_of(np.stack([np.cos(phases), np.sin(phases)]))


def line_table(length, blocks, planes, width):
    kz = np.arange(length)
    out = np.zeros((2, length, blocks, width), np.float64)
    for block in range(blocks):
        z = block * planes + np.arange(planes)
        phases = (kz[:, None] * z[None, :] % length) * (2.0 * np.pi / length)
        out[0, :, block, :planes] = np.cos(phases)
        out[0, :, block, width // 2 : width // 2 + planes] = np.sin(phases)
        out[1, :, block, :planes] = -np.sin(phases)
        out[1, :, block, width // 2 : width // 2 + planes] = np.cos(phases)
    return pieces_of(out.reshape(2, length, blocks * width))


def split(values):
    head = values.astype(BF16)
    return head, (values - head.astype(F32)).astype(BF16)


def stacked(values):
    head, rest = split(values)
    return jnp.concatenate([head.astype(F32), rest.astype(F32)], axis=0).astype(BF16)


def doubled(values):
    values = values.astype(BF16)
    return jnp.concatenate([values, values], axis=1)


def dot(left, right):
    return lax.dot_general(left, right, (((1,), (0,)), ((), ())), preferred_element_type=F32)


def dot_nt(left, right):
    return lax.dot_general(left, right, (((1,), (1,)), ((), ())), preferred_element_type=F32)


def lane_ids(rows):
    return lax.broadcasted_iota(jnp.int32, (rows, LANES), 1)


def used_slots(count_ref, slots):
    used = count_ref[lax.axis_index("ga")] - lax.axis_index("band") * slots
    return lax.broadcasted_iota(jnp.int32, (slots, 1), 0) < used


def project_kernel(
    sizes,
    count_hbm,
    orbitals_hbm,
    projectors_hbm,
    table_hbm,
    site_hbm,
    grid_hbm,
    out_ref,
    x_ref,
    plus_ref,
    minus_ref,
    *scratch,
):
    blocks, groups, orbitals, slots, length, projectors, width = sizes
    count_ref, orbitals_ref, projectors_ref, table_ref, site_ref, grid_ref, coef, spread, small_sems, sems = scratch
    kinds = orbitals * 2
    devices = blocks * groups
    share = projectors // devices
    small = [
        pltpu.make_async_copy(count_hbm, count_ref, small_sems.at[0]),
        pltpu.make_async_copy(orbitals_hbm, orbitals_ref, small_sems.at[1]),
        pltpu.make_async_copy(site_hbm, site_ref, small_sems.at[2]),
        pltpu.make_async_copy(grid_hbm, grid_ref, small_sems.at[3]),
        pltpu.make_async_copy(table_hbm, table_ref, small_sems.at[4]),
    ]
    copies = []
    for piece in range(2 * slots):
        rows = pl.ds(piece * length, length)
        copies.append(pltpu.make_async_copy(projectors_hbm.at[rows], projectors_ref.at[rows], sems.at[piece]))
    for copy in small + copies:
        copy.start()
    small[0].wait()
    small[1].wait()
    used = used_slots(count_ref, slots)
    for n in range(orbitals):
        for part in range(2):
            values = jnp.where(used, orbitals_ref[n, part].astype(F32), 0.0)
            at = (n * 2 + part) * slots
            coef[0, at : at + slots, :] = values
            at = (n * 2 + 1 - part) * slots
            coef[1, at : at + slots, :] = values if part == 1 else -values
            at = n * slots
            coef[2 + part, at : at + slots, :] = values
    small[2].wait()
    small[3].wait()
    make_tables(site_ref, grid_ref, x_ref, plus_ref, minus_ref)
    small[4].wait()
    columns = jnp.zeros((orbitals * slots, blocks * width), F32)
    for part in range(2):
        left = coef[2 + part, : orbitals * slots, :].astype(BF16)
        columns += dot(left, table_ref[0, part]) + dot(left, table_ref[1, part])
    row_slot = lax.broadcasted_iota(jnp.int32, (kinds * slots, length), 0) % slots
    sums = jnp.zeros((kinds * slots, projectors), F32)
    for part in range(2):
        rows = coef[part]
        for slot in range(slots):
            piece = part * slots + slot
            left = jnp.where(row_slot == slot, rows, 0.0).astype(BF16)
            copies[piece].wait()
            sums += dot(left, projectors_ref[piece * length : (piece + 1) * length, :])
    for row in range(kinds):
        spread[row : row + 1, :] = jnp.sum(sums[row * slots : (row + 1) * slots, :], axis=0, keepdims=True)
    lanes = lane_ids(slots)
    groups_of_rows = kinds // slots
    for block in range(blocks):
        at = block * width
        base = at // LANES * LANES
        chunk = pltpu.roll(columns[:, base : base + LANES], (base - at) % LANES, 1)
        for group in range(groups):
            device = block * groups + group
            piece = jnp.where(lanes < width, chunk[group * slots : (group + 1) * slots, :], 0.0)
            first = device * share
            base = first // LANES * LANES
            for rows in range(groups_of_rows):
                low = width + rows * share
                own = spread[rows * slots : (rows + 1) * slots, base : base + LANES]
                own = pltpu.roll(own, (base + low - first) % LANES, 1)
                piece = jnp.where((lanes >= low) & (lanes < low + share), own, piece)
            out_ref[device] = piece


def couple_kernel(projectors, atom_ref, couplings_ref, coupled_ref):
    eye = lax.broadcasted_iota(jnp.int32, (LANES, LANES), 0) == lane_ids(LANES)
    atoms = atom_ref[...].astype(F32)
    for at in range(0, projectors, LANES):
        along = jnp.sum(jnp.where(eye, atoms[:, at : at + LANES], 0.0), axis=1, keepdims=True)
        masked = jnp.where(along == atoms, couplings_ref[at : at + LANES, :], 0.0)
        for other in range(0, projectors, LANES):
            head, rest = split(masked[:, other : other + LANES].T)
            coupled_ref[0, other : other + LANES, at : at + LANES] = head
            coupled_ref[1, other : other + LANES, at : at + LANES] = rest


def make_tables(site_ref, grid_ref, x_ref, plus_ref, minus_ref):
    columns = site_ref.shape[1]
    length = x_ref.shape[0]
    wide = minus_ref.shape[0] // 4
    eye = lax.broadcasted_iota(jnp.int32, (LANES, LANES), 0) == lane_ids(LANES)
    plus_ref[:, length:wide] = jnp.zeros((4 * columns, wide - length), BF16)
    plus_ref[:, wide + length :] = jnp.zeros((4 * columns, wide - length), BF16)
    for part in range(4):
        minus_ref[part * wide + length : (part + 1) * wide, :] = jnp.zeros((wide - length, 2 * columns), BF16)
    row_ids = lax.broadcasted_iota(jnp.int32, (length, LANES), 0).astype(F32)
    column_ids = lax.broadcasted_iota(jnp.int32, (LANES, length), 1).astype(F32)
    for at in range(0, columns, LANES):
        site = site_ref[:, at : at + LANES].astype(F32)
        site_x = jnp.floor((site + 0.5) * (1.0 / length))
        site_y = site - site_x * length
        hot_x = (row_ids == site_x).astype(F32).astype(BF16)
        hot_y = (row_ids == site_y).astype(F32).astype(BF16)
        along = jnp.sum(jnp.where(eye, site_y, 0.0), axis=1, keepdims=True)
        hot_y_rows = (column_ids == along).astype(F32).astype(BF16)
        for part in range(2):
            value = dot(grid_ref[0, part], hot_x) + dot(grid_ref[1, part], hot_x)
            x_ref[:, part * columns + at : part * columns + at + LANES] = value
        for piece in range(2):
            cosine = dot(hot_y_rows, grid_ref[piece, 0])
            sine = dot(hot_y_rows, grid_ref[piece, 1])
            rows = pl.ds(piece * 2 * columns + at, LANES)
            plus_ref[rows, :length] = cosine.astype(BF16)
            plus_ref[rows, wide : wide + length] = sine.astype(BF16)
            rows = pl.ds((piece * 2 + 1) * columns + at, LANES)
            plus_ref[rows, :length] = (-sine).astype(BF16)
            plus_ref[rows, wide : wide + length] = cosine.astype(BF16)
            cosine = dot(grid_ref[piece, 0], hot_y)
            sine = dot(grid_ref[piece, 1], hot_y)
            rows = pl.ds(piece * 2 * wide, length)
            minus_ref[rows, at : at + LANES] = cosine.astype(BF16)
            minus_ref[rows, columns + at : columns + at + LANES] = (-sine).astype(BF16)
            rows = pl.ds((piece * 2 + 1) * wide, length)
            minus_ref[rows, at : at + LANES] = sine.astype(BF16)
            minus_ref[rows, columns + at : columns + at + LANES] = cosine.astype(BF16)


def plane_kernel(sizes, columns_ref, x_ref, plus_ref, minus_ref, potential_ref, out_ref, gathered, lines, back):
    devices, slots, planes, length, wide, width, carried, batch = sizes
    count = devices * slots
    total = jnp.zeros((slots, LANES), F32)
    for device in range(devices):
        piece = columns_ref[device]
        gathered[device * slots : (device + 1) * slots, :] = piece
        total += piece
    for at in range(0, count, LANES):
        lines[:, at : at + LANES] = gathered[at : at + LANES, :].T
    back[...] = jnp.zeros_like(back)
    cosine = x_ref[:, :count]
    sine = x_ref[:, count:]
    padding = jnp.zeros((length, wide - length), F32)
    for i in range(planes // batch):
        left = []
        for plane in range(i * batch, (i + 1) * batch):
            real = lines[plane : plane + 1, :]
            imag = lines[plane + width // 2 : plane + width // 2 + 1, :]
            left.append(jnp.concatenate([cosine * real - sine * imag, cosine * imag + sine * real], axis=1))
        left = doubled(jnp.concatenate(left, axis=0))
        field = dot(left, plus_ref[...])
        weights = []
        for plane in range(i * batch, (i + 1) * batch):
            own = jnp.concatenate([potential_ref[plane], padding], axis=1)
            weights.append(jnp.concatenate([own, own], axis=1))
        left = doubled(field * jnp.concatenate(weights, axis=0))
        half = dot(left, minus_ref[...])
        for j in range(batch):
            plane = i * batch + j
            real = half[j * length : (j + 1) * length, :count]
            imag = half[j * length : (j + 1) * length, count:]
            back[plane : plane + 1, :] = jnp.sum(cosine * real + sine * imag, axis=0, keepdims=True)
            at = plane + width // 2
            back[at : at + 1, :] = jnp.sum(cosine * imag - sine * real, axis=0, keepdims=True)
    for at in range(0, count, LANES):
        gathered[at : at + LANES, :] = back[:, at : at + LANES].T
    lanes = lane_ids(slots)
    for device in range(devices):
        piece = gathered[device * slots : (device + 1) * slots, :]
        out_ref[device] = jnp.where((lanes >= width) & (lanes < carried), total, piece)


def finish_kernel(sizes, count_ref, columns_ref, coupled_ref, projectors_ref, table_ref, out_ref, summed, lined, mixed):
    blocks, groups, orbitals, slots, length, projectors, width, normalizer = sizes
    kinds = orbitals * 2
    devices = blocks * groups
    share = projectors // devices
    groups_of_rows = kinds // slots
    lanes = lane_ids(slots)
    for chunk in range(projectors // LANES):
        in_chunk = range(chunk * LANES // share, (chunk + 1) * LANES // share)
        for rows in range(groups_of_rows):
            low = width + rows * share
            total = jnp.zeros((slots, LANES), F32)
            for device in in_chunk:
                own = columns_ref[device]
                own = pltpu.roll(jnp.where((lanes >= low) & (lanes < low + share), own, 0.0), (device * share - low) % LANES, 1)
                total += own
            summed[rows * slots : (rows + 1) * slots, chunk * LANES : (chunk + 1) * LANES] = total
    for n in range(orbitals):
        at = kinds + n * 2
        summed[at : at + 1, :] = -summed[n * 2 + 1 : n * 2 + 2, :]
        summed[at + 1 : at + 2, :] = summed[n * 2 : n * 2 + 1, :]
    both = stacked(summed[...])
    head = dot(both, coupled_ref[0])
    rest = dot(both, coupled_ref[1])
    weighted = (head[: 2 * kinds] + (head[2 * kinds :] + rest[: 2 * kinds])).astype(BF16)
    for slot in range(slots):
        rows = projectors_ref[slot * length : (slot + 1) * length, :]
        value = dot_nt(weighted, rows)[:kinds]
        rows = projectors_ref[(slots + slot) * length : (slots + slot + 1) * length, :]
        mixed[slot * kinds : (slot + 1) * kinds, :] = value + dot_nt(weighted, rows)[kinds:]
    for chunk in range(blocks * width // LANES):
        for group in range(groups):
            total = jnp.zeros((slots, LANES), F32)
            for inner in range(LANES // width):
                block = chunk * (LANES // width) + inner
                own = jnp.where(lanes < width, columns_ref[block * groups + group], 0.0)
                total += pltpu.roll(own, inner * width, 1)
            lined[group * slots : (group + 1) * slots, chunk * LANES : (chunk + 1) * LANES] = total
    both = stacked(lined[...])
    rows_of_lines = groups * slots
    used = used_slots(count_ref, slots)
    for part in range(2):
        head = dot_nt(both, table_ref[0, part])
        rest = dot_nt(both, table_ref[1, part])
        local = (head[:rows_of_lines] + (head[rows_of_lines:] + rest[:rows_of_lines])) * normalizer
        for n in range(orbitals):
            row = n * 2 + part
            for slot in range(slots):
                at = n * slots + slot
                value = local[at : at + 1, :] + mixed[slot * kinds + row : slot * kinds + row + 1, :]
                out_ref[n, part, slot : slot + 1, :] = value
            out_ref[n, part] = jnp.where(used, out_ref[n, part], 0.0)


def on_device(orbitals, projectors, potential, couplings, atom_index, column_site, column_count):
    blocks = lax.axis_size("ga")
    groups = lax.axis_size("band")
    devices = blocks * groups
    orbital_count, _, slots, length = orbitals.shape
    planes = potential.shape[0]
    projector_count = projectors.shape[0]
    columns = column_site.shape[0]
    kinds = orbital_count * 2
    assert orbital_count == groups and kinds % slots == 0 and columns % LANES == 0
    share = projector_count // devices
    width = 2
    while width < 2 * planes:
        width *= 2
    carried = width + kinds // slots * share
    assert carried <= LANES and width <= LANES and share * devices == projector_count
    wide = -(-length // LANES) * LANES
    flat = jnp.transpose(projectors, (1, 2, 3, 0)).reshape(2 * slots * length, projector_count)
    z_table = line_table(length, blocks, planes, width)
    batch = next(i for i in (4, 3, 2, 1) if planes % i == 0) if columns <= 512 else 1
    smem = pl.BlockSpec(memory_space=pltpu.SMEM)
    vmem = pl.BlockSpec(memory_space=pltpu.VMEM)
    hbm = pl.BlockSpec(memory_space=pltpu.HBM)
    params = pltpu.CompilerParams(vmem_limit_bytes=56 * 1024 * 1024)
    small = pltpu.CompilerParams(vmem_limit_bytes=40 * 1024 * 1024)
    payload = jax.ShapeDtypeStruct((devices, slots, LANES), F32)

    grid = grid_table(length)
    sites = column_site.reshape(1, columns)
    sent, x_rows, plus, minus = pl.pallas_call(
        functools.partial(
            project_kernel, (blocks, groups, orbital_count, slots, length, projector_count, width)
        ),
        out_shape=(
            payload,
            jax.ShapeDtypeStruct((length, 2 * columns), F32),
            jax.ShapeDtypeStruct((4 * columns, 2 * wide), BF16),
            jax.ShapeDtypeStruct((4 * wide, 2 * columns), BF16),
        ),
        in_specs=[hbm] * 6,
        out_specs=(vmem,) * 4,
        scratch_shapes=[
            pltpu.SMEM(column_count.shape, jnp.int32),
            pltpu.VMEM(orbitals.shape, BF16),
            pltpu.VMEM(flat.shape, BF16),
            pltpu.VMEM(z_table.shape, BF16),
            pltpu.VMEM(sites.shape, jnp.int32),
            pltpu.VMEM(grid.shape, BF16),
            pltpu.VMEM((4, kinds * slots, length), F32),
            pltpu.VMEM((kinds, projector_count), F32),
            pltpu.SemaphoreType.DMA((5,)),
            pltpu.SemaphoreType.DMA((2 * slots,)),
        ],
        compiler_params=params,
        name="project",
    )(column_count, orbitals, flat, z_table, sites, grid)
    arrived = lax.all_to_all(sent, ("ga", "band"), split_axis=0, concat_axis=0, tiled=True)

    coupled = pl.pallas_call(
        functools.partial(couple_kernel, projector_count),
        out_shape=jax.ShapeDtypeStruct((2, projector_count, projector_count), BF16),
        in_specs=[vmem] * 2,
        out_specs=vmem,
        compiler_params=params,
        name="couple",
    )(atom_index.reshape(1, projector_count), couplings)

    sent = pl.pallas_call(
        functools.partial(plane_kernel, (devices, slots, planes, length, wide, width, carried, batch)),
        out_shape=payload,
        in_specs=[vmem] * 5,
        out_specs=vmem,
        scratch_shapes=[
            pltpu.VMEM((columns, LANES), F32),
            pltpu.VMEM((LANES, columns), F32),
            pltpu.VMEM((LANES, columns), F32),
        ],
        compiler_params=small,
        name="planes",
    )(arrived, x_rows, plus, minus, potential)
    arrived = lax.all_to_all(sent, ("ga", "band"), split_axis=0, concat_axis=0, tiled=True)

    normalizer = 1.0 / float(length**3)
    return pl.pallas_call(
        functools.partial(
            finish_kernel,
            (blocks, groups, orbital_count, slots, length, projector_count, width, normalizer),
        ),
        out_shape=jax.ShapeDtypeStruct(orbitals.shape, F32),
        in_specs=[smem] + [vmem] * 4,
        out_specs=vmem,
        scratch_shapes=[
            pltpu.VMEM((2 * kinds, projector_count), F32),
            pltpu.VMEM((groups * slots, blocks * width), F32),
            pltpu.VMEM((slots * kinds, length), F32),
        ],
        compiler_params=small,
        name="finish",
    )(column_count, arrived, coupled, flat, z_table)


def solution(mesh):
    return jax.shard_map(
        on_device,
        mesh=mesh,
        in_specs=(
            P(None, None, ("ga", "band"), None),
            P(None, None, ("ga", "band"), None),
            P("ga", None, None),
            P(),
            P(),
            P(),
            P(),
        ),
        out_specs=P(None, None, ("ga", "band"), None),
        check_vma=False,
    )
```

```python
import functools

import jax
import jax.numpy as jnp
import ml_dtypes
import numpy as np
from jax import lax
from jax.experimental import pallas as pl
from jax.experimental.pallas import tpu as pltpu
from jax.sharding import PartitionSpec as P

LANES = 128
BF16 = jnp.bfloat16
F32 = jnp.float32


def pieces_of(table):
    table = np.asarray(table, np.float32)
    head = table.astype(ml_dtypes.bfloat16)
    return np.stack([head, (table - head.astype(np.float32)).astype(ml_dtypes.bfloat16)])


def grid_table(length):
    points = np.arange(length)
    phases = (points[:, None] * points[None, :] % length) * (2.0 * np.pi / length)
    return pieces_of(np.stack([np.cos(phases), np.sin(phases)]))


def line_table(length, blocks, planes, width):
    kz = np.arange(length)
    out = np.zeros((2, length, blocks, width), np.float64)
    for block in range(blocks):
        z = block * planes + np.arange(planes)
        phases = (kz[:, None] * z[None, :] % length) * (2.0 * np.pi / length)
        out[0, :, block, :planes] = np.cos(phases)
        out[0, :, block, width // 2 : width // 2 + planes] = np.sin(phases)
        out[1, :, block, :planes] = -np.sin(phases)
        out[1, :, block, width // 2 : width // 2 + planes] = np.cos(phases)
    return pieces_of(out.reshape(2, length, blocks * width))


def split(values):
    head = values.astype(BF16)
    return head, (values - head.astype(F32)).astype(BF16)


def stacked(values):
    head, rest = split(values)
    return jnp.concatenate([head.astype(F32), rest.astype(F32)], axis=0).astype(BF16)


def doubled(values):
    values = values.astype(BF16)
    return jnp.concatenate([values, values], axis=1)


def dot(left, right):
    return lax.dot_general(left, right, (((1,), (0,)), ((), ())), preferred_element_type=F32)


def dot_nt(left, right):
    return lax.dot_general(left, right, (((1,), (1,)), ((), ())), preferred_element_type=F32)


def lane_ids(rows):
    return lax.broadcasted_iota(jnp.int32, (rows, LANES), 1)


def used_slots(count_ref, slots):
    used = count_ref[lax.axis_index("ga")] - lax.axis_index("band") * slots
    return lax.broadcasted_iota(jnp.int32, (slots, 1), 0) < used


def project_kernel(
    sizes,
    count_hbm,
    orbitals_hbm,
    projectors_hbm,
    table_hbm,
    site_hbm,
    grid_hbm,
    out_ref,
    x_hbm,
    plus_hbm,
    minus_hbm,
    *scratch,
):
    blocks, groups, orbitals, slots, length, projectors, width = sizes
    count_ref, orbitals_ref, projectors_ref, table_ref, site_ref, grid_ref, *scratch = scratch
    x_ref, plus_ref, minus_ref, coef, spread, small_sems, sems, out_sems = scratch
    kinds = orbitals * 2
    devices = blocks * groups
    share = projectors // devices
    small = [
        pltpu.make_async_copy(count_hbm, count_ref, small_sems.at[0]),
        pltpu.make_async_copy(orbitals_hbm, orbitals_ref, small_sems.at[1]),
        pltpu.make_async_copy(site_hbm, site_ref, small_sems.at[2]),
        pltpu.make_async_copy(grid_hbm, grid_ref, small_sems.at[3]),
        pltpu.make_async_copy(table_hbm, table_ref, small_sems.at[4]),
    ]
    copies = []
    for piece in range(2 * slots):
        rows = pl.ds(piece * length, length)
        copies.append(pltpu.make_async_copy(projectors_hbm.at[rows], projectors_ref.at[rows], sems.at[piece]))
    for copy in small + copies:
        copy.start()
    small[0].wait()
    small[1].wait()
    used = used_slots(count_ref, slots)
    for n in range(orbitals):
        for part in range(2):
            values = jnp.where(used, orbitals_ref[n, part].astype(F32), 0.0)
            at = (n * 2 + part) * slots
            coef[0, at : at + slots, :] = values
            at = (n * 2 + 1 - part) * slots
            coef[1, at : at + slots, :] = values if part == 1 else -values
            at = n * slots
            coef[2 + part, at : at + slots, :] = values
    small[2].wait()
    small[3].wait()
    make_tables(site_ref, grid_ref, x_ref, plus_ref, minus_ref)
    pairs = ((x_ref, x_hbm), (plus_ref, plus_hbm), (minus_ref, minus_hbm))
    outgoing = [pltpu.make_async_copy(source, target, out_sems.at[i]) for i, (source, target) in enumerate(pairs)]
    for copy in outgoing:
        copy.start()
    small[4].wait()
    columns = jnp.zeros((orbitals * slots, blocks * width), F32)
    for part in range(2):
        left = coef[2 + part, : orbitals * slots, :].astype(BF16)
        columns += dot(left, table_ref[0, part]) + dot(left, table_ref[1, part])
    row_slot = lax.broadcasted_iota(jnp.int32, (kinds * slots, length), 0) % slots
    sums = jnp.zeros((kinds * slots, projectors), F32)
    for part in range(2):
        rows = coef[part]
        for slot in range(slots):
            piece = part * slots + slot
            left = jnp.where(row_slot == slot, rows, 0.0).astype(BF16)
            copies[piece].wait()
            sums += dot(left, projectors_ref[piece * length : (piece + 1) * length, :])
    for row in range(kinds):
        spread[row : row + 1, :] = jnp.sum(sums[row * slots : (row + 1) * slots, :], axis=0, keepdims=True)
    lanes = lane_ids(slots)
    groups_of_rows = kinds // slots
    for block in range(blocks):
        at = block * width
        base = at // LANES * LANES
        chunk = pltpu.roll(columns[:, base : base + LANES], (base - at) % LANES, 1)
        for group in range(groups):
            device = block * groups + group
            piece = jnp.where(lanes < width, chunk[group * slots : (group + 1) * slots, :], 0.0)
            first = device * share
            base = first // LANES * LANES
            for rows in range(groups_of_rows):
                low = width + rows * share
                own = spread[rows * slots : (rows + 1) * slots, base : base + LANES]
                own = pltpu.roll(own, (base + low - first) % LANES, 1)
                piece = jnp.where((lanes >= low) & (lanes < low + share), own, piece)
            out_ref[device] = piece
    for copy in outgoing:
        copy.wait()


def make_tables(site_ref, grid_ref, x_ref, plus_ref, minus_ref):
    columns = site_ref.shape[1]
    length = x_ref.shape[0]
    wide = minus_ref.shape[0] // 4
    eye = lax.broadcasted_iota(jnp.int32, (LANES, LANES), 0) == lane_ids(LANES)
    plus_ref[:, length:wide] = jnp.zeros((4 * columns, wide - length), BF16)
    plus_ref[:, wide + length :] = jnp.zeros((4 * columns, wide - length), BF16)
    for part in range(4):
        minus_ref[part * wide + length : (part + 1) * wide, :] = jnp.zeros((wide - length, 2 * columns), BF16)
    row_ids = lax.broadcasted_iota(jnp.int32, (length, LANES), 0).astype(F32)
    column_ids = lax.broadcasted_iota(jnp.int32, (LANES, length), 1).astype(F32)
    for at in range(0, columns, LANES):
        site = site_ref[:, at : at + LANES].astype(F32)
        site_x = jnp.floor((site + 0.5) * (1.0 / length))
        site_y = site - site_x * length
        hot_x = (row_ids == site_x).astype(F32).astype(BF16)
        hot_y = (row_ids == site_y).astype(F32).astype(BF16)
        along = jnp.sum(jnp.where(eye, site_y, 0.0), axis=1, keepdims=True)
        hot_y_rows = (column_ids == along).astype(F32).astype(BF16)
        for part in range(2):
            value = dot(grid_ref[0, part], hot_x) + dot(grid_ref[1, part], hot_x)
            x_ref[:, part * columns + at : part * columns + at + LANES] = value
        for piece in range(2):
            cosine = dot(hot_y_rows, grid_ref[piece, 0])
            sine = dot(hot_y_rows, grid_ref[piece, 1])
            rows = pl.ds(piece * 2 * columns + at, LANES)
            plus_ref[rows, :length] = cosine.astype(BF16)
            plus_ref[rows, wide : wide + length] = sine.astype(BF16)
            rows = pl.ds((piece * 2 + 1) * columns + at, LANES)
            plus_ref[rows, :length] = (-sine).astype(BF16)
            plus_ref[rows, wide : wide + length] = cosine.astype(BF16)
            cosine = dot(grid_ref[piece, 0], hot_y)
            sine = dot(grid_ref[piece, 1], hot_y)
            rows = pl.ds(piece * 2 * wide, length)
            minus_ref[rows, at : at + LANES] = cosine.astype(BF16)
            minus_ref[rows, columns + at : columns + at + LANES] = (-sine).astype(BF16)
            rows = pl.ds((piece * 2 + 1) * wide, length)
            minus_ref[rows, at : at + LANES] = sine.astype(BF16)
            minus_ref[rows, columns + at : columns + at + LANES] = cosine.astype(BF16)


def plane_kernel(sizes, columns_hbm, x_hbm, plus_hbm, minus_hbm, potential_hbm, out_ref, *scratch):
    devices, slots, planes, length, wide, width, carried, batch = sizes
    columns_ref, x_ref, plus_ref, minus_ref, potential_ref, gathered, lines, back, table_sems, sems = scratch
    count = devices * slots
    pairs = ((columns_hbm, columns_ref), (x_hbm, x_ref), (plus_hbm, plus_ref), (minus_hbm, minus_ref))
    tables = [pltpu.make_async_copy(source, target, table_sems.at[i]) for i, (source, target) in enumerate(pairs)]
    copies = []
    for i in range(planes // batch):
        some = pl.ds(i * batch, batch)
        copies.append(pltpu.make_async_copy(potential_hbm.at[some], potential_ref.at[some], sems.at[i]))
    for copy in tables[:3] + copies[:1] + tables[3:] + copies[1:]:
        copy.start()
    tables[0].wait()
    total = jnp.zeros((slots, LANES), F32)
    for device in range(devices):
        piece = columns_ref[device]
        gathered[device * slots : (device + 1) * slots, :] = piece
        total += piece
    for at in range(0, count, LANES):
        lines[:, at : at + LANES] = gathered[at : at + LANES, :].T
    back[...] = jnp.zeros_like(back)
    tables[1].wait()
    cosine = x_ref[:, :count]
    sine = x_ref[:, count:]
    padding = jnp.zeros((length, wide - length), F32)
    for i in range(planes // batch):
        left = []
        for plane in range(i * batch, (i + 1) * batch):
            real = lines[plane : plane + 1, :]
            imag = lines[plane + width // 2 : plane + width // 2 + 1, :]
            left.append(jnp.concatenate([cosine * real - sine * imag, cosine * imag + sine * real], axis=1))
        left = doubled(jnp.concatenate(left, axis=0))
        if i == 0:
            tables[2].wait()
        field = dot(left, plus_ref[...])
        copies[i].wait()
        weights = []
        for plane in range(i * batch, (i + 1) * batch):
            own = jnp.concatenate([potential_ref[plane], padding], axis=1)
            weights.append(jnp.concatenate([own, own], axis=1))
        left = doubled(field * jnp.concatenate(weights, axis=0))
        if i == 0:
            tables[3].wait()
        half = dot(left, minus_ref[...])
        for j in range(batch):
            plane = i * batch + j
            real = half[j * length : (j + 1) * length, :count]
            imag = half[j * length : (j + 1) * length, count:]
            back[plane : plane + 1, :] = jnp.sum(cosine * real + sine * imag, axis=0, keepdims=True)
            at = plane + width // 2
            back[at : at + 1, :] = jnp.sum(cosine * imag - sine * real, axis=0, keepdims=True)
    for at in range(0, count, LANES):
        gathered[at : at + LANES, :] = back[:, at : at + LANES].T
    lanes = lane_ids(slots)
    for device in range(devices):
        piece = gathered[device * slots : (device + 1) * slots, :]
        out_ref[device] = jnp.where((lanes >= width) & (lanes < carried), total, piece)


def finish_kernel(
    sizes, count_ref, columns_ref, atom_ref, couplings_ref, projectors_ref, table_ref, out_ref, summed, lined, mixed
):
    blocks, groups, orbitals, slots, length, projectors, width, normalizer = sizes
    kinds = orbitals * 2
    devices = blocks * groups
    share = projectors // devices
    groups_of_rows = kinds // slots
    lanes = lane_ids(slots)
    for chunk in range(projectors // LANES):
        in_chunk = range(chunk * LANES // share, (chunk + 1) * LANES // share)
        for rows in range(groups_of_rows):
            low = width + rows * share
            total = jnp.zeros((slots, LANES), F32)
            for device in in_chunk:
                own = columns_ref[device]
                own = pltpu.roll(jnp.where((lanes >= low) & (lanes < low + share), own, 0.0), (device * share - low) % LANES, 1)
                total += own
            summed[rows * slots : (rows + 1) * slots, chunk * LANES : (chunk + 1) * LANES] = total
    for n in range(orbitals):
        at = kinds + n * 2
        summed[at : at + 1, :] = -summed[n * 2 + 1 : n * 2 + 2, :]
        summed[at + 1 : at + 2, :] = summed[n * 2 : n * 2 + 1, :]
    both = stacked(summed[...])
    atoms = atom_ref[...].astype(F32)
    eye = lax.broadcasted_iota(jnp.int32, (LANES, LANES), 0) == lane_ids(LANES)
    along = []
    for at in range(0, projectors, LANES):
        along.append(jnp.sum(jnp.where(eye, atoms[:, at : at + LANES], 0.0), axis=1, keepdims=True))
    head, rest = split(jnp.where(jnp.concatenate(along, axis=0) == atoms, couplings_ref[...], 0.0))
    head = dot_nt(both, head)
    rest = dot_nt(both, rest)
    weighted = (head[: 2 * kinds] + (head[2 * kinds :] + rest[: 2 * kinds])).astype(BF16)
    for slot in range(slots):
        rows = projectors_ref[slot * length : (slot + 1) * length, :]
        value = dot_nt(weighted, rows)[:kinds]
        rows = projectors_ref[(slots + slot) * length : (slots + slot + 1) * length, :]
        mixed[slot * kinds : (slot + 1) * kinds, :] = value + dot_nt(weighted, rows)[kinds:]
    for chunk in range(blocks * width // LANES):
        for group in range(groups):
            total = jnp.zeros((slots, LANES), F32)
            for inner in range(LANES // width):
                block = chunk * (LANES // width) + inner
                own = jnp.where(lanes < width, columns_ref[block * groups + group], 0.0)
                total += pltpu.roll(own, inner * width, 1)
            lined[group * slots : (group + 1) * slots, chunk * LANES : (chunk + 1) * LANES] = total
    both = stacked(lined[...])
    rows_of_lines = groups * slots
    used = used_slots(count_ref, slots)
    for part in range(2):
        head = dot_nt(both, table_ref[0, part])
        rest = dot_nt(both, table_ref[1, part])
        local = (head[:rows_of_lines] + (head[rows_of_lines:] + rest[:rows_of_lines])) * normalizer
        for n in range(orbitals):
            row = n * 2 + part
            for slot in range(slots):
                at = n * slots + slot
                value = local[at : at + 1, :] + mixed[slot * kinds + row : slot * kinds + row + 1, :]
                out_ref[n, part, slot : slot + 1, :] = value
            out_ref[n, part] = jnp.where(used, out_ref[n, part], 0.0)


def on_device(orbitals, projectors, potential, couplings, atom_index, column_site, column_count):
    blocks = lax.axis_size("ga")
    groups = lax.axis_size("band")
    devices = blocks * groups
    orbital_count, _, slots, length = orbitals.shape
    planes = potential.shape[0]
    projector_count = projectors.shape[0]
    columns = column_site.shape[0]
    kinds = orbital_count * 2
    assert orbital_count == groups and kinds % slots == 0 and columns % LANES == 0
    share = projector_count // devices
    width = 2
    while width < 2 * planes:
        width *= 2
    carried = width + kinds // slots * share
    assert carried <= LANES and width <= LANES and share * devices == projector_count
    wide = -(-length // LANES) * LANES
    flat = jnp.transpose(projectors, (1, 2, 3, 0)).reshape(2 * slots * length, projector_count)
    z_table = line_table(length, blocks, planes, width)
    batch = next(i for i in (4, 3, 2, 1) if planes % i == 0) if columns <= 512 else 1
    smem = pl.BlockSpec(memory_space=pltpu.SMEM)
    vmem = pl.BlockSpec(memory_space=pltpu.VMEM)
    hbm = pl.BlockSpec(memory_space=pltpu.HBM)
    params = pltpu.CompilerParams(vmem_limit_bytes=56 * 1024 * 1024)
    small = pltpu.CompilerParams(vmem_limit_bytes=40 * 1024 * 1024)
    payload = jax.ShapeDtypeStruct((devices, slots, LANES), F32)

    grid = grid_table(length)
    sites = column_site.reshape(1, columns)
    tables = (
        jax.ShapeDtypeStruct((length, 2 * columns), F32),
        jax.ShapeDtypeStruct((4 * columns, 2 * wide), BF16),
        jax.ShapeDtypeStruct((4 * wide, 2 * columns), BF16),
    )
    sent, x_rows, plus, minus = pl.pallas_call(
        functools.partial(
            project_kernel, (blocks, groups, orbital_count, slots, length, projector_count, width)
        ),
        out_shape=(payload,) + tables,
        in_specs=[hbm] * 6,
        out_specs=(vmem,) + (hbm,) * 3,
        scratch_shapes=[
            pltpu.SMEM(column_count.shape, jnp.int32),
            pltpu.VMEM(orbitals.shape, BF16),
            pltpu.VMEM(flat.shape, BF16),
            pltpu.VMEM(z_table.shape, BF16),
            pltpu.VMEM(sites.shape, jnp.int32),
            pltpu.VMEM(grid.shape, BF16),
        ]
        + [pltpu.VMEM(table.shape, table.dtype) for table in tables]
        + [
            pltpu.VMEM((4, kinds * slots, length), F32),
            pltpu.VMEM((kinds, projector_count), F32),
            pltpu.SemaphoreType.DMA((5,)),
            pltpu.SemaphoreType.DMA((2 * slots,)),
            pltpu.SemaphoreType.DMA((3,)),
        ],
        compiler_params=params,
        name="project",
    )(column_count, orbitals, flat, z_table, sites, grid)
    arrived = lax.all_to_all(sent, ("ga", "band"), split_axis=0, concat_axis=0, tiled=True)

    sent = pl.pallas_call(
        functools.partial(plane_kernel, (devices, slots, planes, length, wide, width, carried, batch)),
        out_shape=payload,
        in_specs=[hbm] * 5,
        out_specs=vmem,
        scratch_shapes=[pltpu.VMEM(payload.shape, F32)]
        + [pltpu.VMEM(table.shape, table.dtype) for table in tables]
        + [
            pltpu.VMEM(potential.shape, F32),
            pltpu.VMEM((columns, LANES), F32),
            pltpu.VMEM((LANES, columns), F32),
            pltpu.VMEM((LANES, columns), F32),
            pltpu.SemaphoreType.DMA((4,)),
            pltpu.SemaphoreType.DMA((planes // batch,)),
        ],
        compiler_params=pltpu.CompilerParams(vmem_limit_bytes=60 * 1024 * 1024),
        name="planes",
    )(arrived, x_rows, plus, minus, potential)
    arrived = lax.all_to_all(sent, ("ga", "band"), split_axis=0, concat_axis=0, tiled=True)

    normalizer = 1.0 / float(length**3)
    return pl.pallas_call(
        functools.partial(
            finish_kernel,
            (blocks, groups, orbital_count, slots, length, projector_count, width, normalizer),
        ),
        out_shape=jax.ShapeDtypeStruct(orbitals.shape, F32),
        in_specs=[smem] + [vmem] * 5,
        out_specs=vmem,
        scratch_shapes=[
            pltpu.VMEM((2 * kinds, projector_count), F32),
            pltpu.VMEM((groups * slots, blocks * width), F32),
            pltpu.VMEM((slots * kinds, length), F32),
        ],
        compiler_params=small,
        name="finish",
    )(column_count, arrived, atom_index.reshape(1, projector_count), couplings, flat, z_table)


def solution(mesh):
    return jax.shard_map(
        on_device,
        mesh=mesh,
        in_specs=(
            P(None, None, ("ga", "band"), None),
            P(None, None, ("ga", "band"), None),
            P("ga", None, None),
            P(),
            P(),
            P(),
            P(),
        ),
        out_specs=P(None, None, ("ga", "band"), None),
        check_vma=False,
    )
```

```python
import functools

import jax
import jax.numpy as jnp
import ml_dtypes
import numpy as np
from jax import lax
from jax.experimental import pallas as pl
from jax.experimental.pallas import tpu as pltpu
from jax.sharding import PartitionSpec as P

LANES = 128
BF16 = jnp.bfloat16
F32 = jnp.float32


def pieces_of(table):
    table = np.asarray(table, np.float32)
    head = table.astype(ml_dtypes.bfloat16)
    return np.stack([head, (table - head.astype(np.float32)).astype(ml_dtypes.bfloat16)])


def line_table(length, blocks, planes, width):
    kz = np.arange(length)
    out = np.zeros((2, length, blocks, width), np.float64)
    for block in range(blocks):
        z = block * planes + np.arange(planes)
        phases = (kz[:, None] * z[None, :] % length) * (2.0 * np.pi / length)
        out[0, :, block, :planes] = np.cos(phases)
        out[0, :, block, width // 2 : width // 2 + planes] = np.sin(phases)
        out[1, :, block, :planes] = -np.sin(phases)
        out[1, :, block, width // 2 : width // 2 + planes] = np.cos(phases)
    return pieces_of(out.reshape(2, length, blocks * width))


def split(values):
    head = values.astype(BF16)
    return head, (values - head.astype(F32)).astype(BF16)


def stacked(values):
    head, rest = split(values)
    return jnp.concatenate([head.astype(F32), rest.astype(F32)], axis=0).astype(BF16)


def doubled(values):
    values = values.astype(BF16)
    return jnp.concatenate([values, values], axis=1)


def dot(left, right):
    return lax.dot_general(left, right, (((1,), (0,)), ((), ())), preferred_element_type=F32)


def dot_nt(left, right):
    return lax.dot_general(left, right, (((1,), (1,)), ((), ())), preferred_element_type=F32)


def lane_ids(rows):
    return lax.broadcasted_iota(jnp.int32, (rows, LANES), 1)


def used_slots(count_ref, slots):
    used = count_ref[lax.axis_index("ga")] - lax.axis_index("band") * slots
    return lax.broadcasted_iota(jnp.int32, (slots, 1), 0) < used


def project_kernel(sizes, count_hbm, orbitals_hbm, projectors_hbm, table_hbm, out_ref, *scratch):
    blocks, groups, orbitals, slots, length, projectors, width = sizes
    count_ref, orbitals_ref, projectors_ref, table_ref, coef, spread, small_sems, sems = scratch
    kinds = orbitals * 2
    devices = blocks * groups
    share = projectors // devices
    small = [
        pltpu.make_async_copy(count_hbm, count_ref, small_sems.at[0]),
        pltpu.make_async_copy(orbitals_hbm, orbitals_ref, small_sems.at[1]),
        pltpu.make_async_copy(table_hbm, table_ref, small_sems.at[2]),
    ]
    copies = []
    for piece in range(2 * slots):
        rows = pl.ds(piece * length, length)
        copies.append(pltpu.make_async_copy(projectors_hbm.at[rows], projectors_ref.at[rows], sems.at[piece]))
    for copy in small + copies:
        copy.start()
    small[0].wait()
    small[1].wait()
    used = used_slots(count_ref, slots)
    for n in range(orbitals):
        for part in range(2):
            values = jnp.where(used, orbitals_ref[n, part].astype(F32), 0.0)
            at = (n * 2 + part) * slots
            coef[0, at : at + slots, :] = values
            at = (n * 2 + 1 - part) * slots
            coef[1, at : at + slots, :] = values if part == 1 else -values
            at = n * slots
            coef[2 + part, at : at + slots, :] = values
    small[2].wait()
    columns = jnp.zeros((orbitals * slots, blocks * width), F32)
    for part in range(2):
        left = coef[2 + part, : orbitals * slots, :].astype(BF16)
        columns += dot(left, table_ref[0, part]) + dot(left, table_ref[1, part])
    row_slot = lax.broadcasted_iota(jnp.int32, (kinds * slots, length), 0) % slots
    sums = jnp.zeros((kinds * slots, projectors), F32)
    for part in range(2):
        rows = coef[part]
        for slot in range(slots):
            piece = part * slots + slot
            left = jnp.where(row_slot == slot, rows, 0.0).astype(BF16)
            copies[piece].wait()
            sums += dot(left, projectors_ref[piece * length : (piece + 1) * length, :])
    for row in range(kinds):
        spread[row : row + 1, :] = jnp.sum(sums[row * slots : (row + 1) * slots, :], axis=0, keepdims=True)
    lanes = lane_ids(slots)
    groups_of_rows = kinds // slots
    for block in range(blocks):
        at = block * width
        base = at // LANES * LANES
        chunk = pltpu.roll(columns[:, base : base + LANES], (base - at) % LANES, 1)
        for group in range(groups):
            device = block * groups + group
            piece = jnp.where(lanes < width, chunk[group * slots : (group + 1) * slots, :], 0.0)
            first = device * share
            base = first // LANES * LANES
            for rows in range(groups_of_rows):
                low = width + rows * share
                own = spread[rows * slots : (rows + 1) * slots, base : base + LANES]
                own = pltpu.roll(own, (base + low - first) % LANES, 1)
                piece = jnp.where((lanes >= low) & (lanes < low + share), own, piece)
            out_ref[device] = piece


def cosine_and_sine(phases, length):
    quarter = jnp.floor(phases * (4.0 / length) + 0.5)
    angle = (phases - quarter * (length / 4.0)) * (2.0 * np.pi / length)
    square = angle * angle
    sine = 1.0 / 362880.0
    for term in (-1.0 / 5040.0, 1.0 / 120.0, -1.0 / 6.0, 1.0):
        sine = sine * square + term
    sine = sine * angle
    cosine = -1.0 / 3628800.0
    for term in (1.0 / 40320.0, -1.0 / 720.0, 1.0 / 24.0, -0.5, 1.0):
        cosine = cosine * square + term
    quarter = quarter - 4.0 * jnp.floor(quarter * 0.25)
    odd = (quarter == 1.0) | (quarter == 3.0)
    first = jnp.where(odd, sine, cosine)
    second = jnp.where(odd, cosine, sine)
    first = jnp.where((quarter == 1.0) | (quarter == 2.0), -first, first)
    return first, jnp.where(quarter >= 2.0, -second, second)


def make_tables(length, wide, site_ref, x_ref, plus_ref, minus_ref):
    columns = site_ref.shape[1]
    eye = lax.broadcasted_iota(jnp.int32, (LANES, LANES), 0) == lane_ids(LANES)
    row_ids = lax.broadcasted_iota(jnp.int32, (length, LANES), 0).astype(F32)
    lanes = lax.broadcasted_iota(jnp.int32, (LANES, wide), 1)
    inside = lanes < length
    lanes = lanes.astype(F32)
    for at in range(0, columns, LANES):
        site = site_ref[:, at : at + LANES].astype(F32)
        site_x = jnp.floor((site + 0.5) * (1.0 / length))
        site_y = site - site_x * length
        cosine, sine = cosine_and_sine(row_ids * site_x, length)
        x_ref[:, at : at + LANES] = cosine
        x_ref[:, columns + at : columns + at + LANES] = sine
        along = jnp.sum(jnp.where(eye, site_y, 0.0), axis=1, keepdims=True)
        cosine, sine = cosine_and_sine(lanes * along, length)
        cosine = jnp.where(inside, cosine, 0.0)
        sine = jnp.where(inside, sine, 0.0)
        across = jnp.concatenate([cosine[:, i : i + LANES].T for i in range(0, wide, LANES)], axis=0)
        aside = jnp.concatenate([sine[:, i : i + LANES].T for i in range(0, wide, LANES)], axis=0)
        for piece, (own_cosine, own_sine) in enumerate(zip(split(cosine), split(sine))):
            rows = pl.ds(piece * 2 * columns + at, LANES)
            plus_ref[rows, :wide] = own_cosine
            plus_ref[rows, wide:] = own_sine
            rows = pl.ds((piece * 2 + 1) * columns + at, LANES)
            plus_ref[rows, :wide] = -own_sine
            plus_ref[rows, wide:] = own_cosine
        for piece, (own_cosine, own_sine) in enumerate(zip(split(across), split(aside))):
            rows = pl.ds(piece * 2 * wide, wide)
            minus_ref[rows, at : at + LANES] = own_cosine
            minus_ref[rows, columns + at : columns + at + LANES] = -own_sine
            rows = pl.ds((piece * 2 + 1) * wide, wide)
            minus_ref[rows, at : at + LANES] = own_sine
            minus_ref[rows, columns + at : columns + at + LANES] = own_cosine


def plane_kernel(sizes, columns_ref, site_ref, potential_ref, out_ref, x_ref, plus_ref, minus_ref, gathered, lines, back):
    devices, slots, planes, length, wide, width, carried, batch = sizes
    count = devices * slots
    make_tables(length, wide, site_ref, x_ref, plus_ref, minus_ref)
    total = jnp.zeros((slots, LANES), F32)
    for device in range(devices):
        piece = columns_ref[device]
        gathered[device * slots : (device + 1) * slots, :] = piece
        total += piece
    for at in range(0, count, LANES):
        lines[:, at : at + LANES] = gathered[at : at + LANES, :].T
    back[...] = jnp.zeros_like(back)
    cosine = x_ref[:, :count]
    sine = x_ref[:, count:]
    padding = jnp.zeros((length, wide - length), F32)
    for i in range(planes // batch):
        left = []
        for plane in range(i * batch, (i + 1) * batch):
            real = lines[plane : plane + 1, :]
            imag = lines[plane + width // 2 : plane + width // 2 + 1, :]
            left.append(jnp.concatenate([cosine * real - sine * imag, cosine * imag + sine * real], axis=1))
        left = doubled(jnp.concatenate(left, axis=0))
        field = dot(left, plus_ref[...])
        weights = []
        for plane in range(i * batch, (i + 1) * batch):
            own = jnp.concatenate([potential_ref[plane], padding], axis=1)
            weights.append(jnp.concatenate([own, own], axis=1))
        left = doubled(field * jnp.concatenate(weights, axis=0))
        half = dot(left, minus_ref[...])
        for j in range(batch):
            plane = i * batch + j
            real = half[j * length : (j + 1) * length, :count]
            imag = half[j * length : (j + 1) * length, count:]
            back[plane : plane + 1, :] = jnp.sum(cosine * real + sine * imag, axis=0, keepdims=True)
            at = plane + width // 2
            back[at : at + 1, :] = jnp.sum(cosine * imag - sine * real, axis=0, keepdims=True)
    for at in range(0, count, LANES):
        gathered[at : at + LANES, :] = back[:, at : at + LANES].T
    lanes = lane_ids(slots)
    for device in range(devices):
        piece = gathered[device * slots : (device + 1) * slots, :]
        out_ref[device] = jnp.where((lanes >= width) & (lanes < carried), total, piece)


def finish_kernel(
    sizes, count_ref, columns_ref, atom_ref, couplings_ref, projectors_ref, table_ref, out_ref, summed, lined, mixed
):
    blocks, groups, orbitals, slots, length, projectors, width, normalizer = sizes
    kinds = orbitals * 2
    devices = blocks * groups
    share = projectors // devices
    groups_of_rows = kinds // slots
    lanes = lane_ids(slots)
    for chunk in range(projectors // LANES):
        in_chunk = range(chunk * LANES // share, (chunk + 1) * LANES // share)
        for rows in range(groups_of_rows):
            low = width + rows * share
            total = jnp.zeros((slots, LANES), F32)
            for device in in_chunk:
                own = columns_ref[device]
                own = pltpu.roll(jnp.where((lanes >= low) & (lanes < low + share), own, 0.0), (device * share - low) % LANES, 1)
                total += own
            summed[rows * slots : (rows + 1) * slots, chunk * LANES : (chunk + 1) * LANES] = total
    for n in range(orbitals):
        at = kinds + n * 2
        summed[at : at + 1, :] = -summed[n * 2 + 1 : n * 2 + 2, :]
        summed[at + 1 : at + 2, :] = summed[n * 2 : n * 2 + 1, :]
    both = stacked(summed[...])
    atoms = atom_ref[...].astype(F32)
    eye = lax.broadcasted_iota(jnp.int32, (LANES, LANES), 0) == lane_ids(LANES)
    along = []
    for at in range(0, projectors, LANES):
        along.append(jnp.sum(jnp.where(eye, atoms[:, at : at + LANES], 0.0), axis=1, keepdims=True))
    head, rest = split(jnp.where(jnp.concatenate(along, axis=0) == atoms, couplings_ref[...], 0.0))
    head = dot_nt(both, head)
    rest = dot_nt(both, rest)
    weighted = (head[: 2 * kinds] + (head[2 * kinds :] + rest[: 2 * kinds])).astype(BF16)
    for slot in range(slots):
        rows = projectors_ref[slot * length : (slot + 1) * length, :]
        value = dot_nt(weighted, rows)[:kinds]
        rows = projectors_ref[(slots + slot) * length : (slots + slot + 1) * length, :]
        mixed[slot * kinds : (slot + 1) * kinds, :] = value + dot_nt(weighted, rows)[kinds:]
    for chunk in range(blocks * width // LANES):
        for group in range(groups):
            total = jnp.zeros((slots, LANES), F32)
            for inner in range(LANES // width):
                block = chunk * (LANES // width) + inner
                own = jnp.where(lanes < width, columns_ref[block * groups + group], 0.0)
                total += pltpu.roll(own, inner * width, 1)
            lined[group * slots : (group + 1) * slots, chunk * LANES : (chunk + 1) * LANES] = total
    both = stacked(lined[...])
    rows_of_lines = groups * slots
    used = used_slots(count_ref, slots)
    for part in range(2):
        head = dot_nt(both, table_ref[0, part])
        rest = dot_nt(both, table_ref[1, part])
        local = (head[:rows_of_lines] + (head[rows_of_lines:] + rest[:rows_of_lines])) * normalizer
        for n in range(orbitals):
            row = n * 2 + part
            for slot in range(slots):
                at = n * slots + slot
                value = local[at : at + 1, :] + mixed[slot * kinds + row : slot * kinds + row + 1, :]
                out_ref[n, part, slot : slot + 1, :] = value
            out_ref[n, part] = jnp.where(used, out_ref[n, part], 0.0)


def on_device(orbitals, projectors, potential, couplings, atom_index, column_site, column_count):
    blocks = lax.axis_size("ga")
    groups = lax.axis_size("band")
    devices = blocks * groups
    orbital_count, _, slots, length = orbitals.shape
    planes = potential.shape[0]
    projector_count = projectors.shape[0]
    columns = column_site.shape[0]
    kinds = orbital_count * 2
    assert orbital_count == groups and kinds % slots == 0 and columns % LANES == 0
    share = projector_count // devices
    width = 2
    while width < 2 * planes:
        width *= 2
    carried = width + kinds // slots * share
    assert carried <= LANES and width <= LANES and share * devices == projector_count
    wide = -(-length // LANES) * LANES
    flat = jnp.transpose(projectors, (1, 2, 3, 0)).reshape(2 * slots * length, projector_count)
    z_table = line_table(length, blocks, planes, width)
    batch = next(i for i in (4, 3, 2, 1) if planes % i == 0) if columns <= 512 else 1
    smem = pl.BlockSpec(memory_space=pltpu.SMEM)
    vmem = pl.BlockSpec(memory_space=pltpu.VMEM)
    hbm = pl.BlockSpec(memory_space=pltpu.HBM)
    params = pltpu.CompilerParams(vmem_limit_bytes=56 * 1024 * 1024)
    small = pltpu.CompilerParams(vmem_limit_bytes=40 * 1024 * 1024)
    payload = jax.ShapeDtypeStruct((devices, slots, LANES), F32)

    sent = pl.pallas_call(
        functools.partial(
            project_kernel, (blocks, groups, orbital_count, slots, length, projector_count, width)
        ),
        out_shape=payload,
        in_specs=[hbm] * 4,
        out_specs=vmem,
        scratch_shapes=[
            pltpu.SMEM(column_count.shape, jnp.int32),
            pltpu.VMEM(orbitals.shape, BF16),
            pltpu.VMEM(flat.shape, BF16),
            pltpu.VMEM(z_table.shape, BF16),
            pltpu.VMEM((4, kinds * slots, length), F32),
            pltpu.VMEM((kinds, projector_count), F32),
            pltpu.SemaphoreType.DMA((3,)),
            pltpu.SemaphoreType.DMA((2 * slots,)),
        ],
        compiler_params=params,
        name="project",
    )(column_count, orbitals, flat, z_table)
    arrived = lax.all_to_all(sent, ("ga", "band"), split_axis=0, concat_axis=0, tiled=True)

    sent = pl.pallas_call(
        functools.partial(plane_kernel, (devices, slots, planes, length, wide, width, carried, batch)),
        out_shape=payload,
        in_specs=[vmem] * 3,
        out_specs=vmem,
        scratch_shapes=[
            pltpu.VMEM((length, 2 * columns), F32),
            pltpu.VMEM((4 * columns, 2 * wide), BF16),
            pltpu.VMEM((4 * wide, 2 * columns), BF16),
            pltpu.VMEM((columns, LANES), F32),
            pltpu.VMEM((LANES, columns), F32),
            pltpu.VMEM((LANES, columns), F32),
        ],
        compiler_params=small,
        name="planes",
    )(arrived, column_site.reshape(1, columns), potential)
    arrived = lax.all_to_all(sent, ("ga", "band"), split_axis=0, concat_axis=0, tiled=True)

    normalizer = 1.0 / float(length**3)
    return pl.pallas_call(
        functools.partial(
            finish_kernel,
            (blocks, groups, orbital_count, slots, length, projector_count, width, normalizer),
        ),
        out_shape=jax.ShapeDtypeStruct(orbitals.shape, F32),
        in_specs=[smem] + [vmem] * 5,
        out_specs=vmem,
        scratch_shapes=[
            pltpu.VMEM((2 * kinds, projector_count), F32),
            pltpu.VMEM((groups * slots, blocks * width), F32),
            pltpu.VMEM((slots * kinds, length), F32),
        ],
        compiler_params=small,
        name="finish",
    )(column_count, arrived, atom_index.reshape(1, projector_count), couplings, flat, z_table)


def solution(mesh):
    return jax.shard_map(
        on_device,
        mesh=mesh,
        in_specs=(
            P(None, None, ("ga", "band"), None),
            P(None, None, ("ga", "band"), None),
            P("ga", None, None),
            P(),
            P(),
            P(),
            P(),
        ),
        out_specs=P(None, None, ("ga", "band"), None),
        check_vma=False,
    )
```

```python
import functools

import jax
import jax.numpy as jnp
import ml_dtypes
import numpy as np
from jax import lax
from jax.experimental import pallas as pl
from jax.experimental.pallas import tpu as pltpu
from jax.sharding import PartitionSpec as P

LANES = 128
BF16 = jnp.bfloat16
F32 = jnp.float32


def pieces_of(table):
    table = np.asarray(table, np.float32)
    head = table.astype(ml_dtypes.bfloat16)
    return np.stack([head, (table - head.astype(np.float32)).astype(ml_dtypes.bfloat16)])


def line_table(length, blocks, planes, width):
    kz = np.arange(length)
    out = np.zeros((2, length, blocks, width), np.float64)
    for block in range(blocks):
        z = block * planes + np.arange(planes)
        phases = (kz[:, None] * z[None, :] % length) * (2.0 * np.pi / length)
        out[0, :, block, :planes] = np.cos(phases)
        out[0, :, block, width // 2 : width // 2 + planes] = np.sin(phases)
        out[1, :, block, :planes] = -np.sin(phases)
        out[1, :, block, width // 2 : width // 2 + planes] = np.cos(phases)
    return pieces_of(out.reshape(2, length, blocks * width))


def split(values):
    head = values.astype(BF16)
    return head, (values - head.astype(F32)).astype(BF16)


def stacked(values):
    head, rest = split(values)
    return jnp.concatenate([head.astype(F32), rest.astype(F32)], axis=0).astype(BF16)


def doubled(values):
    values = values.astype(BF16)
    return jnp.concatenate([values, values], axis=1)


def dot(left, right):
    return lax.dot_general(left, right, (((1,), (0,)), ((), ())), preferred_element_type=F32)


def dot_nt(left, right):
    return lax.dot_general(left, right, (((1,), (1,)), ((), ())), preferred_element_type=F32)


def lane_ids(rows):
    return lax.broadcasted_iota(jnp.int32, (rows, LANES), 1)


def used_slots(count_ref, slots):
    used = count_ref[lax.axis_index("ga")] - lax.axis_index("band") * slots
    return lax.broadcasted_iota(jnp.int32, (slots, 1), 0) < used


def project_kernel(sizes, count_hbm, orbitals_hbm, projectors_hbm, table_hbm, out_ref, *scratch):
    blocks, groups, orbitals, slots, length, projectors, width = sizes
    count_ref, orbitals_ref, projectors_ref, table_ref, coef, spread, small_sems, sems = scratch
    kinds = orbitals * 2
    devices = blocks * groups
    share = projectors // devices
    small = [
        pltpu.make_async_copy(count_hbm, count_ref, small_sems.at[0]),
        pltpu.make_async_copy(orbitals_hbm, orbitals_ref, small_sems.at[1]),
        pltpu.make_async_copy(table_hbm, table_ref, small_sems.at[2]),
    ]
    copies = []
    for piece in range(2 * slots):
        rows = pl.ds(piece * length, length)
        copies.append(pltpu.make_async_copy(projectors_hbm.at[rows], projectors_ref.at[rows], sems.at[piece]))
    for copy in small + copies:
        copy.start()
    small[0].wait()
    small[1].wait()
    used = used_slots(count_ref, slots)
    for n in range(orbitals):
        for part in range(2):
            values = jnp.where(used, orbitals_ref[n, part].astype(F32), 0.0)
            at = (n * 2 + part) * slots
            coef[0, at : at + slots, :] = values
            at = (n * 2 + 1 - part) * slots
            coef[1, at : at + slots, :] = values if part == 1 else -values
            at = n * slots
            coef[2 + part, at : at + slots, :] = values
    small[2].wait()
    columns = jnp.zeros((orbitals * slots, blocks * width), F32)
    for part in range(2):
        left = coef[2 + part, : orbitals * slots, :].astype(BF16)
        columns += dot(left, table_ref[0, part]) + dot(left, table_ref[1, part])
    row_slot = lax.broadcasted_iota(jnp.int32, (kinds * slots, length), 0) % slots
    sums = jnp.zeros((kinds * slots, projectors), F32)
    for part in range(2):
        rows = coef[part]
        for slot in range(slots):
            piece = part * slots + slot
            left = jnp.where(row_slot == slot, rows, 0.0).astype(BF16)
            copies[piece].wait()
            sums += dot(left, projectors_ref[piece * length : (piece + 1) * length, :])
    for row in range(kinds):
        spread[row : row + 1, :] = jnp.sum(sums[row * slots : (row + 1) * slots, :], axis=0, keepdims=True)
    lanes = lane_ids(slots)
    groups_of_rows = kinds // slots
    for block in range(blocks):
        at = block * width
        base = at // LANES * LANES
        chunk = pltpu.roll(columns[:, base : base + LANES], (base - at) % LANES, 1)
        for group in range(groups):
            device = block * groups + group
            piece = jnp.where(lanes < width, chunk[group * slots : (group + 1) * slots, :], 0.0)
            first = device * share
            base = first // LANES * LANES
            for rows in range(groups_of_rows):
                low = width + rows * share
                own = spread[rows * slots : (rows + 1) * slots, base : base + LANES]
                own = pltpu.roll(own, (base + low - first) % LANES, 1)
                piece = jnp.where((lanes >= low) & (lanes < low + share), own, piece)
            out_ref[device] = piece


def cosine_and_sine(phases, length):
    quarter = jnp.floor(phases * (4.0 / length) + 0.5)
    angle = (phases - quarter * (length / 4.0)) * (2.0 * np.pi / length)
    square = angle * angle
    sine = 1.0 / 362880.0
    for term in (-1.0 / 5040.0, 1.0 / 120.0, -1.0 / 6.0, 1.0):
        sine = sine * square + term
    sine = sine * angle
    cosine = -1.0 / 3628800.0
    for term in (1.0 / 40320.0, -1.0 / 720.0, 1.0 / 24.0, -0.5, 1.0):
        cosine = cosine * square + term
    quarter = quarter - 4.0 * jnp.floor(quarter * 0.25)
    odd = (quarter == 1.0) | (quarter == 3.0)
    first = jnp.where(odd, sine, cosine)
    second = jnp.where(odd, cosine, sine)
    first = jnp.where((quarter == 1.0) | (quarter == 2.0), -first, first)
    return first, jnp.where(quarter >= 2.0, -second, second)


def make_tables(length, wide, site_ref, x_ref, plus_ref, minus_ref):
    columns = site_ref.shape[1]
    eye = lax.broadcasted_iota(jnp.int32, (LANES, LANES), 0) == lane_ids(LANES)
    row_ids = lax.broadcasted_iota(jnp.int32, (length, LANES), 0).astype(F32)
    lanes = lax.broadcasted_iota(jnp.int32, (LANES, wide), 1)
    inside = lanes < length
    lanes = lanes.astype(F32)
    for at in range(0, columns, LANES):
        site = site_ref[:, at : at + LANES].astype(F32)
        site_x = jnp.floor((site + 0.5) * (1.0 / length))
        site_y = site - site_x * length
        cosine, sine = cosine_and_sine(row_ids * site_x, length)
        x_ref[:, at : at + LANES] = cosine
        x_ref[:, columns + at : columns + at + LANES] = sine
        along = jnp.sum(jnp.where(eye, site_y, 0.0), axis=1, keepdims=True)
        cosine, sine = cosine_and_sine(lanes * along, length)
        cosine = jnp.where(inside, cosine, 0.0)
        sine = jnp.where(inside, sine, 0.0)
        across = jnp.concatenate([cosine[:, i : i + LANES].T for i in range(0, wide, LANES)], axis=0)
        aside = jnp.concatenate([sine[:, i : i + LANES].T for i in range(0, wide, LANES)], axis=0)
        for piece, (own_cosine, own_sine) in enumerate(zip(split(cosine), split(sine))):
            rows = pl.ds(piece * 2 * columns + at, LANES)
            plus_ref[rows, :wide] = own_cosine
            plus_ref[rows, wide:] = own_sine
            rows = pl.ds((piece * 2 + 1) * columns + at, LANES)
            plus_ref[rows, :wide] = -own_sine
            plus_ref[rows, wide:] = own_cosine
        for piece, (own_cosine, own_sine) in enumerate(zip(split(across), split(aside))):
            rows = pl.ds(piece * 2 * wide, wide)
            minus_ref[rows, at : at + LANES] = own_cosine
            minus_ref[rows, columns + at : columns + at + LANES] = -own_sine
            rows = pl.ds((piece * 2 + 1) * wide, wide)
            minus_ref[rows, at : at + LANES] = own_sine
            minus_ref[rows, columns + at : columns + at + LANES] = own_cosine


def plane_kernel(sizes, columns_ref, site_ref, potential_ref, out_ref, x_ref, plus_ref, minus_ref, gathered, lines, back):
    devices, slots, planes, length, wide, width, carried, batch = sizes
    count = devices * slots
    make_tables(length, wide, site_ref, x_ref, plus_ref, minus_ref)
    total = jnp.zeros((slots, LANES), F32)
    for device in range(devices):
        piece = columns_ref[device]
        gathered[device * slots : (device + 1) * slots, :] = piece
        total += piece
    for at in range(0, count, LANES):
        lines[:, at : at + LANES] = gathered[at : at + LANES, :].T
    back[...] = jnp.zeros_like(back)
    cosine = x_ref[:, :count]
    sine = x_ref[:, count:]
    padding = jnp.zeros((length, wide - length), F32)
    for i in range(planes // batch):
        left = []
        for plane in range(i * batch, (i + 1) * batch):
            real = lines[plane : plane + 1, :]
            imag = lines[plane + width // 2 : plane + width // 2 + 1, :]
            left.append(jnp.concatenate([cosine * real - sine * imag, cosine * imag + sine * real], axis=1))
        left = doubled(jnp.concatenate(left, axis=0))
        field = dot(left, plus_ref[...])
        weights = []
        for plane in range(i * batch, (i + 1) * batch):
            own = jnp.concatenate([potential_ref[plane], padding], axis=1)
            weights.append(jnp.concatenate([own, own], axis=1))
        left = doubled(field * jnp.concatenate(weights, axis=0))
        half = dot(left, minus_ref[...])
        for j in range(batch):
            plane = i * batch + j
            real = half[j * length : (j + 1) * length, :count]
            imag = half[j * length : (j + 1) * length, count:]
            back[plane : plane + 1, :] = jnp.sum(cosine * real + sine * imag, axis=0, keepdims=True)
            at = plane + width // 2
            back[at : at + 1, :] = jnp.sum(cosine * imag - sine * real, axis=0, keepdims=True)
    for at in range(0, count, LANES):
        gathered[at : at + LANES, :] = back[:, at : at + LANES].T
    lanes = lane_ids(slots)
    for device in range(devices):
        piece = gathered[device * slots : (device + 1) * slots, :]
        out_ref[device] = jnp.where((lanes >= width) & (lanes < carried), total, piece)


def finish_kernel(
    sizes, count_ref, columns_ref, atom_ref, couplings_ref, projectors_ref, table_ref, out_ref, summed, lined, mixed
):
    blocks, groups, orbitals, slots, length, projectors, width, normalizer = sizes
    kinds = orbitals * 2
    devices = blocks * groups
    share = projectors // devices
    groups_of_rows = kinds // slots
    lanes = lane_ids(slots)
    for chunk in range(projectors // LANES):
        in_chunk = range(chunk * LANES // share, (chunk + 1) * LANES // share)
        for rows in range(groups_of_rows):
            low = width + rows * share
            total = jnp.zeros((slots, LANES), F32)
            for device in in_chunk:
                own = columns_ref[device]
                own = pltpu.roll(jnp.where((lanes >= low) & (lanes < low + share), own, 0.0), (device * share - low) % LANES, 1)
                total += own
            summed[rows * slots : (rows + 1) * slots, chunk * LANES : (chunk + 1) * LANES] = total
    for n in range(orbitals):
        at = kinds + n * 2
        summed[at : at + 1, :] = -summed[n * 2 + 1 : n * 2 + 2, :]
        summed[at + 1 : at + 2, :] = summed[n * 2 : n * 2 + 1, :]
    both = stacked(summed[...])
    atoms = atom_ref[...].astype(F32)
    eye = lax.broadcasted_iota(jnp.int32, (LANES, LANES), 0) == lane_ids(LANES)
    along = []
    for at in range(0, projectors, LANES):
        along.append(jnp.sum(jnp.where(eye, atoms[:, at : at + LANES], 0.0), axis=1, keepdims=True))
    head, rest = split(jnp.where(jnp.concatenate(along, axis=0) == atoms, couplings_ref[...], 0.0))
    head = dot_nt(both, head)
    rest = dot_nt(both, rest)
    weighted = (head[: 2 * kinds] + (head[2 * kinds :] + rest[: 2 * kinds])).astype(BF16)
    for slot in range(slots):
        rows = projectors_ref[slot * length : (slot + 1) * length, :]
        value = dot_nt(weighted, rows)[:kinds]
        rows = projectors_ref[(slots + slot) * length : (slots + slot + 1) * length, :]
        mixed[slot * kinds : (slot + 1) * kinds, :] = value + dot_nt(weighted, rows)[kinds:]
    for chunk in range(blocks * width // LANES):
        for group in range(groups):
            total = jnp.zeros((slots, LANES), F32)
            for inner in range(LANES // width):
                block = chunk * (LANES // width) + inner
                own = jnp.where(lanes < width, columns_ref[block * groups + group], 0.0)
                total += pltpu.roll(own, inner * width, 1)
            lined[group * slots : (group + 1) * slots, chunk * LANES : (chunk + 1) * LANES] = total
    both = stacked(lined[...])
    rows_of_lines = groups * slots
    used = used_slots(count_ref, slots)
    for part in range(2):
        head = dot_nt(both, table_ref[0, part])
        rest = dot_nt(both, table_ref[1, part])
        local = (head[:rows_of_lines] + (head[rows_of_lines:] + rest[:rows_of_lines])) * normalizer
        for n in range(orbitals):
            row = n * 2 + part
            for slot in range(slots):
                at = n * slots + slot
                value = local[at : at + 1, :] + mixed[slot * kinds + row : slot * kinds + row + 1, :]
                out_ref[n, part, slot : slot + 1, :] = value
            out_ref[n, part] = jnp.where(used, out_ref[n, part], 0.0)


def on_device(orbitals, projectors, potential, couplings, atom_index, column_site, column_count):
    blocks = lax.axis_size("ga")
    groups = lax.axis_size("band")
    devices = blocks * groups
    orbital_count, _, slots, length = orbitals.shape
    planes = potential.shape[0]
    projector_count = projectors.shape[0]
    columns = column_site.shape[0]
    kinds = orbital_count * 2
    assert orbital_count == groups and kinds % slots == 0 and columns % LANES == 0
    share = projector_count // devices
    width = 2
    while width < 2 * planes:
        width *= 2
    carried = width + kinds // slots * share
    assert carried <= LANES and width <= LANES and share * devices == projector_count
    wide = -(-length // LANES) * LANES
    flat = jnp.transpose(projectors, (1, 2, 3, 0)).reshape(2 * slots * length, projector_count)
    z_table = line_table(length, blocks, planes, width)
    batch = next(i for i in (4, 3, 2, 1) if planes % i == 0) if columns <= 512 else 1
    smem = pl.BlockSpec(memory_space=pltpu.SMEM)
    vmem = pl.BlockSpec(memory_space=pltpu.VMEM)
    hbm = pl.BlockSpec(memory_space=pltpu.HBM)
    params = pltpu.CompilerParams(vmem_limit_bytes=56 * 1024 * 1024)
    small = pltpu.CompilerParams(vmem_limit_bytes=40 * 1024 * 1024)
    payload = jax.ShapeDtypeStruct((devices, slots, LANES), F32)

    sent = pl.pallas_call(
        functools.partial(
            project_kernel, (blocks, groups, orbital_count, slots, length, projector_count, width)
        ),
        out_shape=payload,
        in_specs=[hbm] * 4,
        out_specs=vmem,
        scratch_shapes=[
            pltpu.SMEM(column_count.shape, jnp.int32),
            pltpu.VMEM(orbitals.shape, BF16),
            pltpu.VMEM(flat.shape, BF16),
            pltpu.VMEM(z_table.shape, BF16),
            pltpu.VMEM((4, kinds * slots, length), F32),
            pltpu.VMEM((kinds, projector_count), F32),
            pltpu.SemaphoreType.DMA((3,)),
            pltpu.SemaphoreType.DMA((2 * slots,)),
        ],
        compiler_params=params,
        cost_estimate=pl.CostEstimate(
            flops=2 * flat.size * kinds * slots + 4 * z_table.size * orbital_count * slots,
            bytes_accessed=2 * (flat.size + z_table.size + orbitals.size) + 4 * devices * slots * LANES,
            transcendentals=0,
        ),
        name="project",
    )(column_count, orbitals, flat, z_table)
    arrived = lax.all_to_all(sent, ("ga", "band"), split_axis=0, concat_axis=0, tiled=True)

    sent = pl.pallas_call(
        functools.partial(plane_kernel, (devices, slots, planes, length, wide, width, carried, batch)),
        out_shape=payload,
        in_specs=[vmem] * 3,
        out_specs=vmem,
        scratch_shapes=[
            pltpu.VMEM((length, 2 * columns), F32),
            pltpu.VMEM((4 * columns, 2 * wide), BF16),
            pltpu.VMEM((4 * wide, 2 * columns), BF16),
            pltpu.VMEM((columns, LANES), F32),
            pltpu.VMEM((LANES, columns), F32),
            pltpu.VMEM((LANES, columns), F32),
        ],
        compiler_params=small,
        cost_estimate=pl.CostEstimate(
            flops=16 * planes * length * wide * 2 * columns,
            bytes_accessed=4 * (potential.size + 2 * devices * slots * LANES),
            transcendentals=2 * (length + wide) * columns,
        ),
        name="planes",
    )(arrived, column_site.reshape(1, columns), potential)
    arrived = lax.all_to_all(sent, ("ga", "band"), split_axis=0, concat_axis=0, tiled=True)

    normalizer = 1.0 / float(length**3)
    return pl.pallas_call(
        functools.partial(
            finish_kernel,
            (blocks, groups, orbital_count, slots, length, projector_count, width, normalizer),
        ),
        out_shape=jax.ShapeDtypeStruct(orbitals.shape, F32),
        in_specs=[smem] + [vmem] * 5,
        out_specs=vmem,
        scratch_shapes=[
            pltpu.VMEM((2 * kinds, projector_count), F32),
            pltpu.VMEM((groups * slots, blocks * width), F32),
            pltpu.VMEM((slots * kinds, length), F32),
        ],
        compiler_params=small,
        cost_estimate=pl.CostEstimate(
            flops=4 * kinds * (4 * couplings.size + flat.size) + 4 * z_table.size * orbital_count * slots,
            bytes_accessed=4 * couplings.size + 2 * (flat.size + z_table.size) + 4 * orbitals.size,
            transcendentals=0,
        ),
        name="finish",
    )(column_count, arrived, atom_index.reshape(1, projector_count), couplings, flat, z_table)


def solution(mesh):
    return jax.shard_map(
        on_device,
        mesh=mesh,
        in_specs=(
            P(None, None, ("ga", "band"), None),
            P(None, None, ("ga", "band"), None),
            P("ga", None, None),
            P(),
            P(),
            P(),
            P(),
        ),
        out_specs=P(None, None, ("ga", "band"), None),
        check_vma=False,
    )
```

```python
import functools

import jax
import jax.numpy as jnp
import ml_dtypes
import numpy as np
from jax import lax
from jax.experimental import pallas as pl
from jax.experimental.pallas import tpu as pltpu
from jax.sharding import PartitionSpec as P

LANES = 128
BF16 = jnp.bfloat16
F32 = jnp.float32


def pieces_of(table):
    table = np.asarray(table, np.float32)
    head = table.astype(ml_dtypes.bfloat16)
    return np.stack([head, (table - head.astype(np.float32)).astype(ml_dtypes.bfloat16)])


def line_table(length, blocks, planes, width):
    kz = np.arange(length)
    out = np.zeros((2, length, blocks, width), np.float64)
    for block in range(blocks):
        z = block * planes + np.arange(planes)
        phases = (kz[:, None] * z[None, :] % length) * (2.0 * np.pi / length)
        out[0, :, block, :planes] = np.cos(phases)
        out[0, :, block, width // 2 : width // 2 + planes] = np.sin(phases)
        out[1, :, block, :planes] = -np.sin(phases)
        out[1, :, block, width // 2 : width // 2 + planes] = np.cos(phases)
    return pieces_of(out.reshape(2, length, blocks * width))


def split(values):
    head = values.astype(BF16)
    return head, (values - head.astype(F32)).astype(BF16)


def stacked(values):
    head, rest = split(values)
    return jnp.concatenate([head.astype(F32), rest.astype(F32)], axis=0).astype(BF16)


def doubled(values):
    values = values.astype(BF16)
    return jnp.concatenate([values, values], axis=1)


def dot(left, right):
    return lax.dot_general(left, right, (((1,), (0,)), ((), ())), preferred_element_type=F32)


def dot_nt(left, right):
    return lax.dot_general(left, right, (((1,), (1,)), ((), ())), preferred_element_type=F32)


def lane_ids(rows):
    return lax.broadcasted_iota(jnp.int32, (rows, LANES), 1)


def used_slots(count_ref, slots):
    used = count_ref[lax.axis_index("ga")] - lax.axis_index("band") * slots
    return lax.broadcasted_iota(jnp.int32, (slots, 1), 0) < used


def project_kernel(sizes, count_hbm, orbitals_hbm, projectors_hbm, table_hbm, out_ref, *scratch):
    blocks, groups, orbitals, slots, length, projectors, width = sizes
    count_ref, orbitals_ref, projectors_ref, table_ref, coef, lines, small_sems, sems = scratch
    kinds = orbitals * 2
    devices = blocks * groups
    share = projectors // devices
    small = [
        pltpu.make_async_copy(count_hbm, count_ref, small_sems.at[0]),
        pltpu.make_async_copy(orbitals_hbm, orbitals_ref, small_sems.at[1]),
        pltpu.make_async_copy(table_hbm, table_ref, small_sems.at[2]),
    ]
    copies = []
    for piece in range(2 * slots):
        rows = pl.ds(piece * length, length)
        copies.append(pltpu.make_async_copy(projectors_hbm.at[rows], projectors_ref.at[rows], sems.at[piece]))
    for copy in small + copies:
        copy.start()
    coef[...] = jnp.zeros_like(coef)
    small[0].wait()
    small[1].wait()
    used = used_slots(count_ref, slots)
    for n in range(orbitals):
        for part in range(2):
            values = jnp.where(used, orbitals_ref[n, part].astype(F32), 0.0)
            lines[part, n * slots : (n + 1) * slots, :] = values
            turned = values if part == 1 else -values
            for slot in range(slots):
                row = n * 2 + part
                coef[slot, row : row + 1, :] = values[slot : slot + 1, :]
                row = n * 2 + 1 - part
                coef[slots + slot, row : row + 1, :] = turned[slot : slot + 1, :]
    small[2].wait()
    columns = jnp.zeros((orbitals * slots, blocks * width), F32)
    for part in range(2):
        left = lines[part].astype(BF16)
        columns += dot(left, table_ref[0, part]) + dot(left, table_ref[1, part])
    for block in range(blocks):
        at = block * width
        base = at // LANES * LANES
        chunk = pltpu.roll(columns[:, base : base + LANES], (base - at) % LANES, 1)
        for group in range(groups):
            out_ref[block * groups + group] = chunk[group * slots : (group + 1) * slots, :]
    sums = jnp.zeros((coef.shape[1], projectors), F32)
    for piece in range(2 * slots):
        left = coef[piece].astype(BF16)
        copies[piece].wait()
        sums += dot(left, projectors_ref[piece * length : (piece + 1) * length, :])
    lanes = lane_ids(slots)
    for device in range(devices):
        piece = jnp.where(lanes < width, out_ref[device], 0.0)
        first = device * share
        base = first // LANES * LANES
        for rows in range(kinds // slots):
            low = width + rows * share
            own = pltpu.roll(sums[rows * slots : (rows + 1) * slots, base : base + LANES], (base + low - first) % LANES, 1)
            piece = jnp.where((lanes >= low) & (lanes < low + share), own, piece)
        out_ref[device] = piece


def cosine_and_sine(phases, length):
    quarter = jnp.floor(phases * (4.0 / length) + 0.5)
    angle = (phases - quarter * (length / 4.0)) * (2.0 * np.pi / length)
    square = angle * angle
    sine = 1.0 / 362880.0
    for term in (-1.0 / 5040.0, 1.0 / 120.0, -1.0 / 6.0, 1.0):
        sine = sine * square + term
    sine = sine * angle
    cosine = -1.0 / 3628800.0
    for term in (1.0 / 40320.0, -1.0 / 720.0, 1.0 / 24.0, -0.5, 1.0):
        cosine = cosine * square + term
    quarter = quarter - 4.0 * jnp.floor(quarter * 0.25)
    odd = (quarter == 1.0) | (quarter == 3.0)
    first = jnp.where(odd, sine, cosine)
    second = jnp.where(odd, cosine, sine)
    first = jnp.where((quarter == 1.0) | (quarter == 2.0), -first, first)
    return first, jnp.where(quarter >= 2.0, -second, second)


def make_tables(length, wide, site_ref, x_ref, plus_ref, minus_ref):
    columns = site_ref.shape[1]
    eye = lax.broadcasted_iota(jnp.int32, (LANES, LANES), 0) == lane_ids(LANES)
    row_ids = lax.broadcasted_iota(jnp.int32, (length, LANES), 0).astype(F32)
    lanes = lax.broadcasted_iota(jnp.int32, (LANES, wide), 1)
    inside = lanes < length
    lanes = lanes.astype(F32)
    for at in range(0, columns, LANES):
        site = site_ref[:, at : at + LANES].astype(F32)
        site_x = jnp.floor((site + 0.5) * (1.0 / length))
        site_y = site - site_x * length
        cosine, sine = cosine_and_sine(row_ids * site_x, length)
        x_ref[:, at : at + LANES] = cosine
        x_ref[:, columns + at : columns + at + LANES] = sine
        along = jnp.sum(jnp.where(eye, site_y, 0.0), axis=1, keepdims=True)
        cosine, sine = cosine_and_sine(lanes * along, length)
        cosine = jnp.where(inside, cosine, 0.0)
        sine = jnp.where(inside, sine, 0.0)
        across = jnp.concatenate([cosine[:, i : i + LANES].T for i in range(0, wide, LANES)], axis=0)
        aside = jnp.concatenate([sine[:, i : i + LANES].T for i in range(0, wide, LANES)], axis=0)
        for piece, (own_cosine, own_sine) in enumerate(zip(split(cosine), split(sine))):
            rows = pl.ds(piece * 2 * columns + at, LANES)
            plus_ref[rows, :wide] = own_cosine
            plus_ref[rows, wide:] = own_sine
            rows = pl.ds((piece * 2 + 1) * columns + at, LANES)
            plus_ref[rows, :wide] = -own_sine
            plus_ref[rows, wide:] = own_cosine
        for piece, (own_cosine, own_sine) in enumerate(zip(split(across), split(aside))):
            rows = pl.ds(piece * 2 * wide, wide)
            minus_ref[rows, at : at + LANES] = own_cosine
            minus_ref[rows, columns + at : columns + at + LANES] = -own_sine
            rows = pl.ds((piece * 2 + 1) * wide, wide)
            minus_ref[rows, at : at + LANES] = own_sine
            minus_ref[rows, columns + at : columns + at + LANES] = own_cosine


def plane_kernel(sizes, columns_ref, site_ref, potential_ref, out_ref, x_ref, plus_ref, minus_ref, gathered, lines, back):
    devices, slots, planes, length, wide, width, carried, batch = sizes
    count = devices * slots
    make_tables(length, wide, site_ref, x_ref, plus_ref, minus_ref)
    total = jnp.zeros((slots, LANES), F32)
    for device in range(devices):
        piece = columns_ref[device]
        gathered[device * slots : (device + 1) * slots, :] = piece
        total += piece
    for at in range(0, count, LANES):
        lines[:, at : at + LANES] = gathered[at : at + LANES, :].T
    back[...] = jnp.zeros_like(back)
    cosine = x_ref[:, :count]
    sine = x_ref[:, count:]
    padding = jnp.zeros((length, wide - length), F32)
    for i in range(planes // batch):
        left = []
        for plane in range(i * batch, (i + 1) * batch):
            real = lines[plane : plane + 1, :]
            imag = lines[plane + width // 2 : plane + width // 2 + 1, :]
            left.append(jnp.concatenate([cosine * real - sine * imag, cosine * imag + sine * real], axis=1))
        left = doubled(jnp.concatenate(left, axis=0))
        field = dot(left, plus_ref[...])
        weights = []
        for plane in range(i * batch, (i + 1) * batch):
            own = jnp.concatenate([potential_ref[plane], padding], axis=1)
            weights.append(jnp.concatenate([own, own], axis=1))
        left = doubled(field * jnp.concatenate(weights, axis=0))
        half = dot(left, minus_ref[...])
        for j in range(batch):
            plane = i * batch + j
            real = half[j * length : (j + 1) * length, :count]
            imag = half[j * length : (j + 1) * length, count:]
            back[plane : plane + 1, :] = jnp.sum(cosine * real + sine * imag, axis=0, keepdims=True)
            at = plane + width // 2
            back[at : at + 1, :] = jnp.sum(cosine * imag - sine * real, axis=0, keepdims=True)
    for at in range(0, count, LANES):
        gathered[at : at + LANES, :] = back[:, at : at + LANES].T
    lanes = lane_ids(slots)
    for device in range(devices):
        piece = gathered[device * slots : (device + 1) * slots, :]
        out_ref[device] = jnp.where((lanes >= width) & (lanes < carried), total, piece)


def finish_kernel(
    sizes, count_ref, columns_ref, atom_ref, couplings_ref, projectors_ref, table_ref, out_ref, summed, lined, mixed
):
    blocks, groups, orbitals, slots, length, projectors, width, normalizer = sizes
    kinds = orbitals * 2
    devices = blocks * groups
    share = projectors // devices
    groups_of_rows = kinds // slots
    lanes = lane_ids(slots)
    for chunk in range(projectors // LANES):
        in_chunk = range(chunk * LANES // share, (chunk + 1) * LANES // share)
        for rows in range(groups_of_rows):
            low = width + rows * share
            total = jnp.zeros((slots, LANES), F32)
            for device in in_chunk:
                own = columns_ref[device]
                own = pltpu.roll(jnp.where((lanes >= low) & (lanes < low + share), own, 0.0), (device * share - low) % LANES, 1)
                total += own
            summed[rows * slots : (rows + 1) * slots, chunk * LANES : (chunk + 1) * LANES] = total
    for n in range(orbitals):
        at = kinds + n * 2
        summed[at : at + 1, :] = -summed[n * 2 + 1 : n * 2 + 2, :]
        summed[at + 1 : at + 2, :] = summed[n * 2 : n * 2 + 1, :]
    both = stacked(summed[...])
    atoms = atom_ref[...].astype(F32)
    eye = lax.broadcasted_iota(jnp.int32, (LANES, LANES), 0) == lane_ids(LANES)
    along = []
    for at in range(0, projectors, LANES):
        along.append(jnp.sum(jnp.where(eye, atoms[:, at : at + LANES], 0.0), axis=1, keepdims=True))
    head, rest = split(jnp.where(jnp.concatenate(along, axis=0) == atoms, couplings_ref[...], 0.0))
    head = dot_nt(both, head)
    rest = dot_nt(both, rest)
    weighted = (head[: 2 * kinds] + (head[2 * kinds :] + rest[: 2 * kinds])).astype(BF16)
    for slot in range(slots):
        rows = projectors_ref[slot * length : (slot + 1) * length, :]
        value = dot_nt(weighted, rows)[:kinds]
        rows = projectors_ref[(slots + slot) * length : (slots + slot + 1) * length, :]
        value = value + dot_nt(weighted, rows)[kinds:]
        for row in range(kinds):
            mixed[row, slot : slot + 1, :] = value[row : row + 1, :]
    for chunk in range(blocks * width // LANES):
        for group in range(groups):
            total = jnp.zeros((slots, LANES), F32)
            for inner in range(LANES // width):
                block = chunk * (LANES // width) + inner
                own = jnp.where(lanes < width, columns_ref[block * groups + group], 0.0)
                total += pltpu.roll(own, inner * width, 1)
            lined[group * slots : (group + 1) * slots, chunk * LANES : (chunk + 1) * LANES] = total
    both = stacked(lined[...])
    rows_of_lines = groups * slots
    used = used_slots(count_ref, slots)
    for part in range(2):
        head = dot_nt(both, table_ref[0, part])
        rest = dot_nt(both, table_ref[1, part])
        local = (head[:rows_of_lines] + (head[rows_of_lines:] + rest[:rows_of_lines])) * normalizer
        for n in range(orbitals):
            value = local[n * slots : (n + 1) * slots, :] + mixed[n * 2 + part]
            out_ref[n, part] = jnp.where(used, value, 0.0)


def on_device(orbitals, projectors, potential, couplings, atom_index, column_site, column_count):
    blocks = lax.axis_size("ga")
    groups = lax.axis_size("band")
    devices = blocks * groups
    orbital_count, _, slots, length = orbitals.shape
    planes = potential.shape[0]
    projector_count = projectors.shape[0]
    columns = column_site.shape[0]
    kinds = orbital_count * 2
    assert orbital_count == groups and kinds % slots == 0 and columns % LANES == 0
    share = projector_count // devices
    width = 2
    while width < 2 * planes:
        width *= 2
    carried = width + kinds // slots * share
    assert carried <= LANES and width <= LANES and share * devices == projector_count
    wide = -(-length // LANES) * LANES
    flat = jnp.transpose(projectors, (1, 2, 3, 0)).reshape(2 * slots * length, projector_count)
    z_table = line_table(length, blocks, planes, width)
    batch = next(i for i in (4, 3, 2, 1) if planes % i == 0) if columns <= 512 else 1
    smem = pl.BlockSpec(memory_space=pltpu.SMEM)
    vmem = pl.BlockSpec(memory_space=pltpu.VMEM)
    hbm = pl.BlockSpec(memory_space=pltpu.HBM)
    params = pltpu.CompilerParams(vmem_limit_bytes=56 * 1024 * 1024)
    small = pltpu.CompilerParams(vmem_limit_bytes=40 * 1024 * 1024)
    payload = jax.ShapeDtypeStruct((devices, slots, LANES), F32)

    sent = pl.pallas_call(
        functools.partial(
            project_kernel, (blocks, groups, orbital_count, slots, length, projector_count, width)
        ),
        out_shape=payload,
        in_specs=[hbm] * 4,
        out_specs=vmem,
        scratch_shapes=[
            pltpu.SMEM(column_count.shape, jnp.int32),
            pltpu.VMEM(orbitals.shape, BF16),
            pltpu.VMEM(flat.shape, BF16),
            pltpu.VMEM(z_table.shape, BF16),
            pltpu.VMEM((2 * slots, -(-kinds // 8) * 8, length), F32),
            pltpu.VMEM((2, orbital_count * slots, length), F32),
            pltpu.SemaphoreType.DMA((3,)),
            pltpu.SemaphoreType.DMA((2 * slots,)),
        ],
        compiler_params=params,
        cost_estimate=pl.CostEstimate(
            flops=2 * flat.size * kinds * slots + 4 * z_table.size * orbital_count * slots,
            bytes_accessed=2 * (flat.size + z_table.size + orbitals.size) + 4 * devices * slots * LANES,
            transcendentals=0,
        ),
        name="project",
    )(column_count, orbitals, flat, z_table)
    arrived = lax.all_to_all(sent, ("ga", "band"), split_axis=0, concat_axis=0, tiled=True)

    sent = pl.pallas_call(
        functools.partial(plane_kernel, (devices, slots, planes, length, wide, width, carried, batch)),
        out_shape=payload,
        in_specs=[vmem] * 3,
        out_specs=vmem,
        scratch_shapes=[
            pltpu.VMEM((length, 2 * columns), F32),
            pltpu.VMEM((4 * columns, 2 * wide), BF16),
            pltpu.VMEM((4 * wide, 2 * columns), BF16),
            pltpu.VMEM((columns, LANES), F32),
            pltpu.VMEM((LANES, columns), F32),
            pltpu.VMEM((LANES, columns), F32),
        ],
        compiler_params=small,
        cost_estimate=pl.CostEstimate(
            flops=16 * planes * length * wide * 2 * columns,
            bytes_accessed=4 * (potential.size + 2 * devices * slots * LANES),
            transcendentals=2 * (length + wide) * columns,
        ),
        name="planes",
    )(arrived, column_site.reshape(1, columns), potential)
    arrived = lax.all_to_all(sent, ("ga", "band"), split_axis=0, concat_axis=0, tiled=True)

    normalizer = 1.0 / float(length**3)
    return pl.pallas_call(
        functools.partial(
            finish_kernel,
            (blocks, groups, orbital_count, slots, length, projector_count, width, normalizer),
        ),
        out_shape=jax.ShapeDtypeStruct(orbitals.shape, F32),
        in_specs=[smem] + [vmem] * 5,
        out_specs=vmem,
        scratch_shapes=[
            pltpu.VMEM((2 * kinds, projector_count), F32),
            pltpu.VMEM((groups * slots, blocks * width), F32),
            pltpu.VMEM((kinds, slots, length), F32),
        ],
        compiler_params=small,
        cost_estimate=pl.CostEstimate(
            flops=4 * kinds * (4 * couplings.size + flat.size) + 4 * z_table.size * orbital_count * slots,
            bytes_accessed=4 * couplings.size + 2 * (flat.size + z_table.size) + 4 * orbitals.size,
            transcendentals=0,
        ),
        name="finish",
    )(column_count, arrived, atom_index.reshape(1, projector_count), couplings, flat, z_table)


def solution(mesh):
    return jax.shard_map(
        on_device,
        mesh=mesh,
        in_specs=(
            P(None, None, ("ga", "band"), None),
            P(None, None, ("ga", "band"), None),
            P("ga", None, None),
            P(),
            P(),
            P(),
            P(),
        ),
        out_specs=P(None, None, ("ga", "band"), None),
        check_vma=False,
    )
```

```python
import functools

import jax
import jax.numpy as jnp
import ml_dtypes
import numpy as np
from jax import lax
from jax.experimental import pallas as pl
from jax.experimental.pallas import tpu as pltpu
from jax.sharding import PartitionSpec as P

LANES = 128
BF16 = jnp.bfloat16
F32 = jnp.float32


def pieces_of(table):
    table = np.asarray(table, np.float32)
    head = table.astype(ml_dtypes.bfloat16)
    return np.stack([head, (table - head.astype(np.float32)).astype(ml_dtypes.bfloat16)])


def line_table(length, wide, blocks, planes, width):
    kz = np.arange(length)
    out = np.zeros((blocks, 2, width // 2, 2, wide), np.float64)
    for block in range(blocks):
        z = block * planes + np.arange(planes)
        phases = (z[:, None] * kz[None, :] % length) * (2.0 * np.pi / length)
        out[block, 0, :planes, 0, :length] = np.cos(phases)
        out[block, 1, :planes, 0, :length] = np.sin(phases)
        out[block, 0, :planes, 1, :length] = -np.sin(phases)
        out[block, 1, :planes, 1, :length] = np.cos(phases)
    return pieces_of(out.reshape(blocks * width, 2 * wide))


def split(values):
    head = values.astype(BF16)
    return head, (values - head.astype(F32)).astype(BF16)


def stacked(values):
    head, rest = split(values)
    return jnp.concatenate([head.astype(F32), rest.astype(F32)], axis=0).astype(BF16)


def doubled(values):
    values = values.astype(BF16)
    return jnp.concatenate([values, values], axis=1)


def dot(left, right):
    return lax.dot_general(left, right, (((1,), (0,)), ((), ())), preferred_element_type=F32)


def lane_ids(rows):
    return lax.broadcasted_iota(jnp.int32, (rows, LANES), 1)


def used_slots(count_ref, slots):
    used = count_ref[lax.axis_index("ga")] - lax.axis_index("band") * slots
    return lax.broadcasted_iota(jnp.int32, (slots, 1), 0) < used


def cosine_and_sine(phases, length):
    quarter = jnp.floor(phases * (4.0 / length) + 0.5)
    angle = (phases - quarter * (length / 4.0)) * (2.0 * np.pi / length)
    square = angle * angle
    sine = 1.0 / 362880.0
    for term in (-1.0 / 5040.0, 1.0 / 120.0, -1.0 / 6.0, 1.0):
        sine = sine * square + term
    sine = sine * angle
    cosine = -1.0 / 3628800.0
    for term in (1.0 / 40320.0, -1.0 / 720.0, 1.0 / 24.0, -0.5, 1.0):
        cosine = cosine * square + term
    quarter = quarter - 4.0 * jnp.floor(quarter * 0.25)
    odd = (quarter == 1.0) | (quarter == 3.0)
    first = jnp.where(odd, sine, cosine)
    second = jnp.where(odd, cosine, sine)
    first = jnp.where((quarter == 1.0) | (quarter == 2.0), -first, first)
    return first, jnp.where(quarter >= 2.0, -second, second)


def project_kernel(sizes, count_hbm, orbitals_hbm, projectors_hbm, out_ref, *scratch):
    blocks, groups, orbitals, slots, length, projectors, planes, width = sizes
    count_ref, orbitals_ref, projectors_ref, coef, lines, small_sems, sems = scratch
    kinds = orbitals * 2
    devices = blocks * groups
    share = projectors // devices
    small = [
        pltpu.make_async_copy(count_hbm, count_ref, small_sems.at[0]),
        pltpu.make_async_copy(orbitals_hbm, orbitals_ref, small_sems.at[1]),
    ]
    copies = []
    for piece in range(2 * slots):
        rows = pl.ds(piece * length, length)
        copies.append(pltpu.make_async_copy(projectors_hbm.at[rows], projectors_ref.at[rows], sems.at[piece]))
    for copy in small + copies:
        copy.start()
    half = width // 2
    lanes = lax.broadcasted_iota(jnp.int32, (length, blocks * half), 1)
    plane = (lanes >> (half.bit_length() - 1)) * planes + (lanes & (half - 1))
    kz = lax.broadcasted_iota(jnp.int32, (length, blocks * half), 0)
    table = split(jnp.concatenate(cosine_and_sine(kz.astype(F32) * plane.astype(F32), length), axis=1))
    coef[...] = jnp.zeros_like(coef)
    small[0].wait()
    small[1].wait()
    used = used_slots(count_ref, slots)
    for n in range(orbitals):
        for part in range(2):
            values = jnp.where(used, orbitals_ref[n, part].astype(F32), 0.0)
            at = (part * orbitals + n) * slots
            lines[at : at + slots, :] = values
            turned = values if part == 1 else -values
            for slot in range(slots):
                row = n * 2 + part
                coef[slot, row : row + 1, :] = values[slot : slot + 1, :]
                row = n * 2 + 1 - part
                coef[slots + slot, row : row + 1, :] = turned[slot : slot + 1, :]
    left = lines[...].astype(BF16)
    both = dot(left, table[0]) + dot(left, table[1])
    rows = orbitals * slots
    points = blocks * half
    real = both[:rows, :points] - both[rows:, points:]
    imag = both[:rows, points:] + both[rows:, :points]
    lanes = lane_ids(rows)
    for block in range(blocks):
        at = block * half
        base = at // LANES * LANES
        chunk = pltpu.roll(imag[:, base : base + LANES], (base - at + half) % LANES, 1)
        chunk = jnp.where(lanes < half, pltpu.roll(real[:, base : base + LANES], (base - at) % LANES, 1), chunk)
        for group in range(groups):
            out_ref[block * groups + group] = chunk[group * slots : (group + 1) * slots, :]
    sums = jnp.zeros((coef.shape[1], projectors), F32)
    for piece in range(2 * slots):
        left = coef[piece].astype(BF16)
        copies[piece].wait()
        sums += dot(left, projectors_ref[piece * length : (piece + 1) * length, :])
    lanes = lane_ids(slots)
    for device in range(devices):
        piece = jnp.where(lanes < width, out_ref[device], 0.0)
        first = device * share
        base = first // LANES * LANES
        for rows in range(kinds // slots):
            low = width + rows * share
            own = pltpu.roll(sums[rows * slots : (rows + 1) * slots, base : base + LANES], (base + low - first) % LANES, 1)
            piece = jnp.where((lanes >= low) & (lanes < low + share), own, piece)
        out_ref[device] = piece


def make_tables(length, wide, site_ref, x_ref, plus_ref, minus_ref):
    columns = site_ref.shape[1]
    eye = lax.broadcasted_iota(jnp.int32, (LANES, LANES), 0) == lane_ids(LANES)
    row_ids = lax.broadcasted_iota(jnp.int32, (length, LANES), 0).astype(F32)
    lanes = lax.broadcasted_iota(jnp.int32, (LANES, wide), 1)
    inside = lanes < length
    lanes = lanes.astype(F32)
    for at in range(0, columns, LANES):
        site = site_ref[:, at : at + LANES].astype(F32)
        site_x = jnp.floor((site + 0.5) * (1.0 / length))
        site_y = site - site_x * length
        cosine, sine = cosine_and_sine(row_ids * site_x, length)
        x_ref[:, at : at + LANES] = cosine
        x_ref[:, columns + at : columns + at + LANES] = sine
        along = jnp.sum(jnp.where(eye, site_y, 0.0), axis=1, keepdims=True)
        cosine, sine = cosine_and_sine(lanes * along, length)
        cosine = jnp.where(inside, cosine, 0.0)
        sine = jnp.where(inside, sine, 0.0)
        across = jnp.concatenate([cosine[:, i : i + LANES].T for i in range(0, wide, LANES)], axis=0)
        aside = jnp.concatenate([sine[:, i : i + LANES].T for i in range(0, wide, LANES)], axis=0)
        for piece, (own_cosine, own_sine) in enumerate(zip(split(cosine), split(sine))):
            rows = pl.ds(piece * 2 * columns + at, LANES)
            plus_ref[rows, :wide] = own_cosine
            plus_ref[rows, wide:] = own_sine
            rows = pl.ds((piece * 2 + 1) * columns + at, LANES)
            plus_ref[rows, :wide] = -own_sine
            plus_ref[rows, wide:] = own_cosine
        for piece, (own_cosine, own_sine) in enumerate(zip(split(across), split(aside))):
            rows = pl.ds(piece * 2 * wide, wide)
            minus_ref[rows, at : at + LANES] = own_cosine
            minus_ref[rows, columns + at : columns + at + LANES] = -own_sine
            rows = pl.ds((piece * 2 + 1) * wide, wide)
            minus_ref[rows, at : at + LANES] = own_sine
            minus_ref[rows, columns + at : columns + at + LANES] = own_cosine


def plane_kernel(sizes, columns_ref, site_ref, potential_ref, out_ref, x_ref, plus_ref, minus_ref, gathered, lines, back):
    devices, slots, planes, length, wide, width, carried, batch = sizes
    count = devices * slots
    make_tables(length, wide, site_ref, x_ref, plus_ref, minus_ref)
    total = jnp.zeros((slots, LANES), F32)
    for device in range(devices):
        piece = columns_ref[device]
        gathered[device * slots : (device + 1) * slots, :] = piece
        total += piece
    for at in range(0, count, LANES):
        lines[:, at : at + LANES] = gathered[at : at + LANES, :].T
    back[...] = jnp.zeros_like(back)
    cosine = x_ref[:, :count]
    sine = x_ref[:, count:]
    padding = jnp.zeros((length, wide - length), F32)
    for i in range(planes // batch):
        left = []
        for plane in range(i * batch, (i + 1) * batch):
            real = lines[plane : plane + 1, :]
            imag = lines[plane + width // 2 : plane + width // 2 + 1, :]
            left.append(jnp.concatenate([cosine * real - sine * imag, cosine * imag + sine * real], axis=1))
        left = doubled(jnp.concatenate(left, axis=0))
        field = dot(left, plus_ref[...])
        weights = []
        for plane in range(i * batch, (i + 1) * batch):
            own = jnp.concatenate([potential_ref[plane], padding], axis=1)
            weights.append(jnp.concatenate([own, own], axis=1))
        left = doubled(field * jnp.concatenate(weights, axis=0))
        half = dot(left, minus_ref[...])
        for j in range(batch):
            plane = i * batch + j
            real = half[j * length : (j + 1) * length, :count]
            imag = half[j * length : (j + 1) * length, count:]
            back[plane : plane + 1, :] = jnp.sum(cosine * real + sine * imag, axis=0, keepdims=True)
            at = plane + width // 2
            back[at : at + 1, :] = jnp.sum(cosine * imag - sine * real, axis=0, keepdims=True)
    for at in range(0, count, LANES):
        gathered[at : at + LANES, :] = back[:, at : at + LANES].T
    lanes = lane_ids(slots)
    for device in range(devices):
        piece = gathered[device * slots : (device + 1) * slots, :]
        out_ref[device] = jnp.where((lanes >= width) & (lanes < carried), total, piece)


def finish_kernel(
    sizes, count_ref, columns_ref, atom_ref, couplings_ref, projectors_ref, table_ref, out_ref, summed, lined, mixed
):
    blocks, groups, orbitals, slots, length, projectors, width, normalizer = sizes
    kinds = orbitals * 2
    devices = blocks * groups
    share = projectors // devices
    groups_of_rows = kinds // slots
    lanes = lane_ids(slots)
    for chunk in range(projectors // LANES):
        in_chunk = range(chunk * LANES // share, (chunk + 1) * LANES // share)
        for rows in range(groups_of_rows):
            low = width + rows * share
            total = jnp.zeros((slots, LANES), F32)
            for device in in_chunk:
                own = columns_ref[device]
                own = pltpu.roll(jnp.where((lanes >= low) & (lanes < low + share), own, 0.0), (device * share - low) % LANES, 1)
                total += own
            summed[rows * slots : (rows + 1) * slots, chunk * LANES : (chunk + 1) * LANES] = total
    for n in range(orbitals):
        at = kinds + n * 2
        summed[at : at + 1, :] = -summed[n * 2 + 1 : n * 2 + 2, :]
        summed[at + 1 : at + 2, :] = summed[n * 2 : n * 2 + 1, :]
    across = stacked(summed[...])
    summed_rows = across.shape[0]
    across = jnp.concatenate([across.astype(F32), jnp.zeros((LANES - summed_rows, projectors), F32)], axis=0)
    across = jnp.concatenate([across[:, at : at + LANES].T for at in range(0, projectors, LANES)], axis=0).astype(BF16)
    atoms = atom_ref[...].astype(F32)
    eye = lax.broadcasted_iota(jnp.int32, (LANES, LANES), 0) == lane_ids(LANES)
    along = []
    for at in range(0, projectors, LANES):
        along.append(jnp.sum(jnp.where(eye, atoms[:, at : at + LANES], 0.0), axis=1, keepdims=True))
    head, rest = split(jnp.where(jnp.concatenate(along, axis=0) == atoms, couplings_ref[...], 0.0))
    head = dot(head, across)
    weighted = head + (pltpu.roll(head, LANES - 2 * kinds, 1) + dot(rest, across))
    value = dot(projectors_ref[...], weighted.astype(BF16))
    value = value[: slots * length] + pltpu.roll(value[slots * length :], LANES - kinds, 1)
    for slot in range(slots):
        rows = value[slot * length : (slot + 1) * length, :].T
        for row in range(kinds):
            mixed[row, slot : slot + 1, :] = rows[row : row + 1, :]
    for chunk in range(blocks * width // LANES):
        for group in range(groups):
            total = jnp.zeros((slots, LANES), F32)
            for inner in range(LANES // width):
                block = chunk * (LANES // width) + inner
                own = jnp.where(lanes < width, columns_ref[block * groups + group], 0.0)
                total += pltpu.roll(own, inner * width, 1)
            lined[group * slots : (group + 1) * slots, chunk * LANES : (chunk + 1) * LANES] = total
    both = stacked(lined[...])
    rows_of_lines = groups * slots
    used = used_slots(count_ref, slots)
    head = dot(both, table_ref[0])
    rest = dot(both, table_ref[1])
    local = (head[:rows_of_lines] + (head[rows_of_lines:] + rest[:rows_of_lines])) * normalizer
    wide = local.shape[1] // 2
    for part in range(2):
        for n in range(orbitals):
            value = local[n * slots : (n + 1) * slots, part * wide : part * wide + length] + mixed[n * 2 + part]
            out_ref[n, part] = jnp.where(used, value, 0.0)


def on_device(orbitals, projectors, potential, couplings, atom_index, column_site, column_count):
    blocks = lax.axis_size("ga")
    groups = lax.axis_size("band")
    devices = blocks * groups
    orbital_count, _, slots, length = orbitals.shape
    planes = potential.shape[0]
    projector_count = projectors.shape[0]
    columns = column_site.shape[0]
    kinds = orbital_count * 2
    assert orbital_count == groups and kinds % slots == 0 and columns % LANES == 0
    share = projector_count // devices
    width = 2
    while width < 2 * planes:
        width *= 2
    carried = width + kinds // slots * share
    assert carried <= LANES and width <= LANES and share * devices == projector_count
    wide = -(-length // LANES) * LANES
    flat = jnp.transpose(projectors, (1, 2, 3, 0)).reshape(2 * slots * length, projector_count)
    z_table = line_table(length, wide, blocks, planes, width)
    batch = next(i for i in (4, 3, 2, 1) if planes % i == 0) if columns <= 512 else 1
    smem = pl.BlockSpec(memory_space=pltpu.SMEM)
    vmem = pl.BlockSpec(memory_space=pltpu.VMEM)
    hbm = pl.BlockSpec(memory_space=pltpu.HBM)
    params = pltpu.CompilerParams(vmem_limit_bytes=56 * 1024 * 1024)
    small = pltpu.CompilerParams(vmem_limit_bytes=40 * 1024 * 1024)
    payload = jax.ShapeDtypeStruct((devices, slots, LANES), F32)

    sent = pl.pallas_call(
        functools.partial(
            project_kernel,
                (blocks, groups, orbital_count, slots, length, projector_count, planes, width),
        ),
        out_shape=payload,
        in_specs=[hbm] * 3,
        out_specs=vmem,
        scratch_shapes=[
            pltpu.SMEM(column_count.shape, jnp.int32),
            pltpu.VMEM(orbitals.shape, BF16),
            pltpu.VMEM(flat.shape, BF16),
            pltpu.VMEM((2 * slots, -(-kinds // 8) * 8, length), F32),
            pltpu.VMEM((kinds * slots, length), F32),
            pltpu.SemaphoreType.DMA((2,)),
            pltpu.SemaphoreType.DMA((2 * slots,)),
        ],
        compiler_params=params,
        cost_estimate=pl.CostEstimate(
            flops=2 * flat.size * kinds + 8 * length * blocks * width * kinds * slots,
            bytes_accessed=2 * (flat.size + orbitals.size) + 4 * devices * slots * LANES,
            transcendentals=length * blocks * width,
        ),
        name="project",
    )(column_count, orbitals, flat)
    arrived = lax.all_to_all(sent, ("ga", "band"), split_axis=0, concat_axis=0, tiled=True)

    sent = pl.pallas_call(
        functools.partial(plane_kernel, (devices, slots, planes, length, wide, width, carried, batch)),
        out_shape=payload,
        in_specs=[vmem] * 3,
        out_specs=vmem,
        scratch_shapes=[
            pltpu.VMEM((length, 2 * columns), F32),
            pltpu.VMEM((4 * columns, 2 * wide), BF16),
            pltpu.VMEM((4 * wide, 2 * columns), BF16),
            pltpu.VMEM((columns, LANES), F32),
            pltpu.VMEM((LANES, columns), F32),
            pltpu.VMEM((LANES, columns), F32),
        ],
        compiler_params=small,
        cost_estimate=pl.CostEstimate(
            flops=16 * planes * length * wide * 2 * columns,
            bytes_accessed=4 * (potential.size + 2 * devices * slots * LANES),
            transcendentals=2 * (length + wide) * columns,
        ),
        name="planes",
    )(arrived, column_site.reshape(1, columns), potential)
    arrived = lax.all_to_all(sent, ("ga", "band"), split_axis=0, concat_axis=0, tiled=True)

    normalizer = 1.0 / float(length**3)
    return pl.pallas_call(
        functools.partial(
            finish_kernel,
            (blocks, groups, orbital_count, slots, length, projector_count, width, normalizer),
        ),
        out_shape=jax.ShapeDtypeStruct(orbitals.shape, F32),
        in_specs=[smem] + [vmem] * 5,
        out_specs=vmem,
        scratch_shapes=[
            pltpu.VMEM((2 * kinds, projector_count), F32),
            pltpu.VMEM((groups * slots, blocks * width), F32),
            pltpu.VMEM((kinds, slots, length), F32),
        ],
        compiler_params=small,
        cost_estimate=pl.CostEstimate(
            flops=4 * kinds * (4 * couplings.size + flat.size) + 4 * z_table.size * orbital_count * slots,
            bytes_accessed=4 * couplings.size + 2 * (flat.size + z_table.size) + 4 * orbitals.size,
            transcendentals=0,
        ),
        name="finish",
    )(column_count, arrived, atom_index.reshape(1, projector_count), couplings, flat, z_table)


def solution(mesh):
    return jax.shard_map(
        on_device,
        mesh=mesh,
        in_specs=(
            P(None, None, ("ga", "band"), None),
            P(None, None, ("ga", "band"), None),
            P("ga", None, None),
            P(),
            P(),
            P(),
            P(),
        ),
        out_specs=P(None, None, ("ga", "band"), None),
        check_vma=False,
    )
```

```python
import functools

import jax
import jax.numpy as jnp
import ml_dtypes
import numpy as np
from jax import lax
from jax.experimental import pallas as pl
from jax.experimental.pallas import tpu as pltpu
from jax.sharding import PartitionSpec as P

LANES = 128
BF16 = jnp.bfloat16
F32 = jnp.float32


def pieces_of(table):
    table = np.asarray(table, np.float32)
    head = table.astype(ml_dtypes.bfloat16)
    return np.stack([head, (table - head.astype(np.float32)).astype(ml_dtypes.bfloat16)])


def line_table(length, blocks, planes, width):
    kz = np.arange(length)
    out = np.zeros((2, length, blocks, width), np.float64)
    for block in range(blocks):
        z = block * planes + np.arange(planes)
        phases = (kz[:, None] * z[None, :] % length) * (2.0 * np.pi / length)
        out[0, :, block, :planes] = np.cos(phases)
        out[0, :, block, width // 2 : width // 2 + planes] = np.sin(phases)
        out[1, :, block, :planes] = -np.sin(phases)
        out[1, :, block, width // 2 : width // 2 + planes] = np.cos(phases)
    return pieces_of(out.reshape(2, length, blocks * width))


def split(values):
    head = values.astype(BF16)
    return head, (values - head.astype(F32)).astype(BF16)


def stacked(values):
    head, rest = split(values)
    return jnp.concatenate([head.astype(F32), rest.astype(F32)], axis=0).astype(BF16)


def doubled(values):
    values = values.astype(BF16)
    return jnp.concatenate([values, values], axis=1)


def dot(left, right):
    return lax.dot_general(left, right, (((1,), (0,)), ((), ())), preferred_element_type=F32)


def dot_nt(left, right):
    return lax.dot_general(left, right, (((1,), (1,)), ((), ())), preferred_element_type=F32)


def lane_ids(rows):
    return lax.broadcasted_iota(jnp.int32, (rows, LANES), 1)


def used_slots(count_ref, slots):
    used = count_ref[lax.axis_index("ga")] - lax.axis_index("band") * slots
    return lax.broadcasted_iota(jnp.int32, (slots, 1), 0) < used


def cosine_and_sine(phases, length):
    quarter = jnp.floor(phases * (4.0 / length) + 0.5)
    angle = (phases - quarter * (length / 4.0)) * (2.0 * np.pi / length)
    square = angle * angle
    sine = 1.0 / 362880.0
    for term in (-1.0 / 5040.0, 1.0 / 120.0, -1.0 / 6.0, 1.0):
        sine = sine * square + term
    sine = sine * angle
    cosine = -1.0 / 3628800.0
    for term in (1.0 / 40320.0, -1.0 / 720.0, 1.0 / 24.0, -0.5, 1.0):
        cosine = cosine * square + term
    quarter = quarter - 4.0 * jnp.floor(quarter * 0.25)
    odd = (quarter == 1.0) | (quarter == 3.0)
    first = jnp.where(odd, sine, cosine)
    second = jnp.where(odd, cosine, sine)
    first = jnp.where((quarter == 1.0) | (quarter == 2.0), -first, first)
    return first, jnp.where(quarter >= 2.0, -second, second)


def project_kernel(sizes, count_hbm, orbitals_hbm, projectors_hbm, out_ref, *scratch):
    blocks, groups, orbitals, slots, length, projectors, planes, width = sizes
    count_ref, orbitals_ref, projectors_ref, coef, lines, small_sems, sems = scratch
    kinds = orbitals * 2
    devices = blocks * groups
    share = projectors // devices
    small = [
        pltpu.make_async_copy(count_hbm, count_ref, small_sems.at[0]),
        pltpu.make_async_copy(orbitals_hbm, orbitals_ref, small_sems.at[1]),
    ]
    copies = []
    for piece in range(2 * slots):
        rows = pl.ds(piece * length, length)
        copies.append(pltpu.make_async_copy(projectors_hbm.at[rows], projectors_ref.at[rows], sems.at[piece]))
    for copy in small + copies:
        copy.start()
    half = width // 2
    lanes = lax.broadcasted_iota(jnp.int32, (length, blocks * half), 1)
    plane = (lanes >> (half.bit_length() - 1)) * planes + (lanes & (half - 1))
    kz = lax.broadcasted_iota(jnp.int32, (length, blocks * half), 0)
    table = split(jnp.concatenate(cosine_and_sine(kz.astype(F32) * plane.astype(F32), length), axis=1))
    coef[...] = jnp.zeros_like(coef)
    small[0].wait()
    small[1].wait()
    used = used_slots(count_ref, slots)
    for n in range(orbitals):
        for part in range(2):
            values = jnp.where(used, orbitals_ref[n, part].astype(F32), 0.0)
            at = (part * orbitals + n) * slots
            lines[at : at + slots, :] = values
            turned = values if part == 1 else -values
            for slot in range(slots):
                row = n * 2 + part
                coef[slot, row : row + 1, :] = values[slot : slot + 1, :]
                row = n * 2 + 1 - part
                coef[slots + slot, row : row + 1, :] = turned[slot : slot + 1, :]
    left = lines[...].astype(BF16)
    both = dot(left, table[0]) + dot(left, table[1])
    rows = orbitals * slots
    points = blocks * half
    real = both[:rows, :points] - both[rows:, points:]
    imag = both[:rows, points:] + both[rows:, :points]
    lanes = lane_ids(rows)
    for block in range(blocks):
        at = block * half
        base = at // LANES * LANES
        chunk = pltpu.roll(imag[:, base : base + LANES], (base - at + half) % LANES, 1)
        chunk = jnp.where(lanes < half, pltpu.roll(real[:, base : base + LANES], (base - at) % LANES, 1), chunk)
        for group in range(groups):
            out_ref[block * groups + group] = chunk[group * slots : (group + 1) * slots, :]
    sums = jnp.zeros((coef.shape[1], projectors), F32)
    for piece in range(2 * slots):
        left = coef[piece].astype(BF16)
        copies[piece].wait()
        sums += dot(left, projectors_ref[piece * length : (piece + 1) * length, :])
    lanes = lane_ids(slots)
    for device in range(devices):
        piece = jnp.where(lanes < width, out_ref[device], 0.0)
        first = device * share
        base = first // LANES * LANES
        for rows in range(kinds // slots):
            low = width + rows * share
            own = pltpu.roll(sums[rows * slots : (rows + 1) * slots, base : base + LANES], (base + low - first) % LANES, 1)
            piece = jnp.where((lanes >= low) & (lanes < low + share), own, piece)
        out_ref[device] = piece


def make_tables(length, wide, site_ref, x_ref, plus_ref, minus_ref):
    columns = site_ref.shape[1]
    eye = lax.broadcasted_iota(jnp.int32, (LANES, LANES), 0) == lane_ids(LANES)
    row_ids = lax.broadcasted_iota(jnp.int32, (length, LANES), 0).astype(F32)
    lanes = lax.broadcasted_iota(jnp.int32, (LANES, wide), 1)
    inside = lanes < length
    lanes = lanes.astype(F32)
    for at in range(0, columns, LANES):
        site = site_ref[:, at : at + LANES].astype(F32)
        site_x = jnp.floor((site + 0.5) * (1.0 / length))
        site_y = site - site_x * length
        cosine, sine = cosine_and_sine(row_ids * site_x, length)
        x_ref[:, at : at + LANES] = cosine
        x_ref[:, columns + at : columns + at + LANES] = sine
        along = jnp.sum(jnp.where(eye, site_y, 0.0), axis=1, keepdims=True)
        cosine, sine = cosine_and_sine(lanes * along, length)
        cosine = jnp.where(inside, cosine, 0.0)
        sine = jnp.where(inside, sine, 0.0)
        across = jnp.concatenate([cosine[:, i : i + LANES].T for i in range(0, wide, LANES)], axis=0)
        aside = jnp.concatenate([sine[:, i : i + LANES].T for i in range(0, wide, LANES)], axis=0)
        for piece, (own_cosine, own_sine) in enumerate(zip(split(cosine), split(sine))):
            rows = pl.ds(piece * 2 * columns + at, LANES)
            plus_ref[rows, :wide] = own_cosine
            plus_ref[rows, wide:] = own_sine
            rows = pl.ds((piece * 2 + 1) * columns + at, LANES)
            plus_ref[rows, :wide] = -own_sine
            plus_ref[rows, wide:] = own_cosine
        for piece, (own_cosine, own_sine) in enumerate(zip(split(across), split(aside))):
            rows = pl.ds(piece * 2 * wide, wide)
            minus_ref[rows, at : at + LANES] = own_cosine
            minus_ref[rows, columns + at : columns + at + LANES] = -own_sine
            rows = pl.ds((piece * 2 + 1) * wide, wide)
            minus_ref[rows, at : at + LANES] = own_sine
            minus_ref[rows, columns + at : columns + at + LANES] = own_cosine


def plane_kernel(sizes, columns_ref, site_ref, potential_ref, out_ref, x_ref, plus_ref, minus_ref, gathered, lines, back):
    devices, slots, planes, length, wide, width, carried, batch = sizes
    count = devices * slots
    make_tables(length, wide, site_ref, x_ref, plus_ref, minus_ref)
    total = jnp.zeros((slots, LANES), F32)
    for device in range(devices):
        piece = columns_ref[device]
        gathered[device * slots : (device + 1) * slots, :] = piece
        total += piece
    for at in range(0, count, LANES):
        lines[:, at : at + LANES] = gathered[at : at + LANES, :].T
    back[...] = jnp.zeros_like(back)
    cosine = x_ref[:, :count]
    sine = x_ref[:, count:]
    padding = jnp.zeros((length, wide - length), F32)
    for i in range(planes // batch):
        left = []
        for plane in range(i * batch, (i + 1) * batch):
            real = lines[plane : plane + 1, :]
            imag = lines[plane + width // 2 : plane + width // 2 + 1, :]
            left.append(jnp.concatenate([cosine * real - sine * imag, cosine * imag + sine * real], axis=1))
        left = doubled(jnp.concatenate(left, axis=0))
        field = dot(left, plus_ref[...])
        weights = []
        for plane in range(i * batch, (i + 1) * batch):
            own = jnp.concatenate([potential_ref[plane], padding], axis=1)
            weights.append(jnp.concatenate([own, own], axis=1))
        left = doubled(field * jnp.concatenate(weights, axis=0))
        half = dot(left, minus_ref[...])
        for j in range(batch):
            plane = i * batch + j
            real = half[j * length : (j + 1) * length, :count]
            imag = half[j * length : (j + 1) * length, count:]
            back[plane : plane + 1, :] = jnp.sum(cosine * real + sine * imag, axis=0, keepdims=True)
            at = plane + width // 2
            back[at : at + 1, :] = jnp.sum(cosine * imag - sine * real, axis=0, keepdims=True)
    for at in range(0, count, LANES):
        gathered[at : at + LANES, :] = back[:, at : at + LANES].T
    lanes = lane_ids(slots)
    for device in range(devices):
        piece = gathered[device * slots : (device + 1) * slots, :]
        out_ref[device] = jnp.where((lanes >= width) & (lanes < carried), total, piece)


def finish_kernel(
    sizes, count_ref, columns_ref, atom_ref, couplings_ref, projectors_ref, table_ref, out_ref, summed, lined, mixed
):
    blocks, groups, orbitals, slots, length, projectors, width, normalizer = sizes
    kinds = orbitals * 2
    devices = blocks * groups
    share = projectors // devices
    groups_of_rows = kinds // slots
    lanes = lane_ids(slots)
    for chunk in range(projectors // LANES):
        in_chunk = range(chunk * LANES // share, (chunk + 1) * LANES // share)
        for rows in range(groups_of_rows):
            low = width + rows * share
            total = jnp.zeros((slots, LANES), F32)
            for device in in_chunk:
                own = columns_ref[device]
                own = pltpu.roll(jnp.where((lanes >= low) & (lanes < low + share), own, 0.0), (device * share - low) % LANES, 1)
                total += own
            summed[rows * slots : (rows + 1) * slots, chunk * LANES : (chunk + 1) * LANES] = total
    for n in range(orbitals):
        at = kinds + n * 2
        summed[at : at + 1, :] = -summed[n * 2 + 1 : n * 2 + 2, :]
        summed[at + 1 : at + 2, :] = summed[n * 2 : n * 2 + 1, :]
    both = stacked(summed[...])
    atoms = atom_ref[...].astype(F32)
    eye = lax.broadcasted_iota(jnp.int32, (LANES, LANES), 0) == lane_ids(LANES)
    along = []
    for at in range(0, projectors, LANES):
        along.append(jnp.sum(jnp.where(eye, atoms[:, at : at + LANES], 0.0), axis=1, keepdims=True))
    head, rest = split(jnp.where(jnp.concatenate(along, axis=0) == atoms, couplings_ref[...], 0.0))
    head = dot_nt(both, head)
    rest = dot_nt(both, rest)
    weighted = (head[: 2 * kinds] + (head[2 * kinds :] + rest[: 2 * kinds])).astype(BF16)
    for slot in range(slots):
        rows = projectors_ref[slot * length : (slot + 1) * length, :]
        value = dot_nt(weighted, rows)[:kinds]
        rows = projectors_ref[(slots + slot) * length : (slots + slot + 1) * length, :]
        value = value + dot_nt(weighted, rows)[kinds:]
        for row in range(kinds):
            mixed[row, slot : slot + 1, :] = value[row : row + 1, :]
    for chunk in range(blocks * width // LANES):
        for group in range(groups):
            total = jnp.zeros((slots, LANES), F32)
            for inner in range(LANES // width):
                block = chunk * (LANES // width) + inner
                own = jnp.where(lanes < width, columns_ref[block * groups + group], 0.0)
                total += pltpu.roll(own, inner * width, 1)
            lined[group * slots : (group + 1) * slots, chunk * LANES : (chunk + 1) * LANES] = total
    both = stacked(lined[...])
    rows_of_lines = groups * slots
    used = used_slots(count_ref, slots)
    for part in range(2):
        head = dot_nt(both, table_ref[0, part])
        rest = dot_nt(both, table_ref[1, part])
        local = (head[:rows_of_lines] + (head[rows_of_lines:] + rest[:rows_of_lines])) * normalizer
        for n in range(orbitals):
            value = local[n * slots : (n + 1) * slots, :] + mixed[n * 2 + part]
            out_ref[n, part] = jnp.where(used, value, 0.0)


def on_device(orbitals, projectors, potential, couplings, atom_index, column_site, column_count):
    blocks = lax.axis_size("ga")
    groups = lax.axis_size("band")
    devices = blocks * groups
    orbital_count, _, slots, length = orbitals.shape
    planes = potential.shape[0]
    projector_count = projectors.shape[0]
    columns = column_site.shape[0]
    kinds = orbital_count * 2
    assert orbital_count == groups and kinds % slots == 0 and columns % LANES == 0
    share = projector_count // devices
    width = 2
    while width < 2 * planes:
        width *= 2
    carried = width + kinds // slots * share
    assert carried <= LANES and width <= LANES and share * devices == projector_count
    wide = -(-length // LANES) * LANES
    flat = jnp.transpose(projectors, (1, 2, 3, 0)).reshape(2 * slots * length, projector_count)
    z_table = line_table(length, blocks, planes, width)
    batch = next(i for i in (4, 3, 2, 1) if planes % i == 0) if columns <= 512 else 1
    smem = pl.BlockSpec(memory_space=pltpu.SMEM)
    vmem = pl.BlockSpec(memory_space=pltpu.VMEM)
    hbm = pl.BlockSpec(memory_space=pltpu.HBM)
    params = pltpu.CompilerParams(vmem_limit_bytes=56 * 1024 * 1024)
    small = pltpu.CompilerParams(vmem_limit_bytes=40 * 1024 * 1024)
    payload = jax.ShapeDtypeStruct((devices, slots, LANES), F32)

    sent = pl.pallas_call(
        functools.partial(
            project_kernel,
                (blocks, groups, orbital_count, slots, length, projector_count, planes, width),
        ),
        out_shape=payload,
        in_specs=[hbm] * 3,
        out_specs=vmem,
        scratch_shapes=[
            pltpu.SMEM(column_count.shape, jnp.int32),
            pltpu.VMEM(orbitals.shape, BF16),
            pltpu.VMEM(flat.shape, BF16),
            pltpu.VMEM((2 * slots, -(-kinds // 8) * 8, length), F32),
            pltpu.VMEM((kinds * slots, length), F32),
            pltpu.SemaphoreType.DMA((2,)),
            pltpu.SemaphoreType.DMA((2 * slots,)),
        ],
        compiler_params=params,
        cost_estimate=pl.CostEstimate(
            flops=2 * flat.size * kinds * slots + 4 * z_table.size * orbital_count * slots,
            bytes_accessed=2 * (flat.size + z_table.size + orbitals.size) + 4 * devices * slots * LANES,
            transcendentals=length * blocks * width,
        ),
        name="project",
    )(column_count, orbitals, flat)
    arrived = lax.all_to_all(sent, ("ga", "band"), split_axis=0, concat_axis=0, tiled=True)

    sent = pl.pallas_call(
        functools.partial(plane_kernel, (devices, slots, planes, length, wide, width, carried, batch)),
        out_shape=payload,
        in_specs=[vmem] * 3,
        out_specs=vmem,
        scratch_shapes=[
            pltpu.VMEM((length, 2 * columns), F32),
            pltpu.VMEM((4 * columns, 2 * wide), BF16),
            pltpu.VMEM((4 * wide, 2 * columns), BF16),
            pltpu.VMEM((columns, LANES), F32),
            pltpu.VMEM((LANES, columns), F32),
            pltpu.VMEM((LANES, columns), F32),
        ],
        compiler_params=small,
        cost_estimate=pl.CostEstimate(
            flops=16 * planes * length * wide * 2 * columns,
            bytes_accessed=4 * (potential.size + 2 * devices * slots * LANES),
            transcendentals=2 * (length + wide) * columns,
        ),
        name="planes",
    )(arrived, column_site.reshape(1, columns), potential)
    arrived = lax.all_to_all(sent, ("ga", "band"), split_axis=0, concat_axis=0, tiled=True)

    normalizer = 1.0 / float(length**3)
    return pl.pallas_call(
        functools.partial(
            finish_kernel,
            (blocks, groups, orbital_count, slots, length, projector_count, width, normalizer),
        ),
        out_shape=jax.ShapeDtypeStruct(orbitals.shape, F32),
        in_specs=[smem] + [vmem] * 5,
        out_specs=vmem,
        scratch_shapes=[
            pltpu.VMEM((2 * kinds, projector_count), F32),
            pltpu.VMEM((groups * slots, blocks * width), F32),
            pltpu.VMEM((kinds, slots, length), F32),
        ],
        compiler_params=small,
        cost_estimate=pl.CostEstimate(
            flops=4 * kinds * (4 * couplings.size + flat.size) + 4 * z_table.size * orbital_count * slots,
            bytes_accessed=4 * couplings.size + 2 * (flat.size + z_table.size) + 4 * orbitals.size,
            transcendentals=0,
        ),
        name="finish",
    )(column_count, arrived, atom_index.reshape(1, projector_count), couplings, flat, z_table)


def solution(mesh):
    return jax.shard_map(
        on_device,
        mesh=mesh,
        in_specs=(
            P(None, None, ("ga", "band"), None),
            P(None, None, ("ga", "band"), None),
            P("ga", None, None),
            P(),
            P(),
            P(),
            P(),
        ),
        out_specs=P(None, None, ("ga", "band"), None),
        check_vma=False,
    )
```

```python
import functools

import jax
import jax.numpy as jnp
import ml_dtypes
import numpy as np
from jax import lax
from jax.experimental import pallas as pl
from jax.experimental.pallas import tpu as pltpu
from jax.sharding import PartitionSpec as P

LANES = 128
BF16 = jnp.bfloat16
F32 = jnp.float32


def pieces_of(table):
    table = np.asarray(table, np.float32)
    head = table.astype(ml_dtypes.bfloat16)
    return np.stack([head, (table - head.astype(np.float32)).astype(ml_dtypes.bfloat16)])


def line_table(length, blocks, planes, width):
    kz = np.arange(length)
    out = np.zeros((2, length, blocks, width), np.float64)
    for block in range(blocks):
        z = block * planes + np.arange(planes)
        phases = (kz[:, None] * z[None, :] % length) * (2.0 * np.pi / length)
        out[0, :, block, :planes] = np.cos(phases)
        out[0, :, block, width // 2 : width // 2 + planes] = np.sin(phases)
        out[1, :, block, :planes] = -np.sin(phases)
        out[1, :, block, width // 2 : width // 2 + planes] = np.cos(phases)
    return pieces_of(out.reshape(2, length, blocks * width))


def split(values):
    head = values.astype(BF16)
    return head, (values - head.astype(F32)).astype(BF16)


def stacked(values):
    head, rest = split(values)
    return jnp.concatenate([head.astype(F32), rest.astype(F32)], axis=0).astype(BF16)


def doubled(values):
    values = values.astype(BF16)
    return jnp.concatenate([values, values], axis=1)


def dot(left, right):
    return lax.dot_general(left, right, (((1,), (0,)), ((), ())), preferred_element_type=F32)


def dot_nt(left, right):
    return lax.dot_general(left, right, (((1,), (1,)), ((), ())), preferred_element_type=F32)


def lane_ids(rows):
    return lax.broadcasted_iota(jnp.int32, (rows, LANES), 1)


def used_slots(count_ref, slots):
    used = count_ref[lax.axis_index("ga")] - lax.axis_index("band") * slots
    return lax.broadcasted_iota(jnp.int32, (slots, 1), 0) < used


def cosine_and_sine(phases, length):
    quarter = jnp.floor(phases * (4.0 / length) + 0.5)
    angle = (phases - quarter * (length / 4.0)) * (2.0 * np.pi / length)
    square = angle * angle
    sine = 1.0 / 362880.0
    for term in (-1.0 / 5040.0, 1.0 / 120.0, -1.0 / 6.0, 1.0):
        sine = sine * square + term
    sine = sine * angle
    cosine = -1.0 / 3628800.0
    for term in (1.0 / 40320.0, -1.0 / 720.0, 1.0 / 24.0, -0.5, 1.0):
        cosine = cosine * square + term
    quarter = quarter - 4.0 * jnp.floor(quarter * 0.25)
    odd = (quarter == 1.0) | (quarter == 3.0)
    first = jnp.where(odd, sine, cosine)
    second = jnp.where(odd, cosine, sine)
    first = jnp.where((quarter == 1.0) | (quarter == 2.0), -first, first)
    return first, jnp.where(quarter >= 2.0, -second, second)


def project_kernel(sizes, count_hbm, orbitals_hbm, projectors_hbm, out_ref, *scratch):
    blocks, groups, orbitals, slots, length, projectors, planes, width = sizes
    count_ref, orbitals_ref, projectors_ref, coef, lines, small_sems, sems = scratch
    kinds = orbitals * 2
    devices = blocks * groups
    share = projectors // devices
    small = [
        pltpu.make_async_copy(count_hbm, count_ref, small_sems.at[0]),
        pltpu.make_async_copy(orbitals_hbm, orbitals_ref, small_sems.at[1]),
    ]
    copies = []
    for piece in range(2 * slots):
        rows = pl.ds(piece * length, length)
        copies.append(pltpu.make_async_copy(projectors_hbm.at[rows], projectors_ref.at[rows], sems.at[piece]))
    for copy in small + copies:
        copy.start()
    half = width // 2
    lanes = lax.broadcasted_iota(jnp.int32, (length, blocks * half), 1)
    plane = (lanes >> (half.bit_length() - 1)) * planes + (lanes & (half - 1))
    kz = lax.broadcasted_iota(jnp.int32, (length, blocks * half), 0)
    table = split(jnp.concatenate(cosine_and_sine(kz.astype(F32) * plane.astype(F32), length), axis=1))
    coef[...] = jnp.zeros_like(coef)
    small[0].wait()
    small[1].wait()
    used = used_slots(count_ref, slots)
    for n in range(orbitals):
        for part in range(2):
            values = jnp.where(used, orbitals_ref[n, part].astype(F32), 0.0)
            at = (part * orbitals + n) * slots
            lines[at : at + slots, :] = values
            turned = values if part == 1 else -values
            for slot in range(slots):
                row = n * 2 + part
                coef[slot, row : row + 1, :] = values[slot : slot + 1, :]
                row = n * 2 + 1 - part
                coef[slots + slot, row : row + 1, :] = turned[slot : slot + 1, :]
    left = lines[...].astype(BF16)
    both = dot(left, table[0]) + dot(left, table[1])
    rows = orbitals * slots
    points = blocks * half
    real = both[:rows, :points] - both[rows:, points:]
    imag = both[:rows, points:] + both[rows:, :points]
    lanes = lane_ids(rows)
    for block in range(blocks):
        at = block * half
        base = at // LANES * LANES
        chunk = pltpu.roll(imag[:, base : base + LANES], (base - at + half) % LANES, 1)
        chunk = jnp.where(lanes < half, pltpu.roll(real[:, base : base + LANES], (base - at) % LANES, 1), chunk)
        for group in range(groups):
            out_ref[block * groups + group] = chunk[group * slots : (group + 1) * slots, :]
    sums = jnp.zeros((coef.shape[1], projectors), F32)
    for piece in range(2 * slots):
        left = coef[piece].astype(BF16)
        copies[piece].wait()
        sums += dot(left, projectors_ref[piece * length : (piece + 1) * length, :])
    lanes = lane_ids(slots)
    for device in range(devices):
        piece = jnp.where(lanes < width, out_ref[device], 0.0)
        first = device * share
        base = first // LANES * LANES
        for rows in range(kinds // slots):
            low = width + rows * share
            own = pltpu.roll(sums[rows * slots : (rows + 1) * slots, base : base + LANES], (base + low - first) % LANES, 1)
            piece = jnp.where((lanes >= low) & (lanes < low + share), own, piece)
        out_ref[device] = piece


def make_tables(length, wide, site_ref, x_ref, plus_ref, minus_ref):
    columns = site_ref.shape[1]
    eye = lax.broadcasted_iota(jnp.int32, (LANES, LANES), 0) == lane_ids(LANES)
    row_ids = lax.broadcasted_iota(jnp.int32, (length, LANES), 0).astype(F32)
    lanes = lax.broadcasted_iota(jnp.int32, (LANES, wide), 1)
    inside = lanes < length
    lanes = lanes.astype(F32)
    for at in range(0, columns, LANES):
        site = site_ref[:, at : at + LANES].astype(F32)
        site_x = jnp.floor((site + 0.5) * (1.0 / length))
        site_y = site - site_x * length
        cosine, sine = cosine_and_sine(row_ids * site_x, length)
        x_ref[:, at : at + LANES] = cosine
        x_ref[:, columns + at : columns + at + LANES] = sine
        along = jnp.sum(jnp.where(eye, site_y, 0.0), axis=1, keepdims=True)
        cosine, sine = cosine_and_sine(lanes * along, length)
        cosine = jnp.where(inside, cosine, 0.0)
        sine = jnp.where(inside, sine, 0.0)
        across = jnp.concatenate([cosine[:, i : i + LANES].T for i in range(0, wide, LANES)], axis=0)
        aside = jnp.concatenate([sine[:, i : i + LANES].T for i in range(0, wide, LANES)], axis=0)
        for piece, (own_cosine, own_sine) in enumerate(zip(split(cosine), split(sine))):
            rows = pl.ds(piece * 2 * columns + at, LANES)
            plus_ref[rows, :wide] = own_cosine
            plus_ref[rows, wide:] = own_sine
            rows = pl.ds((piece * 2 + 1) * columns + at, LANES)
            plus_ref[rows, :wide] = -own_sine
            plus_ref[rows, wide:] = own_cosine
        for piece, (own_cosine, own_sine) in enumerate(zip(split(across), split(aside))):
            rows = pl.ds(piece * 2 * wide, wide)
            minus_ref[rows, at : at + LANES] = own_cosine
            minus_ref[rows, columns + at : columns + at + LANES] = -own_sine
            rows = pl.ds((piece * 2 + 1) * wide, wide)
            minus_ref[rows, at : at + LANES] = own_sine
            minus_ref[rows, columns + at : columns + at + LANES] = own_cosine


def plane_kernel(sizes, columns_ref, site_ref, potential_ref, out_ref, x_ref, plus_ref, minus_ref, gathered, lines, back):
    devices, slots, planes, length, wide, width, carried, batch = sizes
    count = devices * slots
    make_tables(length, wide, site_ref, x_ref, plus_ref, minus_ref)
    total = jnp.zeros((slots, LANES), F32)
    for device in range(devices):
        piece = columns_ref[device]
        gathered[device * slots : (device + 1) * slots, :] = piece
        total += piece
    for at in range(0, count, LANES):
        lines[:, at : at + LANES] = gathered[at : at + LANES, :].T
    back[...] = jnp.zeros_like(back)
    cosine = x_ref[:, :count]
    sine = x_ref[:, count:]
    padding = jnp.zeros((length, wide - length), F32)
    for i in range(planes // batch):
        left = []
        for plane in range(i * batch, (i + 1) * batch):
            real = lines[plane : plane + 1, :]
            imag = lines[plane + width // 2 : plane + width // 2 + 1, :]
            left.append(jnp.concatenate([cosine * real - sine * imag, cosine * imag + sine * real], axis=1))
        left = doubled(jnp.concatenate(left, axis=0))
        field = dot(left, plus_ref[...])
        weights = []
        for plane in range(i * batch, (i + 1) * batch):
            own = jnp.concatenate([potential_ref[plane], padding], axis=1)
            weights.append(jnp.concatenate([own, own], axis=1))
        left = doubled(field * jnp.concatenate(weights, axis=0))
        half = dot(left, minus_ref[...])
        for j in range(batch):
            plane = i * batch + j
            real = half[j * length : (j + 1) * length, :count]
            imag = half[j * length : (j + 1) * length, count:]
            back[plane : plane + 1, :] = jnp.sum(cosine * real + sine * imag, axis=0, keepdims=True)
            at = plane + width // 2
            back[at : at + 1, :] = jnp.sum(cosine * imag - sine * real, axis=0, keepdims=True)
    for at in range(0, count, LANES):
        gathered[at : at + LANES, :] = back[:, at : at + LANES].T
    lanes = lane_ids(slots)
    for device in range(devices):
        piece = gathered[device * slots : (device + 1) * slots, :]
        out_ref[device] = jnp.where((lanes >= width) & (lanes < carried), total, piece)


def finish_kernel(
    sizes, count_ref, columns_ref, atom_ref, couplings_ref, projectors_ref, table_ref, out_ref, summed, lined, mixed
):
    blocks, groups, orbitals, slots, length, projectors, width, normalizer = sizes
    kinds = orbitals * 2
    devices = blocks * groups
    share = projectors // devices
    groups_of_rows = kinds // slots
    lanes = lane_ids(slots)
    for chunk in range(projectors // LANES):
        in_chunk = range(chunk * LANES // share, (chunk + 1) * LANES // share)
        for rows in range(groups_of_rows):
            low = width + rows * share
            total = jnp.zeros((slots, LANES), F32)
            for device in in_chunk:
                own = columns_ref[device]
                own = pltpu.roll(jnp.where((lanes >= low) & (lanes < low + share), own, 0.0), (device * share - low) % LANES, 1)
                total += own
            summed[rows * slots : (rows + 1) * slots, chunk * LANES : (chunk + 1) * LANES] = total
    for n in range(orbitals):
        at = kinds + n * 2
        summed[at : at + 1, :] = -summed[n * 2 + 1 : n * 2 + 2, :]
        summed[at + 1 : at + 2, :] = summed[n * 2 : n * 2 + 1, :]
    both = stacked(summed[...])
    atoms = atom_ref[...].astype(F32)
    eye = lax.broadcasted_iota(jnp.int32, (LANES, LANES), 0) == lane_ids(LANES)
    along = []
    for at in range(0, projectors, LANES):
        along.append(jnp.sum(jnp.where(eye, atoms[:, at : at + LANES], 0.0), axis=1, keepdims=True))
    head, rest = split(jnp.where(jnp.concatenate(along, axis=0) == atoms, couplings_ref[...], 0.0))
    head = dot_nt(both, head)
    rest = dot_nt(both, rest)
    weighted = (head[: 2 * kinds] + (head[2 * kinds :] + rest[: 2 * kinds])).astype(BF16)
    for slot in range(slots):
        rows = projectors_ref[slot * length : (slot + 1) * length, :]
        value = dot_nt(weighted, rows)[:kinds]
        rows = projectors_ref[(slots + slot) * length : (slots + slot + 1) * length, :]
        value = value + dot_nt(weighted, rows)[kinds:]
        for row in range(kinds):
            mixed[row, slot : slot + 1, :] = value[row : row + 1, :]
    for chunk in range(blocks * width // LANES):
        for group in range(groups):
            total = jnp.zeros((slots, LANES), F32)
            for inner in range(LANES // width):
                block = chunk * (LANES // width) + inner
                own = jnp.where(lanes < width, columns_ref[block * groups + group], 0.0)
                total += pltpu.roll(own, inner * width, 1)
            lined[group * slots : (group + 1) * slots, chunk * LANES : (chunk + 1) * LANES] = total
    both = stacked(lined[...])
    rows_of_lines = groups * slots
    held = lax.broadcasted_iota(jnp.int32, (1, blocks), 1) == lax.axis_index("ga")
    used = jnp.sum(jnp.where(held, count_ref[...], 0).astype(F32), axis=1, keepdims=True)
    slot_ids = lax.broadcasted_iota(jnp.int32, (slots, 1), 0) + lax.axis_index("band") * slots
    used = slot_ids.astype(F32) < used
    for part in range(2):
        head = dot_nt(both, table_ref[0, part])
        rest = dot_nt(both, table_ref[1, part])
        local = (head[:rows_of_lines] + (head[rows_of_lines:] + rest[:rows_of_lines])) * normalizer
        for n in range(orbitals):
            value = local[n * slots : (n + 1) * slots, :] + mixed[n * 2 + part]
            out_ref[n, part] = jnp.where(used, value, 0.0)


def on_device(orbitals, projectors, potential, couplings, atom_index, column_site, column_count):
    blocks = lax.axis_size("ga")
    groups = lax.axis_size("band")
    devices = blocks * groups
    orbital_count, _, slots, length = orbitals.shape
    planes = potential.shape[0]
    projector_count = projectors.shape[0]
    columns = column_site.shape[0]
    kinds = orbital_count * 2
    assert orbital_count == groups and kinds % slots == 0 and columns % LANES == 0
    share = projector_count // devices
    width = 2
    while width < 2 * planes:
        width *= 2
    carried = width + kinds // slots * share
    assert carried <= LANES and width <= LANES and share * devices == projector_count
    wide = -(-length // LANES) * LANES
    flat = jnp.transpose(projectors, (1, 2, 3, 0)).reshape(2 * slots * length, projector_count)
    z_table = line_table(length, blocks, planes, width)
    batch = next(i for i in (6, 4, 3, 2, 1) if planes % i == 0) if columns <= 512 else 1
    vmem = pl.BlockSpec(memory_space=pltpu.VMEM)
    hbm = pl.BlockSpec(memory_space=pltpu.HBM)
    params = pltpu.CompilerParams(vmem_limit_bytes=56 * 1024 * 1024)
    small = pltpu.CompilerParams(vmem_limit_bytes=40 * 1024 * 1024)
    payload = jax.ShapeDtypeStruct((devices, slots, LANES), F32)

    sent = pl.pallas_call(
        functools.partial(
            project_kernel,
                (blocks, groups, orbital_count, slots, length, projector_count, planes, width),
        ),
        out_shape=payload,
        in_specs=[hbm] * 3,
        out_specs=vmem,
        scratch_shapes=[
            pltpu.SMEM(column_count.shape, jnp.int32),
            pltpu.VMEM(orbitals.shape, BF16),
            pltpu.VMEM(flat.shape, BF16),
            pltpu.VMEM((2 * slots, -(-kinds // 8) * 8, length), F32),
            pltpu.VMEM((kinds * slots, length), F32),
            pltpu.SemaphoreType.DMA((2,)),
            pltpu.SemaphoreType.DMA((2 * slots,)),
        ],
        compiler_params=params,
        cost_estimate=pl.CostEstimate(
            flops=2 * flat.size * LANES * slots,
            bytes_accessed=2 * (flat.size + z_table.size + orbitals.size) + 4 * devices * slots * LANES,
            transcendentals=length * blocks * width,
        ),
        name="project",
    )(column_count, orbitals, flat)
    arrived = lax.all_to_all(sent, ("ga", "band"), split_axis=0, concat_axis=0, tiled=True)

    sent = pl.pallas_call(
        functools.partial(plane_kernel, (devices, slots, planes, length, wide, width, carried, batch)),
        out_shape=payload,
        in_specs=[vmem] * 3,
        out_specs=vmem,
        scratch_shapes=[
            pltpu.VMEM((length, 2 * columns), F32),
            pltpu.VMEM((4 * columns, 2 * wide), BF16),
            pltpu.VMEM((4 * wide, 2 * columns), BF16),
            pltpu.VMEM((columns, LANES), F32),
            pltpu.VMEM((LANES, columns), F32),
            pltpu.VMEM((LANES, columns), F32),
        ],
        compiler_params=small,
        cost_estimate=pl.CostEstimate(
            flops=16 * planes * length * wide * 2 * columns,
            bytes_accessed=4 * (potential.size + 2 * devices * slots * LANES),
            transcendentals=2 * (length + wide) * columns,
        ),
        name="planes",
    )(arrived, column_site.reshape(1, columns), potential)
    arrived = lax.all_to_all(sent, ("ga", "band"), split_axis=0, concat_axis=0, tiled=True)

    normalizer = 1.0 / float(length**3)
    return pl.pallas_call(
        functools.partial(
            finish_kernel,
            (blocks, groups, orbital_count, slots, length, projector_count, width, normalizer),
        ),
        out_shape=jax.ShapeDtypeStruct(orbitals.shape, F32),
        in_specs=[vmem] * 6,
        out_specs=vmem,
        scratch_shapes=[
            pltpu.VMEM((2 * kinds, projector_count), F32),
            pltpu.VMEM((groups * slots, blocks * width), F32),
            pltpu.VMEM((kinds, slots, length), F32),
        ],
        compiler_params=small,
        cost_estimate=pl.CostEstimate(
            flops=4 * kinds * (4 * couplings.size + flat.size) + 4 * z_table.size * orbital_count * slots,
            bytes_accessed=4 * couplings.size + 2 * (flat.size + z_table.size) + 4 * orbitals.size,
            transcendentals=0,
        ),
        name="finish",
    )(column_count.reshape(1, blocks), arrived, atom_index.reshape(1, projector_count), couplings, flat, z_table)


def solution(mesh):
    return jax.shard_map(
        on_device,
        mesh=mesh,
        in_specs=(
            P(None, None, ("ga", "band"), None),
            P(None, None, ("ga", "band"), None),
            P("ga", None, None),
            P(),
            P(),
            P(),
            P(),
        ),
        out_specs=P(None, None, ("ga", "band"), None),
        check_vma=False,
    )
```

```python
import functools

import jax
import jax.numpy as jnp
import ml_dtypes
import numpy as np
from jax import lax
from jax.experimental import pallas as pl
from jax.experimental.pallas import tpu as pltpu
from jax.sharding import PartitionSpec as P

LANES = 128
BF16 = jnp.bfloat16
F32 = jnp.float32


def pieces_of(table):
    table = np.asarray(table, np.float32)
    head = table.astype(ml_dtypes.bfloat16)
    return np.stack([head, (table - head.astype(np.float32)).astype(ml_dtypes.bfloat16)])


def line_table(length, blocks, planes, width):
    kz = np.arange(length)
    out = np.zeros((2, length, blocks, width), np.float64)
    for block in range(blocks):
        z = block * planes + np.arange(planes)
        phases = (kz[:, None] * z[None, :] % length) * (2.0 * np.pi / length)
        out[0, :, block, :planes] = np.cos(phases)
        out[0, :, block, width // 2 : width // 2 + planes] = np.sin(phases)
        out[1, :, block, :planes] = -np.sin(phases)
        out[1, :, block, width // 2 : width // 2 + planes] = np.cos(phases)
    return pieces_of(out.reshape(2, length, blocks * width))


def split(values):
    head = values.astype(BF16)
    return head, (values - head.astype(F32)).astype(BF16)


def stacked(values):
    head, rest = split(values)
    return jnp.concatenate([head.astype(F32), rest.astype(F32)], axis=0).astype(BF16)


def doubled(values):
    values = values.astype(BF16)
    return jnp.concatenate([values, values], axis=1)


def dot(left, right):
    return lax.dot_general(left, right, (((1,), (0,)), ((), ())), preferred_element_type=F32)


def dot_nt(left, right):
    return lax.dot_general(left, right, (((1,), (1,)), ((), ())), preferred_element_type=F32)


def lane_ids(rows):
    return lax.broadcasted_iota(jnp.int32, (rows, LANES), 1)


def used_slots(count_ref, slots):
    used = count_ref[lax.axis_index("ga")] - lax.axis_index("band") * slots
    return lax.broadcasted_iota(jnp.int32, (slots, 1), 0) < used


def cosine_and_sine(phases, length):
    quarter = jnp.floor(phases * (4.0 / length) + 0.5)
    angle = (phases - quarter * (length / 4.0)) * (2.0 * np.pi / length)
    square = angle * angle
    sine = 1.0 / 362880.0
    for term in (-1.0 / 5040.0, 1.0 / 120.0, -1.0 / 6.0, 1.0):
        sine = sine * square + term
    sine = sine * angle
    cosine = -1.0 / 3628800.0
    for term in (1.0 / 40320.0, -1.0 / 720.0, 1.0 / 24.0, -0.5, 1.0):
        cosine = cosine * square + term
    quarter = quarter - 4.0 * jnp.floor(quarter * 0.25)
    odd = (quarter == 1.0) | (quarter == 3.0)
    first = jnp.where(odd, sine, cosine)
    second = jnp.where(odd, cosine, sine)
    first = jnp.where((quarter == 1.0) | (quarter == 2.0), -first, first)
    return first, jnp.where(quarter >= 2.0, -second, second)


def project_kernel(sizes, count_hbm, orbitals_hbm, projectors_hbm, out_ref, *scratch):
    blocks, groups, orbitals, slots, length, projectors, planes, width = sizes
    count_ref, orbitals_ref, projectors_ref, coef, lines, small_sems, sems = scratch
    kinds = orbitals * 2
    devices = blocks * groups
    share = projectors // devices
    small = [
        pltpu.make_async_copy(count_hbm, count_ref, small_sems.at[0]),
        pltpu.make_async_copy(orbitals_hbm, orbitals_ref, small_sems.at[1]),
    ]
    copies = []
    for piece in range(2 * slots):
        rows = pl.ds(piece * length, length)
        copies.append(pltpu.make_async_copy(projectors_hbm.at[rows], projectors_ref.at[rows], sems.at[piece]))
    for copy in small + copies:
        copy.start()
    half = width // 2
    lanes = lax.broadcasted_iota(jnp.int32, (length, blocks * half), 1)
    plane = (lanes >> (half.bit_length() - 1)) * planes + (lanes & (half - 1))
    kz = lax.broadcasted_iota(jnp.int32, (length, blocks * half), 0)
    table = split(jnp.concatenate(cosine_and_sine(kz.astype(F32) * plane.astype(F32), length), axis=1))
    coef[...] = jnp.zeros_like(coef)
    small[0].wait()
    small[1].wait()
    used = used_slots(count_ref, slots)
    for n in range(orbitals):
        for part in range(2):
            values = jnp.where(used, orbitals_ref[n, part].astype(F32), 0.0)
            at = (part * orbitals + n) * slots
            lines[at : at + slots, :] = values
            turned = values if part == 1 else -values
            for slot in range(slots):
                row = n * 2 + part
                coef[slot, row : row + 1, :] = values[slot : slot + 1, :]
                row = n * 2 + 1 - part
                coef[slots + slot, row : row + 1, :] = turned[slot : slot + 1, :]
    left = lines[...].astype(BF16)
    both = dot(left, table[0]) + dot(left, table[1])
    rows = orbitals * slots
    points = blocks * half
    real = both[:rows, :points] - both[rows:, points:]
    imag = both[:rows, points:] + both[rows:, :points]
    lanes = lane_ids(rows)
    for block in range(blocks):
        at = block * half
        base = at // LANES * LANES
        chunk = pltpu.roll(imag[:, base : base + LANES], (base - at + half) % LANES, 1)
        chunk = jnp.where(lanes < half, pltpu.roll(real[:, base : base + LANES], (base - at) % LANES, 1), chunk)
        for group in range(groups):
            out_ref[block * groups + group] = chunk[group * slots : (group + 1) * slots, :]
    sums = jnp.zeros((coef.shape[1], projectors), F32)
    for piece in range(2 * slots):
        left = coef[piece].astype(BF16)
        copies[piece].wait()
        sums += dot(left, projectors_ref[piece * length : (piece + 1) * length, :])
    lanes = lane_ids(slots)
    for device in range(devices):
        piece = jnp.where(lanes < width, out_ref[device], 0.0)
        first = device * share
        base = first // LANES * LANES
        for rows in range(kinds // slots):
            low = width + rows * share
            own = pltpu.roll(sums[rows * slots : (rows + 1) * slots, base : base + LANES], (base + low - first) % LANES, 1)
            piece = jnp.where((lanes >= low) & (lanes < low + share), own, piece)
        out_ref[device] = piece


def make_tables(length, wide, site_ref, x_ref, plus_ref, minus_ref):
    columns = site_ref.shape[1]
    eye = lax.broadcasted_iota(jnp.int32, (LANES, LANES), 0) == lane_ids(LANES)
    row_ids = lax.broadcasted_iota(jnp.int32, (length, LANES), 0).astype(F32)
    lanes = lax.broadcasted_iota(jnp.int32, (LANES, wide), 1)
    inside = lanes < length
    lanes = lanes.astype(F32)
    for at in range(0, columns, LANES):
        site = site_ref[:, at : at + LANES].astype(F32)
        site_x = jnp.floor((site + 0.5) * (1.0 / length))
        site_y = site - site_x * length
        cosine, sine = cosine_and_sine(row_ids * site_x, length)
        x_ref[:, at : at + LANES] = cosine
        x_ref[:, columns + at : columns + at + LANES] = sine
        along = jnp.sum(jnp.where(eye, site_y, 0.0), axis=1, keepdims=True)
        cosine, sine = cosine_and_sine(lanes * along, length)
        cosine = jnp.where(inside, cosine, 0.0)
        sine = jnp.where(inside, sine, 0.0)
        across = jnp.concatenate([cosine[:, i : i + LANES].T for i in range(0, wide, LANES)], axis=0)
        aside = jnp.concatenate([sine[:, i : i + LANES].T for i in range(0, wide, LANES)], axis=0)
        for piece, (own_cosine, own_sine) in enumerate(zip(split(cosine), split(sine))):
            rows = pl.ds(piece * 2 * columns + at, LANES)
            plus_ref[rows, :wide] = own_cosine
            plus_ref[rows, wide:] = own_sine
            rows = pl.ds((piece * 2 + 1) * columns + at, LANES)
            plus_ref[rows, :wide] = -own_sine
            plus_ref[rows, wide:] = own_cosine
        for piece, (own_cosine, own_sine) in enumerate(zip(split(across), split(aside))):
            rows = pl.ds(piece * 2 * wide, wide)
            minus_ref[rows, at : at + LANES] = own_cosine
            minus_ref[rows, columns + at : columns + at + LANES] = -own_sine
            rows = pl.ds((piece * 2 + 1) * wide, wide)
            minus_ref[rows, at : at + LANES] = own_sine
            minus_ref[rows, columns + at : columns + at + LANES] = own_cosine


def plane_kernel(sizes, columns_ref, site_ref, potential_ref, out_ref, x_ref, plus_ref, minus_ref, gathered, lines, back):
    devices, slots, planes, length, wide, width, carried, batch = sizes
    count = devices * slots
    make_tables(length, wide, site_ref, x_ref, plus_ref, minus_ref)
    total = jnp.zeros((slots, LANES), F32)
    for device in range(devices):
        piece = columns_ref[device]
        gathered[device * slots : (device + 1) * slots, :] = piece
        total += piece
    for at in range(0, count, LANES):
        lines[:, at : at + LANES] = gathered[at : at + LANES, :].T
    back[...] = jnp.zeros_like(back)
    cosine = x_ref[:, :count]
    sine = x_ref[:, count:]
    padding = jnp.zeros((length, wide - length), F32)
    for i in range(planes // batch):
        left = []
        for plane in range(i * batch, (i + 1) * batch):
            real = lines[plane : plane + 1, :]
            imag = lines[plane + width // 2 : plane + width // 2 + 1, :]
            left.append(jnp.concatenate([cosine * real - sine * imag, cosine * imag + sine * real], axis=1))
        left = doubled(jnp.concatenate(left, axis=0))
        field = dot(left, plus_ref[...])
        weights = []
        for plane in range(i * batch, (i + 1) * batch):
            own = jnp.concatenate([potential_ref[plane], padding], axis=1)
            weights.append(jnp.concatenate([own, own], axis=1))
        left = doubled(field * jnp.concatenate(weights, axis=0))
        half = dot(left, minus_ref[...])
        for j in range(batch):
            plane = i * batch + j
            real = half[j * length : (j + 1) * length, :count]
            imag = half[j * length : (j + 1) * length, count:]
            back[plane : plane + 1, :] = jnp.sum(cosine * real + sine * imag, axis=0, keepdims=True)
            at = plane + width // 2
            back[at : at + 1, :] = jnp.sum(cosine * imag - sine * real, axis=0, keepdims=True)
    for at in range(0, count, LANES):
        gathered[at : at + LANES, :] = back[:, at : at + LANES].T
    lanes = lane_ids(slots)
    for device in range(devices):
        piece = gathered[device * slots : (device + 1) * slots, :]
        out_ref[device] = jnp.where((lanes >= width) & (lanes < carried), total, piece)


def finish_kernel(
    sizes, count_ref, columns_ref, atom_ref, couplings_ref, projectors_ref, table_ref, out_ref, summed, lined, mixed
):
    blocks, groups, orbitals, slots, length, projectors, width, normalizer = sizes
    kinds = orbitals * 2
    devices = blocks * groups
    share = projectors // devices
    groups_of_rows = kinds // slots
    lanes = lane_ids(slots)
    for chunk in range(projectors // LANES):
        in_chunk = range(chunk * LANES // share, (chunk + 1) * LANES // share)
        for rows in range(groups_of_rows):
            low = width + rows * share
            total = jnp.zeros((slots, LANES), F32)
            for device in in_chunk:
                own = columns_ref[device]
                own = pltpu.roll(jnp.where((lanes >= low) & (lanes < low + share), own, 0.0), (device * share - low) % LANES, 1)
                total += own
            summed[rows * slots : (rows + 1) * slots, chunk * LANES : (chunk + 1) * LANES] = total
    for n in range(orbitals):
        at = kinds + n * 2
        summed[at : at + 1, :] = -summed[n * 2 + 1 : n * 2 + 2, :]
        summed[at + 1 : at + 2, :] = summed[n * 2 : n * 2 + 1, :]
    both = stacked(summed[...])
    atoms = atom_ref[...].astype(F32)
    eye = lax.broadcasted_iota(jnp.int32, (LANES, LANES), 0) == lane_ids(LANES)
    along = []
    for at in range(0, projectors, LANES):
        along.append(jnp.sum(jnp.where(eye, atoms[:, at : at + LANES], 0.0), axis=1, keepdims=True))
    head, rest = split(jnp.where(jnp.concatenate(along, axis=0) == atoms, couplings_ref[...], 0.0))
    head = dot_nt(both, head)
    rest = dot_nt(both, rest)
    weighted = (head[: 2 * kinds] + (head[2 * kinds :] + rest[: 2 * kinds])).astype(BF16)
    for slot in range(slots):
        rows = projectors_ref[slot * length : (slot + 1) * length, :]
        value = dot_nt(weighted, rows)[:kinds]
        rows = projectors_ref[(slots + slot) * length : (slots + slot + 1) * length, :]
        value = value + dot_nt(weighted, rows)[kinds:]
        for row in range(kinds):
            mixed[row, slot : slot + 1, :] = value[row : row + 1, :]
    for chunk in range(blocks * width // LANES):
        for group in range(groups):
            total = jnp.zeros((slots, LANES), F32)
            for inner in range(LANES // width):
                block = chunk * (LANES // width) + inner
                own = jnp.where(lanes < width, columns_ref[block * groups + group], 0.0)
                total += pltpu.roll(own, inner * width, 1)
            lined[group * slots : (group + 1) * slots, chunk * LANES : (chunk + 1) * LANES] = total
    both = stacked(lined[...])
    rows_of_lines = groups * slots
    held = lax.broadcasted_iota(jnp.int32, (1, blocks), 1) == lax.axis_index("ga")
    used = jnp.sum(jnp.where(held, count_ref[...], 0).astype(F32), axis=1, keepdims=True)
    slot_ids = lax.broadcasted_iota(jnp.int32, (slots, 1), 0) + lax.axis_index("band") * slots
    used = slot_ids.astype(F32) < used
    for part in range(2):
        head = dot_nt(both, table_ref[0, part])
        rest = dot_nt(both, table_ref[1, part])
        local = (head[:rows_of_lines] + (head[rows_of_lines:] + rest[:rows_of_lines])) * normalizer
        for n in range(orbitals):
            value = local[n * slots : (n + 1) * slots, :] + mixed[n * 2 + part]
            out_ref[n, part] = jnp.where(used, value, 0.0)


def on_device(orbitals, projectors, potential, couplings, atom_index, column_site, column_count):
    blocks = lax.axis_size("ga")
    groups = lax.axis_size("band")
    devices = blocks * groups
    orbital_count, _, slots, length = orbitals.shape
    planes = potential.shape[0]
    projector_count = projectors.shape[0]
    columns = column_site.shape[0]
    kinds = orbital_count * 2
    assert orbital_count == groups and kinds % slots == 0 and columns % LANES == 0
    share = projector_count // devices
    width = 2
    while width < 2 * planes:
        width *= 2
    carried = width + kinds // slots * share
    assert carried <= LANES and width <= LANES and share * devices == projector_count
    wide = -(-length // LANES) * LANES
    flat = jnp.transpose(projectors, (1, 2, 3, 0)).reshape(2 * slots * length, projector_count)
    z_table = line_table(length, blocks, planes, width)
    batch = next(i for i in (2, 3, 1) if planes % i == 0) if columns <= 512 else 1
    vmem = pl.BlockSpec(memory_space=pltpu.VMEM)
    hbm = pl.BlockSpec(memory_space=pltpu.HBM)
    params = pltpu.CompilerParams(vmem_limit_bytes=56 * 1024 * 1024)
    small = pltpu.CompilerParams(vmem_limit_bytes=40 * 1024 * 1024)
    payload = jax.ShapeDtypeStruct((devices, slots, LANES), F32)

    sent = pl.pallas_call(
        functools.partial(
            project_kernel,
                (blocks, groups, orbital_count, slots, length, projector_count, planes, width),
        ),
        out_shape=payload,
        in_specs=[hbm] * 3,
        out_specs=vmem,
        scratch_shapes=[
            pltpu.SMEM(column_count.shape, jnp.int32),
            pltpu.VMEM(orbitals.shape, BF16),
            pltpu.VMEM(flat.shape, BF16),
            pltpu.VMEM((2 * slots, -(-kinds // 8) * 8, length), F32),
            pltpu.VMEM((kinds * slots, length), F32),
            pltpu.SemaphoreType.DMA((2,)),
            pltpu.SemaphoreType.DMA((2 * slots,)),
        ],
        compiler_params=params,
        cost_estimate=pl.CostEstimate(
            flops=2 * flat.size * LANES * slots,
            bytes_accessed=2 * (flat.size + z_table.size + orbitals.size) + 4 * devices * slots * LANES,
            transcendentals=length * blocks * width,
        ),
        name="project",
    )(column_count, orbitals, flat)
    arrived = lax.all_to_all(sent, ("ga", "band"), split_axis=0, concat_axis=0, tiled=True)

    sent = pl.pallas_call(
        functools.partial(plane_kernel, (devices, slots, planes, length, wide, width, carried, batch)),
        out_shape=payload,
        in_specs=[vmem] * 3,
        out_specs=vmem,
        scratch_shapes=[
            pltpu.VMEM((length, 2 * columns), F32),
            pltpu.VMEM((4 * columns, 2 * wide), BF16),
            pltpu.VMEM((4 * wide, 2 * columns), BF16),
            pltpu.VMEM((columns, LANES), F32),
            pltpu.VMEM((LANES, columns), F32),
            pltpu.VMEM((LANES, columns), F32),
        ],
        compiler_params=small,
        cost_estimate=pl.CostEstimate(
            flops=16 * planes * length * wide * 2 * columns,
            bytes_accessed=4 * (potential.size + 2 * devices * slots * LANES),
            transcendentals=2 * (length + wide) * columns,
        ),
        name="planes",
    )(arrived, column_site.reshape(1, columns), potential)
    arrived = lax.all_to_all(sent, ("ga", "band"), split_axis=0, concat_axis=0, tiled=True)

    normalizer = 1.0 / float(length**3)
    return pl.pallas_call(
        functools.partial(
            finish_kernel,
            (blocks, groups, orbital_count, slots, length, projector_count, width, normalizer),
        ),
        out_shape=jax.ShapeDtypeStruct(orbitals.shape, F32),
        in_specs=[vmem] * 6,
        out_specs=vmem,
        scratch_shapes=[
            pltpu.VMEM((2 * kinds, projector_count), F32),
            pltpu.VMEM((groups * slots, blocks * width), F32),
            pltpu.VMEM((kinds, slots, length), F32),
        ],
        compiler_params=small,
        cost_estimate=pl.CostEstimate(
            flops=4 * kinds * (4 * couplings.size + flat.size) + 4 * z_table.size * orbital_count * slots,
            bytes_accessed=4 * couplings.size + 2 * (flat.size + z_table.size) + 4 * orbitals.size,
            transcendentals=0,
        ),
        name="finish",
    )(column_count.reshape(1, blocks), arrived, atom_index.reshape(1, projector_count), couplings, flat, z_table)


def solution(mesh):
    return jax.shard_map(
        on_device,
        mesh=mesh,
        in_specs=(
            P(None, None, ("ga", "band"), None),
            P(None, None, ("ga", "band"), None),
            P("ga", None, None),
            P(),
            P(),
            P(),
            P(),
        ),
        out_specs=P(None, None, ("ga", "band"), None),
        check_vma=False,
    )
```

```python
import functools

import jax
import jax.numpy as jnp
import ml_dtypes
import numpy as np
from jax import lax
from jax.experimental import pallas as pl
from jax.experimental.pallas import tpu as pltpu
from jax.sharding import PartitionSpec as P

LANES = 128
BF16 = jnp.bfloat16
F32 = jnp.float32


def pieces_of(table):
    table = np.asarray(table, np.float32)
    head = table.astype(ml_dtypes.bfloat16)
    return np.stack([head, (table - head.astype(np.float32)).astype(ml_dtypes.bfloat16)])


def line_table(length, blocks, planes, width):
    kz = np.arange(length)
    out = np.zeros((2, length, blocks, width), np.float64)
    for block in range(blocks):
        z = block * planes + np.arange(planes)
        phases = (kz[:, None] * z[None, :] % length) * (2.0 * np.pi / length)
        out[0, :, block, :planes] = np.cos(phases)
        out[0, :, block, width // 2 : width // 2 + planes] = np.sin(phases)
        out[1, :, block, :planes] = -np.sin(phases)
        out[1, :, block, width // 2 : width // 2 + planes] = np.cos(phases)
    return pieces_of(out.reshape(2, length, blocks * width))


def split(values):
    head = values.astype(BF16)
    return head, (values - head.astype(F32)).astype(BF16)


def stacked(values):
    head, rest = split(values)
    return jnp.concatenate([head.astype(F32), rest.astype(F32)], axis=0).astype(BF16)


def doubled(values):
    values = values.astype(BF16)
    return jnp.concatenate([values, values], axis=1)


def dot(left, right):
    return lax.dot_general(left, right, (((1,), (0,)), ((), ())), preferred_element_type=F32)


def dot_nt(left, right):
    return lax.dot_general(left, right, (((1,), (1,)), ((), ())), preferred_element_type=F32)


def lane_ids(rows):
    return lax.broadcasted_iota(jnp.int32, (rows, LANES), 1)


def used_slots(count_ref, slots):
    used = count_ref[lax.axis_index("ga")] - lax.axis_index("band") * slots
    return lax.broadcasted_iota(jnp.int32, (slots, 1), 0) < used


def cosine_and_sine(phases, length):
    quarter = jnp.floor(phases * (4.0 / length) + 0.5)
    angle = (phases - quarter * (length / 4.0)) * (2.0 * np.pi / length)
    square = angle * angle
    sine = 1.0 / 362880.0
    for term in (-1.0 / 5040.0, 1.0 / 120.0, -1.0 / 6.0, 1.0):
        sine = sine * square + term
    sine = sine * angle
    cosine = -1.0 / 3628800.0
    for term in (1.0 / 40320.0, -1.0 / 720.0, 1.0 / 24.0, -0.5, 1.0):
        cosine = cosine * square + term
    quarter = quarter - 4.0 * jnp.floor(quarter * 0.25)
    odd = (quarter == 1.0) | (quarter == 3.0)
    first = jnp.where(odd, sine, cosine)
    second = jnp.where(odd, cosine, sine)
    first = jnp.where((quarter == 1.0) | (quarter == 2.0), -first, first)
    return first, jnp.where(quarter >= 2.0, -second, second)


def project_kernel(sizes, count_hbm, orbitals_hbm, projectors_hbm, out_ref, *scratch):
    blocks, groups, orbitals, slots, length, projectors, planes, width = sizes
    count_ref, orbitals_ref, projectors_ref, coef, lines, small_sems, sems = scratch
    kinds = orbitals * 2
    devices = blocks * groups
    share = projectors // devices
    small = [
        pltpu.make_async_copy(count_hbm, count_ref, small_sems.at[0]),
        pltpu.make_async_copy(orbitals_hbm, orbitals_ref, small_sems.at[1]),
    ]
    copies = []
    for piece in range(2 * slots):
        rows = pl.ds(piece * length, length)
        copies.append(pltpu.make_async_copy(projectors_hbm.at[rows], projectors_ref.at[rows], sems.at[piece]))
    for copy in small + copies:
        copy.start()
    half = width // 2
    lanes = lax.broadcasted_iota(jnp.int32, (length, blocks * half), 1)
    plane = (lanes >> (half.bit_length() - 1)) * planes + (lanes & (half - 1))
    kz = lax.broadcasted_iota(jnp.int32, (length, blocks * half), 0)
    table = split(jnp.concatenate(cosine_and_sine(kz.astype(F32) * plane.astype(F32), length), axis=1))
    coef[...] = jnp.zeros_like(coef)
    small[0].wait()
    small[1].wait()
    used = used_slots(count_ref, slots)
    for n in range(orbitals):
        for part in range(2):
            values = jnp.where(used, orbitals_ref[n, part].astype(F32), 0.0)
            at = (part * orbitals + n) * slots
            lines[at : at + slots, :] = values
            turned = values if part == 1 else -values
            for slot in range(slots):
                row = n * 2 + part
                coef[slot, row : row + 1, :] = values[slot : slot + 1, :]
                row = n * 2 + 1 - part
                coef[slots + slot, row : row + 1, :] = turned[slot : slot + 1, :]
    left = lines[...].astype(BF16)
    both = dot(left, table[0]) + dot(left, table[1])
    rows = orbitals * slots
    points = blocks * half
    real = both[:rows, :points] - both[rows:, points:]
    imag = both[:rows, points:] + both[rows:, :points]
    lanes = lane_ids(rows)
    for block in range(blocks):
        at = block * half
        base = at // LANES * LANES
        chunk = pltpu.roll(imag[:, base : base + LANES], (base - at + half) % LANES, 1)
        chunk = jnp.where(lanes < half, pltpu.roll(real[:, base : base + LANES], (base - at) % LANES, 1), chunk)
        for group in range(groups):
            out_ref[block * groups + group] = chunk[group * slots : (group + 1) * slots, :]
    sums = jnp.zeros((coef.shape[1], projectors), F32)
    for piece in range(2 * slots):
        left = coef[piece].astype(BF16)
        copies[piece].wait()
        sums += dot(left, projectors_ref[piece * length : (piece + 1) * length, :])
    lanes = lane_ids(slots)
    for device in range(devices):
        piece = jnp.where(lanes < width, out_ref[device], 0.0)
        first = device * share
        base = first // LANES * LANES
        for rows in range(kinds // slots):
            low = width + rows * share
            own = pltpu.roll(sums[rows * slots : (rows + 1) * slots, base : base + LANES], (base + low - first) % LANES, 1)
            piece = jnp.where((lanes >= low) & (lanes < low + share), own, piece)
        out_ref[device] = piece


def table_kernel(length, wide, site_ref, x_ref, plus_ref):
    columns = site_ref.shape[1]
    eye = lax.broadcasted_iota(jnp.int32, (LANES, LANES), 0) == lane_ids(LANES)
    row_ids = lax.broadcasted_iota(jnp.int32, (length, LANES), 0).astype(F32)
    lanes = lax.broadcasted_iota(jnp.int32, (LANES, wide), 1)
    inside = lanes < length
    lanes = lanes.astype(F32)
    for at in range(0, columns, LANES):
        site = site_ref[:, at : at + LANES].astype(F32)
        site_x = jnp.floor((site + 0.5) * (1.0 / length))
        site_y = site - site_x * length
        cosine, sine = cosine_and_sine(row_ids * site_x, length)
        x_ref[:, at : at + LANES] = cosine
        x_ref[:, columns + at : columns + at + LANES] = sine
        along = jnp.sum(jnp.where(eye, site_y, 0.0), axis=1, keepdims=True)
        cosine, sine = cosine_and_sine(lanes * along, length)
        cosine = jnp.where(inside, cosine, 0.0)
        sine = jnp.where(inside, sine, 0.0)
        for piece, (own_cosine, own_sine) in enumerate(zip(split(cosine), split(sine))):
            rows = pl.ds(piece * 2 * columns + at, LANES)
            plus_ref[rows, :wide] = own_cosine
            plus_ref[rows, wide:] = own_sine
            rows = pl.ds((piece * 2 + 1) * columns + at, LANES)
            plus_ref[rows, :wide] = -own_sine
            plus_ref[rows, wide:] = own_cosine


def plane_kernel(sizes, columns_ref, x_ref, plus_ref, potential_ref, out_ref, gathered, lines, back):
    devices, slots, planes, length, wide, width, carried, batch = sizes
    count = devices * slots
    total = jnp.zeros((slots, LANES), F32)
    for device in range(devices):
        piece = columns_ref[device]
        gathered[device * slots : (device + 1) * slots, :] = piece
        total += piece
    for at in range(0, count, LANES):
        lines[:, at : at + LANES] = gathered[at : at + LANES, :].T
    back[...] = jnp.zeros_like(back)
    cosine = x_ref[:, :count]
    sine = x_ref[:, count:]
    padding = jnp.zeros((length, wide - length), F32)
    for i in range(planes // batch):
        left = []
        for plane in range(i * batch, (i + 1) * batch):
            real = lines[plane : plane + 1, :]
            imag = lines[plane + width // 2 : plane + width // 2 + 1, :]
            left.append(jnp.concatenate([cosine * real - sine * imag, cosine * imag + sine * real], axis=1))
        left = doubled(jnp.concatenate(left, axis=0))
        field = dot(left, plus_ref[...])
        weights = []
        for plane in range(i * batch, (i + 1) * batch):
            own = jnp.concatenate([potential_ref[plane], padding], axis=1)
            weights.append(jnp.concatenate([own, own], axis=1))
        left = (field * jnp.concatenate(weights, axis=0)).astype(BF16)
        half = dot_nt(left, plus_ref[: 2 * count, :]) + dot_nt(left, plus_ref[2 * count :, :])
        for j in range(batch):
            plane = i * batch + j
            real = half[j * length : (j + 1) * length, :count]
            imag = half[j * length : (j + 1) * length, count:]
            back[plane : plane + 1, :] = jnp.sum(cosine * real + sine * imag, axis=0, keepdims=True)
            at = plane + width // 2
            back[at : at + 1, :] = jnp.sum(cosine * imag - sine * real, axis=0, keepdims=True)
    for at in range(0, count, LANES):
        gathered[at : at + LANES, :] = back[:, at : at + LANES].T
    lanes = lane_ids(slots)
    for device in range(devices):
        piece = gathered[device * slots : (device + 1) * slots, :]
        out_ref[device] = jnp.where((lanes >= width) & (lanes < carried), total, piece)


def finish_kernel(
    sizes, count_ref, columns_ref, atom_ref, couplings_ref, projectors_ref, table_ref, out_ref, summed, lined, mixed
):
    blocks, groups, orbitals, slots, length, projectors, width, normalizer = sizes
    kinds = orbitals * 2
    devices = blocks * groups
    share = projectors // devices
    groups_of_rows = kinds // slots
    lanes = lane_ids(slots)
    for chunk in range(projectors // LANES):
        in_chunk = range(chunk * LANES // share, (chunk + 1) * LANES // share)
        for rows in range(groups_of_rows):
            low = width + rows * share
            total = jnp.zeros((slots, LANES), F32)
            for device in in_chunk:
                own = columns_ref[device]
                own = pltpu.roll(jnp.where((lanes >= low) & (lanes < low + share), own, 0.0), (device * share - low) % LANES, 1)
                total += own
            summed[rows * slots : (rows + 1) * slots, chunk * LANES : (chunk + 1) * LANES] = total
    for n in range(orbitals):
        at = kinds + n * 2
        summed[at : at + 1, :] = -summed[n * 2 + 1 : n * 2 + 2, :]
        summed[at + 1 : at + 2, :] = summed[n * 2 : n * 2 + 1, :]
    both = stacked(summed[...])
    atoms = atom_ref[...].astype(F32)
    eye = lax.broadcasted_iota(jnp.int32, (LANES, LANES), 0) == lane_ids(LANES)
    along = []
    for at in range(0, projectors, LANES):
        along.append(jnp.sum(jnp.where(eye, atoms[:, at : at + LANES], 0.0), axis=1, keepdims=True))
    head, rest = split(jnp.where(jnp.concatenate(along, axis=0) == atoms, couplings_ref[...], 0.0))
    head = dot_nt(both, head)
    rest = dot_nt(both, rest)
    weighted = (head[: 2 * kinds] + (head[2 * kinds :] + rest[: 2 * kinds])).astype(BF16)
    for slot in range(slots):
        rows = projectors_ref[slot * length : (slot + 1) * length, :]
        value = dot_nt(weighted, rows)[:kinds]
        rows = projectors_ref[(slots + slot) * length : (slots + slot + 1) * length, :]
        value = value + dot_nt(weighted, rows)[kinds:]
        for row in range(kinds):
            mixed[row, slot : slot + 1, :] = value[row : row + 1, :]
    for chunk in range(blocks * width // LANES):
        for group in range(groups):
            total = jnp.zeros((slots, LANES), F32)
            for inner in range(LANES // width):
                block = chunk * (LANES // width) + inner
                own = jnp.where(lanes < width, columns_ref[block * groups + group], 0.0)
                total += pltpu.roll(own, inner * width, 1)
            lined[group * slots : (group + 1) * slots, chunk * LANES : (chunk + 1) * LANES] = total
    both = stacked(lined[...])
    rows_of_lines = groups * slots
    held = lax.broadcasted_iota(jnp.int32, (1, blocks), 1) == lax.axis_index("ga")
    used = jnp.sum(jnp.where(held, count_ref[...], 0).astype(F32), axis=1, keepdims=True)
    slot_ids = lax.broadcasted_iota(jnp.int32, (slots, 1), 0) + lax.axis_index("band") * slots
    used = slot_ids.astype(F32) < used
    for part in range(2):
        head = dot_nt(both, table_ref[0, part])
        rest = dot_nt(both, table_ref[1, part])
        local = (head[:rows_of_lines] + (head[rows_of_lines:] + rest[:rows_of_lines])) * normalizer
        for n in range(orbitals):
            value = local[n * slots : (n + 1) * slots, :] + mixed[n * 2 + part]
            out_ref[n, part] = jnp.where(used, value, 0.0)


def on_device(orbitals, projectors, potential, couplings, atom_index, column_site, column_count):
    blocks = lax.axis_size("ga")
    groups = lax.axis_size("band")
    devices = blocks * groups
    orbital_count, _, slots, length = orbitals.shape
    planes = potential.shape[0]
    projector_count = projectors.shape[0]
    columns = column_site.shape[0]
    kinds = orbital_count * 2
    assert orbital_count == groups and kinds % slots == 0 and columns % LANES == 0
    share = projector_count // devices
    width = 2
    while width < 2 * planes:
        width *= 2
    carried = width + kinds // slots * share
    assert carried <= LANES and width <= LANES and share * devices == projector_count
    wide = -(-length // LANES) * LANES
    flat = jnp.transpose(projectors, (1, 2, 3, 0)).reshape(2 * slots * length, projector_count)
    z_table = line_table(length, blocks, planes, width)
    batch = next(i for i in (2, 3, 1) if planes % i == 0) if columns <= 512 else 1
    vmem = pl.BlockSpec(memory_space=pltpu.VMEM)
    hbm = pl.BlockSpec(memory_space=pltpu.HBM)
    params = pltpu.CompilerParams(vmem_limit_bytes=56 * 1024 * 1024)
    small = pltpu.CompilerParams(vmem_limit_bytes=40 * 1024 * 1024)
    payload = jax.ShapeDtypeStruct((devices, slots, LANES), F32)

    sent = pl.pallas_call(
        functools.partial(
            project_kernel,
                (blocks, groups, orbital_count, slots, length, projector_count, planes, width),
        ),
        out_shape=payload,
        in_specs=[hbm] * 3,
        out_specs=vmem,
        scratch_shapes=[
            pltpu.SMEM(column_count.shape, jnp.int32),
            pltpu.VMEM(orbitals.shape, BF16),
            pltpu.VMEM(flat.shape, BF16),
            pltpu.VMEM((2 * slots, -(-kinds // 8) * 8, length), F32),
            pltpu.VMEM((kinds * slots, length), F32),
            pltpu.SemaphoreType.DMA((2,)),
            pltpu.SemaphoreType.DMA((2 * slots,)),
        ],
        compiler_params=params,
        cost_estimate=pl.CostEstimate(
            flops=2 * flat.size * LANES * slots,
            bytes_accessed=2 * (flat.size + z_table.size + orbitals.size) + 4 * devices * slots * LANES,
            transcendentals=length * blocks * width,
        ),
        name="project",
    )(column_count, orbitals, flat)
    arrived = lax.all_to_all(sent, ("ga", "band"), split_axis=0, concat_axis=0, tiled=True)

    x_rows, plus = pl.pallas_call(
        functools.partial(table_kernel, length, wide),
        out_shape=(
            jax.ShapeDtypeStruct((length, 2 * columns), F32),
            jax.ShapeDtypeStruct((4 * columns, 2 * wide), BF16),
        ),
        in_specs=[vmem],
        out_specs=(vmem,) * 2,
        compiler_params=small,
        cost_estimate=pl.CostEstimate(
            flops=32 * (length + wide) * columns,
            bytes_accessed=8 * (length + 2 * wide) * columns,
            transcendentals=2 * (length + wide) * columns,
        ),
        name="tables",
    )(column_site.reshape(1, columns))

    sent = pl.pallas_call(
        functools.partial(plane_kernel, (devices, slots, planes, length, wide, width, carried, batch)),
        out_shape=payload,
        in_specs=[vmem] * 4,
        out_specs=vmem,
        scratch_shapes=[
            pltpu.VMEM((columns, LANES), F32),
            pltpu.VMEM((LANES, columns), F32),
            pltpu.VMEM((LANES, columns), F32),
        ],
        compiler_params=small,
        cost_estimate=pl.CostEstimate(
            flops=16 * planes * length * wide * 2 * columns,
            bytes_accessed=4 * (potential.size + 2 * devices * slots * LANES),
            transcendentals=0,
        ),
        name="planes",
    )(arrived, x_rows, plus, potential)
    arrived = lax.all_to_all(sent, ("ga", "band"), split_axis=0, concat_axis=0, tiled=True)

    normalizer = 1.0 / float(length**3)
    return pl.pallas_call(
        functools.partial(
            finish_kernel,
            (blocks, groups, orbital_count, slots, length, projector_count, width, normalizer),
        ),
        out_shape=jax.ShapeDtypeStruct(orbitals.shape, F32),
        in_specs=[vmem] * 6,
        out_specs=vmem,
        scratch_shapes=[
            pltpu.VMEM((2 * kinds, projector_count), F32),
            pltpu.VMEM((groups * slots, blocks * width), F32),
            pltpu.VMEM((kinds, slots, length), F32),
        ],
        compiler_params=small,
        cost_estimate=pl.CostEstimate(
            flops=4 * kinds * (4 * couplings.size + flat.size) + 4 * z_table.size * orbital_count * slots,
            bytes_accessed=4 * couplings.size + 2 * (flat.size + z_table.size) + 4 * orbitals.size,
            transcendentals=0,
        ),
        name="finish",
    )(column_count.reshape(1, blocks), arrived, atom_index.reshape(1, projector_count), couplings, flat, z_table)


def solution(mesh):
    return jax.shard_map(
        on_device,
        mesh=mesh,
        in_specs=(
            P(None, None, ("ga", "band"), None),
            P(None, None, ("ga", "band"), None),
            P("ga", None, None),
            P(),
            P(),
            P(),
            P(),
        ),
        out_specs=P(None, None, ("ga", "band"), None),
        check_vma=False,
    )
```

```python
import functools

import jax
import jax.numpy as jnp
import ml_dtypes
import numpy as np
from jax import lax
from jax.experimental import pallas as pl
from jax.experimental.pallas import tpu as pltpu
from jax.sharding import PartitionSpec as P

LANES = 128
BF16 = jnp.bfloat16
F32 = jnp.float32


def pieces_of(table):
    table = np.asarray(table, np.float32)
    head = table.astype(ml_dtypes.bfloat16)
    return np.stack([head, (table - head.astype(np.float32)).astype(ml_dtypes.bfloat16)])


def line_table(length, blocks, planes, width):
    kz = np.arange(length)
    out = np.zeros((2, length, blocks, width), np.float64)
    for block in range(blocks):
        z = block * planes + np.arange(planes)
        phases = (kz[:, None] * z[None, :] % length) * (2.0 * np.pi / length)
        out[0, :, block, :planes] = np.cos(phases)
        out[0, :, block, width // 2 : width // 2 + planes] = np.sin(phases)
        out[1, :, block, :planes] = -np.sin(phases)
        out[1, :, block, width // 2 : width // 2 + planes] = np.cos(phases)
    return pieces_of(out.reshape(2, length, blocks * width))


def split(values):
    head = values.astype(BF16)
    return head, (values - head.astype(F32)).astype(BF16)


def stacked(values):
    head, rest = split(values)
    return jnp.concatenate([head.astype(F32), rest.astype(F32)], axis=0).astype(BF16)


def doubled(values):
    values = values.astype(BF16)
    return jnp.concatenate([values, values], axis=1)


def dot(left, right):
    return lax.dot_general(left, right, (((1,), (0,)), ((), ())), preferred_element_type=F32)


def dot_nt(left, right):
    return lax.dot_general(left, right, (((1,), (1,)), ((), ())), preferred_element_type=F32)


def lane_ids(rows):
    return lax.broadcasted_iota(jnp.int32, (rows, LANES), 1)


def used_slots(count_ref, slots):
    used = count_ref[lax.axis_index("ga")] - lax.axis_index("band") * slots
    return lax.broadcasted_iota(jnp.int32, (slots, 1), 0) < used


def cosine_and_sine(phases, length):
    quarter = jnp.floor(phases * (4.0 / length) + 0.5)
    angle = (phases - quarter * (length / 4.0)) * (2.0 * np.pi / length)
    square = angle * angle
    sine = 1.0 / 362880.0
    for term in (-1.0 / 5040.0, 1.0 / 120.0, -1.0 / 6.0, 1.0):
        sine = sine * square + term
    sine = sine * angle
    cosine = -1.0 / 3628800.0
    for term in (1.0 / 40320.0, -1.0 / 720.0, 1.0 / 24.0, -0.5, 1.0):
        cosine = cosine * square + term
    quarter = quarter - 4.0 * jnp.floor(quarter * 0.25)
    odd = (quarter == 1.0) | (quarter == 3.0)
    first = jnp.where(odd, sine, cosine)
    second = jnp.where(odd, cosine, sine)
    first = jnp.where((quarter == 1.0) | (quarter == 2.0), -first, first)
    return first, jnp.where(quarter >= 2.0, -second, second)


def project_kernel(sizes, count_hbm, orbitals_hbm, projectors_hbm, out_ref, *scratch):
    blocks, groups, orbitals, slots, length, projectors, planes, width = sizes
    count_ref, orbitals_ref, projectors_ref, coef, lines, small_sems, sems = scratch
    kinds = orbitals * 2
    devices = blocks * groups
    share = projectors // devices
    small = [
        pltpu.make_async_copy(count_hbm, count_ref, small_sems.at[0]),
        pltpu.make_async_copy(orbitals_hbm, orbitals_ref, small_sems.at[1]),
    ]
    copies = []
    for piece in range(2 * slots):
        rows = pl.ds(piece * length, length)
        copies.append(pltpu.make_async_copy(projectors_hbm.at[rows], projectors_ref.at[rows], sems.at[piece]))
    for copy in small + copies:
        copy.start()
    half = width // 2
    lanes = lax.broadcasted_iota(jnp.int32, (length, blocks * half), 1)
    plane = (lanes >> (half.bit_length() - 1)) * planes + (lanes & (half - 1))
    kz = lax.broadcasted_iota(jnp.int32, (length, blocks * half), 0)
    table = split(jnp.concatenate(cosine_and_sine(kz.astype(F32) * plane.astype(F32), length), axis=1))
    coef[...] = jnp.zeros_like(coef)
    small[0].wait()
    small[1].wait()
    used = used_slots(count_ref, slots)
    for n in range(orbitals):
        for part in range(2):
            values = jnp.where(used, orbitals_ref[n, part].astype(F32), 0.0)
            at = (part * orbitals + n) * slots
            lines[at : at + slots, :] = values
            turned = values if part == 1 else -values
            for slot in range(slots):
                row = n * 2 + part
                coef[slot, row : row + 1, :] = values[slot : slot + 1, :]
                row = n * 2 + 1 - part
                coef[slots + slot, row : row + 1, :] = turned[slot : slot + 1, :]
    left = lines[...].astype(BF16)
    both = dot(left, table[0]) + dot(left, table[1])
    rows = orbitals * slots
    points = blocks * half
    real = both[:rows, :points] - both[rows:, points:]
    imag = both[:rows, points:] + both[rows:, :points]
    lanes = lane_ids(rows)
    for block in range(blocks):
        at = block * half
        base = at // LANES * LANES
        chunk = pltpu.roll(imag[:, base : base + LANES], (base - at + half) % LANES, 1)
        chunk = jnp.where(lanes < half, pltpu.roll(real[:, base : base + LANES], (base - at) % LANES, 1), chunk)
        for group in range(groups):
            out_ref[block * groups + group] = chunk[group * slots : (group + 1) * slots, :]
    sums = jnp.zeros((coef.shape[1], projectors), F32)
    for piece in range(2 * slots):
        left = coef[piece].astype(BF16)
        copies[piece].wait()
        sums += dot(left, projectors_ref[piece * length : (piece + 1) * length, :])
    lanes = lane_ids(slots)
    for device in range(devices):
        piece = jnp.where(lanes < width, out_ref[device], 0.0)
        first = device * share
        base = first // LANES * LANES
        for rows in range(kinds // slots):
            low = width + rows * share
            own = pltpu.roll(sums[rows * slots : (rows + 1) * slots, base : base + LANES], (base + low - first) % LANES, 1)
            piece = jnp.where((lanes >= low) & (lanes < low + share), own, piece)
        out_ref[device] = piece


def table_kernel(length, wide, site_ref, x_ref, plus_ref):
    columns = site_ref.shape[1]
    eye = lax.broadcasted_iota(jnp.int32, (LANES, LANES), 0) == lane_ids(LANES)
    row_ids = lax.broadcasted_iota(jnp.int32, (length, LANES), 0).astype(F32)
    lanes = lax.broadcasted_iota(jnp.int32, (LANES, wide), 1)
    inside = lanes < length
    lanes = lanes.astype(F32)
    for at in range(0, columns, LANES):
        site = site_ref[:, at : at + LANES].astype(F32)
        site_x = jnp.floor((site + 0.5) * (1.0 / length))
        site_y = site - site_x * length
        cosine, sine = cosine_and_sine(row_ids * site_x, length)
        x_ref[:, at : at + LANES] = cosine
        x_ref[:, columns + at : columns + at + LANES] = sine
        along = jnp.sum(jnp.where(eye, site_y, 0.0), axis=1, keepdims=True)
        cosine, sine = cosine_and_sine(lanes * along, length)
        cosine = jnp.where(inside, cosine, 0.0)
        sine = jnp.where(inside, sine, 0.0)
        for piece, (own_cosine, own_sine) in enumerate(zip(split(cosine), split(sine))):
            rows = pl.ds(piece * 2 * columns + at, LANES)
            plus_ref[rows, :wide] = own_cosine
            plus_ref[rows, wide:] = own_sine
            rows = pl.ds((piece * 2 + 1) * columns + at, LANES)
            plus_ref[rows, :wide] = -own_sine
            plus_ref[rows, wide:] = own_cosine


def plane_kernel(sizes, columns_ref, x_ref, plus_ref, potential_ref, out_ref, gathered, lines, back):
    devices, slots, planes, length, wide, width, carried, batch = sizes
    count = devices * slots
    total = jnp.zeros((slots, LANES), F32)
    for device in range(devices):
        piece = columns_ref[device]
        gathered[device * slots : (device + 1) * slots, :] = piece
        total += piece
    for at in range(0, count, LANES):
        lines[:, at : at + LANES] = gathered[at : at + LANES, :].T
    back[...] = jnp.zeros_like(back)
    cosine = x_ref[:, :count]
    sine = x_ref[:, count:]
    padding = jnp.zeros((length, wide - length), F32)
    for i in range(planes // batch):
        left = []
        for plane in range(i * batch, (i + 1) * batch):
            real = lines[plane : plane + 1, :]
            imag = lines[plane + width // 2 : plane + width // 2 + 1, :]
            left.append(jnp.concatenate([cosine * real - sine * imag, cosine * imag + sine * real], axis=1))
        left = doubled(jnp.concatenate(left, axis=0))
        field = dot(left, plus_ref[...])
        weights = []
        for plane in range(i * batch, (i + 1) * batch):
            own = jnp.concatenate([potential_ref[plane], padding], axis=1)
            weights.append(jnp.concatenate([own, own], axis=1))
        left = (field * jnp.concatenate(weights, axis=0)).astype(BF16)
        half = dot_nt(left, plus_ref[: 2 * count, :])
        for j in range(batch):
            plane = i * batch + j
            real = half[j * length : (j + 1) * length, :count]
            imag = half[j * length : (j + 1) * length, count:]
            back[plane : plane + 1, :] = jnp.sum(cosine * real + sine * imag, axis=0, keepdims=True)
            at = plane + width // 2
            back[at : at + 1, :] = jnp.sum(cosine * imag - sine * real, axis=0, keepdims=True)
    for at in range(0, count, LANES):
        gathered[at : at + LANES, :] = back[:, at : at + LANES].T
    lanes = lane_ids(slots)
    for device in range(devices):
        piece = gathered[device * slots : (device + 1) * slots, :]
        out_ref[device] = jnp.where((lanes >= width) & (lanes < carried), total, piece)


def finish_kernel(
    sizes, count_ref, columns_ref, atom_ref, couplings_ref, projectors_ref, table_ref, out_ref, summed, lined, mixed
):
    blocks, groups, orbitals, slots, length, projectors, width, normalizer = sizes
    kinds = orbitals * 2
    devices = blocks * groups
    share = projectors // devices
    groups_of_rows = kinds // slots
    lanes = lane_ids(slots)
    for chunk in range(projectors // LANES):
        in_chunk = range(chunk * LANES // share, (chunk + 1) * LANES // share)
        for rows in range(groups_of_rows):
            low = width + rows * share
            total = jnp.zeros((slots, LANES), F32)
            for device in in_chunk:
                own = columns_ref[device]
                own = pltpu.roll(jnp.where((lanes >= low) & (lanes < low + share), own, 0.0), (device * share - low) % LANES, 1)
                total += own
            summed[rows * slots : (rows + 1) * slots, chunk * LANES : (chunk + 1) * LANES] = total
    for n in range(orbitals):
        at = kinds + n * 2
        summed[at : at + 1, :] = -summed[n * 2 + 1 : n * 2 + 2, :]
        summed[at + 1 : at + 2, :] = summed[n * 2 : n * 2 + 1, :]
    both = stacked(summed[...])
    atoms = atom_ref[...].astype(F32)
    eye = lax.broadcasted_iota(jnp.int32, (LANES, LANES), 0) == lane_ids(LANES)
    along = []
    for at in range(0, projectors, LANES):
        along.append(jnp.sum(jnp.where(eye, atoms[:, at : at + LANES], 0.0), axis=1, keepdims=True))
    head, rest = split(jnp.where(jnp.concatenate(along, axis=0) == atoms, couplings_ref[...], 0.0))
    head = dot_nt(both, head)
    rest = dot_nt(both, rest)
    weighted = (head[: 2 * kinds] + (head[2 * kinds :] + rest[: 2 * kinds])).astype(BF16)
    for slot in range(slots):
        rows = projectors_ref[slot * length : (slot + 1) * length, :]
        value = dot_nt(weighted, rows)[:kinds]
        rows = projectors_ref[(slots + slot) * length : (slots + slot + 1) * length, :]
        value = value + dot_nt(weighted, rows)[kinds:]
        for row in range(kinds):
            mixed[row, slot : slot + 1, :] = value[row : row + 1, :]
    for chunk in range(blocks * width // LANES):
        for group in range(groups):
            total = jnp.zeros((slots, LANES), F32)
            for inner in range(LANES // width):
                block = chunk * (LANES // width) + inner
                own = jnp.where(lanes < width, columns_ref[block * groups + group], 0.0)
                total += pltpu.roll(own, inner * width, 1)
            lined[group * slots : (group + 1) * slots, chunk * LANES : (chunk + 1) * LANES] = total
    both = stacked(lined[...])
    rows_of_lines = groups * slots
    held = lax.broadcasted_iota(jnp.int32, (1, blocks), 1) == lax.axis_index("ga")
    used = jnp.sum(jnp.where(held, count_ref[...], 0).astype(F32), axis=1, keepdims=True)
    slot_ids = lax.broadcasted_iota(jnp.int32, (slots, 1), 0) + lax.axis_index("band") * slots
    used = slot_ids.astype(F32) < used
    for part in range(2):
        head = dot_nt(both, table_ref[0, part])
        rest = dot_nt(both, table_ref[1, part])
        local = (head[:rows_of_lines] + (head[rows_of_lines:] + rest[:rows_of_lines])) * normalizer
        for n in range(orbitals):
            value = local[n * slots : (n + 1) * slots, :] + mixed[n * 2 + part]
            out_ref[n, part] = jnp.where(used, value, 0.0)


def on_device(orbitals, projectors, potential, couplings, atom_index, column_site, column_count):
    blocks = lax.axis_size("ga")
    groups = lax.axis_size("band")
    devices = blocks * groups
    orbital_count, _, slots, length = orbitals.shape
    planes = potential.shape[0]
    projector_count = projectors.shape[0]
    columns = column_site.shape[0]
    kinds = orbital_count * 2
    assert orbital_count == groups and kinds % slots == 0 and columns % LANES == 0
    share = projector_count // devices
    width = 2
    while width < 2 * planes:
        width *= 2
    carried = width + kinds // slots * share
    assert carried <= LANES and width <= LANES and share * devices == projector_count
    wide = -(-length // LANES) * LANES
    flat = jnp.transpose(projectors, (1, 2, 3, 0)).reshape(2 * slots * length, projector_count)
    z_table = line_table(length, blocks, planes, width)
    batch = next(i for i in (2, 3, 1) if planes % i == 0) if columns <= 512 else 1
    vmem = pl.BlockSpec(memory_space=pltpu.VMEM)
    hbm = pl.BlockSpec(memory_space=pltpu.HBM)
    params = pltpu.CompilerParams(vmem_limit_bytes=56 * 1024 * 1024)
    small = pltpu.CompilerParams(vmem_limit_bytes=40 * 1024 * 1024)
    payload = jax.ShapeDtypeStruct((devices, slots, LANES), F32)

    sent = pl.pallas_call(
        functools.partial(
            project_kernel,
                (blocks, groups, orbital_count, slots, length, projector_count, planes, width),
        ),
        out_shape=payload,
        in_specs=[hbm] * 3,
        out_specs=vmem,
        scratch_shapes=[
            pltpu.SMEM(column_count.shape, jnp.int32),
            pltpu.VMEM(orbitals.shape, BF16),
            pltpu.VMEM(flat.shape, BF16),
            pltpu.VMEM((2 * slots, -(-kinds // 8) * 8, length), F32),
            pltpu.VMEM((kinds * slots, length), F32),
            pltpu.SemaphoreType.DMA((2,)),
            pltpu.SemaphoreType.DMA((2 * slots,)),
        ],
        compiler_params=params,
        cost_estimate=pl.CostEstimate(
            flops=2 * flat.size * LANES * slots,
            bytes_accessed=2 * (flat.size + z_table.size + orbitals.size) + 4 * devices * slots * LANES,
            transcendentals=length * blocks * width,
        ),
        name="project",
    )(column_count, orbitals, flat)
    arrived = lax.all_to_all(sent, ("ga", "band"), split_axis=0, concat_axis=0, tiled=True)

    x_rows, plus = pl.pallas_call(
        functools.partial(table_kernel, length, wide),
        out_shape=(
            jax.ShapeDtypeStruct((length, 2 * columns), F32),
            jax.ShapeDtypeStruct((4 * columns, 2 * wide), BF16),
        ),
        in_specs=[vmem],
        out_specs=(vmem,) * 2,
        compiler_params=small,
        cost_estimate=pl.CostEstimate(
            flops=4096 * potential.size,
            bytes_accessed=8 * (length + 2 * wide) * columns,
            transcendentals=2 * (length + wide) * columns,
        ),
        name="tables",
    )(column_site.reshape(1, columns))

    sent = pl.pallas_call(
        functools.partial(plane_kernel, (devices, slots, planes, length, wide, width, carried, batch)),
        out_shape=payload,
        in_specs=[vmem] * 4,
        out_specs=vmem,
        scratch_shapes=[
            pltpu.VMEM((columns, LANES), F32),
            pltpu.VMEM((LANES, columns), F32),
            pltpu.VMEM((LANES, columns), F32),
        ],
        compiler_params=small,
        cost_estimate=pl.CostEstimate(
            flops=12 * planes * length * wide * 2 * columns,
            bytes_accessed=4 * (potential.size + 2 * devices * slots * LANES),
            transcendentals=0,
        ),
        name="planes",
    )(arrived, x_rows, plus, potential)
    arrived = lax.all_to_all(sent, ("ga", "band"), split_axis=0, concat_axis=0, tiled=True)

    normalizer = 1.0 / float(length**3)
    return pl.pallas_call(
        functools.partial(
            finish_kernel,
            (blocks, groups, orbital_count, slots, length, projector_count, width, normalizer),
        ),
        out_shape=jax.ShapeDtypeStruct(orbitals.shape, F32),
        in_specs=[vmem] * 6,
        out_specs=vmem,
        scratch_shapes=[
            pltpu.VMEM((2 * kinds, projector_count), F32),
            pltpu.VMEM((groups * slots, blocks * width), F32),
            pltpu.VMEM((kinds, slots, length), F32),
        ],
        compiler_params=small,
        cost_estimate=pl.CostEstimate(
            flops=4 * kinds * (4 * couplings.size + flat.size) + 4 * z_table.size * orbital_count * slots,
            bytes_accessed=4 * couplings.size + 2 * (flat.size + z_table.size) + 4 * orbitals.size,
            transcendentals=0,
        ),
        name="finish",
    )(column_count.reshape(1, blocks), arrived, atom_index.reshape(1, projector_count), couplings, flat, z_table)


def solution(mesh):
    return jax.shard_map(
        on_device,
        mesh=mesh,
        in_specs=(
            P(None, None, ("ga", "band"), None),
            P(None, None, ("ga", "band"), None),
            P("ga", None, None),
            P(),
            P(),
            P(),
            P(),
        ),
        out_specs=P(None, None, ("ga", "band"), None),
        check_vma=False,
    )
```

```python
import functools

import jax
import jax.numpy as jnp
import ml_dtypes
import numpy as np
from jax import lax
from jax.experimental import pallas as pl
from jax.experimental.pallas import tpu as pltpu
from jax.sharding import PartitionSpec as P

LANES = 128
BF16 = jnp.bfloat16
F32 = jnp.float32


def pieces_of(table):
    table = np.asarray(table, np.float32)
    head = table.astype(ml_dtypes.bfloat16)
    return np.stack([head, (table - head.astype(np.float32)).astype(ml_dtypes.bfloat16)])


def line_table(length, blocks, planes, width):
    kz = np.arange(length)
    out = np.zeros((2, length, blocks, width), np.float64)
    for block in range(blocks):
        z = block * planes + np.arange(planes)
        phases = (kz[:, None] * z[None, :] % length) * (2.0 * np.pi / length)
        out[0, :, block, :planes] = np.cos(phases)
        out[0, :, block, width // 2 : width // 2 + planes] = np.sin(phases)
        out[1, :, block, :planes] = -np.sin(phases)
        out[1, :, block, width // 2 : width // 2 + planes] = np.cos(phases)
    return pieces_of(out.reshape(2, length, blocks * width))


def split(values):
    head = values.astype(BF16)
    return head, (values - head.astype(F32)).astype(BF16)


def stacked(values):
    head, rest = split(values)
    return jnp.concatenate([head.astype(F32), rest.astype(F32)], axis=0).astype(BF16)


def both_pieces(values):
    return jnp.concatenate(split(values), axis=1)


def dot(left, right):
    return lax.dot_general(left, right, (((1,), (0,)), ((), ())), preferred_element_type=F32)


def dot_nt(left, right):
    return lax.dot_general(left, right, (((1,), (1,)), ((), ())), preferred_element_type=F32)


def lane_ids(rows):
    return lax.broadcasted_iota(jnp.int32, (rows, LANES), 1)


def used_slots(count_ref, slots):
    used = count_ref[lax.axis_index("ga")] - lax.axis_index("band") * slots
    return lax.broadcasted_iota(jnp.int32, (slots, 1), 0) < used


def cosine_and_sine(phases, length):
    quarter = jnp.floor(phases * (4.0 / length) + 0.5)
    angle = (phases - quarter * (length / 4.0)) * (2.0 * np.pi / length)
    square = angle * angle
    sine = 1.0 / 362880.0
    for term in (-1.0 / 5040.0, 1.0 / 120.0, -1.0 / 6.0, 1.0):
        sine = sine * square + term
    sine = sine * angle
    cosine = -1.0 / 3628800.0
    for term in (1.0 / 40320.0, -1.0 / 720.0, 1.0 / 24.0, -0.5, 1.0):
        cosine = cosine * square + term
    quarter = quarter - 4.0 * jnp.floor(quarter * 0.25)
    odd = (quarter == 1.0) | (quarter == 3.0)
    first = jnp.where(odd, sine, cosine)
    second = jnp.where(odd, cosine, sine)
    first = jnp.where((quarter == 1.0) | (quarter == 2.0), -first, first)
    return first, jnp.where(quarter >= 2.0, -second, second)


def project_kernel(sizes, count_hbm, orbitals_hbm, projectors_hbm, out_ref, *scratch):
    blocks, groups, orbitals, slots, length, projectors, planes, width = sizes
    count_ref, orbitals_ref, projectors_ref, coef, lines, small_sems, sems = scratch
    kinds = orbitals * 2
    devices = blocks * groups
    share = projectors // devices
    small = [
        pltpu.make_async_copy(count_hbm, count_ref, small_sems.at[0]),
        pltpu.make_async_copy(orbitals_hbm, orbitals_ref, small_sems.at[1]),
    ]
    copies = []
    for piece in range(2 * slots):
        rows = pl.ds(piece * length, length)
        copies.append(pltpu.make_async_copy(projectors_hbm.at[rows], projectors_ref.at[rows], sems.at[piece]))
    for copy in small + copies:
        copy.start()
    half = width // 2
    lanes = lax.broadcasted_iota(jnp.int32, (length, blocks * half), 1)
    plane = (lanes >> (half.bit_length() - 1)) * planes + (lanes & (half - 1))
    kz = lax.broadcasted_iota(jnp.int32, (length, blocks * half), 0)
    table = split(jnp.concatenate(cosine_and_sine(kz.astype(F32) * plane.astype(F32), length), axis=1))
    coef[...] = jnp.zeros_like(coef)
    small[0].wait()
    small[1].wait()
    used = used_slots(count_ref, slots)
    for n in range(orbitals):
        for part in range(2):
            values = jnp.where(used, orbitals_ref[n, part].astype(F32), 0.0)
            at = (part * orbitals + n) * slots
            lines[at : at + slots, :] = values
            turned = values if part == 1 else -values
            for slot in range(slots):
                row = n * 2 + part
                coef[slot, row : row + 1, :] = values[slot : slot + 1, :]
                row = n * 2 + 1 - part
                coef[slots + slot, row : row + 1, :] = turned[slot : slot + 1, :]
    left = lines[...].astype(BF16)
    both = dot(left, table[0]) + dot(left, table[1])
    rows = orbitals * slots
    points = blocks * half
    real = both[:rows, :points] - both[rows:, points:]
    imag = both[:rows, points:] + both[rows:, :points]
    lanes = lane_ids(rows)
    for block in range(blocks):
        at = block * half
        base = at // LANES * LANES
        chunk = pltpu.roll(imag[:, base : base + LANES], (base - at + half) % LANES, 1)
        chunk = jnp.where(lanes < half, pltpu.roll(real[:, base : base + LANES], (base - at) % LANES, 1), chunk)
        for group in range(groups):
            out_ref[block * groups + group] = chunk[group * slots : (group + 1) * slots, :]
    sums = jnp.zeros((coef.shape[1], projectors), F32)
    for piece in range(2 * slots):
        left = coef[piece].astype(BF16)
        copies[piece].wait()
        sums += dot(left, projectors_ref[piece * length : (piece + 1) * length, :])
    lanes = lane_ids(slots)
    for device in range(devices):
        piece = jnp.where(lanes < width, out_ref[device], 0.0)
        first = device * share
        base = first // LANES * LANES
        for rows in range(kinds // slots):
            low = width + rows * share
            own = pltpu.roll(sums[rows * slots : (rows + 1) * slots, base : base + LANES], (base + low - first) % LANES, 1)
            piece = jnp.where((lanes >= low) & (lanes < low + share), own, piece)
        out_ref[device] = piece


def table_kernel(length, wide, site_ref, x_ref, plus_ref):
    columns = site_ref.shape[1]
    eye = lax.broadcasted_iota(jnp.int32, (LANES, LANES), 0) == lane_ids(LANES)
    row_ids = lax.broadcasted_iota(jnp.int32, (length, LANES), 0).astype(F32)
    lanes = lax.broadcasted_iota(jnp.int32, (LANES, wide), 1)
    inside = lanes < length
    lanes = lanes.astype(F32)
    for at in range(0, columns, LANES):
        site = site_ref[:, at : at + LANES].astype(F32)
        site_x = jnp.floor((site + 0.5) * (1.0 / length))
        site_y = site - site_x * length
        cosine, sine = cosine_and_sine(row_ids * site_x, length)
        x_ref[:, at : at + LANES] = cosine
        x_ref[:, columns + at : columns + at + LANES] = sine
        along = jnp.sum(jnp.where(eye, site_y, 0.0), axis=1, keepdims=True)
        cosine, sine = cosine_and_sine(lanes * along, length)
        cosine = jnp.where(inside, cosine, 0.0)
        sine = jnp.where(inside, sine, 0.0)
        cosine = cosine.astype(BF16)
        sine = sine.astype(BF16)
        for piece in range(2):
            rows = pl.ds(piece * 2 * columns + at, LANES)
            plus_ref[rows, :wide] = cosine
            plus_ref[rows, wide:] = sine
            rows = pl.ds((piece * 2 + 1) * columns + at, LANES)
            plus_ref[rows, :wide] = -sine
            plus_ref[rows, wide:] = cosine


def plane_kernel(sizes, columns_ref, x_ref, plus_ref, potential_ref, out_ref, gathered, lines, back):
    devices, slots, planes, length, wide, width, carried, batch = sizes
    count = devices * slots
    total = jnp.zeros((slots, LANES), F32)
    for device in range(devices):
        piece = columns_ref[device]
        gathered[device * slots : (device + 1) * slots, :] = piece
        total += piece
    for at in range(0, count, LANES):
        lines[:, at : at + LANES] = gathered[at : at + LANES, :].T
    back[...] = jnp.zeros_like(back)
    cosine = x_ref[:, :count]
    sine = x_ref[:, count:]
    padding = jnp.zeros((length, wide - length), F32)
    for i in range(planes // batch):
        left = []
        for plane in range(i * batch, (i + 1) * batch):
            real = lines[plane : plane + 1, :]
            imag = lines[plane + width // 2 : plane + width // 2 + 1, :]
            left.append(jnp.concatenate([cosine * real - sine * imag, cosine * imag + sine * real], axis=1))
        left = both_pieces(jnp.concatenate(left, axis=0))
        field = dot(left, plus_ref[...])
        weights = []
        for plane in range(i * batch, (i + 1) * batch):
            own = jnp.concatenate([potential_ref[plane], padding], axis=1)
            weights.append(jnp.concatenate([own, own], axis=1))
        left = (field * jnp.concatenate(weights, axis=0)).astype(BF16)
        half = dot_nt(left, plus_ref[: 2 * count, :])
        for j in range(batch):
            plane = i * batch + j
            real = half[j * length : (j + 1) * length, :count]
            imag = half[j * length : (j + 1) * length, count:]
            back[plane : plane + 1, :] = jnp.sum(cosine * real + sine * imag, axis=0, keepdims=True)
            at = plane + width // 2
            back[at : at + 1, :] = jnp.sum(cosine * imag - sine * real, axis=0, keepdims=True)
    for at in range(0, count, LANES):
        gathered[at : at + LANES, :] = back[:, at : at + LANES].T
    lanes = lane_ids(slots)
    for device in range(devices):
        piece = gathered[device * slots : (device + 1) * slots, :]
        out_ref[device] = jnp.where((lanes >= width) & (lanes < carried), total, piece)


def finish_kernel(
    sizes, count_ref, columns_ref, atom_ref, couplings_ref, projectors_ref, table_ref, out_ref, summed, lined, mixed
):
    blocks, groups, orbitals, slots, length, projectors, width, normalizer = sizes
    kinds = orbitals * 2
    devices = blocks * groups
    share = projectors // devices
    groups_of_rows = kinds // slots
    lanes = lane_ids(slots)
    for chunk in range(projectors // LANES):
        in_chunk = range(chunk * LANES // share, (chunk + 1) * LANES // share)
        for rows in range(groups_of_rows):
            low = width + rows * share
            total = jnp.zeros((slots, LANES), F32)
            for device in in_chunk:
                own = columns_ref[device]
                own = pltpu.roll(jnp.where((lanes >= low) & (lanes < low + share), own, 0.0), (device * share - low) % LANES, 1)
                total += own
            summed[rows * slots : (rows + 1) * slots, chunk * LANES : (chunk + 1) * LANES] = total
    for n in range(orbitals):
        at = kinds + n * 2
        summed[at : at + 1, :] = -summed[n * 2 + 1 : n * 2 + 2, :]
        summed[at + 1 : at + 2, :] = summed[n * 2 : n * 2 + 1, :]
    both = stacked(summed[...])
    atoms = atom_ref[...].astype(F32)
    eye = lax.broadcasted_iota(jnp.int32, (LANES, LANES), 0) == lane_ids(LANES)
    along = []
    for at in range(0, projectors, LANES):
        along.append(jnp.sum(jnp.where(eye, atoms[:, at : at + LANES], 0.0), axis=1, keepdims=True))
    head, rest = split(jnp.where(jnp.concatenate(along, axis=0) == atoms, couplings_ref[...], 0.0))
    head = dot_nt(both, head)
    rest = dot_nt(both, rest)
    weighted = (head[: 2 * kinds] + (head[2 * kinds :] + rest[: 2 * kinds])).astype(BF16)
    for slot in range(slots):
        rows = projectors_ref[slot * length : (slot + 1) * length, :]
        value = dot_nt(weighted, rows)[:kinds]
        rows = projectors_ref[(slots + slot) * length : (slots + slot + 1) * length, :]
        value = value + dot_nt(weighted, rows)[kinds:]
        for row in range(kinds):
            mixed[row, slot : slot + 1, :] = value[row : row + 1, :]
    for chunk in range(blocks * width // LANES):
        for group in range(groups):
            total = jnp.zeros((slots, LANES), F32)
            for inner in range(LANES // width):
                block = chunk * (LANES // width) + inner
                own = jnp.where(lanes < width, columns_ref[block * groups + group], 0.0)
                total += pltpu.roll(own, inner * width, 1)
            lined[group * slots : (group + 1) * slots, chunk * LANES : (chunk + 1) * LANES] = total
    both = stacked(lined[...])
    rows_of_lines = groups * slots
    held = lax.broadcasted_iota(jnp.int32, (1, blocks), 1) == lax.axis_index("ga")
    used = jnp.sum(jnp.where(held, count_ref[...], 0).astype(F32), axis=1, keepdims=True)
    slot_ids = lax.broadcasted_iota(jnp.int32, (slots, 1), 0) + lax.axis_index("band") * slots
    used = slot_ids.astype(F32) < used
    for part in range(2):
        head = dot_nt(both, table_ref[0, part])
        rest = dot_nt(both, table_ref[1, part])
        local = (head[:rows_of_lines] + (head[rows_of_lines:] + rest[:rows_of_lines])) * normalizer
        for n in range(orbitals):
            value = local[n * slots : (n + 1) * slots, :] + mixed[n * 2 + part]
            out_ref[n, part] = jnp.where(used, value, 0.0)


def on_device(orbitals, projectors, potential, couplings, atom_index, column_site, column_count):
    blocks = lax.axis_size("ga")
    groups = lax.axis_size("band")
    devices = blocks * groups
    orbital_count, _, slots, length = orbitals.shape
    planes = potential.shape[0]
    projector_count = projectors.shape[0]
    columns = column_site.shape[0]
    kinds = orbital_count * 2
    assert orbital_count == groups and kinds % slots == 0 and columns % LANES == 0
    share = projector_count // devices
    width = 2
    while width < 2 * planes:
        width *= 2
    carried = width + kinds // slots * share
    assert carried <= LANES and width <= LANES and share * devices == projector_count
    wide = -(-length // LANES) * LANES
    flat = jnp.transpose(projectors, (1, 2, 3, 0)).reshape(2 * slots * length, projector_count)
    z_table = line_table(length, blocks, planes, width)
    batch = next(i for i in (2, 3, 1) if planes % i == 0) if columns <= 512 else 1
    vmem = pl.BlockSpec(memory_space=pltpu.VMEM)
    hbm = pl.BlockSpec(memory_space=pltpu.HBM)
    params = pltpu.CompilerParams(vmem_limit_bytes=56 * 1024 * 1024)
    small = pltpu.CompilerParams(vmem_limit_bytes=40 * 1024 * 1024)
    payload = jax.ShapeDtypeStruct((devices, slots, LANES), F32)

    sent = pl.pallas_call(
        functools.partial(
            project_kernel,
                (blocks, groups, orbital_count, slots, length, projector_count, planes, width),
        ),
        out_shape=payload,
        in_specs=[hbm] * 3,
        out_specs=vmem,
        scratch_shapes=[
            pltpu.SMEM(column_count.shape, jnp.int32),
            pltpu.VMEM(orbitals.shape, BF16),
            pltpu.VMEM(flat.shape, BF16),
            pltpu.VMEM((2 * slots, -(-kinds // 8) * 8, length), F32),
            pltpu.VMEM((kinds * slots, length), F32),
            pltpu.SemaphoreType.DMA((2,)),
            pltpu.SemaphoreType.DMA((2 * slots,)),
        ],
        compiler_params=params,
        cost_estimate=pl.CostEstimate(
            flops=2 * flat.size * LANES * slots,
            bytes_accessed=2 * (flat.size + z_table.size + orbitals.size) + 4 * devices * slots * LANES,
            transcendentals=length * blocks * width,
        ),
        name="project",
    )(column_count, orbitals, flat)
    arrived = lax.all_to_all(sent, ("ga", "band"), split_axis=0, concat_axis=0, tiled=True)

    x_rows, plus = pl.pallas_call(
        functools.partial(table_kernel, length, wide),
        out_shape=(
            jax.ShapeDtypeStruct((length, 2 * columns), F32),
            jax.ShapeDtypeStruct((4 * columns, 2 * wide), BF16),
        ),
        in_specs=[vmem],
        out_specs=(vmem,) * 2,
        compiler_params=small,
        cost_estimate=pl.CostEstimate(
            flops=4096 * potential.size,
            bytes_accessed=8 * (length + 2 * wide) * columns,
            transcendentals=2 * (length + wide) * columns,
        ),
        name="tables",
    )(column_site.reshape(1, columns))

    sent = pl.pallas_call(
        functools.partial(plane_kernel, (devices, slots, planes, length, wide, width, carried, batch)),
        out_shape=payload,
        in_specs=[vmem] * 4,
        out_specs=vmem,
        scratch_shapes=[
            pltpu.VMEM((columns, LANES), F32),
            pltpu.VMEM((LANES, columns), F32),
            pltpu.VMEM((LANES, columns), F32),
        ],
        compiler_params=small,
        cost_estimate=pl.CostEstimate(
            flops=12 * planes * length * wide * 2 * columns,
            bytes_accessed=4 * (potential.size + 2 * devices * slots * LANES),
            transcendentals=0,
        ),
        name="planes",
    )(arrived, x_rows, plus, potential)
    arrived = lax.all_to_all(sent, ("ga", "band"), split_axis=0, concat_axis=0, tiled=True)

    normalizer = 1.0 / float(length**3)
    return pl.pallas_call(
        functools.partial(
            finish_kernel,
            (blocks, groups, orbital_count, slots, length, projector_count, width, normalizer),
        ),
        out_shape=jax.ShapeDtypeStruct(orbitals.shape, F32),
        in_specs=[vmem] * 6,
        out_specs=vmem,
        scratch_shapes=[
            pltpu.VMEM((2 * kinds, projector_count), F32),
            pltpu.VMEM((groups * slots, blocks * width), F32),
            pltpu.VMEM((kinds, slots, length), F32),
        ],
        compiler_params=small,
        cost_estimate=pl.CostEstimate(
            flops=4 * kinds * (4 * couplings.size + flat.size) + 4 * z_table.size * orbital_count * slots,
            bytes_accessed=4 * couplings.size + 2 * (flat.size + z_table.size) + 4 * orbitals.size,
            transcendentals=0,
        ),
        name="finish",
    )(column_count.reshape(1, blocks), arrived, atom_index.reshape(1, projector_count), couplings, flat, z_table)


def solution(mesh):
    return jax.shard_map(
        on_device,
        mesh=mesh,
        in_specs=(
            P(None, None, ("ga", "band"), None),
            P(None, None, ("ga", "band"), None),
            P("ga", None, None),
            P(),
            P(),
            P(),
            P(),
        ),
        out_specs=P(None, None, ("ga", "band"), None),
        check_vma=False,
    )
```

```python
import functools

import jax
import jax.numpy as jnp
import ml_dtypes
import numpy as np
from jax import lax
from jax.experimental import pallas as pl
from jax.experimental.pallas import tpu as pltpu
from jax.sharding import PartitionSpec as P

LANES = 128
BF16 = jnp.bfloat16
F32 = jnp.float32


def pieces_of(table):
    table = np.asarray(table, np.float32)
    head = table.astype(ml_dtypes.bfloat16)
    return np.stack([head, (table - head.astype(np.float32)).astype(ml_dtypes.bfloat16)])


def line_table(length, blocks, planes, width):
    kz = np.arange(length)
    out = np.zeros((2, length, blocks, width), np.float64)
    for block in range(blocks):
        z = block * planes + np.arange(planes)
        phases = (kz[:, None] * z[None, :] % length) * (2.0 * np.pi / length)
        out[0, :, block, :planes] = np.cos(phases)
        out[0, :, block, width // 2 : width // 2 + planes] = np.sin(phases)
        out[1, :, block, :planes] = -np.sin(phases)
        out[1, :, block, width // 2 : width // 2 + planes] = np.cos(phases)
    return pieces_of(out.reshape(2, length, blocks * width))


def split(values):
    head = values.astype(BF16)
    return head, (values - head.astype(F32)).astype(BF16)


def stacked(values):
    head, rest = split(values)
    return jnp.concatenate([head.astype(F32), rest.astype(F32)], axis=0).astype(BF16)


def both_pieces(values):
    return jnp.concatenate(split(values), axis=1)


def dot(left, right):
    return lax.dot_general(left, right, (((1,), (0,)), ((), ())), preferred_element_type=F32)


def dot_nt(left, right):
    return lax.dot_general(left, right, (((1,), (1,)), ((), ())), preferred_element_type=F32)


def lane_ids(rows):
    return lax.broadcasted_iota(jnp.int32, (rows, LANES), 1)


def used_slots(count_ref, slots):
    used = count_ref[lax.axis_index("ga")] - lax.axis_index("band") * slots
    return lax.broadcasted_iota(jnp.int32, (slots, 1), 0) < used


def cosine_and_sine(phases, length):
    quarter = jnp.floor(phases * (4.0 / length) + 0.5)
    angle = (phases - quarter * (length / 4.0)) * (2.0 * np.pi / length)
    square = angle * angle
    sine = 1.0 / 362880.0
    for term in (-1.0 / 5040.0, 1.0 / 120.0, -1.0 / 6.0, 1.0):
        sine = sine * square + term
    sine = sine * angle
    cosine = -1.0 / 3628800.0
    for term in (1.0 / 40320.0, -1.0 / 720.0, 1.0 / 24.0, -0.5, 1.0):
        cosine = cosine * square + term
    quarter = quarter - 4.0 * jnp.floor(quarter * 0.25)
    odd = (quarter == 1.0) | (quarter == 3.0)
    first = jnp.where(odd, sine, cosine)
    second = jnp.where(odd, cosine, sine)
    first = jnp.where((quarter == 1.0) | (quarter == 2.0), -first, first)
    return first, jnp.where(quarter >= 2.0, -second, second)


def project_kernel(sizes, count_hbm, orbitals_hbm, projectors_hbm, out_ref, *scratch):
    blocks, groups, orbitals, slots, length, projectors, planes, width = sizes
    count_ref, orbitals_ref, projectors_ref, coef, lines, small_sems, sems = scratch
    kinds = orbitals * 2
    devices = blocks * groups
    share = projectors // devices
    small = [
        pltpu.make_async_copy(count_hbm, count_ref, small_sems.at[0]),
        pltpu.make_async_copy(orbitals_hbm, orbitals_ref, small_sems.at[1]),
    ]
    copies = []
    for piece in range(2 * slots):
        rows = pl.ds(piece * length, length)
        copies.append(pltpu.make_async_copy(projectors_hbm.at[rows], projectors_ref.at[rows], sems.at[piece]))
    for copy in small + copies:
        copy.start()
    half = width // 2
    lanes = lax.broadcasted_iota(jnp.int32, (length, blocks * half), 1)
    plane = (lanes >> (half.bit_length() - 1)) * planes + (lanes & (half - 1))
    kz = lax.broadcasted_iota(jnp.int32, (length, blocks * half), 0)
    table = split(jnp.concatenate(cosine_and_sine(kz.astype(F32) * plane.astype(F32), length), axis=1))
    coef[...] = jnp.zeros_like(coef)
    small[0].wait()
    small[1].wait()
    used = used_slots(count_ref, slots)
    for n in range(orbitals):
        for part in range(2):
            values = jnp.where(used, orbitals_ref[n, part].astype(F32), 0.0)
            at = (part * orbitals + n) * slots
            lines[at : at + slots, :] = values
            turned = values if part == 1 else -values
            for slot in range(slots):
                row = n * 2 + part
                coef[slot, row : row + 1, :] = values[slot : slot + 1, :]
                row = n * 2 + 1 - part
                coef[slots + slot, row : row + 1, :] = turned[slot : slot + 1, :]
    left = lines[...].astype(BF16)
    both = dot(left, table[0]) + dot(left, table[1])
    rows = orbitals * slots
    points = blocks * half
    real = both[:rows, :points] - both[rows:, points:]
    imag = both[:rows, points:] + both[rows:, :points]
    lanes = lane_ids(rows)
    rows_each = slots // 2
    piece_lanes = lane_ids(rows_each)
    for block in range(blocks):
        at = block * half
        base = at // LANES * LANES
        chunk = pltpu.roll(imag[:, base : base + LANES], (base - at + half) % LANES, 1)
        chunk = jnp.where(lanes < half, pltpu.roll(real[:, base : base + LANES], (base - at) % LANES, 1), chunk)
        aside = pltpu.roll(chunk, width, 1)
        for group in range(groups):
            at = group * slots
            piece = jnp.where(piece_lanes < width, chunk[at : at + rows_each, :], aside[at + rows_each : at + slots, :])
            out_ref[block * groups + group] = piece
    sums = jnp.zeros((coef.shape[1], projectors), F32)
    for piece in range(2 * slots):
        left = coef[piece].astype(BF16)
        copies[piece].wait()
        sums += dot(left, projectors_ref[piece * length : (piece + 1) * length, :])
    for device in range(devices):
        piece = jnp.where(piece_lanes < 2 * width, out_ref[device], 0.0)
        first = device * share
        base = first // LANES * LANES
        for group in range(kinds // rows_each):
            low = 2 * width + group * share
            own = sums[group * rows_each : (group + 1) * rows_each, base : base + LANES]
            own = pltpu.roll(own, (base + low - first) % LANES, 1)
            piece = jnp.where((piece_lanes >= low) & (piece_lanes < low + share), own, piece)
        out_ref[device] = piece


def table_kernel(length, wide, slots, site_ref, x_ref, plus_ref):
    columns = site_ref.shape[1]
    each = slots // 2
    eye = lax.broadcasted_iota(jnp.int32, (LANES, LANES), 0) == lane_ids(LANES)
    row_ids = lax.broadcasted_iota(jnp.int32, (length, LANES), 0).astype(F32)
    lanes = lax.broadcasted_iota(jnp.int32, (LANES, wide), 1)
    inside = lanes < length
    lanes = lanes.astype(F32)
    sites = site_ref[...].astype(F32)
    stored = lax.broadcasted_iota(jnp.int32, (LANES, columns), 1)
    for at in range(0, columns, LANES):
        order = lax.broadcasted_iota(jnp.int32, (LANES, columns), 0) + at
        second = order >= columns // 2
        order = jnp.where(second, order - columns // 2, order)
        wanted = (order >> (each.bit_length() - 1)) * slots + (order & (each - 1)) + jnp.where(second, each, 0)
        along = jnp.sum(jnp.where(stored == wanted, sites, 0.0), axis=1, keepdims=True)
        site = jnp.sum(jnp.where(eye, along, 0.0), axis=0, keepdims=True)
        site_x = jnp.floor((site + 0.5) * (1.0 / length))
        along = along - jnp.floor((along + 0.5) * (1.0 / length)) * length
        cosine, sine = cosine_and_sine(row_ids * site_x, length)
        x_ref[:, at : at + LANES] = cosine
        x_ref[:, columns + at : columns + at + LANES] = sine
        cosine, sine = cosine_and_sine(lanes * along, length)
        cosine = jnp.where(inside, cosine, 0.0)
        sine = jnp.where(inside, sine, 0.0)
        cosine = cosine.astype(BF16)
        sine = sine.astype(BF16)
        for piece in range(2):
            rows = pl.ds(piece * 2 * columns + at, LANES)
            plus_ref[rows, :wide] = cosine
            plus_ref[rows, wide:] = sine
            rows = pl.ds((piece * 2 + 1) * columns + at, LANES)
            plus_ref[rows, :wide] = -sine
            plus_ref[rows, wide:] = cosine


def plane_kernel(sizes, columns_ref, x_ref, plus_ref, potential_ref, out_ref, gathered, lines, back, turning):
    devices, slots, planes, length, wide, width, carried, batch = sizes
    count = devices * slots
    each = slots // 2
    middle = count // 2
    total = jnp.zeros((each, LANES), F32)
    for device in range(devices):
        piece = columns_ref[device]
        gathered[device * each : (device + 1) * each, :] = piece
        total += piece
    for at in range(0, middle, LANES):
        size = min(LANES, middle - at)
        turned = gathered[at : at + LANES, :].T
        for side in range(2):
            lines[:, side * middle + at : side * middle + at + size] = turned[side * width : (side + 1) * width, :size]
    back[...] = jnp.zeros_like(back)
    cosine = x_ref[:, :count]
    sine = x_ref[:, count:]
    padding = jnp.zeros((length, wide - length), F32)
    for i in range(planes // batch):
        left = []
        for plane in range(i * batch, (i + 1) * batch):
            real = lines[plane : plane + 1, :]
            imag = lines[plane + width // 2 : plane + width // 2 + 1, :]
            left.append(jnp.concatenate([cosine * real - sine * imag, cosine * imag + sine * real], axis=1))
        left = both_pieces(jnp.concatenate(left, axis=0))
        field = dot(left, plus_ref[...])
        weights = []
        for plane in range(i * batch, (i + 1) * batch):
            own = jnp.concatenate([potential_ref[plane], padding], axis=1)
            weights.append(jnp.concatenate([own, own], axis=1))
        left = (field * jnp.concatenate(weights, axis=0)).astype(BF16)
        half = dot_nt(left, plus_ref[: 2 * count, :])
        for j in range(batch):
            plane = i * batch + j
            real = half[j * length : (j + 1) * length, :count]
            imag = half[j * length : (j + 1) * length, count:]
            back[plane : plane + 1, :] = jnp.sum(cosine * real + sine * imag, axis=0, keepdims=True)
            at = plane + width // 2
            back[at : at + 1, :] = jnp.sum(cosine * imag - sine * real, axis=0, keepdims=True)
    for at in range(0, middle, LANES):
        size = min(LANES, middle - at)
        for side in range(2):
            turning[side * width : (side + 1) * width, :size] = back[:, side * middle + at : side * middle + at + size]
        gathered[at : at + LANES, :] = turning[...].T
    lanes = lane_ids(each)
    for device in range(devices):
        piece = gathered[device * each : (device + 1) * each, :]
        out_ref[device] = jnp.where((lanes >= 2 * width) & (lanes < carried), total, piece)


def finish_kernel(
    sizes, count_ref, columns_ref, atom_ref, couplings_ref, projectors_ref, table_ref, out_ref, summed, lined, mixed
):
    blocks, groups, orbitals, slots, length, projectors, width, normalizer = sizes
    kinds = orbitals * 2
    devices = blocks * groups
    share = projectors // devices
    each = slots // 2
    lanes = lane_ids(each)
    for chunk in range(projectors // LANES):
        in_chunk = range(chunk * LANES // share, (chunk + 1) * LANES // share)
        for rows in range(kinds // each):
            low = 2 * width + rows * share
            total = jnp.zeros((each, LANES), F32)
            for device in in_chunk:
                own = columns_ref[device]
                own = pltpu.roll(jnp.where((lanes >= low) & (lanes < low + share), own, 0.0), (device * share - low) % LANES, 1)
                total += own
            summed[rows * each : (rows + 1) * each, chunk * LANES : (chunk + 1) * LANES] = total
    for n in range(orbitals):
        at = kinds + n * 2
        summed[at : at + 1, :] = -summed[n * 2 + 1 : n * 2 + 2, :]
        summed[at + 1 : at + 2, :] = summed[n * 2 : n * 2 + 1, :]
    both = stacked(summed[...])
    atoms = atom_ref[...].astype(F32)
    eye = lax.broadcasted_iota(jnp.int32, (LANES, LANES), 0) == lane_ids(LANES)
    along = []
    for at in range(0, projectors, LANES):
        along.append(jnp.sum(jnp.where(eye, atoms[:, at : at + LANES], 0.0), axis=1, keepdims=True))
    head, rest = split(jnp.where(jnp.concatenate(along, axis=0) == atoms, couplings_ref[...], 0.0))
    head = dot_nt(both, head)
    rest = dot_nt(both, rest)
    weighted = (head[: 2 * kinds] + (head[2 * kinds :] + rest[: 2 * kinds])).astype(BF16)
    for slot in range(slots):
        rows = projectors_ref[slot * length : (slot + 1) * length, :]
        value = dot_nt(weighted, rows)[:kinds]
        rows = projectors_ref[(slots + slot) * length : (slots + slot + 1) * length, :]
        value = value + dot_nt(weighted, rows)[kinds:]
        for row in range(kinds):
            mixed[row, slot : slot + 1, :] = value[row : row + 1, :]
    for chunk in range(blocks * width // LANES):
        for group in range(groups):
            for side in range(2):
                low = side * width
                total = jnp.zeros((each, LANES), F32)
                for inner in range(LANES // width):
                    block = chunk * (LANES // width) + inner
                    own = columns_ref[block * groups + group]
                    own = jnp.where((lanes >= low) & (lanes < low + width), own, 0.0)
                    total += pltpu.roll(own, (inner * width - low) % LANES, 1)
                at = group * slots + side * each
                lined[at : at + each, chunk * LANES : (chunk + 1) * LANES] = total
    both = stacked(lined[...])
    rows_of_lines = groups * slots
    held = lax.broadcasted_iota(jnp.int32, (1, blocks), 1) == lax.axis_index("ga")
    used = jnp.sum(jnp.where(held, count_ref[...], 0).astype(F32), axis=1, keepdims=True)
    slot_ids = lax.broadcasted_iota(jnp.int32, (slots, 1), 0) + lax.axis_index("band") * slots
    used = slot_ids.astype(F32) < used
    for part in range(2):
        head = dot_nt(both, table_ref[0, part])
        rest = dot_nt(both, table_ref[1, part])
        local = (head[:rows_of_lines] + (head[rows_of_lines:] + rest[:rows_of_lines])) * normalizer
        for n in range(orbitals):
            value = local[n * slots : (n + 1) * slots, :] + mixed[n * 2 + part]
            out_ref[n, part] = jnp.where(used, value, 0.0)


def on_device(orbitals, projectors, potential, couplings, atom_index, column_site, column_count):
    blocks = lax.axis_size("ga")
    groups = lax.axis_size("band")
    devices = blocks * groups
    orbital_count, _, slots, length = orbitals.shape
    planes = potential.shape[0]
    projector_count = projectors.shape[0]
    columns = column_site.shape[0]
    kinds = orbital_count * 2
    assert orbital_count == groups and slots % 2 == 0 and kinds % (slots // 2) == 0 and columns % LANES == 0
    share = projector_count // devices
    width = 2
    while width < 2 * planes:
        width *= 2
    carried = 2 * width + kinds // (slots // 2) * share
    assert carried <= LANES and width <= LANES and share * devices == projector_count
    wide = -(-length // LANES) * LANES
    flat = jnp.transpose(projectors, (1, 2, 3, 0)).reshape(2 * slots * length, projector_count)
    z_table = line_table(length, blocks, planes, width)
    batch = next(i for i in (2, 3, 1) if planes % i == 0) if columns <= 512 else 1
    vmem = pl.BlockSpec(memory_space=pltpu.VMEM)
    hbm = pl.BlockSpec(memory_space=pltpu.HBM)
    params = pltpu.CompilerParams(vmem_limit_bytes=56 * 1024 * 1024)
    small = pltpu.CompilerParams(vmem_limit_bytes=40 * 1024 * 1024)
    payload = jax.ShapeDtypeStruct((devices, slots // 2, LANES), F32)

    sent = pl.pallas_call(
        functools.partial(
            project_kernel,
                (blocks, groups, orbital_count, slots, length, projector_count, planes, width),
        ),
        out_shape=payload,
        in_specs=[hbm] * 3,
        out_specs=vmem,
        scratch_shapes=[
            pltpu.SMEM(column_count.shape, jnp.int32),
            pltpu.VMEM(orbitals.shape, BF16),
            pltpu.VMEM(flat.shape, BF16),
            pltpu.VMEM((2 * slots, -(-kinds // 8) * 8, length), F32),
            pltpu.VMEM((kinds * slots, length), F32),
            pltpu.SemaphoreType.DMA((2,)),
            pltpu.SemaphoreType.DMA((2 * slots,)),
        ],
        compiler_params=params,
        cost_estimate=pl.CostEstimate(
            flops=2 * flat.size * LANES * slots,
            bytes_accessed=2 * (flat.size + z_table.size + orbitals.size) + 4 * payload.size,
            transcendentals=length * blocks * width,
        ),
        name="project",
    )(column_count, orbitals, flat)
    arrived = lax.all_to_all(sent, ("ga", "band"), split_axis=0, concat_axis=0, tiled=True)

    x_rows, plus = pl.pallas_call(
        functools.partial(table_kernel, length, wide, slots),
        out_shape=(
            jax.ShapeDtypeStruct((length, 2 * columns), F32),
            jax.ShapeDtypeStruct((4 * columns, 2 * wide), BF16),
        ),
        in_specs=[vmem],
        out_specs=(vmem,) * 2,
        compiler_params=small,
        cost_estimate=pl.CostEstimate(
            flops=4096 * potential.size,
            bytes_accessed=8 * (length + 2 * wide) * columns,
            transcendentals=2 * (length + wide) * columns,
        ),
        name="tables",
    )(column_site.reshape(1, columns))

    sent = pl.pallas_call(
        functools.partial(plane_kernel, (devices, slots, planes, length, wide, width, carried, batch)),
        out_shape=payload,
        in_specs=[vmem] * 4,
        out_specs=vmem,
        scratch_shapes=[
            pltpu.VMEM((-(-columns // (2 * LANES)) * LANES, LANES), F32),
            pltpu.VMEM((width, columns), F32),
            pltpu.VMEM((width, columns), F32),
            pltpu.VMEM((LANES, LANES), F32),
        ],
        compiler_params=small,
        cost_estimate=pl.CostEstimate(
            flops=12 * planes * length * wide * 2 * columns,
            bytes_accessed=4 * (potential.size + 2 * payload.size),
            transcendentals=0,
        ),
        name="planes",
    )(arrived, x_rows, plus, potential)
    arrived = lax.all_to_all(sent, ("ga", "band"), split_axis=0, concat_axis=0, tiled=True)

    normalizer = 1.0 / float(length**3)
    return pl.pallas_call(
        functools.partial(
            finish_kernel,
            (blocks, groups, orbital_count, slots, length, projector_count, width, normalizer),
        ),
        out_shape=jax.ShapeDtypeStruct(orbitals.shape, F32),
        in_specs=[vmem] * 6,
        out_specs=vmem,
        scratch_shapes=[
            pltpu.VMEM((2 * kinds, projector_count), F32),
            pltpu.VMEM((groups * slots, blocks * width), F32),
            pltpu.VMEM((kinds, slots, length), F32),
        ],
        compiler_params=small,
        cost_estimate=pl.CostEstimate(
            flops=4 * kinds * (4 * couplings.size + flat.size) + 4 * z_table.size * orbital_count * slots,
            bytes_accessed=4 * couplings.size + 2 * (flat.size + z_table.size) + 4 * orbitals.size,
            transcendentals=0,
        ),
        name="finish",
    )(column_count.reshape(1, blocks), arrived, atom_index.reshape(1, projector_count), couplings, flat, z_table)


def solution(mesh):
    return jax.shard_map(
        on_device,
        mesh=mesh,
        in_specs=(
            P(None, None, ("ga", "band"), None),
            P(None, None, ("ga", "band"), None),
            P("ga", None, None),
            P(),
            P(),
            P(),
            P(),
        ),
        out_specs=P(None, None, ("ga", "band"), None),
        check_vma=False,
    )
```

```python
import functools

import jax
import jax.numpy as jnp
import ml_dtypes
import numpy as np
from jax import lax
from jax.experimental import pallas as pl
from jax.experimental.pallas import tpu as pltpu
from jax.sharding import PartitionSpec as P

LANES = 128
BF16 = jnp.bfloat16
F32 = jnp.float32


def pieces_of(table):
    table = np.asarray(table, np.float32)
    head = table.astype(ml_dtypes.bfloat16)
    return np.stack([head, (table - head.astype(np.float32)).astype(ml_dtypes.bfloat16)])


def line_table(length, blocks, planes, width):
    kz = np.arange(length)
    out = np.zeros((2, length, blocks, width), np.float64)
    for block in range(blocks):
        z = block * planes + np.arange(planes)
        phases = (kz[:, None] * z[None, :] % length) * (2.0 * np.pi / length)
        out[0, :, block, :planes] = np.cos(phases)
        out[0, :, block, width // 2 : width // 2 + planes] = np.sin(phases)
        out[1, :, block, :planes] = -np.sin(phases)
        out[1, :, block, width // 2 : width // 2 + planes] = np.cos(phases)
    return pieces_of(out.reshape(2, length, blocks * width))


def split(values):
    head = values.astype(BF16)
    return head, (values - head.astype(F32)).astype(BF16)


def stacked(values):
    head, rest = split(values)
    return jnp.concatenate([head.astype(F32), rest.astype(F32)], axis=0).astype(BF16)


def both_pieces(values):
    return jnp.concatenate(split(values), axis=1)


def dot(left, right):
    return lax.dot_general(left, right, (((1,), (0,)), ((), ())), preferred_element_type=F32)


def dot_nt(left, right):
    return lax.dot_general(left, right, (((1,), (1,)), ((), ())), preferred_element_type=F32)


def lane_ids(rows):
    return lax.broadcasted_iota(jnp.int32, (rows, LANES), 1)


def used_slots(count_ref, slots):
    used = count_ref[lax.axis_index("ga")] - lax.axis_index("band") * slots
    return lax.broadcasted_iota(jnp.int32, (slots, 1), 0) < used


def cosine_and_sine(phases, length):
    quarter = jnp.floor(phases * (4.0 / length) + 0.5)
    angle = (phases - quarter * (length / 4.0)) * (2.0 * np.pi / length)
    square = angle * angle
    sine = 1.0 / 362880.0
    for term in (-1.0 / 5040.0, 1.0 / 120.0, -1.0 / 6.0, 1.0):
        sine = sine * square + term
    sine = sine * angle
    cosine = -1.0 / 3628800.0
    for term in (1.0 / 40320.0, -1.0 / 720.0, 1.0 / 24.0, -0.5, 1.0):
        cosine = cosine * square + term
    quarter = quarter - 4.0 * jnp.floor(quarter * 0.25)
    odd = (quarter == 1.0) | (quarter == 3.0)
    first = jnp.where(odd, sine, cosine)
    second = jnp.where(odd, cosine, sine)
    first = jnp.where((quarter == 1.0) | (quarter == 2.0), -first, first)
    return first, jnp.where(quarter >= 2.0, -second, second)


def project_kernel(sizes, count_hbm, orbitals_hbm, projectors_hbm, out_ref, *scratch):
    blocks, groups, orbitals, slots, length, projectors, planes, width = sizes
    count_ref, orbitals_ref, projectors_ref, coef, lines, small_sems, sems = scratch
    kinds = orbitals * 2
    devices = blocks * groups
    share = projectors // devices
    small = [
        pltpu.make_async_copy(count_hbm, count_ref, small_sems.at[0]),
        pltpu.make_async_copy(orbitals_hbm, orbitals_ref, small_sems.at[1]),
    ]
    copies = []
    for piece in range(2 * slots):
        rows = pl.ds(piece * length, length)
        copies.append(pltpu.make_async_copy(projectors_hbm.at[rows], projectors_ref.at[rows], sems.at[piece]))
    for copy in small + copies:
        copy.start()
    half = width // 2
    lanes = lax.broadcasted_iota(jnp.int32, (length, blocks * half), 1)
    plane = (lanes >> (half.bit_length() - 1)) * planes + (lanes & (half - 1))
    kz = lax.broadcasted_iota(jnp.int32, (length, blocks * half), 0)
    table = split(jnp.concatenate(cosine_and_sine(kz.astype(F32) * plane.astype(F32), length), axis=1))
    coef[...] = jnp.zeros_like(coef)
    small[0].wait()
    small[1].wait()
    used = used_slots(count_ref, slots)
    for n in range(orbitals):
        for part in range(2):
            values = jnp.where(used, orbitals_ref[n, part].astype(F32), 0.0)
            at = (part * orbitals + n) * slots
            lines[at : at + slots, :] = values
            turned = values if part == 1 else -values
            for slot in range(slots):
                row = n * 2 + part
                coef[slot, row : row + 1, :] = values[slot : slot + 1, :]
                row = n * 2 + 1 - part
                coef[slots + slot, row : row + 1, :] = turned[slot : slot + 1, :]
    left = lines[...].astype(BF16)
    both = dot(left, table[0]) + dot(left, table[1])
    rows = orbitals * slots
    points = blocks * half
    real = both[:rows, :points] - both[rows:, points:]
    imag = both[:rows, points:] + both[rows:, :points]
    lanes = lane_ids(rows)
    rows_each = slots // 2
    piece_lanes = lane_ids(rows_each)
    for block in range(blocks):
        at = block * half
        base = at // LANES * LANES
        chunk = pltpu.roll(imag[:, base : base + LANES], (base - at + half) % LANES, 1)
        chunk = jnp.where(lanes < half, pltpu.roll(real[:, base : base + LANES], (base - at) % LANES, 1), chunk)
        aside = pltpu.roll(chunk, width, 1)
        for group in range(groups):
            at = group * slots
            piece = jnp.where(piece_lanes < width, chunk[at : at + rows_each, :], aside[at + rows_each : at + slots, :])
            out_ref[block * groups + group] = piece
    sums = jnp.zeros((coef.shape[1], projectors), F32)
    for piece in range(2 * slots):
        left = coef[piece].astype(BF16)
        copies[piece].wait()
        sums += dot(left, projectors_ref[piece * length : (piece + 1) * length, :])
    for device in range(devices):
        piece = jnp.where(piece_lanes < 2 * width, out_ref[device], 0.0)
        first = device * share
        base = first // LANES * LANES
        for group in range(kinds // rows_each):
            low = 2 * width + group * share
            own = sums[group * rows_each : (group + 1) * rows_each, base : base + LANES]
            own = pltpu.roll(own, (base + low - first) % LANES, 1)
            piece = jnp.where((piece_lanes >= low) & (piece_lanes < low + share), own, piece)
        out_ref[device] = piece


def table_kernel(length, wide, slots, site_ref, x_ref, plus_ref):
    columns = site_ref.shape[1]
    each = slots // 2
    eye = lax.broadcasted_iota(jnp.int32, (LANES, LANES), 0) == lane_ids(LANES)
    row_ids = lax.broadcasted_iota(jnp.int32, (length, LANES), 0).astype(F32)
    lanes = lax.broadcasted_iota(jnp.int32, (LANES, wide), 1)
    inside = lanes < length
    lanes = lanes.astype(F32)
    sites = site_ref[...].astype(F32)
    stored = lax.broadcasted_iota(jnp.int32, (LANES, columns), 1)
    for at in range(0, columns, LANES):
        order = lax.broadcasted_iota(jnp.int32, (LANES, columns), 0) + at
        second = order >= columns // 2
        order = jnp.where(second, order - columns // 2, order)
        wanted = (order >> (each.bit_length() - 1)) * slots + (order & (each - 1)) + jnp.where(second, each, 0)
        along = jnp.sum(jnp.where(stored == wanted, sites, 0.0), axis=1, keepdims=True)
        site = jnp.sum(jnp.where(eye, along, 0.0), axis=0, keepdims=True)
        site_x = jnp.floor((site + 0.5) * (1.0 / length))
        along = along - jnp.floor((along + 0.5) * (1.0 / length)) * length
        cosine, sine = cosine_and_sine(row_ids * site_x, length)
        x_ref[:, at : at + LANES] = cosine
        x_ref[:, columns + at : columns + at + LANES] = sine
        cosine, sine = cosine_and_sine(lanes * along, length)
        cosine = jnp.where(inside, cosine, 0.0)
        sine = jnp.where(inside, sine, 0.0)
        cosine = cosine.astype(BF16)
        sine = sine.astype(BF16)
        for piece in range(2):
            rows = pl.ds(piece * 2 * columns + at, LANES)
            plus_ref[rows, :wide] = cosine
            plus_ref[rows, wide:] = sine
            rows = pl.ds((piece * 2 + 1) * columns + at, LANES)
            plus_ref[rows, :wide] = -sine
            plus_ref[rows, wide:] = cosine


def plane_kernel(sizes, columns_ref, x_ref, plus_ref, potential_ref, out_ref, gathered, lines, back, turning):
    devices, slots, planes, length, wide, width, carried, batch = sizes
    count = devices * slots
    each = slots // 2
    middle = count // 2
    total = jnp.zeros((each, LANES), F32)
    for device in range(devices):
        piece = columns_ref[device]
        gathered[device * each : (device + 1) * each, :] = piece
        total += piece
    for at in range(0, middle, LANES):
        size = min(LANES, middle - at)
        turned = gathered[at : at + LANES, :].T
        for side in range(2):
            lines[:, side * middle + at : side * middle + at + size] = turned[side * width : (side + 1) * width, :size]
    back[...] = jnp.zeros_like(back)
    cosine = x_ref[:, :count]
    sine = x_ref[:, count:]
    padding = jnp.zeros((length, wide - length), F32)
    for i in range(planes // batch):
        left = []
        for plane in range(i * batch, (i + 1) * batch):
            real = lines[plane : plane + 1, :]
            imag = lines[plane + width // 2 : plane + width // 2 + 1, :]
            left.append(jnp.concatenate([cosine * real - sine * imag, cosine * imag + sine * real], axis=1))
        left = both_pieces(jnp.concatenate(left, axis=0))
        field = dot(left, plus_ref[...])
        weights = []
        for plane in range(i * batch, (i + 1) * batch):
            own = jnp.concatenate([potential_ref[plane], padding], axis=1)
            weights.append(jnp.concatenate([own, own], axis=1))
        left = (field * jnp.concatenate(weights, axis=0)).astype(BF16)
        half = dot_nt(left, plus_ref[: 2 * count, :])
        for j in range(batch):
            plane = i * batch + j
            real = half[j * length : (j + 1) * length, :count]
            imag = half[j * length : (j + 1) * length, count:]
            back[plane : plane + 1, :] = jnp.sum(cosine * real + sine * imag, axis=0, keepdims=True)
            at = plane + width // 2
            back[at : at + 1, :] = jnp.sum(cosine * imag - sine * real, axis=0, keepdims=True)
    for at in range(0, middle, LANES):
        size = min(LANES, middle - at)
        for side in range(2):
            turning[side * width : (side + 1) * width, :size] = back[:, side * middle + at : side * middle + at + size]
        gathered[at : at + LANES, :] = turning[...].T
    lanes = lane_ids(each)
    for device in range(devices):
        piece = gathered[device * each : (device + 1) * each, :]
        out_ref[device] = jnp.where((lanes >= 2 * width) & (lanes < carried), total, piece)


def finish_kernel(
    sizes, count_ref, columns_ref, atom_ref, couplings_ref, projectors_ref, table_ref, out_ref, summed, lined, mixed
):
    blocks, groups, orbitals, slots, length, projectors, width, normalizer = sizes
    kinds = orbitals * 2
    devices = blocks * groups
    share = projectors // devices
    each = slots // 2
    lanes = lane_ids(each)
    for chunk in range(projectors // LANES):
        in_chunk = range(chunk * LANES // share, (chunk + 1) * LANES // share)
        for rows in range(kinds // each):
            low = 2 * width + rows * share
            total = jnp.zeros((each, LANES), F32)
            for device in in_chunk:
                own = columns_ref[device]
                own = pltpu.roll(jnp.where((lanes >= low) & (lanes < low + share), own, 0.0), (device * share - low) % LANES, 1)
                total += own
            summed[rows * each : (rows + 1) * each, chunk * LANES : (chunk + 1) * LANES] = total
    for n in range(orbitals):
        at = kinds + n * 2
        summed[at : at + 1, :] = -summed[n * 2 + 1 : n * 2 + 2, :]
        summed[at + 1 : at + 2, :] = summed[n * 2 : n * 2 + 1, :]
    both = stacked(summed[...])
    atoms = atom_ref[...].astype(F32)
    eye = lax.broadcasted_iota(jnp.int32, (LANES, LANES), 0) == lane_ids(LANES)
    along = []
    for at in range(0, projectors, LANES):
        along.append(jnp.sum(jnp.where(eye, atoms[:, at : at + LANES], 0.0), axis=1, keepdims=True))
    head, rest = split(jnp.where(jnp.concatenate(along, axis=0) == atoms, couplings_ref[...], 0.0))
    head = dot_nt(both, head)
    rest = dot_nt(both, rest)
    weighted = (head[: 2 * kinds] + (head[2 * kinds :] + rest[: 2 * kinds])).astype(BF16)
    for slot in range(slots):
        rows = projectors_ref[slot * length : (slot + 1) * length, :]
        value = dot_nt(weighted, rows)[:kinds]
        rows = projectors_ref[(slots + slot) * length : (slots + slot + 1) * length, :]
        value = value + dot_nt(weighted, rows)[kinds:]
        for row in range(kinds):
            mixed[row, slot : slot + 1, :] = value[row : row + 1, :]
    for chunk in range(blocks * width // LANES):
        for group in range(groups):
            for side in range(2):
                low = side * width
                total = jnp.zeros((each, LANES), F32)
                for inner in range(LANES // width):
                    block = chunk * (LANES // width) + inner
                    own = columns_ref[block * groups + group]
                    own = jnp.where((lanes >= low) & (lanes < low + width), own, 0.0)
                    total += pltpu.roll(own, (inner * width - low) % LANES, 1)
                at = group * slots + side * each
                lined[at : at + each, chunk * LANES : (chunk + 1) * LANES] = total
    both = stacked(lined[...])
    rows_of_lines = groups * slots
    held = lax.broadcasted_iota(jnp.int32, (1, blocks), 1) == lax.axis_index("ga")
    used = jnp.sum(jnp.where(held, count_ref[...], 0).astype(F32), axis=1, keepdims=True)
    slot_ids = lax.broadcasted_iota(jnp.int32, (slots, 1), 0) + lax.axis_index("band") * slots
    used = slot_ids.astype(F32) < used
    for part in range(2):
        head = dot_nt(both, table_ref[0, part])
        rest = dot_nt(both, table_ref[1, part])
        local = (head[:rows_of_lines] + (head[rows_of_lines:] + rest[:rows_of_lines])) * normalizer
        for n in range(orbitals):
            value = local[n * slots : (n + 1) * slots, :] + mixed[n * 2 + part]
            out_ref[n, part] = jnp.where(used, value, 0.0)


def on_device(orbitals, projectors, potential, couplings, atom_index, column_site, column_count):
    blocks = lax.axis_size("ga")
    groups = lax.axis_size("band")
    devices = blocks * groups
    orbital_count, _, slots, length = orbitals.shape
    planes = potential.shape[0]
    projector_count = projectors.shape[0]
    columns = column_site.shape[0]
    kinds = orbital_count * 2
    assert orbital_count == groups and slots % 2 == 0 and kinds % (slots // 2) == 0 and columns % LANES == 0
    share = projector_count // devices
    width = 2
    while width < 2 * planes:
        width *= 2
    carried = 2 * width + kinds // (slots // 2) * share
    assert carried <= LANES and width <= LANES and share * devices == projector_count
    wide = -(-length // LANES) * LANES
    flat = jnp.transpose(projectors, (1, 2, 3, 0)).reshape(2 * slots * length, projector_count)
    z_table = line_table(length, blocks, planes, width)
    batch = next(i for i in (1,) if planes % i == 0) if columns <= 512 else 1
    vmem = pl.BlockSpec(memory_space=pltpu.VMEM)
    hbm = pl.BlockSpec(memory_space=pltpu.HBM)
    params = pltpu.CompilerParams(vmem_limit_bytes=56 * 1024 * 1024)
    small = pltpu.CompilerParams(vmem_limit_bytes=40 * 1024 * 1024)
    payload = jax.ShapeDtypeStruct((devices, slots // 2, LANES), F32)

    sent = pl.pallas_call(
        functools.partial(
            project_kernel,
                (blocks, groups, orbital_count, slots, length, projector_count, planes, width),
        ),
        out_shape=payload,
        in_specs=[hbm] * 3,
        out_specs=vmem,
        scratch_shapes=[
            pltpu.SMEM(column_count.shape, jnp.int32),
            pltpu.VMEM(orbitals.shape, BF16),
            pltpu.VMEM(flat.shape, BF16),
            pltpu.VMEM((2 * slots, -(-kinds // 8) * 8, length), F32),
            pltpu.VMEM((kinds * slots, length), F32),
            pltpu.SemaphoreType.DMA((2,)),
            pltpu.SemaphoreType.DMA((2 * slots,)),
        ],
        compiler_params=params,
        cost_estimate=pl.CostEstimate(
            flops=2 * flat.size * LANES * slots,
            bytes_accessed=2 * (flat.size + z_table.size + orbitals.size) + 4 * payload.size,
            transcendentals=length * blocks * width,
        ),
        name="project",
    )(column_count, orbitals, flat)
    arrived = lax.all_to_all(sent, ("ga", "band"), split_axis=0, concat_axis=0, tiled=True)

    x_rows, plus = pl.pallas_call(
        functools.partial(table_kernel, length, wide, slots),
        out_shape=(
            jax.ShapeDtypeStruct((length, 2 * columns), F32),
            jax.ShapeDtypeStruct((4 * columns, 2 * wide), BF16),
        ),
        in_specs=[vmem],
        out_specs=(vmem,) * 2,
        compiler_params=small,
        cost_estimate=pl.CostEstimate(
            flops=4096 * potential.size,
            bytes_accessed=8 * (length + 2 * wide) * columns,
            transcendentals=2 * (length + wide) * columns,
        ),
        name="tables",
    )(column_site.reshape(1, columns))

    sent = pl.pallas_call(
        functools.partial(plane_kernel, (devices, slots, planes, length, wide, width, carried, batch)),
        out_shape=payload,
        in_specs=[vmem] * 4,
        out_specs=vmem,
        scratch_shapes=[
            pltpu.VMEM((-(-columns // (2 * LANES)) * LANES, LANES), F32),
            pltpu.VMEM((width, columns), F32),
            pltpu.VMEM((width, columns), F32),
            pltpu.VMEM((LANES, LANES), F32),
        ],
        compiler_params=small,
        cost_estimate=pl.CostEstimate(
            flops=12 * planes * length * wide * 2 * columns,
            bytes_accessed=4 * (potential.size + 2 * payload.size),
            transcendentals=0,
        ),
        name="planes",
    )(arrived, x_rows, plus, potential)
    arrived = lax.all_to_all(sent, ("ga", "band"), split_axis=0, concat_axis=0, tiled=True)

    normalizer = 1.0 / float(length**3)
    return pl.pallas_call(
        functools.partial(
            finish_kernel,
            (blocks, groups, orbital_count, slots, length, projector_count, width, normalizer),
        ),
        out_shape=jax.ShapeDtypeStruct(orbitals.shape, F32),
        in_specs=[vmem] * 6,
        out_specs=vmem,
        scratch_shapes=[
            pltpu.VMEM((2 * kinds, projector_count), F32),
            pltpu.VMEM((groups * slots, blocks * width), F32),
            pltpu.VMEM((kinds, slots, length), F32),
        ],
        compiler_params=small,
        cost_estimate=pl.CostEstimate(
            flops=4 * kinds * (4 * couplings.size + flat.size) + 4 * z_table.size * orbital_count * slots,
            bytes_accessed=4 * couplings.size + 2 * (flat.size + z_table.size) + 4 * orbitals.size,
            transcendentals=0,
        ),
        name="finish",
    )(column_count.reshape(1, blocks), arrived, atom_index.reshape(1, projector_count), couplings, flat, z_table)


def solution(mesh):
    return jax.shard_map(
        on_device,
        mesh=mesh,
        in_specs=(
            P(None, None, ("ga", "band"), None),
            P(None, None, ("ga", "band"), None),
            P("ga", None, None),
            P(),
            P(),
            P(),
            P(),
        ),
        out_specs=P(None, None, ("ga", "band"), None),
        check_vma=False,
    )
```

```python
import functools

import jax
import jax.numpy as jnp
import ml_dtypes
import numpy as np
from jax import lax
from jax.experimental import pallas as pl
from jax.experimental.pallas import tpu as pltpu
from jax.sharding import PartitionSpec as P

LANES = 128
BF16 = jnp.bfloat16
F32 = jnp.float32


def pieces_of(table):
    table = np.asarray(table, np.float32)
    head = table.astype(ml_dtypes.bfloat16)
    return np.stack([head, (table - head.astype(np.float32)).astype(ml_dtypes.bfloat16)])


def line_table(length, blocks, planes, width):
    kz = np.arange(length)
    out = np.zeros((2, length, blocks, width), np.float64)
    for block in range(blocks):
        z = block * planes + np.arange(planes)
        phases = (kz[:, None] * z[None, :] % length) * (2.0 * np.pi / length)
        out[0, :, block, :planes] = np.cos(phases)
        out[0, :, block, width // 2 : width // 2 + planes] = np.sin(phases)
        out[1, :, block, :planes] = -np.sin(phases)
        out[1, :, block, width // 2 : width // 2 + planes] = np.cos(phases)
    return pieces_of(out.reshape(2, length, blocks * width))


def split(values):
    head = values.astype(BF16)
    return head, (values - head.astype(F32)).astype(BF16)


def stacked(values):
    head, rest = split(values)
    return jnp.concatenate([head.astype(F32), rest.astype(F32)], axis=0).astype(BF16)


def both_pieces(values):
    return jnp.concatenate(split(values), axis=1)


def dot(left, right):
    return lax.dot_general(left, right, (((1,), (0,)), ((), ())), preferred_element_type=F32)


def dot_nt(left, right):
    return lax.dot_general(left, right, (((1,), (1,)), ((), ())), preferred_element_type=F32)


def lane_ids(rows):
    return lax.broadcasted_iota(jnp.int32, (rows, LANES), 1)


def used_slots(count_ref, slots):
    used = count_ref[lax.axis_index("ga")] - lax.axis_index("band") * slots
    return lax.broadcasted_iota(jnp.int32, (slots, 1), 0) < used


def cosine_and_sine(phases, length):
    quarter = jnp.floor(phases * (4.0 / length) + 0.5)
    angle = (phases - quarter * (length / 4.0)) * (2.0 * np.pi / length)
    square = angle * angle
    sine = 1.0 / 362880.0
    for term in (-1.0 / 5040.0, 1.0 / 120.0, -1.0 / 6.0, 1.0):
        sine = sine * square + term
    sine = sine * angle
    cosine = -1.0 / 3628800.0
    for term in (1.0 / 40320.0, -1.0 / 720.0, 1.0 / 24.0, -0.5, 1.0):
        cosine = cosine * square + term
    quarter = quarter - 4.0 * jnp.floor(quarter * 0.25)
    odd = (quarter == 1.0) | (quarter == 3.0)
    first = jnp.where(odd, sine, cosine)
    second = jnp.where(odd, cosine, sine)
    first = jnp.where((quarter == 1.0) | (quarter == 2.0), -first, first)
    return first, jnp.where(quarter >= 2.0, -second, second)


def project_kernel(sizes, count_hbm, orbitals_hbm, projectors_hbm, out_ref, *scratch):
    blocks, groups, orbitals, slots, length, projectors, planes, width = sizes
    count_ref, orbitals_ref, projectors_ref, coef, lines, small_sems, sems = scratch
    kinds = orbitals * 2
    devices = blocks * groups
    share = projectors // devices
    small = [
        pltpu.make_async_copy(count_hbm, count_ref, small_sems.at[0]),
        pltpu.make_async_copy(orbitals_hbm, orbitals_ref, small_sems.at[1]),
    ]
    copies = []
    for piece in range(2 * slots):
        rows = pl.ds(piece * length, length)
        copies.append(pltpu.make_async_copy(projectors_hbm.at[rows], projectors_ref.at[rows], sems.at[piece]))
    for copy in small + copies:
        copy.start()
    half = width // 2
    lanes = lax.broadcasted_iota(jnp.int32, (length, blocks * half), 1)
    plane = (lanes >> (half.bit_length() - 1)) * planes + (lanes & (half - 1))
    kz = lax.broadcasted_iota(jnp.int32, (length, blocks * half), 0)
    table = split(jnp.concatenate(cosine_and_sine(kz.astype(F32) * plane.astype(F32), length), axis=1))
    coef[...] = jnp.zeros_like(coef)
    small[0].wait()
    small[1].wait()
    used = used_slots(count_ref, slots)
    for n in range(orbitals):
        for part in range(2):
            values = jnp.where(used, orbitals_ref[n, part].astype(F32), 0.0)
            at = (part * orbitals + n) * slots
            lines[at : at + slots, :] = values
            turned = values if part == 1 else -values
            for slot in range(slots):
                row = n * 2 + part
                coef[slot, row : row + 1, :] = values[slot : slot + 1, :]
                row = n * 2 + 1 - part
                coef[slots + slot, row : row + 1, :] = turned[slot : slot + 1, :]
    left = lines[...].astype(BF16)
    both = dot(left, table[0]) + dot(left, table[1])
    rows = orbitals * slots
    points = blocks * half
    real = both[:rows, :points] - both[rows:, points:]
    imag = both[:rows, points:] + both[rows:, :points]
    lanes = lane_ids(rows)
    rows_each = slots // 2
    piece_lanes = lane_ids(rows_each)
    for block in range(blocks):
        at = block * half
        base = at // LANES * LANES
        chunk = pltpu.roll(imag[:, base : base + LANES], (base - at + half) % LANES, 1)
        chunk = jnp.where(lanes < half, pltpu.roll(real[:, base : base + LANES], (base - at) % LANES, 1), chunk)
        aside = pltpu.roll(chunk, width, 1)
        for group in range(groups):
            at = group * slots
            piece = jnp.where(piece_lanes < width, chunk[at : at + rows_each, :], aside[at + rows_each : at + slots, :])
            out_ref[block * groups + group] = piece
    sums = jnp.zeros((coef.shape[1], projectors), F32)
    for piece in range(2 * slots):
        left = coef[piece].astype(BF16)
        copies[piece].wait()
        sums += dot(left, projectors_ref[piece * length : (piece + 1) * length, :])
    for device in range(devices):
        piece = jnp.where(piece_lanes < 2 * width, out_ref[device], 0.0)
        first = device * share
        base = first // LANES * LANES
        for group in range(kinds // rows_each):
            low = 2 * width + group * share
            own = sums[group * rows_each : (group + 1) * rows_each, base : base + LANES]
            own = pltpu.roll(own, (base + low - first) % LANES, 1)
            piece = jnp.where((piece_lanes >= low) & (piece_lanes < low + share), own, piece)
        out_ref[device] = piece


def table_kernel(length, wide, slots, site_ref, x_ref, plus_ref):
    columns = site_ref.shape[1]
    each = slots // 2
    eye = lax.broadcasted_iota(jnp.int32, (LANES, LANES), 0) == lane_ids(LANES)
    row_ids = lax.broadcasted_iota(jnp.int32, (length, LANES), 0).astype(F32)
    lanes = lax.broadcasted_iota(jnp.int32, (LANES, wide), 1)
    inside = lanes < length
    lanes = lanes.astype(F32)
    sites = site_ref[...].astype(F32)
    stored = lax.broadcasted_iota(jnp.int32, (LANES, columns), 1)
    for at in range(0, columns, LANES):
        order = lax.broadcasted_iota(jnp.int32, (LANES, columns), 0) + at
        second = order >= columns // 2
        order = jnp.where(second, order - columns // 2, order)
        wanted = (order >> (each.bit_length() - 1)) * slots + (order & (each - 1)) + jnp.where(second, each, 0)
        along = jnp.sum(jnp.where(stored == wanted, sites, 0.0), axis=1, keepdims=True)
        site = jnp.sum(jnp.where(eye, along, 0.0), axis=0, keepdims=True)
        site_x = jnp.floor((site + 0.5) * (1.0 / length))
        along = along - jnp.floor((along + 0.5) * (1.0 / length)) * length
        cosine, sine = cosine_and_sine(row_ids * site_x, length)
        x_ref[:, at : at + LANES] = cosine
        x_ref[:, columns + at : columns + at + LANES] = sine
        cosine, sine = cosine_and_sine(lanes * along, length)
        cosine = jnp.where(inside, cosine, 0.0)
        sine = jnp.where(inside, sine, 0.0)
        cosine = cosine.astype(BF16)
        sine = sine.astype(BF16)
        for piece in range(2):
            rows = pl.ds(piece * 2 * columns + at, LANES)
            plus_ref[rows, :wide] = cosine
            plus_ref[rows, wide:] = sine
            rows = pl.ds((piece * 2 + 1) * columns + at, LANES)
            plus_ref[rows, :wide] = -sine
            plus_ref[rows, wide:] = cosine


def plane_kernel(sizes, columns_ref, x_ref, plus_ref, potential_ref, out_ref, gathered, lines, back, turning):
    devices, slots, planes, length, wide, width, carried, batch = sizes
    count = devices * slots
    each = slots // 2
    middle = count // 2
    total = jnp.zeros((each, LANES), F32)
    for device in range(devices):
        piece = columns_ref[device]
        gathered[device * each : (device + 1) * each, :] = piece
        total += piece
    for at in range(0, middle, LANES):
        size = min(LANES, middle - at)
        turned = gathered[at : at + LANES, :].T
        for side in range(2):
            lines[:, side * middle + at : side * middle + at + size] = turned[side * width : (side + 1) * width, :size]
    back[...] = jnp.zeros_like(back)
    cosine = x_ref[:, :count]
    sine = x_ref[:, count:]
    padding = jnp.zeros((length, wide - length), F32)
    for i in range(planes // batch):
        left = []
        for plane in range(i * batch, (i + 1) * batch):
            real = lines[plane : plane + 1, :]
            imag = lines[plane + width // 2 : plane + width // 2 + 1, :]
            left.append(jnp.concatenate([cosine * real - sine * imag, cosine * imag + sine * real], axis=1))
        left = both_pieces(jnp.concatenate(left, axis=0))
        field = dot(left, plus_ref[...])
        weights = []
        for plane in range(i * batch, (i + 1) * batch):
            own = jnp.concatenate([potential_ref[plane], padding], axis=1)
            weights.append(jnp.concatenate([own, own], axis=1))
        left = (field * jnp.concatenate(weights, axis=0)).astype(BF16)
        half = dot_nt(left, plus_ref[: 2 * count, :])
        for j in range(batch):
            plane = i * batch + j
            real = half[j * length : (j + 1) * length, :count]
            imag = half[j * length : (j + 1) * length, count:]
            back[plane : plane + 1, :] = jnp.sum(cosine * real + sine * imag, axis=0, keepdims=True)
            at = plane + width // 2
            back[at : at + 1, :] = jnp.sum(cosine * imag - sine * real, axis=0, keepdims=True)
    for at in range(0, middle, LANES):
        size = min(LANES, middle - at)
        for side in range(2):
            turning[side * width : (side + 1) * width, :size] = back[:, side * middle + at : side * middle + at + size]
        gathered[at : at + LANES, :] = turning[...].T
    lanes = lane_ids(each)
    for device in range(devices):
        piece = gathered[device * each : (device + 1) * each, :]
        out_ref[device] = jnp.where((lanes >= 2 * width) & (lanes < carried), total, piece)


def finish_kernel(
    sizes, count_ref, columns_ref, atom_ref, couplings_ref, projectors_ref, table_ref, out_ref, summed, lined, mixed
):
    blocks, groups, orbitals, slots, length, projectors, width, normalizer = sizes
    kinds = orbitals * 2
    devices = blocks * groups
    share = projectors // devices
    each = slots // 2
    lanes = lane_ids(each)
    for chunk in range(projectors // LANES):
        in_chunk = range(chunk * LANES // share, (chunk + 1) * LANES // share)
        for rows in range(kinds // each):
            low = 2 * width + rows * share
            total = jnp.zeros((each, LANES), F32)
            for device in in_chunk:
                own = columns_ref[device]
                own = pltpu.roll(jnp.where((lanes >= low) & (lanes < low + share), own, 0.0), (device * share - low) % LANES, 1)
                total += own
            summed[rows * each : (rows + 1) * each, chunk * LANES : (chunk + 1) * LANES] = total
    for n in range(orbitals):
        at = kinds + n * 2
        summed[at : at + 1, :] = -summed[n * 2 + 1 : n * 2 + 2, :]
        summed[at + 1 : at + 2, :] = summed[n * 2 : n * 2 + 1, :]
    both = stacked(summed[...])
    atoms = atom_ref[...].astype(F32)
    eye = lax.broadcasted_iota(jnp.int32, (LANES, LANES), 0) == lane_ids(LANES)
    along = []
    for at in range(0, projectors, LANES):
        along.append(jnp.sum(jnp.where(eye, atoms[:, at : at + LANES], 0.0), axis=1, keepdims=True))
    head, rest = split(jnp.where(jnp.concatenate(along, axis=0) == atoms, couplings_ref[...], 0.0))
    head = dot_nt(both, head)
    rest = dot_nt(both, rest)
    weighted = (head[: 2 * kinds] + (head[2 * kinds :] + rest[: 2 * kinds])).astype(BF16)
    for slot in range(slots):
        rows = projectors_ref[slot * length : (slot + 1) * length, :]
        value = dot_nt(weighted, rows)[:kinds]
        rows = projectors_ref[(slots + slot) * length : (slots + slot + 1) * length, :]
        value = value + dot_nt(weighted, rows)[kinds:]
        for row in range(kinds):
            mixed[row, slot : slot + 1, :] = value[row : row + 1, :]
    for chunk in range(blocks * width // LANES):
        for group in range(groups):
            for side in range(2):
                low = side * width
                total = jnp.zeros((each, LANES), F32)
                for inner in range(LANES // width):
                    block = chunk * (LANES // width) + inner
                    own = columns_ref[block * groups + group]
                    own = jnp.where((lanes >= low) & (lanes < low + width), own, 0.0)
                    total += pltpu.roll(own, (inner * width - low) % LANES, 1)
                at = group * slots + side * each
                lined[at : at + each, chunk * LANES : (chunk + 1) * LANES] = total
    both = stacked(lined[...])
    rows_of_lines = groups * slots
    held = lax.broadcasted_iota(jnp.int32, (1, blocks), 1) == lax.axis_index("ga")
    used = jnp.sum(jnp.where(held, count_ref[...], 0).astype(F32), axis=1, keepdims=True)
    slot_ids = lax.broadcasted_iota(jnp.int32, (slots, 1), 0) + lax.axis_index("band") * slots
    used = slot_ids.astype(F32) < used
    for part in range(2):
        head = dot_nt(both, table_ref[0, part])
        rest = dot_nt(both, table_ref[1, part])
        local = (head[:rows_of_lines] + (head[rows_of_lines:] + rest[:rows_of_lines])) * normalizer
        for n in range(orbitals):
            value = local[n * slots : (n + 1) * slots, :] + mixed[n * 2 + part]
            out_ref[n, part] = jnp.where(used, value, 0.0)


def on_device(orbitals, projectors, potential, couplings, atom_index, column_site, column_count):
    blocks = lax.axis_size("ga")
    groups = lax.axis_size("band")
    devices = blocks * groups
    orbital_count, _, slots, length = orbitals.shape
    planes = potential.shape[0]
    projector_count = projectors.shape[0]
    columns = column_site.shape[0]
    kinds = orbital_count * 2
    assert orbital_count == groups and slots % 2 == 0 and kinds % (slots // 2) == 0 and columns % LANES == 0
    share = projector_count // devices
    width = 2
    while width < 2 * planes:
        width *= 2
    carried = 2 * width + kinds // (slots // 2) * share
    assert carried <= LANES and width <= LANES and share * devices == projector_count
    wide = -(-length // LANES) * LANES
    flat = jnp.transpose(projectors, (1, 2, 3, 0)).reshape(2 * slots * length, projector_count)
    z_table = line_table(length, blocks, planes, width)
    batch = next(i for i in (3, 2, 1) if planes % i == 0) if columns <= 512 else 1
    vmem = pl.BlockSpec(memory_space=pltpu.VMEM)
    hbm = pl.BlockSpec(memory_space=pltpu.HBM)
    params = pltpu.CompilerParams(vmem_limit_bytes=56 * 1024 * 1024)
    small = pltpu.CompilerParams(vmem_limit_bytes=40 * 1024 * 1024)
    payload = jax.ShapeDtypeStruct((devices, slots // 2, LANES), F32)

    sent = pl.pallas_call(
        functools.partial(
            project_kernel,
                (blocks, groups, orbital_count, slots, length, projector_count, planes, width),
        ),
        out_shape=payload,
        in_specs=[hbm] * 3,
        out_specs=vmem,
        scratch_shapes=[
            pltpu.SMEM(column_count.shape, jnp.int32),
            pltpu.VMEM(orbitals.shape, BF16),
            pltpu.VMEM(flat.shape, BF16),
            pltpu.VMEM((2 * slots, -(-kinds // 8) * 8, length), F32),
            pltpu.VMEM((kinds * slots, length), F32),
            pltpu.SemaphoreType.DMA((2,)),
            pltpu.SemaphoreType.DMA((2 * slots,)),
        ],
        compiler_params=params,
        cost_estimate=pl.CostEstimate(
            flops=2 * flat.size * LANES * slots,
            bytes_accessed=2 * (flat.size + z_table.size + orbitals.size) + 4 * payload.size,
            transcendentals=length * blocks * width,
        ),
        name="project",
    )(column_count, orbitals, flat)
    arrived = lax.all_to_all(sent, ("ga", "band"), split_axis=0, concat_axis=0, tiled=True)

    x_rows, plus = pl.pallas_call(
        functools.partial(table_kernel, length, wide, slots),
        out_shape=(
            jax.ShapeDtypeStruct((length, 2 * columns), F32),
            jax.ShapeDtypeStruct((4 * columns, 2 * wide), BF16),
        ),
        in_specs=[vmem],
        out_specs=(vmem,) * 2,
        compiler_params=small,
        cost_estimate=pl.CostEstimate(
            flops=4096 * potential.size,
            bytes_accessed=8 * (length + 2 * wide) * columns,
            transcendentals=2 * (length + wide) * columns,
        ),
        name="tables",
    )(column_site.reshape(1, columns))

    sent = pl.pallas_call(
        functools.partial(plane_kernel, (devices, slots, planes, length, wide, width, carried, batch)),
        out_shape=payload,
        in_specs=[vmem] * 4,
        out_specs=vmem,
        scratch_shapes=[
            pltpu.VMEM((-(-columns // (2 * LANES)) * LANES, LANES), F32),
            pltpu.VMEM((width, columns), F32),
            pltpu.VMEM((width, columns), F32),
            pltpu.VMEM((LANES, LANES), F32),
        ],
        compiler_params=small,
        cost_estimate=pl.CostEstimate(
            flops=12 * planes * length * wide * 2 * columns,
            bytes_accessed=4 * (potential.size + 2 * payload.size),
            transcendentals=0,
        ),
        name="planes",
    )(arrived, x_rows, plus, potential)
    arrived = lax.all_to_all(sent, ("ga", "band"), split_axis=0, concat_axis=0, tiled=True)

    normalizer = 1.0 / float(length**3)
    return pl.pallas_call(
        functools.partial(
            finish_kernel,
            (blocks, groups, orbital_count, slots, length, projector_count, width, normalizer),
        ),
        out_shape=jax.ShapeDtypeStruct(orbitals.shape, F32),
        in_specs=[vmem] * 6,
        out_specs=vmem,
        scratch_shapes=[
            pltpu.VMEM((2 * kinds, projector_count), F32),
            pltpu.VMEM((groups * slots, blocks * width), F32),
            pltpu.VMEM((kinds, slots, length), F32),
        ],
        compiler_params=small,
        cost_estimate=pl.CostEstimate(
            flops=4 * kinds * (4 * couplings.size + flat.size) + 4 * z_table.size * orbital_count * slots,
            bytes_accessed=4 * couplings.size + 2 * (flat.size + z_table.size) + 4 * orbitals.size,
            transcendentals=0,
        ),
        name="finish",
    )(column_count.reshape(1, blocks), arrived, atom_index.reshape(1, projector_count), couplings, flat, z_table)


def solution(mesh):
    return jax.shard_map(
        on_device,
        mesh=mesh,
        in_specs=(
            P(None, None, ("ga", "band"), None),
            P(None, None, ("ga", "band"), None),
            P("ga", None, None),
            P(),
            P(),
            P(),
            P(),
        ),
        out_specs=P(None, None, ("ga", "band"), None),
        check_vma=False,
    )
```

```python
import functools

import jax
import jax.numpy as jnp
import ml_dtypes
import numpy as np
from jax import lax
from jax.experimental import pallas as pl
from jax.experimental.pallas import tpu as pltpu
from jax.sharding import PartitionSpec as P

LANES = 128
BF16 = jnp.bfloat16
F32 = jnp.float32


def pieces_of(table):
    table = np.asarray(table, np.float32)
    head = table.astype(ml_dtypes.bfloat16)
    return np.stack([head, (table - head.astype(np.float32)).astype(ml_dtypes.bfloat16)])


def line_table(length, blocks, planes, width):
    kz = np.arange(length)
    out = np.zeros((2, length, blocks, width), np.float64)
    for block in range(blocks):
        z = block * planes + np.arange(planes)
        phases = (kz[:, None] * z[None, :] % length) * (2.0 * np.pi / length)
        out[0, :, block, :planes] = np.cos(phases)
        out[0, :, block, width // 2 : width // 2 + planes] = np.sin(phases)
        out[1, :, block, :planes] = -np.sin(phases)
        out[1, :, block, width // 2 : width // 2 + planes] = np.cos(phases)
    return pieces_of(out.reshape(2, length, blocks * width))


def split(values):
    head = values.astype(BF16)
    return head, (values - head.astype(F32)).astype(BF16)


def stacked(values):
    head, rest = split(values)
    return jnp.concatenate([head.astype(F32), rest.astype(F32)], axis=0).astype(BF16)


def both_pieces(values):
    return jnp.concatenate(split(values), axis=1)


def dot(left, right):
    return lax.dot_general(left, right, (((1,), (0,)), ((), ())), preferred_element_type=F32)


def dot_nt(left, right):
    return lax.dot_general(left, right, (((1,), (1,)), ((), ())), preferred_element_type=F32)


def lane_ids(rows):
    return lax.broadcasted_iota(jnp.int32, (rows, LANES), 1)


def used_slots(count_ref, slots):
    used = count_ref[lax.axis_index("ga")] - lax.axis_index("band") * slots
    return lax.broadcasted_iota(jnp.int32, (slots, 1), 0) < used


def cosine_and_sine(phases, length):
    quarter = jnp.floor(phases * (4.0 / length) + 0.5)
    angle = (phases - quarter * (length / 4.0)) * (2.0 * np.pi / length)
    square = angle * angle
    sine = 1.0 / 362880.0
    for term in (-1.0 / 5040.0, 1.0 / 120.0, -1.0 / 6.0, 1.0):
        sine = sine * square + term
    sine = sine * angle
    cosine = -1.0 / 3628800.0
    for term in (1.0 / 40320.0, -1.0 / 720.0, 1.0 / 24.0, -0.5, 1.0):
        cosine = cosine * square + term
    quarter = quarter - 4.0 * jnp.floor(quarter * 0.25)
    odd = (quarter == 1.0) | (quarter == 3.0)
    first = jnp.where(odd, sine, cosine)
    second = jnp.where(odd, cosine, sine)
    first = jnp.where((quarter == 1.0) | (quarter == 2.0), -first, first)
    return first, jnp.where(quarter >= 2.0, -second, second)


def project_kernel(sizes, count_hbm, orbitals_hbm, projectors_hbm, out_ref, *scratch):
    blocks, groups, orbitals, slots, length, projectors, planes, width = sizes
    count_ref, orbitals_ref, projectors_ref, coef, lines, small_sems, sems = scratch
    kinds = orbitals * 2
    devices = blocks * groups
    share = projectors // devices
    small = [
        pltpu.make_async_copy(count_hbm, count_ref, small_sems.at[0]),
        pltpu.make_async_copy(orbitals_hbm, orbitals_ref, small_sems.at[1]),
    ]
    copies = []
    for piece in range(2 * slots):
        rows = pl.ds(piece * length, length)
        copies.append(pltpu.make_async_copy(projectors_hbm.at[rows], projectors_ref.at[rows], sems.at[piece]))
    for copy in small + copies:
        copy.start()
    half = width // 2
    lanes = lax.broadcasted_iota(jnp.int32, (length, blocks * half), 1)
    plane = (lanes >> (half.bit_length() - 1)) * planes + (lanes & (half - 1))
    kz = lax.broadcasted_iota(jnp.int32, (length, blocks * half), 0)
    table = split(jnp.concatenate(cosine_and_sine(kz.astype(F32) * plane.astype(F32), length), axis=1))
    coef[...] = jnp.zeros_like(coef)
    small[0].wait()
    small[1].wait()
    used = used_slots(count_ref, slots)
    for n in range(orbitals):
        for part in range(2):
            values = jnp.where(used, orbitals_ref[n, part].astype(F32), 0.0)
            at = (part * orbitals + n) * slots
            lines[at : at + slots, :] = values
            turned = values if part == 1 else -values
            for slot in range(slots):
                row = n * 2 + part
                coef[slot, row : row + 1, :] = values[slot : slot + 1, :]
                row = n * 2 + 1 - part
                coef[slots + slot, row : row + 1, :] = turned[slot : slot + 1, :]
    left = lines[...].astype(BF16)
    both = dot(left, table[0]) + dot(left, table[1])
    rows = orbitals * slots
    points = blocks * half
    real = both[:rows, :points] - both[rows:, points:]
    imag = both[:rows, points:] + both[rows:, :points]
    lanes = lane_ids(rows)
    rows_each = slots // 2
    piece_lanes = lane_ids(rows_each)
    for block in range(blocks):
        at = block * half
        base = at // LANES * LANES
        chunk = pltpu.roll(imag[:, base : base + LANES], (base - at + half) % LANES, 1)
        chunk = jnp.where(lanes < half, pltpu.roll(real[:, base : base + LANES], (base - at) % LANES, 1), chunk)
        aside = pltpu.roll(chunk, width, 1)
        for group in range(groups):
            at = group * slots
            piece = jnp.where(piece_lanes < width, chunk[at : at + rows_each, :], aside[at + rows_each : at + slots, :])
            out_ref[block * groups + group] = piece
    sums = jnp.zeros((coef.shape[1], projectors), F32)
    for piece in range(2 * slots):
        left = coef[piece].astype(BF16)
        copies[piece].wait()
        sums += dot(left, projectors_ref[piece * length : (piece + 1) * length, :])
    for device in range(devices):
        piece = jnp.where(piece_lanes < 2 * width, out_ref[device], 0.0)
        first = device * share
        base = first // LANES * LANES
        for group in range(kinds // rows_each):
            low = 2 * width + group * share
            own = sums[group * rows_each : (group + 1) * rows_each, base : base + LANES]
            own = pltpu.roll(own, (base + low - first) % LANES, 1)
            piece = jnp.where((piece_lanes >= low) & (piece_lanes < low + share), own, piece)
        out_ref[device] = piece


def table_kernel(length, wide, slots, site_ref, x_ref, plus_ref):
    columns = site_ref.shape[1]
    each = slots // 2
    eye = lax.broadcasted_iota(jnp.int32, (LANES, LANES), 0) == lane_ids(LANES)
    row_ids = lax.broadcasted_iota(jnp.int32, (length, LANES), 0).astype(F32)
    lanes = lax.broadcasted_iota(jnp.int32, (LANES, wide), 1)
    inside = lanes < length
    lanes = lanes.astype(F32)
    sites = site_ref[...].astype(F32)
    stored = lax.broadcasted_iota(jnp.int32, (LANES, columns), 1)
    for at in range(0, columns, LANES):
        order = lax.broadcasted_iota(jnp.int32, (LANES, columns), 0) + at
        second = order >= columns // 2
        order = jnp.where(second, order - columns // 2, order)
        wanted = (order >> (each.bit_length() - 1)) * slots + (order & (each - 1)) + jnp.where(second, each, 0)
        along = jnp.sum(jnp.where(stored == wanted, sites, 0.0), axis=1, keepdims=True)
        site = jnp.sum(jnp.where(eye, along, 0.0), axis=0, keepdims=True)
        site_x = jnp.floor((site + 0.5) * (1.0 / length))
        along = along - jnp.floor((along + 0.5) * (1.0 / length)) * length
        cosine, sine = cosine_and_sine(row_ids * site_x, length)
        x_ref[:, at : at + LANES] = cosine
        x_ref[:, columns + at : columns + at + LANES] = sine
        cosine, sine = cosine_and_sine(lanes * along, length)
        cosine = jnp.where(inside, cosine, 0.0)
        sine = jnp.where(inside, sine, 0.0)
        cosine = cosine.astype(BF16)
        sine = sine.astype(BF16)
        for piece in range(2):
            rows = pl.ds(piece * 2 * columns + at, LANES)
            plus_ref[rows, :wide] = cosine
            plus_ref[rows, wide:] = sine
            rows = pl.ds((piece * 2 + 1) * columns + at, LANES)
            plus_ref[rows, :wide] = -sine
            plus_ref[rows, wide:] = cosine


def plane_kernel(sizes, columns_ref, x_ref, plus_ref, potential_ref, out_ref, gathered, lines, back, turning):
    devices, slots, planes, length, wide, width, carried, batch = sizes
    count = devices * slots
    each = slots // 2
    middle = count // 2
    total = jnp.zeros((each, LANES), F32)
    for device in range(devices):
        piece = columns_ref[device]
        gathered[device * each : (device + 1) * each, :] = piece
        total += piece
    for at in range(0, middle, LANES):
        size = min(LANES, middle - at)
        turned = gathered[at : at + LANES, :].T
        for side in range(2):
            lines[:, side * middle + at : side * middle + at + size] = turned[side * width : (side + 1) * width, :size]
    back[...] = jnp.zeros_like(back)
    cosine = x_ref[:, :count]
    sine = x_ref[:, count:]
    padding = jnp.zeros((length, wide - length), F32)

    def factors(i):
        left = []
        for plane in range(i * batch, (i + 1) * batch):
            real = lines[plane : plane + 1, :]
            imag = lines[plane + width // 2 : plane + width // 2 + 1, :]
            left.append(jnp.concatenate([cosine * real - sine * imag, cosine * imag + sine * real], axis=1))
        return both_pieces(jnp.concatenate(left, axis=0))

    def weigh(i, field):
        weights = []
        for plane in range(i * batch, (i + 1) * batch):
            own = jnp.concatenate([potential_ref[plane], padding], axis=1)
            weights.append(jnp.concatenate([own, own], axis=1))
        return (field * jnp.concatenate(weights, axis=0)).astype(BF16)

    def collect(i, half):
        for j in range(batch):
            plane = i * batch + j
            real = half[j * length : (j + 1) * length, :count]
            imag = half[j * length : (j + 1) * length, count:]
            back[plane : plane + 1, :] = jnp.sum(cosine * real + sine * imag, axis=0, keepdims=True)
            at = plane + width // 2
            back[at : at + 1, :] = jnp.sum(cosine * imag - sine * real, axis=0, keepdims=True)

    steps = planes // batch
    left = factors(0)
    half = None
    for i in range(steps):
        field = dot(left, plus_ref[...])
        if i + 1 < steps:
            left = factors(i + 1)
        if half is not None:
            collect(i - 1, half)
        half = dot_nt(weigh(i, field), plus_ref[: 2 * count, :])
    collect(steps - 1, half)
    for at in range(0, middle, LANES):
        size = min(LANES, middle - at)
        for side in range(2):
            turning[side * width : (side + 1) * width, :size] = back[:, side * middle + at : side * middle + at + size]
        gathered[at : at + LANES, :] = turning[...].T
    lanes = lane_ids(each)
    for device in range(devices):
        piece = gathered[device * each : (device + 1) * each, :]
        out_ref[device] = jnp.where((lanes >= 2 * width) & (lanes < carried), total, piece)


def finish_kernel(
    sizes, count_ref, columns_ref, atom_ref, couplings_ref, projectors_ref, table_ref, out_ref, summed, lined, mixed
):
    blocks, groups, orbitals, slots, length, projectors, width, normalizer = sizes
    kinds = orbitals * 2
    devices = blocks * groups
    share = projectors // devices
    each = slots // 2
    lanes = lane_ids(each)
    for chunk in range(projectors // LANES):
        in_chunk = range(chunk * LANES // share, (chunk + 1) * LANES // share)
        for rows in range(kinds // each):
            low = 2 * width + rows * share
            total = jnp.zeros((each, LANES), F32)
            for device in in_chunk:
                own = columns_ref[device]
                own = pltpu.roll(jnp.where((lanes >= low) & (lanes < low + share), own, 0.0), (device * share - low) % LANES, 1)
                total += own
            summed[rows * each : (rows + 1) * each, chunk * LANES : (chunk + 1) * LANES] = total
    for n in range(orbitals):
        at = kinds + n * 2
        summed[at : at + 1, :] = -summed[n * 2 + 1 : n * 2 + 2, :]
        summed[at + 1 : at + 2, :] = summed[n * 2 : n * 2 + 1, :]
    both = stacked(summed[...])
    atoms = atom_ref[...].astype(F32)
    eye = lax.broadcasted_iota(jnp.int32, (LANES, LANES), 0) == lane_ids(LANES)
    along = []
    for at in range(0, projectors, LANES):
        along.append(jnp.sum(jnp.where(eye, atoms[:, at : at + LANES], 0.0), axis=1, keepdims=True))
    head, rest = split(jnp.where(jnp.concatenate(along, axis=0) == atoms, couplings_ref[...], 0.0))
    head = dot_nt(both, head)
    rest = dot_nt(both, rest)
    weighted = (head[: 2 * kinds] + (head[2 * kinds :] + rest[: 2 * kinds])).astype(BF16)
    for slot in range(slots):
        rows = projectors_ref[slot * length : (slot + 1) * length, :]
        value = dot_nt(weighted, rows)[:kinds]
        rows = projectors_ref[(slots + slot) * length : (slots + slot + 1) * length, :]
        value = value + dot_nt(weighted, rows)[kinds:]
        for row in range(kinds):
            mixed[row, slot : slot + 1, :] = value[row : row + 1, :]
    for chunk in range(blocks * width // LANES):
        for group in range(groups):
            for side in range(2):
                low = side * width
                total = jnp.zeros((each, LANES), F32)
                for inner in range(LANES // width):
                    block = chunk * (LANES // width) + inner
                    own = columns_ref[block * groups + group]
                    own = jnp.where((lanes >= low) & (lanes < low + width), own, 0.0)
                    total += pltpu.roll(own, (inner * width - low) % LANES, 1)
                at = group * slots + side * each
                lined[at : at + each, chunk * LANES : (chunk + 1) * LANES] = total
    both = stacked(lined[...])
    rows_of_lines = groups * slots
    held = lax.broadcasted_iota(jnp.int32, (1, blocks), 1) == lax.axis_index("ga")
    used = jnp.sum(jnp.where(held, count_ref[...], 0).astype(F32), axis=1, keepdims=True)
    slot_ids = lax.broadcasted_iota(jnp.int32, (slots, 1), 0) + lax.axis_index("band") * slots
    used = slot_ids.astype(F32) < used
    for part in range(2):
        head = dot_nt(both, table_ref[0, part])
        rest = dot_nt(both, table_ref[1, part])
        local = (head[:rows_of_lines] + (head[rows_of_lines:] + rest[:rows_of_lines])) * normalizer
        for n in range(orbitals):
            value = local[n * slots : (n + 1) * slots, :] + mixed[n * 2 + part]
            out_ref[n, part] = jnp.where(used, value, 0.0)


def on_device(orbitals, projectors, potential, couplings, atom_index, column_site, column_count):
    blocks = lax.axis_size("ga")
    groups = lax.axis_size("band")
    devices = blocks * groups
    orbital_count, _, slots, length = orbitals.shape
    planes = potential.shape[0]
    projector_count = projectors.shape[0]
    columns = column_site.shape[0]
    kinds = orbital_count * 2
    assert orbital_count == groups and slots % 2 == 0 and kinds % (slots // 2) == 0 and columns % LANES == 0
    share = projector_count // devices
    width = 2
    while width < 2 * planes:
        width *= 2
    carried = 2 * width + kinds // (slots // 2) * share
    assert carried <= LANES and width <= LANES and share * devices == projector_count
    wide = -(-length // LANES) * LANES
    flat = jnp.transpose(projectors, (1, 2, 3, 0)).reshape(2 * slots * length, projector_count)
    z_table = line_table(length, blocks, planes, width)
    batch = next(i for i in (3, 2, 1) if planes % i == 0) if columns <= 512 else 1
    vmem = pl.BlockSpec(memory_space=pltpu.VMEM)
    hbm = pl.BlockSpec(memory_space=pltpu.HBM)
    params = pltpu.CompilerParams(vmem_limit_bytes=56 * 1024 * 1024)
    small = pltpu.CompilerParams(vmem_limit_bytes=40 * 1024 * 1024)
    payload = jax.ShapeDtypeStruct((devices, slots // 2, LANES), F32)

    sent = pl.pallas_call(
        functools.partial(
            project_kernel,
                (blocks, groups, orbital_count, slots, length, projector_count, planes, width),
        ),
        out_shape=payload,
        in_specs=[hbm] * 3,
        out_specs=vmem,
        scratch_shapes=[
            pltpu.SMEM(column_count.shape, jnp.int32),
            pltpu.VMEM(orbitals.shape, BF16),
            pltpu.VMEM(flat.shape, BF16),
            pltpu.VMEM((2 * slots, -(-kinds // 8) * 8, length), F32),
            pltpu.VMEM((kinds * slots, length), F32),
            pltpu.SemaphoreType.DMA((2,)),
            pltpu.SemaphoreType.DMA((2 * slots,)),
        ],
        compiler_params=params,
        cost_estimate=pl.CostEstimate(
            flops=2 * flat.size * LANES * slots,
            bytes_accessed=2 * (flat.size + z_table.size + orbitals.size) + 4 * payload.size,
            transcendentals=length * blocks * width,
        ),
        name="project",
    )(column_count, orbitals, flat)
    arrived = lax.all_to_all(sent, ("ga", "band"), split_axis=0, concat_axis=0, tiled=True)

    x_rows, plus = pl.pallas_call(
        functools.partial(table_kernel, length, wide, slots),
        out_shape=(
            jax.ShapeDtypeStruct((length, 2 * columns), F32),
            jax.ShapeDtypeStruct((4 * columns, 2 * wide), BF16),
        ),
        in_specs=[vmem],
        out_specs=(vmem,) * 2,
        compiler_params=small,
        cost_estimate=pl.CostEstimate(
            flops=4096 * potential.size,
            bytes_accessed=8 * (length + 2 * wide) * columns,
            transcendentals=2 * (length + wide) * columns,
        ),
        name="tables",
    )(column_site.reshape(1, columns))

    sent = pl.pallas_call(
        functools.partial(plane_kernel, (devices, slots, planes, length, wide, width, carried, batch)),
        out_shape=payload,
        in_specs=[vmem] * 4,
        out_specs=vmem,
        scratch_shapes=[
            pltpu.VMEM((-(-columns // (2 * LANES)) * LANES, LANES), F32),
            pltpu.VMEM((width, columns), F32),
            pltpu.VMEM((width, columns), F32),
            pltpu.VMEM((LANES, LANES), F32),
        ],
        compiler_params=small,
        cost_estimate=pl.CostEstimate(
            flops=12 * planes * length * wide * 2 * columns,
            bytes_accessed=4 * (potential.size + 2 * payload.size),
            transcendentals=0,
        ),
        name="planes",
    )(arrived, x_rows, plus, potential)
    arrived = lax.all_to_all(sent, ("ga", "band"), split_axis=0, concat_axis=0, tiled=True)

    normalizer = 1.0 / float(length**3)
    return pl.pallas_call(
        functools.partial(
            finish_kernel,
            (blocks, groups, orbital_count, slots, length, projector_count, width, normalizer),
        ),
        out_shape=jax.ShapeDtypeStruct(orbitals.shape, F32),
        in_specs=[vmem] * 6,
        out_specs=vmem,
        scratch_shapes=[
            pltpu.VMEM((2 * kinds, projector_count), F32),
            pltpu.VMEM((groups * slots, blocks * width), F32),
            pltpu.VMEM((kinds, slots, length), F32),
        ],
        compiler_params=small,
        cost_estimate=pl.CostEstimate(
            flops=4 * kinds * (4 * couplings.size + flat.size) + 4 * z_table.size * orbital_count * slots,
            bytes_accessed=4 * couplings.size + 2 * (flat.size + z_table.size) + 4 * orbitals.size,
            transcendentals=0,
        ),
        name="finish",
    )(column_count.reshape(1, blocks), arrived, atom_index.reshape(1, projector_count), couplings, flat, z_table)


def solution(mesh):
    return jax.shard_map(
        on_device,
        mesh=mesh,
        in_specs=(
            P(None, None, ("ga", "band"), None),
            P(None, None, ("ga", "band"), None),
            P("ga", None, None),
            P(),
            P(),
            P(),
            P(),
        ),
        out_specs=P(None, None, ("ga", "band"), None),
        check_vma=False,
    )
```

```python
import functools

import jax
import jax.numpy as jnp
import ml_dtypes
import numpy as np
from jax import lax
from jax.experimental import pallas as pl
from jax.experimental.pallas import tpu as pltpu
from jax.sharding import PartitionSpec as P

LANES = 128
BF16 = jnp.bfloat16
F32 = jnp.float32


def pieces_of(table):
    table = np.asarray(table, np.float32)
    head = table.astype(ml_dtypes.bfloat16)
    return np.stack([head, (table - head.astype(np.float32)).astype(ml_dtypes.bfloat16)])


def line_table(length, blocks, planes, width):
    kz = np.arange(length)
    out = np.zeros((2, length, blocks, width), np.float64)
    for block in range(blocks):
        z = block * planes + np.arange(planes)
        phases = (kz[:, None] * z[None, :] % length) * (2.0 * np.pi / length)
        out[0, :, block, :planes] = np.cos(phases)
        out[0, :, block, width // 2 : width // 2 + planes] = np.sin(phases)
        out[1, :, block, :planes] = -np.sin(phases)
        out[1, :, block, width // 2 : width // 2 + planes] = np.cos(phases)
    return pieces_of(out.reshape(2, length, blocks * width))


def split(values):
    head = values.astype(BF16)
    return head, (values - head.astype(F32)).astype(BF16)


def stacked(values):
    head, rest = split(values)
    return jnp.concatenate([head.astype(F32), rest.astype(F32)], axis=0).astype(BF16)


def both_pieces(values):
    return jnp.concatenate(split(values), axis=1)


def dot(left, right):
    return lax.dot_general(left, right, (((1,), (0,)), ((), ())), preferred_element_type=F32)


def dot_nt(left, right):
    return lax.dot_general(left, right, (((1,), (1,)), ((), ())), preferred_element_type=F32)


def lane_ids(rows):
    return lax.broadcasted_iota(jnp.int32, (rows, LANES), 1)


def used_slots(count_ref, slots):
    used = count_ref[lax.axis_index("ga")] - lax.axis_index("band") * slots
    return lax.broadcasted_iota(jnp.int32, (slots, 1), 0) < used


def cosine_and_sine(phases, length):
    quarter = jnp.floor(phases * (4.0 / length) + 0.5)
    angle = (phases - quarter * (length / 4.0)) * (2.0 * np.pi / length)
    square = angle * angle
    sine = 1.0 / 362880.0
    for term in (-1.0 / 5040.0, 1.0 / 120.0, -1.0 / 6.0, 1.0):
        sine = sine * square + term
    sine = sine * angle
    cosine = -1.0 / 3628800.0
    for term in (1.0 / 40320.0, -1.0 / 720.0, 1.0 / 24.0, -0.5, 1.0):
        cosine = cosine * square + term
    quarter = quarter - 4.0 * jnp.floor(quarter * 0.25)
    odd = (quarter == 1.0) | (quarter == 3.0)
    first = jnp.where(odd, sine, cosine)
    second = jnp.where(odd, cosine, sine)
    first = jnp.where((quarter == 1.0) | (quarter == 2.0), -first, first)
    return first, jnp.where(quarter >= 2.0, -second, second)


def project_kernel(sizes, count_hbm, orbitals_hbm, projectors_hbm, out_ref, *scratch):
    blocks, groups, orbitals, slots, length, projectors, planes, width = sizes
    count_ref, orbitals_ref, projectors_ref, coef, lines, small_sems, sems = scratch
    kinds = orbitals * 2
    devices = blocks * groups
    share = projectors // devices
    small = [
        pltpu.make_async_copy(count_hbm, count_ref, small_sems.at[0]),
        pltpu.make_async_copy(orbitals_hbm, orbitals_ref, small_sems.at[1]),
    ]
    copies = []
    for piece in range(2 * slots):
        rows = pl.ds(piece * length, length)
        copies.append(pltpu.make_async_copy(projectors_hbm.at[rows], projectors_ref.at[rows], sems.at[piece]))
    for copy in small + copies:
        copy.start()
    half = width // 2
    lanes = lax.broadcasted_iota(jnp.int32, (length, blocks * half), 1)
    plane = (lanes >> (half.bit_length() - 1)) * planes + (lanes & (half - 1))
    kz = lax.broadcasted_iota(jnp.int32, (length, blocks * half), 0)
    table = split(jnp.concatenate(cosine_and_sine(kz.astype(F32) * plane.astype(F32), length), axis=1))
    coef[...] = jnp.zeros_like(coef)
    small[0].wait()
    small[1].wait()
    used = used_slots(count_ref, slots)
    for n in range(orbitals):
        for part in range(2):
            values = jnp.where(used, orbitals_ref[n, part].astype(F32), 0.0)
            at = (part * orbitals + n) * slots
            lines[at : at + slots, :] = values
            turned = values if part == 1 else -values
            for slot in range(slots):
                row = n * 2 + part
                coef[slot, row : row + 1, :] = values[slot : slot + 1, :]
                row = n * 2 + 1 - part
                coef[slots + slot, row : row + 1, :] = turned[slot : slot + 1, :]
    left = lines[...].astype(BF16)
    both = dot(left, table[0]) + dot(left, table[1])
    rows = orbitals * slots
    points = blocks * half
    real = both[:rows, :points] - both[rows:, points:]
    imag = both[:rows, points:] + both[rows:, :points]
    lanes = lane_ids(rows)
    rows_each = slots // 2
    piece_lanes = lane_ids(rows_each)
    for block in range(blocks):
        at = block * half
        base = at // LANES * LANES
        chunk = pltpu.roll(imag[:, base : base + LANES], (base - at + half) % LANES, 1)
        chunk = jnp.where(lanes < half, pltpu.roll(real[:, base : base + LANES], (base - at) % LANES, 1), chunk)
        aside = pltpu.roll(chunk, width, 1)
        for group in range(groups):
            at = group * slots
            piece = jnp.where(piece_lanes < width, chunk[at : at + rows_each, :], aside[at + rows_each : at + slots, :])
            out_ref[block * groups + group] = piece
    sums = jnp.zeros((coef.shape[1], projectors), F32)
    for piece in range(2 * slots):
        left = coef[piece].astype(BF16)
        copies[piece].wait()
        sums += dot(left, projectors_ref[piece * length : (piece + 1) * length, :])
    for device in range(devices):
        piece = jnp.where(piece_lanes < 2 * width, out_ref[device], 0.0)
        first = device * share
        base = first // LANES * LANES
        for group in range(kinds // rows_each):
            low = 2 * width + group * share
            own = sums[group * rows_each : (group + 1) * rows_each, base : base + LANES]
            own = pltpu.roll(own, (base + low - first) % LANES, 1)
            piece = jnp.where((piece_lanes >= low) & (piece_lanes < low + share), own, piece)
        out_ref[device] = piece


def table_kernel(length, wide, slots, site_ref, x_ref, plus_ref):
    columns = site_ref.shape[1]
    each = slots // 2
    eye = lax.broadcasted_iota(jnp.int32, (LANES, LANES), 0) == lane_ids(LANES)
    row_ids = lax.broadcasted_iota(jnp.int32, (length, LANES), 0).astype(F32)
    lanes = lax.broadcasted_iota(jnp.int32, (LANES, wide), 1)
    inside = lanes < length
    lanes = lanes.astype(F32)
    sites = site_ref[...].astype(F32)
    stored = lax.broadcasted_iota(jnp.int32, (LANES, columns), 1)
    for at in range(0, columns, LANES):
        order = lax.broadcasted_iota(jnp.int32, (LANES, columns), 0) + at
        second = order >= columns // 2
        order = jnp.where(second, order - columns // 2, order)
        wanted = (order >> (each.bit_length() - 1)) * slots + (order & (each - 1)) + jnp.where(second, each, 0)
        along = jnp.sum(jnp.where(stored == wanted, sites, 0.0), axis=1, keepdims=True)
        site = jnp.sum(jnp.where(eye, along, 0.0), axis=0, keepdims=True)
        site_x = jnp.floor((site + 0.5) * (1.0 / length))
        along = along - jnp.floor((along + 0.5) * (1.0 / length)) * length
        cosine, sine = cosine_and_sine(row_ids * site_x, length)
        x_ref[:, at : at + LANES] = cosine
        x_ref[:, columns + at : columns + at + LANES] = sine
        cosine, sine = cosine_and_sine(lanes * along, length)
        cosine = jnp.where(inside, cosine, 0.0)
        sine = jnp.where(inside, sine, 0.0)
        cosine = cosine.astype(BF16)
        sine = sine.astype(BF16)
        for piece in range(2):
            rows = pl.ds(piece * 2 * columns + at, LANES)
            plus_ref[rows, :wide] = cosine
            plus_ref[rows, wide:] = sine
            rows = pl.ds((piece * 2 + 1) * columns + at, LANES)
            plus_ref[rows, :wide] = -sine
            plus_ref[rows, wide:] = cosine


def plane_kernel(sizes, columns_ref, x_ref, plus_ref, potential_ref, out_ref, gathered, lines, back, turning):
    devices, slots, planes, length, wide, width, carried, batch = sizes
    count = devices * slots
    each = slots // 2
    middle = count // 2
    total = jnp.zeros((each, LANES), F32)
    for device in range(devices):
        piece = columns_ref[device]
        gathered[device * each : (device + 1) * each, :] = piece
        total += piece
    for at in range(0, middle, LANES):
        size = min(LANES, middle - at)
        turned = gathered[at : at + LANES, :].T
        for side in range(2):
            lines[:, side * middle + at : side * middle + at + size] = turned[side * width : (side + 1) * width, :size]
    back[...] = jnp.zeros_like(back)
    cosine = x_ref[:, :count]
    sine = x_ref[:, count:]
    padding = jnp.zeros((length, wide - length), F32)
    for i in range(planes // batch):
        left = []
        for plane in range(i * batch, (i + 1) * batch):
            real = lines[plane : plane + 1, :]
            imag = lines[plane + width // 2 : plane + width // 2 + 1, :]
            left.append(jnp.concatenate([cosine * real - sine * imag, cosine * imag + sine * real], axis=1))
        left = both_pieces(jnp.concatenate(left, axis=0))
        field = dot(left, plus_ref[...])
        weights = []
        for plane in range(i * batch, (i + 1) * batch):
            own = jnp.concatenate([potential_ref[plane], padding], axis=1)
            weights.append(jnp.concatenate([own, own], axis=1))
        left = (field * jnp.concatenate(weights, axis=0)).astype(BF16)
        half = dot_nt(left, plus_ref[: 2 * count, :])
        for j in range(batch):
            plane = i * batch + j
            real = half[j * length : (j + 1) * length, :count]
            imag = half[j * length : (j + 1) * length, count:]
            back[plane : plane + 1, :] = jnp.sum(cosine * real + sine * imag, axis=0, keepdims=True)
            at = plane + width // 2
            back[at : at + 1, :] = jnp.sum(cosine * imag - sine * real, axis=0, keepdims=True)
    for at in range(0, middle, LANES):
        size = min(LANES, middle - at)
        for side in range(2):
            turning[side * width : (side + 1) * width, :size] = back[:, side * middle + at : side * middle + at + size]
        gathered[at : at + LANES, :] = turning[...].T
    lanes = lane_ids(each)
    for device in range(devices):
        piece = gathered[device * each : (device + 1) * each, :]
        out_ref[device] = jnp.where((lanes >= 2 * width) & (lanes < carried), total, piece)


def finish_kernel(
    sizes, count_ref, columns_ref, atom_ref, couplings_ref, projectors_ref, table_ref, out_ref, summed, lined, mixed
):
    blocks, groups, orbitals, slots, length, projectors, width, normalizer = sizes
    kinds = orbitals * 2
    devices = blocks * groups
    share = projectors // devices
    each = slots // 2
    lanes = lane_ids(each)
    for chunk in range(projectors // LANES):
        in_chunk = range(chunk * LANES // share, (chunk + 1) * LANES // share)
        for rows in range(kinds // each):
            low = 2 * width + rows * share
            total = jnp.zeros((each, LANES), F32)
            for device in in_chunk:
                own = columns_ref[device]
                own = pltpu.roll(jnp.where((lanes >= low) & (lanes < low + share), own, 0.0), (device * share - low) % LANES, 1)
                total += own
            summed[rows * each : (rows + 1) * each, chunk * LANES : (chunk + 1) * LANES] = total
    for n in range(orbitals):
        at = kinds + n * 2
        summed[at : at + 1, :] = -summed[n * 2 + 1 : n * 2 + 2, :]
        summed[at + 1 : at + 2, :] = summed[n * 2 : n * 2 + 1, :]
    both = stacked(summed[...])
    atoms = atom_ref[...].astype(F32)
    eye = lax.broadcasted_iota(jnp.int32, (LANES, LANES), 0) == lane_ids(LANES)
    along = []
    for at in range(0, projectors, LANES):
        along.append(jnp.sum(jnp.where(eye, atoms[:, at : at + LANES], 0.0), axis=1, keepdims=True))
    head, rest = split(jnp.where(jnp.concatenate(along, axis=0) == atoms, couplings_ref[...], 0.0))
    head = dot_nt(both, head)
    rest = dot_nt(both, rest)
    weighted = (head[: 2 * kinds] + (head[2 * kinds :] + rest[: 2 * kinds])).astype(BF16)
    for slot in range(slots):
        rows = projectors_ref[slot * length : (slot + 1) * length, :]
        value = dot_nt(weighted, rows)[:kinds]
        rows = projectors_ref[(slots + slot) * length : (slots + slot + 1) * length, :]
        value = value + dot_nt(weighted, rows)[kinds:]
        for row in range(kinds):
            mixed[row, slot : slot + 1, :] = value[row : row + 1, :]
    for chunk in range(blocks * width // LANES):
        for group in range(groups):
            for side in range(2):
                low = side * width
                total = jnp.zeros((each, LANES), F32)
                for inner in range(LANES // width):
                    block = chunk * (LANES // width) + inner
                    own = columns_ref[block * groups + group]
                    own = jnp.where((lanes >= low) & (lanes < low + width), own, 0.0)
                    total += pltpu.roll(own, (inner * width - low) % LANES, 1)
                at = group * slots + side * each
                lined[at : at + each, chunk * LANES : (chunk + 1) * LANES] = total
    both = stacked(lined[...])
    rows_of_lines = groups * slots
    held = lax.broadcasted_iota(jnp.int32, (1, blocks), 1) == lax.axis_index("ga")
    used = jnp.sum(jnp.where(held, count_ref[...], 0).astype(F32), axis=1, keepdims=True)
    slot_ids = lax.broadcasted_iota(jnp.int32, (slots, 1), 0) + lax.axis_index("band") * slots
    used = slot_ids.astype(F32) < used
    for part in range(2):
        head = dot_nt(both, table_ref[0, part])
        rest = dot_nt(both, table_ref[1, part])
        local = (head[:rows_of_lines] + (head[rows_of_lines:] + rest[:rows_of_lines])) * normalizer
        for n in range(orbitals):
            value = local[n * slots : (n + 1) * slots, :] + mixed[n * 2 + part]
            out_ref[n, part] = jnp.where(used, value, 0.0)


def on_device(orbitals, projectors, potential, couplings, atom_index, column_site, column_count):
    blocks = lax.axis_size("ga")
    groups = lax.axis_size("band")
    devices = blocks * groups
    orbital_count, _, slots, length = orbitals.shape
    planes = potential.shape[0]
    projector_count = projectors.shape[0]
    columns = column_site.shape[0]
    kinds = orbital_count * 2
    assert orbital_count == groups and slots % 2 == 0 and kinds % (slots // 2) == 0 and columns % LANES == 0
    share = projector_count // devices
    width = 2
    while width < 2 * planes:
        width *= 2
    carried = 2 * width + kinds // (slots // 2) * share
    assert carried <= LANES and width <= LANES and share * devices == projector_count
    wide = -(-length // LANES) * LANES
    flat = jnp.transpose(projectors, (1, 2, 3, 0)).reshape(2 * slots * length, projector_count)
    z_table = line_table(length, blocks, planes, width)
    batch = next(i for i in (4, 3, 2, 1) if planes % i == 0) if columns <= 512 else 1
    vmem = pl.BlockSpec(memory_space=pltpu.VMEM)
    hbm = pl.BlockSpec(memory_space=pltpu.HBM)
    params = pltpu.CompilerParams(vmem_limit_bytes=56 * 1024 * 1024)
    small = pltpu.CompilerParams(vmem_limit_bytes=40 * 1024 * 1024)
    payload = jax.ShapeDtypeStruct((devices, slots // 2, LANES), F32)

    sent = pl.pallas_call(
        functools.partial(
            project_kernel,
                (blocks, groups, orbital_count, slots, length, projector_count, planes, width),
        ),
        out_shape=payload,
        in_specs=[hbm] * 3,
        out_specs=vmem,
        scratch_shapes=[
            pltpu.SMEM(column_count.shape, jnp.int32),
            pltpu.VMEM(orbitals.shape, BF16),
            pltpu.VMEM(flat.shape, BF16),
            pltpu.VMEM((2 * slots, -(-kinds // 8) * 8, length), F32),
            pltpu.VMEM((kinds * slots, length), F32),
            pltpu.SemaphoreType.DMA((2,)),
            pltpu.SemaphoreType.DMA((2 * slots,)),
        ],
        compiler_params=params,
        cost_estimate=pl.CostEstimate(
            flops=2 * flat.size * LANES * slots,
            bytes_accessed=2 * (flat.size + z_table.size + orbitals.size) + 4 * payload.size,
            transcendentals=length * blocks * width,
        ),
        name="project",
    )(column_count, orbitals, flat)
    arrived = lax.all_to_all(sent, ("ga", "band"), split_axis=0, concat_axis=0, tiled=True)

    x_rows, plus = pl.pallas_call(
        functools.partial(table_kernel, length, wide, slots),
        out_shape=(
            jax.ShapeDtypeStruct((length, 2 * columns), F32),
            jax.ShapeDtypeStruct((4 * columns, 2 * wide), BF16),
        ),
        in_specs=[vmem],
        out_specs=(vmem,) * 2,
        compiler_params=small,
        cost_estimate=pl.CostEstimate(
            flops=4096 * potential.size,
            bytes_accessed=8 * (length + 2 * wide) * columns,
            transcendentals=2 * (length + wide) * columns,
        ),
        name="tables",
    )(column_site.reshape(1, columns))

    sent = pl.pallas_call(
        functools.partial(plane_kernel, (devices, slots, planes, length, wide, width, carried, batch)),
        out_shape=payload,
        in_specs=[vmem] * 4,
        out_specs=vmem,
        scratch_shapes=[
            pltpu.VMEM((-(-columns // (2 * LANES)) * LANES, LANES), F32),
            pltpu.VMEM((width, columns), F32),
            pltpu.VMEM((width, columns), F32),
            pltpu.VMEM((LANES, LANES), F32),
        ],
        compiler_params=small,
        cost_estimate=pl.CostEstimate(
            flops=12 * planes * length * wide * 2 * columns,
            bytes_accessed=4 * (potential.size + 2 * payload.size),
            transcendentals=0,
        ),
        name="planes",
    )(arrived, x_rows, plus, potential)
    arrived = lax.all_to_all(sent, ("ga", "band"), split_axis=0, concat_axis=0, tiled=True)

    normalizer = 1.0 / float(length**3)
    return pl.pallas_call(
        functools.partial(
            finish_kernel,
            (blocks, groups, orbital_count, slots, length, projector_count, width, normalizer),
        ),
        out_shape=jax.ShapeDtypeStruct(orbitals.shape, F32),
        in_specs=[vmem] * 6,
        out_specs=vmem,
        scratch_shapes=[
            pltpu.VMEM((2 * kinds, projector_count), F32),
            pltpu.VMEM((groups * slots, blocks * width), F32),
            pltpu.VMEM((kinds, slots, length), F32),
        ],
        compiler_params=small,
        cost_estimate=pl.CostEstimate(
            flops=4 * kinds * (4 * couplings.size + flat.size) + 4 * z_table.size * orbital_count * slots,
            bytes_accessed=4 * couplings.size + 2 * (flat.size + z_table.size) + 4 * orbitals.size,
            transcendentals=0,
        ),
        name="finish",
    )(column_count.reshape(1, blocks), arrived, atom_index.reshape(1, projector_count), couplings, flat, z_table)


def solution(mesh):
    return jax.shard_map(
        on_device,
        mesh=mesh,
        in_specs=(
            P(None, None, ("ga", "band"), None),
            P(None, None, ("ga", "band"), None),
            P("ga", None, None),
            P(),
            P(),
            P(),
            P(),
        ),
        out_specs=P(None, None, ("ga", "band"), None),
        check_vma=False,
    )
```

```python
import functools

import jax
import jax.numpy as jnp
import ml_dtypes
import numpy as np
from jax import lax
from jax.experimental import pallas as pl
from jax.experimental.pallas import tpu as pltpu
from jax.sharding import PartitionSpec as P

LANES = 128
BF16 = jnp.bfloat16
F32 = jnp.float32


def pieces_of(table):
    table = np.asarray(table, np.float32)
    head = table.astype(ml_dtypes.bfloat16)
    return np.stack([head, (table - head.astype(np.float32)).astype(ml_dtypes.bfloat16)])


def line_table(length, blocks, planes, width):
    kz = np.arange(length)
    out = np.zeros((2, length, blocks, width), np.float64)
    for block in range(blocks):
        z = block * planes + np.arange(planes)
        phases = (kz[:, None] * z[None, :] % length) * (2.0 * np.pi / length)
        out[0, :, block, :planes] = np.cos(phases)
        out[0, :, block, width // 2 : width // 2 + planes] = np.sin(phases)
        out[1, :, block, :planes] = -np.sin(phases)
        out[1, :, block, width // 2 : width // 2 + planes] = np.cos(phases)
    return pieces_of(out.reshape(2, length, blocks * width))


def split(values):
    head = values.astype(BF16)
    return head, (values - head.astype(F32)).astype(BF16)


def stacked(values):
    head, rest = split(values)
    return jnp.concatenate([head.astype(F32), rest.astype(F32)], axis=0).astype(BF16)


def both_pieces(values):
    return jnp.concatenate(split(values), axis=1)


def dot(left, right):
    return lax.dot_general(left, right, (((1,), (0,)), ((), ())), preferred_element_type=F32)


def dot_nt(left, right):
    return lax.dot_general(left, right, (((1,), (1,)), ((), ())), preferred_element_type=F32)


def lane_ids(rows):
    return lax.broadcasted_iota(jnp.int32, (rows, LANES), 1)


def used_slots(count_ref, slots):
    used = count_ref[lax.axis_index("ga")] - lax.axis_index("band") * slots
    return lax.broadcasted_iota(jnp.int32, (slots, 1), 0) < used


def cosine_and_sine(phases, length):
    quarter = jnp.floor(phases * (4.0 / length) + 0.5)
    angle = (phases - quarter * (length / 4.0)) * (2.0 * np.pi / length)
    square = angle * angle
    sine = 1.0 / 362880.0
    for term in (-1.0 / 5040.0, 1.0 / 120.0, -1.0 / 6.0, 1.0):
        sine = sine * square + term
    sine = sine * angle
    cosine = -1.0 / 3628800.0
    for term in (1.0 / 40320.0, -1.0 / 720.0, 1.0 / 24.0, -0.5, 1.0):
        cosine = cosine * square + term
    quarter = quarter - 4.0 * jnp.floor(quarter * 0.25)
    odd = (quarter == 1.0) | (quarter == 3.0)
    first = jnp.where(odd, sine, cosine)
    second = jnp.where(odd, cosine, sine)
    first = jnp.where((quarter == 1.0) | (quarter == 2.0), -first, first)
    return first, jnp.where(quarter >= 2.0, -second, second)


def project_kernel(sizes, count_hbm, orbitals_ref, projectors_hbm, out_ref, *scratch):
    blocks, groups, orbitals, slots, length, projectors, planes, width = sizes
    count_ref, projectors_ref, coef, lines, small_sems, sems = scratch
    kinds = orbitals * 2
    devices = blocks * groups
    share = projectors // devices
    small = [
        pltpu.make_async_copy(count_hbm, count_ref, small_sems.at[0]),
    ]
    copies = []
    for piece in range(2 * slots):
        rows = pl.ds(piece * length, length)
        copies.append(pltpu.make_async_copy(projectors_hbm.at[rows], projectors_ref.at[rows], sems.at[piece]))
    for copy in small + copies:
        copy.start()
    half = width // 2
    lanes = lax.broadcasted_iota(jnp.int32, (length, blocks * half), 1)
    plane = (lanes >> (half.bit_length() - 1)) * planes + (lanes & (half - 1))
    kz = lax.broadcasted_iota(jnp.int32, (length, blocks * half), 0)
    table = split(jnp.concatenate(cosine_and_sine(kz.astype(F32) * plane.astype(F32), length), axis=1))
    coef[...] = jnp.zeros_like(coef)
    small[0].wait()
    used = used_slots(count_ref, slots)
    for n in range(orbitals):
        for part in range(2):
            values = jnp.where(used, orbitals_ref[n, part].astype(F32), 0.0)
            at = (part * orbitals + n) * slots
            lines[at : at + slots, :] = values
            turned = values if part == 1 else -values
            for slot in range(slots):
                row = n * 2 + part
                coef[slot, row : row + 1, :] = values[slot : slot + 1, :]
                row = n * 2 + 1 - part
                coef[slots + slot, row : row + 1, :] = turned[slot : slot + 1, :]
    left = lines[...].astype(BF16)
    both = dot(left, table[0]) + dot(left, table[1])
    rows = orbitals * slots
    points = blocks * half
    real = both[:rows, :points] - both[rows:, points:]
    imag = both[:rows, points:] + both[rows:, :points]
    lanes = lane_ids(rows)
    rows_each = slots // 2
    piece_lanes = lane_ids(rows_each)
    for block in range(blocks):
        at = block * half
        base = at // LANES * LANES
        chunk = pltpu.roll(imag[:, base : base + LANES], (base - at + half) % LANES, 1)
        chunk = jnp.where(lanes < half, pltpu.roll(real[:, base : base + LANES], (base - at) % LANES, 1), chunk)
        aside = pltpu.roll(chunk, width, 1)
        for group in range(groups):
            at = group * slots
            piece = jnp.where(piece_lanes < width, chunk[at : at + rows_each, :], aside[at + rows_each : at + slots, :])
            out_ref[block * groups + group] = piece
    sums = jnp.zeros((coef.shape[1], projectors), F32)
    for piece in range(2 * slots):
        left = coef[piece].astype(BF16)
        copies[piece].wait()
        sums += dot(left, projectors_ref[piece * length : (piece + 1) * length, :])
    for device in range(devices):
        piece = jnp.where(piece_lanes < 2 * width, out_ref[device], 0.0)
        first = device * share
        base = first // LANES * LANES
        for group in range(kinds // rows_each):
            low = 2 * width + group * share
            own = sums[group * rows_each : (group + 1) * rows_each, base : base + LANES]
            own = pltpu.roll(own, (base + low - first) % LANES, 1)
            piece = jnp.where((piece_lanes >= low) & (piece_lanes < low + share), own, piece)
        out_ref[device] = piece


def table_kernel(length, wide, slots, site_ref, x_ref, plus_ref):
    columns = site_ref.shape[1]
    each = slots // 2
    eye = lax.broadcasted_iota(jnp.int32, (LANES, LANES), 0) == lane_ids(LANES)
    row_ids = lax.broadcasted_iota(jnp.int32, (length, LANES), 0).astype(F32)
    lanes = lax.broadcasted_iota(jnp.int32, (LANES, wide), 1)
    inside = lanes < length
    lanes = lanes.astype(F32)
    sites = site_ref[...].astype(F32)
    stored = lax.broadcasted_iota(jnp.int32, (LANES, columns), 1)
    for at in range(0, columns, LANES):
        order = lax.broadcasted_iota(jnp.int32, (LANES, columns), 0) + at
        second = order >= columns // 2
        order = jnp.where(second, order - columns // 2, order)
        wanted = (order >> (each.bit_length() - 1)) * slots + (order & (each - 1)) + jnp.where(second, each, 0)
        along = jnp.sum(jnp.where(stored == wanted, sites, 0.0), axis=1, keepdims=True)
        site = jnp.sum(jnp.where(eye, along, 0.0), axis=0, keepdims=True)
        site_x = jnp.floor((site + 0.5) * (1.0 / length))
        along = along - jnp.floor((along + 0.5) * (1.0 / length)) * length
        cosine, sine = cosine_and_sine(row_ids * site_x, length)
        x_ref[:, at : at + LANES] = cosine
        x_ref[:, columns + at : columns + at + LANES] = sine
        cosine, sine = cosine_and_sine(lanes * along, length)
        cosine = jnp.where(inside, cosine, 0.0)
        sine = jnp.where(inside, sine, 0.0)
        cosine = cosine.astype(BF16)
        sine = sine.astype(BF16)
        for piece in range(2):
            rows = pl.ds(piece * 2 * columns + at, LANES)
            plus_ref[rows, :wide] = cosine
            plus_ref[rows, wide:] = sine
            rows = pl.ds((piece * 2 + 1) * columns + at, LANES)
            plus_ref[rows, :wide] = -sine
            plus_ref[rows, wide:] = cosine


def plane_kernel(sizes, columns_ref, x_ref, plus_ref, potential_ref, out_ref, gathered, lines, back, turning):
    devices, slots, planes, length, wide, width, carried, batch = sizes
    count = devices * slots
    each = slots // 2
    middle = count // 2
    total = jnp.zeros((each, LANES), F32)
    for device in range(devices):
        piece = columns_ref[device]
        gathered[device * each : (device + 1) * each, :] = piece
        total += piece
    for at in range(0, middle, LANES):
        size = min(LANES, middle - at)
        turned = gathered[at : at + LANES, :].T
        for side in range(2):
            lines[:, side * middle + at : side * middle + at + size] = turned[side * width : (side + 1) * width, :size]
    back[...] = jnp.zeros_like(back)
    cosine = x_ref[:, :count]
    sine = x_ref[:, count:]
    padding = jnp.zeros((length, wide - length), F32)
    for i in range(planes // batch):
        left = []
        for plane in range(i * batch, (i + 1) * batch):
            real = lines[plane : plane + 1, :]
            imag = lines[plane + width // 2 : plane + width // 2 + 1, :]
            left.append(jnp.concatenate([cosine * real - sine * imag, cosine * imag + sine * real], axis=1))
        left = both_pieces(jnp.concatenate(left, axis=0))
        field = dot(left, plus_ref[...])
        weights = []
        for plane in range(i * batch, (i + 1) * batch):
            own = jnp.concatenate([potential_ref[plane], padding], axis=1)
            weights.append(jnp.concatenate([own, own], axis=1))
        left = (field * jnp.concatenate(weights, axis=0)).astype(BF16)
        half = dot_nt(left, plus_ref[: 2 * count, :])
        for j in range(batch):
            plane = i * batch + j
            real = half[j * length : (j + 1) * length, :count]
            imag = half[j * length : (j + 1) * length, count:]
            back[plane : plane + 1, :] = jnp.sum(cosine * real + sine * imag, axis=0, keepdims=True)
            at = plane + width // 2
            back[at : at + 1, :] = jnp.sum(cosine * imag - sine * real, axis=0, keepdims=True)
    for at in range(0, middle, LANES):
        size = min(LANES, middle - at)
        for side in range(2):
            turning[side * width : (side + 1) * width, :size] = back[:, side * middle + at : side * middle + at + size]
        gathered[at : at + LANES, :] = turning[...].T
    lanes = lane_ids(each)
    for device in range(devices):
        piece = gathered[device * each : (device + 1) * each, :]
        out_ref[device] = jnp.where((lanes >= 2 * width) & (lanes < carried), total, piece)


def finish_kernel(
    sizes, count_ref, columns_ref, atom_ref, couplings_ref, projectors_ref, table_ref, out_ref, summed, lined, mixed
):
    blocks, groups, orbitals, slots, length, projectors, width, normalizer = sizes
    kinds = orbitals * 2
    devices = blocks * groups
    share = projectors // devices
    each = slots // 2
    lanes = lane_ids(each)
    for chunk in range(projectors // LANES):
        in_chunk = range(chunk * LANES // share, (chunk + 1) * LANES // share)
        for rows in range(kinds // each):
            low = 2 * width + rows * share
            total = jnp.zeros((each, LANES), F32)
            for device in in_chunk:
                own = columns_ref[device]
                own = pltpu.roll(jnp.where((lanes >= low) & (lanes < low + share), own, 0.0), (device * share - low) % LANES, 1)
                total += own
            summed[rows * each : (rows + 1) * each, chunk * LANES : (chunk + 1) * LANES] = total
    for n in range(orbitals):
        at = kinds + n * 2
        summed[at : at + 1, :] = -summed[n * 2 + 1 : n * 2 + 2, :]
        summed[at + 1 : at + 2, :] = summed[n * 2 : n * 2 + 1, :]
    both = stacked(summed[...])
    atoms = atom_ref[...].astype(F32)
    eye = lax.broadcasted_iota(jnp.int32, (LANES, LANES), 0) == lane_ids(LANES)
    along = []
    for at in range(0, projectors, LANES):
        along.append(jnp.sum(jnp.where(eye, atoms[:, at : at + LANES], 0.0), axis=1, keepdims=True))
    head, rest = split(jnp.where(jnp.concatenate(along, axis=0) == atoms, couplings_ref[...], 0.0))
    head = dot_nt(both, head)
    rest = dot_nt(both, rest)
    weighted = (head[: 2 * kinds] + (head[2 * kinds :] + rest[: 2 * kinds])).astype(BF16)
    for slot in range(slots):
        rows = projectors_ref[slot * length : (slot + 1) * length, :]
        value = dot_nt(weighted, rows)[:kinds]
        rows = projectors_ref[(slots + slot) * length : (slots + slot + 1) * length, :]
        value = value + dot_nt(weighted, rows)[kinds:]
        for row in range(kinds):
            mixed[row, slot : slot + 1, :] = value[row : row + 1, :]
    for chunk in range(blocks * width // LANES):
        for group in range(groups):
            for side in range(2):
                low = side * width
                total = jnp.zeros((each, LANES), F32)
                for inner in range(LANES // width):
                    block = chunk * (LANES // width) + inner
                    own = columns_ref[block * groups + group]
                    own = jnp.where((lanes >= low) & (lanes < low + width), own, 0.0)
                    total += pltpu.roll(own, (inner * width - low) % LANES, 1)
                at = group * slots + side * each
                lined[at : at + each, chunk * LANES : (chunk + 1) * LANES] = total
    both = stacked(lined[...])
    rows_of_lines = groups * slots
    held = lax.broadcasted_iota(jnp.int32, (1, blocks), 1) == lax.axis_index("ga")
    used = jnp.sum(jnp.where(held, count_ref[...], 0).astype(F32), axis=1, keepdims=True)
    slot_ids = lax.broadcasted_iota(jnp.int32, (slots, 1), 0) + lax.axis_index("band") * slots
    used = slot_ids.astype(F32) < used
    for part in range(2):
        head = dot_nt(both, table_ref[0, part])
        rest = dot_nt(both, table_ref[1, part])
        local = (head[:rows_of_lines] + (head[rows_of_lines:] + rest[:rows_of_lines])) * normalizer
        for n in range(orbitals):
            value = local[n * slots : (n + 1) * slots, :] + mixed[n * 2 + part]
            out_ref[n, part] = jnp.where(used, value, 0.0)


def on_device(orbitals, projectors, potential, couplings, atom_index, column_site, column_count):
    blocks = lax.axis_size("ga")
    groups = lax.axis_size("band")
    devices = blocks * groups
    orbital_count, _, slots, length = orbitals.shape
    planes = potential.shape[0]
    projector_count = projectors.shape[0]
    columns = column_site.shape[0]
    kinds = orbital_count * 2
    assert orbital_count == groups and slots % 2 == 0 and kinds % (slots // 2) == 0 and columns % LANES == 0
    share = projector_count // devices
    width = 2
    while width < 2 * planes:
        width *= 2
    carried = 2 * width + kinds // (slots // 2) * share
    assert carried <= LANES and width <= LANES and share * devices == projector_count
    wide = -(-length // LANES) * LANES
    flat = jnp.transpose(projectors, (1, 2, 3, 0)).reshape(2 * slots * length, projector_count)
    z_table = line_table(length, blocks, planes, width)
    batch = next(i for i in (3, 2, 1) if planes % i == 0) if columns <= 512 else 1
    vmem = pl.BlockSpec(memory_space=pltpu.VMEM)
    hbm = pl.BlockSpec(memory_space=pltpu.HBM)
    params = pltpu.CompilerParams(vmem_limit_bytes=56 * 1024 * 1024)
    small = pltpu.CompilerParams(vmem_limit_bytes=40 * 1024 * 1024)
    payload = jax.ShapeDtypeStruct((devices, slots // 2, LANES), F32)

    sent = pl.pallas_call(
        functools.partial(
            project_kernel,
                (blocks, groups, orbital_count, slots, length, projector_count, planes, width),
        ),
        out_shape=payload,
        in_specs=[hbm, vmem, hbm],
        out_specs=vmem,
        scratch_shapes=[
            pltpu.SMEM(column_count.shape, jnp.int32),
            pltpu.VMEM(flat.shape, BF16),
            pltpu.VMEM((2 * slots, -(-kinds // 8) * 8, length), F32),
            pltpu.VMEM((kinds * slots, length), F32),
            pltpu.SemaphoreType.DMA((1,)),
            pltpu.SemaphoreType.DMA((2 * slots,)),
        ],
        compiler_params=params,
        cost_estimate=pl.CostEstimate(
            flops=2 * flat.size * LANES * slots,
            bytes_accessed=2 * (flat.size + z_table.size + orbitals.size) + 4 * payload.size,
            transcendentals=length * blocks * width,
        ),
        name="project",
    )(column_count, orbitals, flat)
    arrived = lax.all_to_all(sent, ("ga", "band"), split_axis=0, concat_axis=0, tiled=True)

    x_rows, plus = pl.pallas_call(
        functools.partial(table_kernel, length, wide, slots),
        out_shape=(
            jax.ShapeDtypeStruct((length, 2 * columns), F32),
            jax.ShapeDtypeStruct((4 * columns, 2 * wide), BF16),
        ),
        in_specs=[vmem],
        out_specs=(vmem,) * 2,
        compiler_params=small,
        cost_estimate=pl.CostEstimate(
            flops=4096 * potential.size,
            bytes_accessed=8 * (length + 2 * wide) * columns,
            transcendentals=2 * (length + wide) * columns,
        ),
        name="tables",
    )(column_site.reshape(1, columns))

    sent = pl.pallas_call(
        functools.partial(plane_kernel, (devices, slots, planes, length, wide, width, carried, batch)),
        out_shape=payload,
        in_specs=[vmem] * 4,
        out_specs=vmem,
        scratch_shapes=[
            pltpu.VMEM((-(-columns // (2 * LANES)) * LANES, LANES), F32),
            pltpu.VMEM((width, columns), F32),
            pltpu.VMEM((width, columns), F32),
            pltpu.VMEM((LANES, LANES), F32),
        ],
        compiler_params=small,
        cost_estimate=pl.CostEstimate(
            flops=12 * planes * length * wide * 2 * columns,
            bytes_accessed=4 * (potential.size + 2 * payload.size),
            transcendentals=0,
        ),
        name="planes",
    )(arrived, x_rows, plus, potential)
    arrived = lax.all_to_all(sent, ("ga", "band"), split_axis=0, concat_axis=0, tiled=True)

    normalizer = 1.0 / float(length**3)
    return pl.pallas_call(
        functools.partial(
            finish_kernel,
            (blocks, groups, orbital_count, slots, length, projector_count, width, normalizer),
        ),
        out_shape=jax.ShapeDtypeStruct(orbitals.shape, F32),
        in_specs=[vmem] * 6,
        out_specs=vmem,
        scratch_shapes=[
            pltpu.VMEM((2 * kinds, projector_count), F32),
            pltpu.VMEM((groups * slots, blocks * width), F32),
            pltpu.VMEM((kinds, slots, length), F32),
        ],
        compiler_params=small,
        cost_estimate=pl.CostEstimate(
            flops=4 * kinds * (4 * couplings.size + flat.size) + 4 * z_table.size * orbital_count * slots,
            bytes_accessed=4 * couplings.size + 2 * (flat.size + z_table.size) + 4 * orbitals.size,
            transcendentals=0,
        ),
        name="finish",
    )(column_count.reshape(1, blocks), arrived, atom_index.reshape(1, projector_count), couplings, flat, z_table)


def solution(mesh):
    return jax.shard_map(
        on_device,
        mesh=mesh,
        in_specs=(
            P(None, None, ("ga", "band"), None),
            P(None, None, ("ga", "band"), None),
            P("ga", None, None),
            P(),
            P(),
            P(),
            P(),
        ),
        out_specs=P(None, None, ("ga", "band"), None),
        check_vma=False,
    )
```
